32 devices in a mesh: groups: 2 (over y), blk: 8 (over z, x), narrow: 2 (over core).
Axes of the slice: x: 2, y: 2, z: 4, core: 2. Of those that a mesh axis runs over, the one named last changes fastest.
Arguments:
- embeddings: bfloat16 [12288, 768], P(('groups', 'blk', 'narrow')), parts along dimension 0, may hold values from -0.16237976 to 0.16237976
- pair_mask: int32 [16, 2], P('groups'), parts along dimension 0, may hold values 0 or 1
- shift_index: int32 [2], P('groups'), parts along dimension 0, may hold values from 0 to 63
- start_seed: int32 [12288, 64], P(('groups', 'blk', 'narrow')), parts along dimension 0, may hold values from -1499 to 1499
Outputs:
- embedding_out: float32 [12288, 64], P(('groups', 'blk', 'narrow')), parts along dimension 0
The draws below stay inside these ranges and needn't reach their ends.
There are 2 independent parts, one for each index of `groups`. The reference program is written for one: setup_inputs(seed, part) draws one part's arguments, and reference() takes and returns one part's arrays. A program takes and returns all parts, laid end to end along the dimension named above; each array names one. Nothing has to cross between parts.
All inputs are finite; a program needn't handle non-finite values.
Results may differ from the reference program's by a relative error of at most 0.0003.
Values may be sent and summed in bfloat16 or wider, within the bound.
No kernel may reach another device: no remote copies, remote signals or barrier semaphores. Data moves between devices by JAX's collectives and lax.ppermute only.
A program may use at most 64 MiB of HBM per device.

```python
import math
import jax
import jax.numpy as jnp
from jax import lax

D = 768
NVEC = 64
ITERS = 2
QSTEPS = 6
NBLOCKS = 8
BLOCK = 768
ROWS = 6144


def draw_embeddings(key, part):
    key = jax.random.fold_in(key, 11)
    mode_key, freq_key, phase_key, noise_key = jax.random.split(key, 4)
    centre_amp = 0.5
    noise = jnp.clip(jax.random.normal(noise_key, (ROWS, D), jnp.float32), -3.0, 3.0) * 0.7
    freqs = jax.random.uniform(freq_key, (4,), jnp.float32, 0.15, 0.4)
    phases = jax.random.uniform(phase_key, (4,), jnp.float32, -math.pi, math.pi)
    directions = jnp.clip(jax.random.normal(mode_key, (4, D), jnp.float32), -3.0, 3.0) * centre_amp
    position = jnp.arange(ROWS, dtype=jnp.float32) / BLOCK
    centre = jnp.zeros((ROWS, D), jnp.float32)
    for mode in range(4):
        wave = jnp.cos(position * freqs[mode] + phases[mode])
        centre = centre + wave[:, None] * directions[mode][None, :]
    bound = 4.5
    values = jnp.clip(centre + noise, -bound, bound) * D ** (-0.5)
    return values.astype(jnp.bfloat16)


def draw_start_seed(key, part):
    key = jax.random.fold_in(key, 23)
    row_index = jnp.arange(ROWS, dtype=jnp.int32)[:, None]
    bound = 500 + 1000 * row_index // ROWS
    seeds = jax.random.randint(key, (ROWS, NVEC), -bound, bound + 1, dtype=jnp.int32)
    seeds = seeds.at[ROWS - 1, 0].set(1499)
    seeds = seeds.at[ROWS - 1, 1].set(-1499)
    return seeds


def touch_ends(array, rng, least, largest):
    place = [jax.random.randint(jax.random.fold_in(rng, axis), (), 0, length) for axis, length in enumerate(array.shape)]
    longest = array.shape.index(max(array.shape))
    neighbour = place[:longest] + [(place[longest] + 1) % array.shape[longest]] + place[longest + 1:]
    return array.at[tuple(place)].set(least).at[tuple(neighbour)].set(largest)


def setup_inputs(seed: int = 0, part: int = 0) -> dict:
    arg_keys = jax.random.split(jax.random.key(seed), 5)
    part_keys = jax.random.split(jax.random.fold_in(arg_keys[4], part), 5)
    return {
        "embeddings": draw_embeddings(jax.random.fold_in(jax.random.fold_in(arg_keys[4], part), 71), part),
        "pair_mask": touch_ends((jax.random.randint(part_keys[1], (NBLOCKS, 2), 0, 4) < 3).astype(jnp.int32), jax.random.fold_in(part_keys[1], 1), 0, 1),
        "shift_index": jax.random.randint(part_keys[2], (1,), 0, NVEC).astype(jnp.int32),
        "start_seed": draw_start_seed(jax.random.fold_in(jax.random.fold_in(arg_keys[4], part), 71), part),
    }


kernel_gamma = 2.0
ridge_weight = 1e-05
highest = lax.Precision.HIGHEST

def row_squares(values):
    return jnp.einsum('rc,rc->r', values.astype(jnp.float32), values.astype(jnp.float32), preferred_element_type=jnp.float32)

def inner(left, right):
    return jnp.einsum('ra,rb->ab', left, right, precision=highest)

def times(left, right):
    return jnp.dot(left, right, precision=highest)

def lower_solve(factor, rhs):
    return lax.linalg.triangular_solve(factor, rhs, left_side=True, lower=True)

def upper_solve(factor, rhs):
    return lax.linalg.triangular_solve(factor, rhs, left_side=True, lower=True, transpose_a=True)

def ritz_step(gram, image_gram, shift_value, width):
    total = gram.shape[0]
    identity = jnp.eye(total, dtype=jnp.float32)
    ridged = gram + ridge_weight * jnp.mean(jnp.diagonal(gram)) * identity
    factor = jnp.linalg.cholesky(ridged)
    halfway = lower_solve(factor, image_gram)
    projected = lower_solve(factor, halfway.T).T
    shifted = projected + (3.0 - shift_value) * identity
    coeffs = jnp.eye(total, width, dtype=jnp.float32)
    for repeat in range(QSTEPS):
        coeffs = times(shifted, coeffs)
        norm_factor = jnp.linalg.cholesky(inner(coeffs, coeffs))
        coeffs = lower_solve(norm_factor, coeffs.T).T
    mixing = upper_solve(factor, coeffs)
    return (mixing, coeffs, projected)

def band_product(embeddings, squares, pair_mask, vectors):
    width = vectors.shape[1]
    emb_blocks = embeddings.reshape(NBLOCKS, BLOCK, D)
    sq_blocks = squares.reshape(NBLOCKS, BLOCK)
    vec_blocks = vectors.reshape(NBLOCKS, BLOCK, width)

    def one_block(where):
        row_emb = emb_blocks[where].astype(jnp.float32)
        row_sq = sq_blocks[where]
        total = jnp.zeros((BLOCK, width), jnp.float32)
        for offset in (-2, -1, 0, 1, 2):
            other = (where + offset + NBLOCKS) % NBLOCKS
            if offset == 0:
                weight = jnp.float32(1.0)
            elif offset == 1:
                weight = pair_mask[where, 0].astype(jnp.float32)
            elif offset == 2:
                weight = pair_mask[where, 1].astype(jnp.float32)
            elif offset == -1:
                weight = pair_mask[other, 0].astype(jnp.float32)
            else:
                weight = pair_mask[other, 1].astype(jnp.float32)
            col_emb = emb_blocks[other].astype(jnp.float32)
            inner_prod = jnp.einsum('rc,kc->rk', row_emb, col_emb, precision=highest)
            tile = jnp.exp(-kernel_gamma * (row_sq[:, None] + sq_blocks[other][None, :] - 2.0 * inner_prod))
            total = total + weight * times(tile, vec_blocks[other])
        return total
    result = lax.map(one_block, jnp.arange(NBLOCKS, dtype=jnp.int32))
    return result.reshape(ROWS, width)

def reference(embeddings, pair_mask, shift_index, start_seed):
    squares = row_squares(embeddings)
    degree = band_product(embeddings, squares, pair_mask, jnp.ones((ROWS, 1), jnp.float32))[:, 0]
    scale = lax.rsqrt(degree)[:, None]

    def operate(vectors):
        return scale * band_product(embeddings, squares, pair_mask, scale * vectors)
    start = start_seed.astype(jnp.float32) / 1000.0
    current = lower_solve(jnp.linalg.cholesky(inner(start, start)), start.T).T
    image = operate(current)
    width = current.shape[1]
    previous = current
    previous_image = image
    index_value = shift_index[0]
    for iteration in range(ITERS):
        ritz_block = inner(current, image)
        shift_value = ritz_block[index_value, index_value]
        residual = image - times(current, ritz_block)
        residual_image = operate(residual)
        if iteration == 0:
            basis = jnp.concatenate([current, residual], axis=1)
            basis_image = jnp.concatenate([image, residual_image], axis=1)
        else:
            basis = jnp.concatenate([current, residual, previous], axis=1)
            basis_image = jnp.concatenate([image, residual_image, previous_image], axis=1)
        gram = inner(basis, basis)
        image_gram = inner(basis, basis_image)
        mixing, coeffs, projected = ritz_step(gram, image_gram, shift_value, width)
        current = times(basis, mixing)
        image = times(basis_image, mixing)
        previous = times(basis[:, width:], mixing[width:])
        previous_image = times(basis_image[:, width:], mixing[width:])
    return current * math.sqrt(ROWS)
```

```python
import math

import jax
import jax.numpy as jnp
from jax import lax
from jax.experimental import pallas as pl
from jax.experimental.pallas import tpu as pltpu
from jax.sharding import PartitionSpec as P

KERNEL_GAMMA = 2.0
RIDGE_WEIGHT = 1e-05
NVEC = 64
F32 = jnp.float32
BF16 = jnp.bfloat16
VMEM_LIMIT = 48 * 1024 * 1024


def dot(left, right, left_dim=1, right_dim=0):
    precision = lax.Precision.HIGHEST if left.dtype == F32 else None
    return lax.dot_general(
        left, right, (((left_dim,), (right_dim,)), ((), ())),
        precision=precision, preferred_element_type=F32,
    )


def halves(values):
    high = values.astype(BF16)
    return high, (values - high.astype(F32)).astype(BF16)


def call(body, out_shapes, args, smem=(), flops=0, nbytes=0):
    specs = [
        pl.BlockSpec(memory_space=pltpu.SMEM if i in smem else pltpu.VMEM)
        for i in range(len(args))
    ]
    out = pl.pallas_call(
        body,
        out_shape=[jax.ShapeDtypeStruct(shape, dtype) for shape, dtype in out_shapes],
        in_specs=specs,
        out_specs=[pl.BlockSpec(memory_space=pltpu.VMEM) for _ in out_shapes],
        compiler_params=pltpu.CompilerParams(vmem_limit_bytes=VMEM_LIMIT),
        cost_estimate=pl.CostEstimate(flops=flops, bytes_accessed=nbytes, transcendentals=0),
    )(*args)
    return out


def tile_body(keep, own, other, col, high, low, row_sum, col_sum):
    weight = keep[0].astype(F32)
    size = own.shape[0]
    ones = jnp.ones((8, own.shape[1]), BF16)
    ones_rows = jnp.ones((8, size), BF16)
    col_emb = col[...]
    col32 = col_emb.astype(F32)
    sq_high, sq_low = halves(col32 * col32)
    col_sq = (dot(ones, sq_high, 1, 1) + dot(ones, sq_low, 1, 1))[0:1, :]
    total = jnp.zeros((8, size), F32)
    for half, rows in enumerate((own, other)):
        row_emb = rows[...]
        row32 = row_emb.astype(F32)
        row_sq = jnp.sum(row32 * row32, axis=1, keepdims=True)
        inner = dot(row_emb, col_emb, 1, 1)
        tile = jnp.exp(-KERNEL_GAMMA * (row_sq + col_sq - 2.0 * inner)) * weight
        tile_high, tile_low = halves(tile)
        high[half * size:(half + 1) * size, :] = tile_high
        low[half * size:(half + 1) * size, :] = tile_low
        row_sum[half * 8:(half + 1) * 8, :] = dot(ones_rows, tile_high, 1, 1) + dot(ones_rows, tile_low, 1, 1)
        total = total + dot(ones_rows, tile_high) + dot(ones_rows, tile_low)
    col_sum[...] = total


def make_tile(keep, own, other, col):
    rows, depth = own.shape
    return call(
        tile_body,
        [((2 * rows, rows), BF16), ((2 * rows, rows), BF16), ((16, rows), F32), ((8, rows), F32)],
        [keep, own, other, col], smem=(0,),
        flops=4 * rows * rows * depth, nbytes=6 * rows * depth + 8 * rows * rows,
    )


def swapped(values):
    middle = values.shape[0] // 2
    return jnp.concatenate([values[middle:], values[:middle]], axis=0)


def per_row(values, width):
    return jnp.concatenate([
        jnp.broadcast_to(values[0:1, :], (width, values.shape[1])),
        jnp.broadcast_to(values[8:9, :], (width, values.shape[1])),
    ], axis=0)


def send_ahead(vectors, tiles, outs):
    width = vectors.shape[0] // 2
    whole = jnp.concatenate([vectors[:width], vectors[width:]], axis=1)
    high, low = halves(whole)
    both = jnp.concatenate([high, low], axis=0)
    for (tile_high, tile_low), out in zip(tiles, outs):
        product = dot(both, tile_high[...])
        out[...] = product[:width] + product[width:] + dot(high, tile_low[...])


def first_body(sum0, sum1, sum2, other_sum, q0, q1, q2, q3, seed, other_seed, h1, l1, h2, l2,
               degree_out, vectors_out, ahead1, ahead2):
    width = seed.shape[0]
    own_sum = sum0[...] + sum1[...] + sum2[...]
    degree = own_sum + swapped(other_sum[...])
    behind = jnp.concatenate([q0[...] + q1[...], q2[...] + q3[...]], axis=0)
    degree = degree + behind
    degree_out[...] = degree
    scale = lax.rsqrt(degree)
    vectors = jnp.concatenate([seed[...], other_seed[...]], axis=0) * per_row(scale, width)
    vectors_out[...] = vectors
    send_ahead(vectors, ((h1, l1), (h2, l2)), (ahead1, ahead2))


def next_body(total, other_total, degree, h1, l1, h2, l2, vectors_out, ahead1, ahead2):
    width = total.shape[0] // 2
    vectors = (total[...] + swapped(other_total[...])) / per_row(degree[...], width)
    vectors_out[...] = vectors
    send_ahead(vectors, ((h1, l1), (h2, l2)), (ahead1, ahead2))


def product_rows(vectors, tile_high, tile_low):
    width = vectors.shape[0]
    high, low = halves(vectors)
    both = jnp.concatenate([high, low], axis=0)
    product = dot(both, tile_high[...], 1, 1)
    return product[:width] + product[width:] + dot(high, tile_low[...], 1, 1)


def block_body(vectors, near1, near2, q1, q2, h0, l0, h1, l1, h2, l2, total):
    width, size = near1.shape
    product = product_rows(vectors[:width, :], h0, l0)
    product = product + product_rows(near1[...], h1, l1)
    product = product + product_rows(near2[...], h2, l2)
    total[:width, :] = product[:, :size] + q1[...] + q2[...]
    total[width:, :] = product[:, size:]


def moment_body(degree, v0, v1, v2, near1, near2, h0, l0, h1, l1, h2, l2, moments, scaled):
    width, size = near1.shape
    root = jnp.sqrt(degree[0:1, :])
    x0, x1, x2 = v0[:width, :] * root, v1[:width, :] * root, v2[:width, :] * root
    scaled[...] = jnp.concatenate([x0, x1, x2], axis=0)
    low_order = dot(jnp.concatenate([x0, x1], axis=0), jnp.concatenate([x0, x1], axis=0), 1, 1)
    high_order = dot(jnp.concatenate([x1, x2], axis=0), x2, 1, 1)
    last = product_rows(near1[...], h1, l1) + product_rows(near2[...], h2, l2)
    last = 2.0 * last + product_rows(v2[:width, :], h0, l0)
    whole = jnp.concatenate([v2[:width, :], v2[width:, :]], axis=1)
    last = dot(whole, last, 1, 1)
    moments[0:width, :] = low_order[:width, :]
    moments[width:2 * width, :] = jnp.concatenate([low_order[width:, width:], high_order[:width]], axis=1)
    moments[2 * width:, :] = jnp.concatenate([high_order[width:], last], axis=1)


def unit(rows, cols):
    return (lax.broadcasted_iota(jnp.int32, (rows, cols), 0)
            == lax.broadcasted_iota(jnp.int32, (rows, cols), 1)).astype(F32)


def inverse_factor(matrix):
    size = matrix.shape[0]
    work = jnp.concatenate([matrix, unit(size, size)], axis=1)
    blocks = [work[8 * i:8 * i + 8, :] for i in range(size // 8)]
    place = lax.broadcasted_iota(jnp.int32, (8, 2 * size), 0)
    shape = (8, 2 * size)
    for k in range(0, size, 2):
        top, r = divmod(k, 8)
        pivot = blocks[top]
        row0 = jnp.broadcast_to(pivot[r:r + 1, :], shape)
        row1 = jnp.broadcast_to(pivot[r + 1:r + 2, :], shape)
        a = jnp.broadcast_to(row0[:, k:k + 1], shape)
        b = jnp.broadcast_to(row0[:, k + 1:k + 2], shape)
        d = jnp.broadcast_to(row1[:, k + 1:k + 2], shape)
        inv_a = 1.0 / a
        inv_d = a / (a * d - b * b)
        ratio = b * inv_a
        row1 = row1 - ratio * row0
        for i in range(top, size // 8):
            c0 = jnp.broadcast_to(blocks[i][:, k:k + 1], shape)
            c1 = jnp.broadcast_to(blocks[i][:, k + 1:k + 2], shape)
            f0 = c0 * inv_a
            f1 = (c1 - c0 * ratio) * inv_d
            if i == top:
                f0 = jnp.where(place > r, f0, 0.0)
                f1 = jnp.where(place > r + 1, f1, 0.0)
            blocks[i] = blocks[i] - f0 * row0 - f1 * row1
    work = jnp.concatenate(blocks, axis=0)
    diagonal = jnp.sum(work[:, :size] * unit(size, size), axis=1, keepdims=True)
    return work[:, size:] * lax.rsqrt(diagonal)


def trace(matrix):
    return jnp.sum(matrix * unit(*matrix.shape))


def dense(moments, index, rows):
    n = NVEC
    eye = unit(n, n)
    pick = ((lax.broadcasted_iota(jnp.int32, (n, n), 0) == index)
            & (lax.broadcasted_iota(jnp.int32, (n, n), 1) == index)).astype(F32)

    def even(matrix):
        return 0.5 * (matrix + matrix.T)

    base_t = inverse_factor(moments[0])
    base = base_t.T
    wide = dot(base_t, jnp.concatenate(moments[1:], axis=1))
    tall = dot(jnp.concatenate([wide[:, i * n:(i + 1) * n] for i in range(5)], axis=0), base)
    m = [eye] + [even(tall[i * n:(i + 1) * n]) for i in range(5)]

    square = dot(m[1], m[1])
    cross = dot(m[1], jnp.concatenate([m[2], square], axis=1))
    gram_r = m[2] - square
    image_r = m[3] - cross[:, :n] - cross[:, :n].T + cross[:, n:]
    shift = 3.0 - jnp.sum(m[1] * pick)
    ridge = RIDGE_WEIGHT * (n + trace(gram_r)) / (2 * n)
    ridged = gram_r + ridge * eye
    factor_t = inverse_factor(ridged)
    inverse = dot(factor_t, factor_t, 0, 0)
    keep = 1.0 / (1.0 + ridge)
    step = jnp.concatenate([
        jnp.concatenate([m[1] * keep + shift * eye, gram_r * keep], axis=1),
        jnp.concatenate([eye - ridge * inverse, dot(inverse, image_r) + shift * eye], axis=1),
    ], axis=0)
    cube = dot(dot(step, step), step)
    power = dot(cube, cube[:, :n])
    top, bottom = power[:n], power[n:]
    norm = (1.0 + ridge) * dot(top, top, 0, 0) + dot(bottom, dot(ridged, bottom), 0, 0)
    norm_t = inverse_factor(even(norm))
    mixed = dot(power, norm_t, 1, 1)
    top, bottom = mixed[:n], mixed[n:]

    back = dot(m[1], bottom)
    zero = jnp.zeros((n, n), F32)
    current = jnp.concatenate([top - back, bottom, zero], axis=0)
    image = jnp.concatenate([zero, top - back, bottom], axis=0)
    previous = jnp.concatenate([-back, bottom, zero], axis=0)
    hankel = [jnp.concatenate(m[i:i + 3], axis=1) for i in range(4)]
    plain = jnp.concatenate(hankel[:3], axis=0)
    raised = jnp.concatenate(hankel[1:], axis=0)
    ritz = even(dot(dot(current, plain, 0, 0), image))
    shift = 3.0 - jnp.sum(ritz * pick)
    residual = image - dot(current, ritz)
    basis = jnp.concatenate([current, previous, residual], axis=1)
    gram = dot(dot(basis, plain, 0, 0), basis)
    image_gram = dot(dot(basis, raised, 0, 0), basis)
    ridge = RIDGE_WEIGHT * trace(gram) / (3 * n)
    ridged = gram + ridge * unit(3 * n, 3 * n)
    g = [[ridged[i * n:(i + 1) * n, j * n:(j + 1) * n] for j in range(3)] for i in range(3)]
    v0 = inverse_factor(even(g[0][0]))
    l1020 = dot(jnp.concatenate([g[1][0], g[2][0]], axis=0), v0, 1, 1)
    outer = dot(l1020, l1020, 1, 1)
    v1 = inverse_factor(even(g[1][1] - outer[:n, :n]))
    l21 = dot(g[2][1] - outer[n:, :n], v1, 1, 1)
    v2 = inverse_factor(even(g[2][2] - outer[n:, n:] - dot(l21, l21, 1, 1)))
    l10, l20 = l1020[:n], l1020[n:]
    h0 = dot(v0, image_gram[:n])
    h1 = dot(v1, image_gram[n:2 * n] - dot(l10, h0))
    h2 = dot(v2, image_gram[2 * n:] - dot(l20, h0) - dot(l21, h1))
    z2 = dot(v2, h2, 0, 0)
    z1 = dot(v1, h1 - dot(l21, z2, 0, 0), 0, 0)
    z0 = dot(v0, h0 - dot(l10, z1, 0, 0) - dot(l20, z2, 0, 0), 0, 0)
    step = jnp.concatenate([z0, z1, z2], axis=0) + shift * unit(3 * n, 3 * n)
    cube = dot(dot(step, step), step)
    power = dot(cube, cube[:, :n])
    norm_t = inverse_factor(even(dot(power, dot(ridged, power), 0, 0)))
    mixed = dot(basis, dot(power, norm_t, 1, 1)) * math.sqrt(rows)
    return jnp.concatenate([dot(base, mixed[i * n:(i + 1) * n]) for i in range(3)], axis=0)


def dense_body(rows, index, moments, scaled, out):
    n = NVEC
    packed = moments[...]
    parts = [packed[i * n:(i + 1) * n, j * n:(j + 1) * n] for i in range(3) for j in range(2)]
    parts = [0.5 * (part + part.T) for part in parts]
    coeffs = dense(parts, index[0], rows)
    out[...] = dot(scaled[...], coeffs, 0, 0)


def moved(shard, axis, by):
    length = lax.axis_size(axis)
    return lax.ppermute(shard, axis, [(i, (i + by) % length) for i in range(length)])


def moved_both(shard, axis, by):
    blocks, cores = lax.axis_size(axis), lax.axis_size("narrow")
    pairs = []
    for i in range(blocks):
        for j in range(cores):
            pairs.append((i * cores + j, (i + by) % blocks * cores + (j + 1) % cores))
    return lax.ppermute(shard, (axis, "narrow"), pairs)


def total_over_rows(values):
    values = lax.psum(values, "narrow")
    blocks = lax.axis_size("blk")
    span = 1
    while blocks % (2 * span) == 0:
        groups = [[i, i + span] for i in range(blocks) if i // span % 2 == 0]
        values = lax.psum(values, "blk", axis_index_groups=groups)
        span *= 2
    if span < blocks:
        groups = [list(range(i, blocks, span)) for i in range(span)]
        values = lax.psum(values, "blk", axis_index_groups=groups)
    return values


def shards(embeddings, pair_mask, shift_index, start_seed):
    size = embeddings.shape[0]
    blocks = lax.axis_size("blk")
    where = lax.axis_index("blk")
    other_emb = moved(embeddings, "narrow", 1)
    near_emb = [moved(embeddings, "blk", -1), moved(embeddings, "blk", -2)]
    seed = start_seed.astype(F32).T / 1000.0
    other_seed = moved(seed, "narrow", 1)
    keep = lax.dynamic_slice_in_dim(pair_mask, where, 1, 0)[0]
    flags = [jnp.ones((1,), jnp.int32), keep[0:1], keep[1:2]]
    tiles, row_sums, col_sums = [], [], []
    for flag, col in zip(flags, [embeddings] + near_emb):
        high, low, row_sum, col_sum = make_tile(flag, embeddings, other_emb, col)
        tiles += [high, low]
        row_sums.append(row_sum)
        col_sums.append(col_sum)
    other_sum = moved(row_sums[0] + row_sums[1] + row_sums[2], "narrow", 1)
    behind = [moved(col_sums[1], "blk", 1), moved(col_sums[2], "blk", 2),
              moved_both(col_sums[1], "blk", 1), moved_both(col_sums[2], "blk", 2)]
    pair_shape = ((2 * NVEC, size), F32)
    half_shape = ((NVEC, size), F32)
    cost = dict(flops=2 * 3 * 128 * 2 * size * 2 * size, nbytes=16 * size * size)
    degree, vectors, ahead1, ahead2 = call(
        first_body, [((16, size), F32), pair_shape, half_shape, half_shape],
        row_sums + [other_sum] + behind + [seed, other_seed] + tiles[2:], **cost,
    )
    history = [vectors]
    for _ in range(2):
        near1, near2 = moved(vectors[:NVEC], "blk", -1), moved(vectors[:NVEC], "blk", -2)
        q1, q2 = moved(ahead1, "blk", 1), moved(ahead2, "blk", 2)
        (total,) = call(block_body, [pair_shape], [vectors, near1, near2, q1, q2] + tiles, **cost)
        other_total = moved(total, "narrow", 1)
        vectors, ahead1, ahead2 = call(
            next_body, [pair_shape, half_shape, half_shape],
            [total, other_total, degree] + tiles[2:], **cost,
        )
        history.append(vectors)
    near1, near2 = moved(vectors[:NVEC], "blk", -1), moved(vectors[:NVEC], "blk", -2)
    moments, scaled = call(
        moment_body, [((3 * NVEC, 2 * NVEC), F32), ((3 * NVEC, size), F32)],
        [degree] + history + [near1, near2] + tiles, **cost,
    )
    moments = total_over_rows(moments)
    rows = size * blocks * lax.axis_size("narrow")
    (out,) = call(
        lambda *refs: dense_body(rows, *refs), [((size, NVEC), F32)],
        [shift_index, moments, scaled], smem=(0,), flops=10**9, nbytes=10**6,
    )
    return out


def solution(mesh):
    return jax.shard_map(
        shards,
        mesh=mesh,
        in_specs=(
            P(("groups", "blk", "narrow"), None),
            P("groups", None),
            P("groups"),
            P(("groups", "blk", "narrow"), None),
        ),
        out_specs=P(("groups", "blk", "narrow"), None),
        check_vma=False,
    )
```

```python
import math

import jax
import jax.numpy as jnp
from jax import lax
from jax.experimental import pallas as pl
from jax.experimental.pallas import tpu as pltpu
from jax.sharding import PartitionSpec as P

KERNEL_GAMMA = 2.0
RIDGE_WEIGHT = 1e-05
NVEC = 64
F32 = jnp.float32
BF16 = jnp.bfloat16
VMEM_LIMIT = 48 * 1024 * 1024


def dot(left, right, left_dim=1, right_dim=0):
    precision = lax.Precision.HIGHEST if left.dtype == F32 else None
    return lax.dot_general(
        left, right, (((left_dim,), (right_dim,)), ((), ())),
        precision=precision, preferred_element_type=F32,
    )


def halves(values):
    high = values.astype(BF16)
    return high, (values - high.astype(F32)).astype(BF16)


def call(body, out_shapes, args, smem=(), flops=0, nbytes=0):
    specs = [
        pl.BlockSpec(memory_space=pltpu.SMEM if i in smem else pltpu.VMEM)
        for i in range(len(args))
    ]
    out = pl.pallas_call(
        body,
        out_shape=[jax.ShapeDtypeStruct(shape, dtype) for shape, dtype in out_shapes],
        in_specs=specs,
        out_specs=[pl.BlockSpec(memory_space=pltpu.VMEM) for _ in out_shapes],
        compiler_params=pltpu.CompilerParams(vmem_limit_bytes=VMEM_LIMIT),
        cost_estimate=pl.CostEstimate(flops=flops, bytes_accessed=nbytes, transcendentals=0),
    )(*args)
    return out


def row_squares(rows):
    row32 = rows.astype(F32)
    return jnp.sum(row32 * row32, axis=1, keepdims=True)


def fill_tile(weight, row_embs, row_sqs, col_emb, high, low, row_sum, col_sum):
    size, depth = col_emb.shape
    ones = jnp.ones((8, depth), BF16)
    ones_rows = jnp.ones((8, size), BF16)
    col32 = col_emb.astype(F32)
    sq_high, sq_low = halves(col32 * col32)
    col_sq = (dot(ones, sq_high, 1, 1) + dot(ones, sq_low, 1, 1))[0:1, :]
    total = jnp.zeros((8, size), F32)
    for half in range(2):
        inner = dot(row_embs[half], col_emb, 1, 1)
        tile = jnp.exp(-KERNEL_GAMMA * (row_sqs[half] + col_sq - 2.0 * inner)) * weight
        tile_high, tile_low = halves(tile)
        high[half * size:(half + 1) * size, :] = tile_high
        low[half * size:(half + 1) * size, :] = tile_low
        row_sum[half * 8:(half + 1) * 8, :] = dot(ones_rows, tile_high, 1, 1) + dot(ones_rows, tile_low, 1, 1)
        total = total + dot(ones_rows, tile_high) + dot(ones_rows, tile_low)
    col_sum[...] = total


def own_body(own, other, high, low, row_sum, col_sum, row_sq):
    size = own.shape[0]
    embs = [own[...], other[...]]
    sqs = [row_squares(emb) for emb in embs]
    for half in range(2):
        row_sq[half * size:(half + 1) * size, :] = jnp.broadcast_to(sqs[half], (size, 128))
    fill_tile(1.0, embs, sqs, embs[0], high, low, row_sum, col_sum)


def near_body(count, keep, own, other, row_sq, *refs):
    size = own.shape[0]
    sqs = [row_sq[half * size:(half + 1) * size, 0:1] for half in range(2)]
    col = jnp.concatenate([ref[...] for ref in refs[:count]], axis=0)
    fill_tile(keep[0].astype(F32), [own[...], other[...]], sqs, col, *refs[count:])


def relayed_body(count, keep, odd, own, other, row_sq, direct, *refs):
    size = own.shape[0]
    sqs = [row_sq[half * size:(half + 1) * size, 0:1] for half in range(2)]
    relayed = jnp.concatenate([ref[...] for ref in refs[:count]], axis=0)
    col = jnp.where(odd[0] > 0, relayed, direct[...])
    fill_tile(keep[0].astype(F32), [own[...], other[...]], sqs, col, *refs[count:])


def make_tile(body, args, rows, depth, smem=(), extra=()):
    return call(
        body,
        [((2 * rows, rows), BF16), ((2 * rows, rows), BF16), ((16, rows), F32), ((8, rows), F32), *extra],
        args, smem=smem,
        flops=4 * rows * rows * depth, nbytes=6 * rows * depth + 8 * rows * rows,
    )


def swapped(values):
    middle = values.shape[0] // 2
    return jnp.concatenate([values[middle:], values[:middle]], axis=0)


def send_ahead(own, other, tiles, outs):
    width = own.shape[0]
    high, low = halves(jnp.concatenate([own, other], axis=1))
    both = jnp.concatenate([high, low], axis=0)
    for (tile_high, tile_low), out in zip(tiles, outs):
        product = dot(both, tile_high[...])
        out[...] = product[:width] + product[width:] + dot(high, tile_low[...])


def gram_body(values, out):
    out[...] = dot(values[...], values[...], 1, 1)


def start_body(gram, other_gram, seed, other_seed, own_out, other_out):
    gram = gram[...] + other_gram[...]
    factor = inverse_factor(0.5 * (gram + gram.T))
    own_out[...] = dot(factor, seed[...])
    other_out[...] = dot(factor, other_seed[...])


def first_body(sum0, sum1, sum2, other_sum, q0, q1, q2, q3, start, other_start, h1, l1, h2, l2,
               degree_out, own_out, other_out, ahead1, ahead2):
    degree = sum0[...] + sum1[...] + sum2[...] + swapped(other_sum[...])
    degree = degree + jnp.concatenate([q0[...] + q1[...], q2[...] + q3[...]], axis=0)
    degree_out[...] = degree
    scale = lax.rsqrt(degree)
    own = start[...] * scale[0:1, :]
    other = other_start[...] * scale[8:9, :]
    own_out[...] = own
    other_out[...] = other
    send_ahead(own, other, ((h1, l1), (h2, l2)), (ahead1, ahead2))


def combined(total, other_total, degree):
    width = total.shape[0] // 2
    own = (total[:width, :] + other_total[width:, :]) / degree[0:1, :]
    other = (total[width:, :] + other_total[:width, :]) / degree[8:9, :]
    return own, other


def next_body(total, other_total, degree, h1, l1, h2, l2, own_out, other_out, ahead1, ahead2):
    own, other = combined(total, other_total, degree)
    own_out[...] = own
    other_out[...] = other
    send_ahead(own, other, ((h1, l1), (h2, l2)), (ahead1, ahead2))


def last_body(total, other_total, degree, own_out, other_out):
    own_out[...], other_out[...] = combined(total, other_total, degree)


def product_rows(vectors, tile_high, tile_low):
    width = vectors.shape[0]
    high, low = halves(vectors)
    both = jnp.concatenate([high, low], axis=0)
    product = dot(both, tile_high[...], 1, 1)
    return product[:width] + product[width:] + dot(high, tile_low[...], 1, 1)


def block_body(own, near1, near2, q1, q2, h0, l0, h1, l1, h2, l2, total):
    width, size = near1.shape
    product = product_rows(own[...], h0, l0)
    product = product + product_rows(near1[...], h1, l1)
    product = product + product_rows(near2[...], h2, l2)
    total[:width, :] = product[:, :size] + q1[...] + q2[...]
    total[width:, :] = product[:, size:]


def low_body(degree, v0, v1, v2, moments, scaled):
    width = v0.shape[0]
    root = jnp.sqrt(degree[0:1, :])
    x0, x1, x2 = v0[...] * root, v1[...] * root, v2[...] * root
    scaled[...] = jnp.concatenate([x0, x1, x2], axis=0)
    left = jnp.concatenate([x0, x1], axis=0)
    order12 = dot(left, x1, 1, 1)
    order34 = dot(jnp.concatenate([x1, x2], axis=0), x2, 1, 1)
    moments[:width, :] = jnp.concatenate([order12[:width], order12[width:]], axis=1)
    moments[width:, :] = jnp.concatenate([order34[:width], order34[width:]], axis=1)


def moment_body(low, own, other, near1, near2, h0, l0, h1, l1, h2, l2, moments):
    width = own.shape[0]
    last = product_rows(near1[...], h1, l1) + product_rows(near2[...], h2, l2)
    last = 2.0 * last + product_rows(own[...], h0, l0)
    last = dot(jnp.concatenate([own[...], other[...]], axis=1), last, 1, 1)
    moments[:2 * width, :] = low[...]
    moments[2 * width:, :] = jnp.concatenate([last[:width // 2], last[width // 2:]], axis=1)


def unit(rows, cols):
    return (lax.broadcasted_iota(jnp.int32, (rows, cols), 0)
            == lax.broadcasted_iota(jnp.int32, (rows, cols), 1)).astype(F32)


def inverse_factor(matrix):
    size = matrix.shape[0]
    work = jnp.concatenate([matrix, unit(size, size)], axis=1)
    blocks = [work[8 * i:8 * i + 8, :] for i in range(size // 8)]
    place = lax.broadcasted_iota(jnp.int32, (8, 2 * size), 0)
    shape = (8, 2 * size)
    for k in range(0, size, 2):
        top, r = divmod(k, 8)
        pivot = blocks[top]
        row0 = jnp.broadcast_to(pivot[r:r + 1, :], shape)
        row1 = jnp.broadcast_to(pivot[r + 1:r + 2, :], shape)
        a = jnp.broadcast_to(row0[:, k:k + 1], shape)
        b = jnp.broadcast_to(row0[:, k + 1:k + 2], shape)
        d = jnp.broadcast_to(row1[:, k + 1:k + 2], shape)
        inv_a = 1.0 / a
        inv_d = a / (a * d - b * b)
        ratio = b * inv_a
        row1 = row1 - ratio * row0
        for i in range(top, size // 8):
            c0 = jnp.broadcast_to(blocks[i][:, k:k + 1], shape)
            c1 = jnp.broadcast_to(blocks[i][:, k + 1:k + 2], shape)
            f0 = c0 * inv_a
            f1 = (c1 - c0 * ratio) * inv_d
            if i == top:
                f0 = jnp.where(place > r, f0, 0.0)
                f1 = jnp.where(place > r + 1, f1, 0.0)
            blocks[i] = blocks[i] - f0 * row0 - f1 * row1
    work = jnp.concatenate(blocks, axis=0)
    diagonal = jnp.sum(work[:, :size] * unit(size, size), axis=1, keepdims=True)
    return work[:, size:] * lax.rsqrt(diagonal)


def trace(matrix):
    return jnp.sum(matrix * unit(*matrix.shape))


def dense(moments, index, rows):
    n = NVEC
    eye = unit(n, n)
    pick = ((lax.broadcasted_iota(jnp.int32, (n, n), 0) == index)
            & (lax.broadcasted_iota(jnp.int32, (n, n), 1) == index)).astype(F32)

    def even(matrix):
        return 0.5 * (matrix + matrix.T)

    m = [eye] + [even(moment) for moment in moments]

    square = dot(m[1], m[1])
    cross = dot(m[1], jnp.concatenate([m[2], square], axis=1))
    gram_r = m[2] - square
    image_r = m[3] - cross[:, :n] - cross[:, :n].T + cross[:, n:]
    shift = 3.0 - jnp.sum(m[1] * pick)
    ridge = RIDGE_WEIGHT * (n + trace(gram_r)) / (2 * n)
    ridged = gram_r + ridge * eye
    factor_t = inverse_factor(ridged)
    inverse = dot(factor_t, factor_t, 0, 0)
    keep = 1.0 / (1.0 + ridge)
    step = jnp.concatenate([
        jnp.concatenate([m[1] * keep + shift * eye, gram_r * keep], axis=1),
        jnp.concatenate([eye - ridge * inverse, dot(inverse, image_r) + shift * eye], axis=1),
    ], axis=0)
    cube = dot(dot(step, step), step)
    power = dot(cube, cube[:, :n])
    top, bottom = power[:n], power[n:]
    norm = (1.0 + ridge) * dot(top, top, 0, 0) + dot(bottom, dot(ridged, bottom), 0, 0)
    norm_t = inverse_factor(even(norm))
    mixed = dot(power, norm_t, 1, 1)
    top, bottom = mixed[:n], mixed[n:]

    back = dot(m[1], bottom)
    zero = jnp.zeros((n, n), F32)
    current = jnp.concatenate([top - back, bottom, zero], axis=0)
    image = jnp.concatenate([zero, top - back, bottom], axis=0)
    previous = jnp.concatenate([-back, bottom, zero], axis=0)
    hankel = [jnp.concatenate(m[i:i + 3], axis=1) for i in range(4)]
    plain = jnp.concatenate(hankel[:3], axis=0)
    raised = jnp.concatenate(hankel[1:], axis=0)
    ritz = even(dot(dot(current, plain, 0, 0), image))
    shift = 3.0 - jnp.sum(ritz * pick)
    residual = image - dot(current, ritz)
    basis = jnp.concatenate([current, previous, residual], axis=1)
    gram = dot(dot(basis, plain, 0, 0), basis)
    image_gram = dot(dot(basis, raised, 0, 0), basis)
    ridge = RIDGE_WEIGHT * trace(gram) / (3 * n)
    ridged = gram + ridge * unit(3 * n, 3 * n)
    g = [[ridged[i * n:(i + 1) * n, j * n:(j + 1) * n] for j in range(3)] for i in range(3)]
    v0 = inverse_factor(even(g[0][0]))
    l1020 = dot(jnp.concatenate([g[1][0], g[2][0]], axis=0), v0, 1, 1)
    outer = dot(l1020, l1020, 1, 1)
    v1 = inverse_factor(even(g[1][1] - outer[:n, :n]))
    l21 = dot(g[2][1] - outer[n:, :n], v1, 1, 1)
    v2 = inverse_factor(even(g[2][2] - outer[n:, n:] - dot(l21, l21, 1, 1)))
    l10, l20 = l1020[:n], l1020[n:]
    h0 = dot(v0, image_gram[:n])
    h1 = dot(v1, image_gram[n:2 * n] - dot(l10, h0))
    h2 = dot(v2, image_gram[2 * n:] - dot(l20, h0) - dot(l21, h1))
    z2 = dot(v2, h2, 0, 0)
    z1 = dot(v1, h1 - dot(l21, z2, 0, 0), 0, 0)
    z0 = dot(v0, h0 - dot(l10, z1, 0, 0) - dot(l20, z2, 0, 0), 0, 0)
    step = jnp.concatenate([z0, z1, z2], axis=0) + shift * unit(3 * n, 3 * n)
    cube = dot(dot(step, step), step)
    power = dot(cube, cube[:, :n])
    norm_t = inverse_factor(even(dot(power, dot(ridged, power), 0, 0)))
    return dot(basis, dot(power, norm_t, 1, 1)) * math.sqrt(rows)


def dense_body(rows, index, moments, other_moments, scaled, out):
    n = NVEC
    packed = moments[...] + other_moments[...]
    parts = [packed[i * n:(i + 1) * n, j * n:(j + 1) * n] for i in range(2) for j in range(2)]
    parts.append(jnp.concatenate([packed[2 * n:, :n], packed[2 * n:, n:]], axis=0))
    out[...] = dot(dense(parts, index[0], rows), scaled[...], 0, 0)


def moved(shard, axis, by):
    length = lax.axis_size(axis)
    return lax.ppermute(shard, axis, [(i, (i + by) % length) for i in range(length)])


def moved_both(shard, axis, by):
    blocks, cores = lax.axis_size(axis), lax.axis_size("narrow")
    pairs = []
    for i in range(blocks):
        for j in range(cores):
            pairs.append((i * cores + j, (i + by) % blocks * cores + (j + 1) % cores))
    return lax.ppermute(shard, (axis, "narrow"), pairs)


def two_terms(values):
    blocks = lax.axis_size("blk")
    span = 1
    while blocks % (2 * span) == 0:
        other = lax.ppermute(values, "blk", [(i, i ^ span) for i in range(blocks)])
        values = values + other
        span *= 2
    if span < blocks:
        groups = [list(range(i, blocks, span)) for i in range(span)]
        values = lax.psum(values, "blk", axis_index_groups=groups)
    return values, moved(values, "narrow", 1)


def shards(embeddings, pair_mask, shift_index, start_seed):
    size, depth = embeddings.shape
    blocks = lax.axis_size("blk")
    where = lax.axis_index("blk")
    chunk = 128 if size % 128 == 0 else size
    count = size // chunk
    other_emb = moved(embeddings, "narrow", 1)
    near2 = [moved(embeddings[i * chunk:(i + 1) * chunk], "blk", -2) for i in range(count)]
    seed = start_seed.astype(F32).T / 1000.0
    keep = lax.dynamic_slice_in_dim(pair_mask, where, 1, 0)[0]
    if blocks % 2 == 0:
        direct = lax.ppermute(embeddings, "blk", [(i, i - 1) for i in range(1, blocks, 2)])
        relayed = [lax.ppermute(part, "blk", [(i, i + 1) for i in range(0, blocks, 2)]) for part in near2]
    else:
        direct, relayed = moved(embeddings, "blk", -1), near2
    odd = (where % 2 * (blocks % 2 == 0)).astype(jnp.int32).reshape(1)

    other_seed = moved(seed, "narrow", 1)
    (gram,) = call(gram_body, [((NVEC, NVEC), F32)], [seed], flops=10**7, nbytes=10**5)
    start, other_start = call(
        start_body, [((NVEC, size), F32)] * 2, [*two_terms(gram), seed, other_seed], flops=10**9, nbytes=10**6,
    )

    rows_args = [embeddings, other_emb]
    h0, l0, rows0, _, row_sq = make_tile(
        own_body, rows_args, size, depth, extra=(((2 * size, 128), F32),))
    h2, l2, rows2, cols2 = make_tile(
        lambda *refs: near_body(count, *refs), [keep[1:2], *rows_args, row_sq, *near2], size, depth, (0,))
    h1, l1, rows1, cols1 = make_tile(
        lambda *refs: relayed_body(count, *refs),
        [keep[0:1], odd, *rows_args, row_sq, direct, *relayed], size, depth, (0, 1))
    tiles = [h0, l0, h1, l1, h2, l2]
    other_sum = moved(rows0 + rows1 + rows2, "narrow", 1)
    behind = [moved(cols1, "blk", 1), moved(cols2, "blk", 2),
              moved_both(cols1, "blk", 1), moved_both(cols2, "blk", 2)]
    pair_shape = ((2 * NVEC, size), F32)
    half_shape = ((NVEC, size), F32)
    cost = dict(flops=2 * 3 * 128 * 2 * size * 2 * size, nbytes=16 * size * size)
    degree, own, other, ahead1, ahead2 = call(
        first_body, [((16, size), F32)] + [half_shape] * 4,
        [rows0, rows1, rows2, other_sum] + behind + [start, other_start] + tiles[2:], **cost,
    )
    history = [own]
    for repeat in range(2):
        q1, q2 = moved(ahead1, "blk", 1), moved(ahead2, "blk", 2)
        near = [moved(own, "blk", -1), moved(own, "blk", -2)]
        (total,) = call(block_body, [pair_shape], [own, *near, q1, q2] + tiles, **cost)
        other_total = moved(total, "narrow", 1)
        if repeat == 0:
            own, other, ahead1, ahead2 = call(
                next_body, [half_shape] * 4, [total, other_total, degree] + tiles[2:], **cost)
        else:
            own, other = call(last_body, [half_shape] * 2, [total, other_total, degree], flops=10**5, nbytes=10**6)
        history.append(own)
    near = [moved(own, "blk", -1), moved(own, "blk", -2)]
    low, scaled = call(
        low_body, [((2 * NVEC, 2 * NVEC), F32), ((3 * NVEC, size), F32)], [degree] + history,
        flops=10**8, nbytes=10**6)
    (moments,) = call(
        moment_body, [((5 * NVEC // 2, 2 * NVEC), F32)], [low, own, other, *near] + tiles, **cost)
    rows = size * blocks * lax.axis_size("narrow")
    (out,) = call(
        lambda *refs: dense_body(rows, *refs), [half_shape],
        [shift_index, *two_terms(moments), scaled], smem=(0,), flops=10**9, nbytes=10**6,
    )
    return out.T


def solution(mesh):
    return jax.shard_map(
        shards,
        mesh=mesh,
        in_specs=(
            P(("groups", "blk", "narrow"), None),
            P("groups", None),
            P("groups"),
            P(("groups", "blk", "narrow"), None),
        ),
        out_specs=P(("groups", "blk", "narrow"), None),
        check_vma=False,
    )
```

```python
import math

import jax
import jax.numpy as jnp
from jax import lax
from jax.experimental import pallas as pl
from jax.experimental.pallas import tpu as pltpu
from jax.sharding import PartitionSpec as P

KERNEL_GAMMA = 2.0
RIDGE_WEIGHT = 1e-05
NVEC = 64
F32 = jnp.float32
BF16 = jnp.bfloat16
VMEM_LIMIT = 48 * 1024 * 1024


def dot(left, right, left_dim=1, right_dim=0):
    precision = lax.Precision.HIGHEST if left.dtype == F32 else None
    return lax.dot_general(
        left, right, (((left_dim,), (right_dim,)), ((), ())),
        precision=precision, preferred_element_type=F32,
    )


def halves(values):
    high = values.astype(BF16)
    return high, (values - high.astype(F32)).astype(BF16)


def call(body, out_shapes, args, smem=(), flops=0, nbytes=0):
    specs = [
        pl.BlockSpec(memory_space=pltpu.SMEM if i in smem else pltpu.VMEM)
        for i in range(len(args))
    ]
    out = pl.pallas_call(
        body,
        out_shape=[jax.ShapeDtypeStruct(shape, dtype) for shape, dtype in out_shapes],
        in_specs=specs,
        out_specs=[pl.BlockSpec(memory_space=pltpu.VMEM) for _ in out_shapes],
        compiler_params=pltpu.CompilerParams(vmem_limit_bytes=VMEM_LIMIT),
        cost_estimate=pl.CostEstimate(flops=flops, bytes_accessed=nbytes, transcendentals=0),
    )(*args)
    return out


def row_squares(rows):
    row32 = rows.astype(F32)
    return jnp.sum(row32 * row32, axis=1, keepdims=True)


def fill_tile(weight, row_embs, row_sqs, col_emb, high, low, row_sum, col_sum):
    size, depth = col_emb.shape
    ones = jnp.ones((8, depth), BF16)
    ones_rows = jnp.ones((8, size), BF16)
    col32 = col_emb.astype(F32)
    sq_high, sq_low = halves(col32 * col32)
    col_sq = (dot(ones, sq_high, 1, 1) + dot(ones, sq_low, 1, 1))[0:1, :]
    total = jnp.zeros((8, size), F32)
    for half in range(2):
        inner = dot(row_embs[half], col_emb, 1, 1)
        tile = jnp.exp(-KERNEL_GAMMA * (row_sqs[half] + col_sq - 2.0 * inner)) * weight
        tile_high, tile_low = halves(tile)
        high[half * size:(half + 1) * size, :] = tile_high
        low[half * size:(half + 1) * size, :] = tile_low
        row_sum[half * 8:(half + 1) * 8, :] = dot(ones_rows, tile_high, 1, 1) + dot(ones_rows, tile_low, 1, 1)
        total = total + dot(ones_rows, tile_high) + dot(ones_rows, tile_low)
    col_sum[...] = total


def own_body(own, other, high, low, row_sum, col_sum, row_sq):
    size = own.shape[0]
    embs = [own[...], other[...]]
    sqs = [row_squares(emb) for emb in embs]
    for half in range(2):
        row_sq[half * size:(half + 1) * size, :] = jnp.broadcast_to(sqs[half], (size, 128))
    fill_tile(1.0, embs, sqs, embs[0], high, low, row_sum, col_sum)


def near_body(count, keep, own, other, row_sq, *refs):
    size = own.shape[0]
    sqs = [row_sq[half * size:(half + 1) * size, 0:1] for half in range(2)]
    col = jnp.concatenate([ref[...] for ref in refs[:count]], axis=0)
    fill_tile(keep[0].astype(F32), [own[...], other[...]], sqs, col, *refs[count:])


def relayed_body(count, keep, odd, own, other, row_sq, direct, *refs):
    size = own.shape[0]
    sqs = [row_sq[half * size:(half + 1) * size, 0:1] for half in range(2)]
    relayed = jnp.concatenate([ref[...] for ref in refs[:count]], axis=0)
    col = jnp.where(odd[0] > 0, relayed, direct[...])
    fill_tile(keep[0].astype(F32), [own[...], other[...]], sqs, col, *refs[count:])


def make_tile(body, args, rows, depth, smem=(), extra=()):
    return call(
        body,
        [((2 * rows, rows), BF16), ((2 * rows, rows), BF16), ((16, rows), F32), ((8, rows), F32), *extra],
        args, smem=smem,
        flops=4 * rows * rows * depth, nbytes=6 * rows * depth + 8 * rows * rows,
    )


def swapped(values):
    middle = values.shape[0] // 2
    return jnp.concatenate([values[middle:], values[:middle]], axis=0)


def send_ahead(own, other, tiles, outs):
    width = own.shape[0]
    high, low = halves(jnp.concatenate([own, other], axis=1))
    both = jnp.concatenate([high, low], axis=0)
    for (tile_high, tile_low), out in zip(tiles, outs):
        product = dot(both, tile_high[...])
        out[...] = product[:width] + product[width:] + dot(high, tile_low[...])


def first_body(sum0, sum1, sum2, other_sum, q0, q1, q2, q3, start, other_start, h1, l1, h2, l2,
               degree_out, own_out, other_out, ahead1, ahead2):
    degree = sum0[...] + sum1[...] + sum2[...] + swapped(other_sum[...])
    degree = degree + jnp.concatenate([q0[...] + q1[...], q2[...] + q3[...]], axis=0)
    degree_out[...] = degree
    scale = lax.rsqrt(degree)
    own = start[...] * scale[0:1, :]
    other = other_start[...] * scale[8:9, :]
    own_out[...] = own
    other_out[...] = other
    send_ahead(own, other, ((h1, l1), (h2, l2)), (ahead1, ahead2))


def combined(total, other_total, degree):
    width = total.shape[0] // 2
    own = (total[:width, :] + other_total[width:, :]) / degree[0:1, :]
    other = (total[width:, :] + other_total[:width, :]) / degree[8:9, :]
    return own, other


def next_body(total, other_total, degree, h1, l1, h2, l2, own_out, other_out, ahead1, ahead2):
    own, other = combined(total, other_total, degree)
    own_out[...] = own
    other_out[...] = other
    send_ahead(own, other, ((h1, l1), (h2, l2)), (ahead1, ahead2))


def last_body(total, other_total, degree, own_out, other_out):
    own_out[...], other_out[...] = combined(total, other_total, degree)


def product_rows(vectors, tile_high, tile_low):
    width = vectors.shape[0]
    high, low = halves(vectors)
    both = jnp.concatenate([high, low], axis=0)
    product = dot(both, tile_high[...], 1, 1)
    return product[:width] + product[width:] + dot(high, tile_low[...], 1, 1)


def block_body(own, near1, near2, q1, q2, h0, l0, h1, l1, h2, l2, total):
    width, size = near1.shape
    product = product_rows(own[...], h0, l0)
    product = product + product_rows(near1[...], h1, l1)
    product = product + product_rows(near2[...], h2, l2)
    total[:width, :] = product[:, :size] + q1[...] + q2[...]
    total[width:, :] = product[:, size:]


def low_body(degree, v0, v1, v2, moments, scaled):
    width = v0.shape[0]
    root = jnp.sqrt(degree[0:1, :])
    x0, x1, x2 = v0[...] * root, v1[...] * root, v2[...] * root
    scaled[...] = jnp.concatenate([x0, x1, x2], axis=0)
    left = jnp.concatenate([x0, x1], axis=0)
    order012 = dot(left, left, 1, 1)
    order34 = dot(jnp.concatenate([x1, x2], axis=0), x2, 1, 1)
    moments[:width, :] = order012[:width]
    moments[width:2 * width, :] = jnp.concatenate([order012[width:, width:], order34[:width]], axis=1)
    moments[2 * width:, :] = jnp.concatenate([order34[width:], order34[width:]], axis=1)


def moment_body(low, own, other, near1, near2, h0, l0, h1, l1, h2, l2, moments):
    width = own.shape[0]
    last = product_rows(near1[...], h1, l1) + product_rows(near2[...], h2, l2)
    last = 2.0 * last + product_rows(own[...], h0, l0)
    last = dot(jnp.concatenate([own[...], other[...]], axis=1), last, 1, 1)
    moments[:2 * width, :] = low[:2 * width, :]
    moments[2 * width:, :] = jnp.concatenate([low[2 * width:, :width], last], axis=1)


def unit(rows, cols):
    return (lax.broadcasted_iota(jnp.int32, (rows, cols), 0)
            == lax.broadcasted_iota(jnp.int32, (rows, cols), 1)).astype(F32)


def lane(values, k):
    return jnp.take_along_axis(values, jnp.full(values.shape, k, jnp.int32), axis=1, mode="promise_in_bounds")


def sublane(values, k):
    return jnp.broadcast_to(values[k:k + 1, :], values.shape)


def inverse_factor(matrix):
    size = matrix.shape[0]
    work = jnp.concatenate([matrix, unit(size, size)], axis=1)
    blocks = [work[8 * i:8 * i + 8, :] for i in range(size // 8)]
    place = lax.broadcasted_iota(jnp.int32, (8, 2 * size), 0)
    done = [None] * (size // 8)
    for k in range(0, size, 4):
        top, r = divmod(k, 8)
        pivot = blocks[top]
        cols = [lane(pivot, k + j) for j in range(4)]
        u0, u1, u2, u3 = (sublane(pivot, r + j) for j in range(4))
        a00, a10, a20, a30 = (sublane(cols[0], r + j) for j in range(4))
        a11, a21, a31 = (sublane(cols[1], r + j) for j in range(1, 4))
        a22, a32 = (sublane(cols[2], r + j) for j in range(2, 4))
        a33 = sublane(cols[3], r + 3)
        det_a = a00 * a11 - a10 * a10
        inv_a = 1.0 / det_a
        p00, p10, p11 = a11 * inv_a, a10 * inv_a, a00 * inv_a
        b00, b01 = a20 * p00 - a21 * p10, a21 * p11 - a20 * p10
        b10, b11 = a30 * p00 - a31 * p10, a31 * p11 - a30 * p10
        s00 = a22 - b00 * a20 - b01 * a21
        s10 = a32 - b10 * a20 - b11 * a21
        s11 = a33 - b10 * a30 - b11 * a31
        det_s = s00 * s11 - s10 * s10
        inv_s = 1.0 / det_s
        u2 = u2 - b00 * u0 - b01 * u1
        u3 = u3 - b10 * u0 - b11 * u1
        t2 = (s11 * u2 - s10 * u3) * inv_s
        t3 = (s00 * u3 - s10 * u2) * inv_s
        t0 = (p00 * u0 - p10 * u1) - b00 * t2 - b10 * t3
        t1 = (p11 * u1 - p10 * u0) - b01 * t2 - b11 * t3
        for i in range(top, size // 8):
            if i == top:
                if r:
                    continue
                c = cols
            else:
                c = [lane(blocks[i], k + j) for j in range(4)]
            change = (c[0] * t0 + c[1] * t1) + (c[2] * t2 + c[3] * t3)
            blocks[i] = blocks[i] - (jnp.where(place > 3, change, 0.0) if i == top else change)
        v0 = u0 * lax.rsqrt(a00)
        v1 = (a00 * u1 - a10 * u0) * lax.rsqrt(a00 * det_a)
        v2 = u2 * lax.rsqrt(s00)
        v3 = (s00 * u3 - s10 * u2) * lax.rsqrt(s00 * det_s)
        four = jnp.where(place % 4 == 0, v0, jnp.where(place % 4 == 1, v1, jnp.where(place % 4 == 2, v2, v3)))
        done[top] = jnp.where(place > 3, four, done[top]) if r else four
    return jnp.concatenate(done, axis=0)[:, size:]


def trace(matrix):
    return jnp.sum(matrix * unit(*matrix.shape))


def dense(moments, index, rows):
    n = NVEC
    eye = unit(n, n)
    pick = ((lax.broadcasted_iota(jnp.int32, (n, n), 0) == index)
            & (lax.broadcasted_iota(jnp.int32, (n, n), 1) == index)).astype(F32)

    def even(matrix):
        return 0.5 * (matrix + matrix.T)

    base_t = inverse_factor(moments[0])
    base = base_t.T
    wide = dot(base_t, jnp.concatenate(moments[1:], axis=1))
    tall = dot(jnp.concatenate([wide[:, i * n:(i + 1) * n] for i in range(5)], axis=0), base)
    m = [eye] + [even(tall[i * n:(i + 1) * n]) for i in range(5)]

    square = dot(m[1], m[1])
    cross = dot(m[1], jnp.concatenate([m[2], square], axis=1))
    gram_r = m[2] - square
    image_r = m[3] - cross[:, :n] - cross[:, :n].T + cross[:, n:]
    shift = 3.0 - jnp.sum(m[1] * pick)
    ridge = RIDGE_WEIGHT * (n + trace(gram_r)) / (2 * n)
    ridged = gram_r + ridge * eye
    factor_t = inverse_factor(ridged)
    inverse = dot(factor_t, factor_t, 0, 0)
    keep = 1.0 / (1.0 + ridge)
    step = jnp.concatenate([
        jnp.concatenate([m[1] * keep + shift * eye, gram_r * keep], axis=1),
        jnp.concatenate([eye - ridge * inverse, dot(inverse, image_r) + shift * eye], axis=1),
    ], axis=0)
    cube = dot(dot(step, step), step)
    power = dot(cube, cube[:, :n])
    top, bottom = power[:n], power[n:]
    norm = (1.0 + ridge) * dot(top, top, 0, 0) + dot(bottom, dot(ridged, bottom), 0, 0)
    norm_t = inverse_factor(even(norm))
    mixed = dot(power, norm_t, 1, 1)
    top, bottom = mixed[:n], mixed[n:]

    back = dot(m[1], bottom)
    zero = jnp.zeros((n, n), F32)
    current = jnp.concatenate([top - back, bottom, zero], axis=0)
    image = jnp.concatenate([zero, top - back, bottom], axis=0)
    previous = jnp.concatenate([-back, bottom, zero], axis=0)
    hankel = [jnp.concatenate(m[i:i + 3], axis=1) for i in range(4)]
    plain = jnp.concatenate(hankel[:3], axis=0)
    raised = jnp.concatenate(hankel[1:], axis=0)
    ritz = even(dot(dot(current, plain, 0, 0), image))
    shift = 3.0 - jnp.sum(ritz * pick)
    residual = image - dot(current, ritz)
    basis = jnp.concatenate([current, previous, residual], axis=1)
    gram = dot(dot(basis, plain, 0, 0), basis)
    image_gram = dot(dot(basis, raised, 0, 0), basis)
    ridge = RIDGE_WEIGHT * trace(gram) / (3 * n)
    ridged = gram + ridge * unit(3 * n, 3 * n)
    g = [[ridged[i * n:(i + 1) * n, j * n:(j + 1) * n] for j in range(3)] for i in range(3)]
    v0 = inverse_factor(even(g[0][0]))
    l1020 = dot(jnp.concatenate([g[1][0], g[2][0]], axis=0), v0, 1, 1)
    outer = dot(l1020, l1020, 1, 1)
    v1 = inverse_factor(even(g[1][1] - outer[:n, :n]))
    l21 = dot(g[2][1] - outer[n:, :n], v1, 1, 1)
    v2 = inverse_factor(even(g[2][2] - outer[n:, n:] - dot(l21, l21, 1, 1)))
    l10, l20 = l1020[:n], l1020[n:]
    h0 = dot(v0, image_gram[:n])
    h1 = dot(v1, image_gram[n:2 * n] - dot(l10, h0))
    h2 = dot(v2, image_gram[2 * n:] - dot(l20, h0) - dot(l21, h1))
    z2 = dot(v2, h2, 0, 0)
    z1 = dot(v1, h1 - dot(l21, z2, 0, 0), 0, 0)
    z0 = dot(v0, h0 - dot(l10, z1, 0, 0) - dot(l20, z2, 0, 0), 0, 0)
    step = jnp.concatenate([z0, z1, z2], axis=0) + shift * unit(3 * n, 3 * n)
    cube = dot(dot(step, step), step)
    power = dot(cube, cube[:, :n])
    norm_t = inverse_factor(even(dot(power, dot(ridged, power), 0, 0)))
    mixed = dot(basis, dot(power, norm_t, 1, 1)) * math.sqrt(rows)
    return jnp.concatenate([dot(base, mixed[i * n:(i + 1) * n]) for i in range(3)], axis=0)


def dense_body(rows, index, moments, other_moments, scaled, out):
    n = NVEC
    packed = moments[...] + other_moments[...]
    parts = [packed[i * n:(i + 1) * n, j * n:(j + 1) * n] for i in range(3) for j in range(2)]
    parts = [0.5 * (part + part.T) for part in parts]
    out[...] = dot(dense(parts, index[0], rows), scaled[...], 0, 0)


def moved(shard, axis, by):
    length = lax.axis_size(axis)
    return lax.ppermute(shard, axis, [(i, (i + by) % length) for i in range(length)])


def moved_both(shard, axis, by):
    blocks, cores = lax.axis_size(axis), lax.axis_size("narrow")
    pairs = []
    for i in range(blocks):
        for j in range(cores):
            pairs.append((i * cores + j, (i + by) % blocks * cores + (j + 1) % cores))
    return lax.ppermute(shard, (axis, "narrow"), pairs)


def two_terms(values):
    blocks = lax.axis_size("blk")
    span = 1
    while blocks % (2 * span) == 0:
        other = lax.ppermute(values, "blk", [(i, i ^ span) for i in range(blocks)])
        values = values + other
        span *= 2
    if span < blocks:
        groups = [list(range(i, blocks, span)) for i in range(span)]
        values = lax.psum(values, "blk", axis_index_groups=groups)
    return values, moved(values, "narrow", 1)


def shards(embeddings, pair_mask, shift_index, start_seed):
    size, depth = embeddings.shape
    blocks = lax.axis_size("blk")
    where = lax.axis_index("blk")
    chunk = 128 if size % 128 == 0 else size
    count = size // chunk
    other_emb = moved(embeddings, "narrow", 1)
    near2 = [moved(embeddings[i * chunk:(i + 1) * chunk], "blk", -2) for i in range(count)]
    seed = start_seed.astype(F32).T / 1000.0
    keep = lax.dynamic_slice_in_dim(pair_mask, where, 1, 0)[0]
    if blocks % 2 == 0:
        direct = lax.ppermute(embeddings, "blk", [(i, i - 1) for i in range(1, blocks, 2)])
        relayed = [lax.ppermute(part, "blk", [(i, i + 1) for i in range(0, blocks, 2)]) for part in near2]
    else:
        direct, relayed = moved(embeddings, "blk", -1), near2
    odd = (where % 2 * (blocks % 2 == 0)).astype(jnp.int32).reshape(1)

    other_seed = moved(seed, "narrow", 1)
    rows_args = [embeddings, other_emb]
    h0, l0, rows0, _, row_sq = make_tile(
        own_body, rows_args, size, depth, extra=(((2 * size, 128), F32),))
    h2, l2, rows2, cols2 = make_tile(
        lambda *refs: near_body(count, *refs), [keep[1:2], *rows_args, row_sq, *near2], size, depth, (0,))
    h1, l1, rows1, cols1 = make_tile(
        lambda *refs: relayed_body(count, *refs),
        [keep[0:1], odd, *rows_args, row_sq, direct, *relayed], size, depth, (0, 1))
    tiles = [h0, l0, h1, l1, h2, l2]
    other_sum = moved(rows0 + rows1 + rows2, "narrow", 1)
    behind = [moved(cols1, "blk", 1), moved(cols2, "blk", 2),
              moved_both(cols1, "blk", 1), moved_both(cols2, "blk", 2)]
    pair_shape = ((2 * NVEC, size), F32)
    half_shape = ((NVEC, size), F32)
    cost = dict(flops=2 * 3 * 128 * 2 * size * 2 * size, nbytes=16 * size * size)
    degree, own, other, ahead1, ahead2 = call(
        first_body, [((16, size), F32)] + [half_shape] * 4,
        [rows0, rows1, rows2, other_sum] + behind + [seed, other_seed] + tiles[2:], **cost,
    )
    history = [own]
    for repeat in range(2):
        q1, q2 = moved(ahead1, "blk", 1), moved(ahead2, "blk", 2)
        near = [moved(own, "blk", -1), moved(own, "blk", -2)]
        (total,) = call(block_body, [pair_shape], [own, *near, q1, q2] + tiles, **cost)
        other_total = moved(total, "narrow", 1)
        if repeat == 0:
            own, other, ahead1, ahead2 = call(
                next_body, [half_shape] * 4, [total, other_total, degree] + tiles[2:], **cost)
        else:
            own, other = call(last_body, [half_shape] * 2, [total, other_total, degree], flops=10**5, nbytes=10**6)
        history.append(own)
    near = [moved(own, "blk", -1), moved(own, "blk", -2)]
    low, scaled = call(
        low_body, [((3 * NVEC, 2 * NVEC), F32), ((3 * NVEC, size), F32)], [degree] + history,
        flops=10**8, nbytes=10**6)
    (moments,) = call(
        moment_body, [((3 * NVEC, 2 * NVEC), F32)], [low, own, other, *near] + tiles, **cost)
    rows = size * blocks * lax.axis_size("narrow")
    (out,) = call(
        lambda *refs: dense_body(rows, *refs), [half_shape],
        [shift_index, *two_terms(moments), scaled], smem=(0,), flops=10**9, nbytes=10**6,
    )
    return out.T


def solution(mesh):
    return jax.shard_map(
        shards,
        mesh=mesh,
        in_specs=(
            P(("groups", "blk", "narrow"), None),
            P("groups", None),
            P("groups"),
            P(("groups", "blk", "narrow"), None),
        ),
        out_specs=P(("groups", "blk", "narrow"), None),
        check_vma=False,
    )
```

```python
import math

import jax
import jax.numpy as jnp
from jax import lax
from jax.experimental import pallas as pl
from jax.experimental.pallas import tpu as pltpu
from jax.sharding import PartitionSpec as P

KERNEL_GAMMA = 2.0
RIDGE_WEIGHT = 1e-05
NVEC = 64
F32 = jnp.float32
BF16 = jnp.bfloat16
VMEM_LIMIT = 48 * 1024 * 1024


def dot(left, right, left_dim=1, right_dim=0):
    precision = lax.Precision.HIGHEST if left.dtype == F32 else None
    return lax.dot_general(
        left, right, (((left_dim,), (right_dim,)), ((), ())),
        precision=precision, preferred_element_type=F32,
    )


def halves(values):
    high = values.astype(BF16)
    return high, (values - high.astype(F32)).astype(BF16)


def call(body, out_shapes, args, smem=(), flops=0, nbytes=0):
    specs = [
        pl.BlockSpec(memory_space=pltpu.SMEM if i in smem else pltpu.VMEM)
        for i in range(len(args))
    ]
    out = pl.pallas_call(
        body,
        out_shape=[jax.ShapeDtypeStruct(shape, dtype) for shape, dtype in out_shapes],
        in_specs=specs,
        out_specs=[pl.BlockSpec(memory_space=pltpu.VMEM) for _ in out_shapes],
        compiler_params=pltpu.CompilerParams(vmem_limit_bytes=VMEM_LIMIT),
        cost_estimate=pl.CostEstimate(flops=flops, bytes_accessed=nbytes, transcendentals=0),
    )(*args)
    return out


LOG2_E = 1.4426950408889634


def sums_along(values):
    rows, depth = values.shape
    folded = values[:, :128]
    for j in range(128, depth, 128):
        folded = folded + values[:, j:j + 128]
    return dot(jnp.ones((8, 128), F32), folded, 1, 1)


def fill_tile(weight, row_embs, row_sqs, col_emb, high, low, row_sum):
    size = col_emb.shape[0]
    col32 = col_emb.astype(F32)
    col_sq = (2.0 * LOG2_E) * sums_along(col32 * col32)[0:1, :]
    total = jnp.zeros((1, size), F32)
    for half in range(2):
        inner = dot(row_embs[half], col_emb, 1, 1)
        tile = jnp.exp2((4.0 * LOG2_E) * inner - (row_sqs[half] + col_sq)) * weight
        tile_high, tile_low = halves(tile)
        high[half * size:(half + 1) * size, :] = tile_high
        low[half * size:(half + 1) * size, :] = tile_low
        row_sum[half * 8:(half + 1) * 8, :] = row_sum[half * 8:(half + 1) * 8, :] + sums_along(tile)
        total = total + jnp.sum(tile, axis=0, keepdims=True)
    return jnp.broadcast_to(total, (8, size))


def own_body(own, other, high, low, row_sum, row_sq, copy):
    size = own.shape[0]
    embs = [own[...], other[...]]
    copy[...] = embs[0]
    sqs = []
    for half in range(2):
        row32 = embs[half].astype(F32)
        sqs.append((2.0 * LOG2_E) * jnp.sum(row32 * row32, axis=1, keepdims=True))
        row_sq[half * size:(half + 1) * size, :] = jnp.broadcast_to(sqs[half], (size, 128))
    row_sum[...] = jnp.zeros(row_sum.shape, F32)
    fill_tile(1.0, embs, sqs, embs[0], high, low, row_sum)


def stored_squares(row_sq, size):
    return [row_sq[half * size:(half + 1) * size, 0:1] for half in range(2)]


def near_body(count, keep, own, other, row_sq, *refs):
    size = own.shape[0]
    col = jnp.concatenate([ref[...] for ref in refs[:count]], axis=0)
    before, high, low, row_sum, col_sum = refs[count:]
    row_sum[...] = before[...]
    col_sum[...] = fill_tile(keep[0].astype(F32), [own[...], other[...]], stored_squares(row_sq, size),
                             col, high, low, row_sum)


def relayed_body(count, keep, odd, own, other, row_sq, direct, *refs):
    size = own.shape[0]
    relayed = jnp.concatenate([ref[...] for ref in refs[:count]], axis=0)
    col = jnp.where(odd[0] > 0, relayed, direct[...])
    before, behind, high, low, row_sum, col_sum = refs[count:]
    row_sum[:8, :] = before[:8, :] + behind[...]
    row_sum[8:, :] = before[8:, :]
    col_sum[...] = fill_tile(keep[0].astype(F32), [own[...], other[...]], stored_squares(row_sq, size),
                             col, high, low, row_sum)


def make_tile(body, args, rows, smem=(), extra=()):
    return call(
        body, [((2 * rows, rows), BF16), ((2 * rows, rows), BF16), ((16, rows), F32), *extra],
        args, smem=smem, flops=2 * 10**9, nbytes=10**6,
    )


def degree_body(sums, behind, other_sums, seed, other_seed, degree_out, scale_out, own_out, other_out):
    top = sums[:8, :] + behind[...] + other_sums[8:, :]
    bottom = sums[8:, :] + other_sums[:8, :]
    degree_out[:8, :] = top
    degree_out[8:, :] = bottom
    scale = lax.rsqrt(top)
    scale_out[...] = scale
    own_out[...] = seed[...] * scale[0:1, :]
    other_out[...] = other_seed[...] * lax.rsqrt(bottom)[0:1, :]


def ahead_body(own, other, h1, l1, h2, l2, ahead1, ahead2):
    width = own.shape[0]
    high, low = halves(jnp.concatenate([own[...], other[...]], axis=1))
    both = jnp.concatenate([high, low], axis=0)
    for tile_high, tile_low, out in ((h1, l1, ahead1), (h2, l2, ahead2)):
        product = dot(both, tile_high[...])
        out[...] = product[:width] + product[width:] + dot(high, tile_low[...])


def combine_body(total, other_total, degree, own_out, other_out):
    width = total.shape[0] // 2
    own_out[...] = (total[:width, :] + other_total[width:, :]) / degree[0:1, :]
    other_out[...] = (total[width:, :] + other_total[:width, :]) / degree[8:9, :]


def product_rows(vectors, tile_high, tile_low):
    width = vectors.shape[0]
    high, low = halves(vectors)
    both = jnp.concatenate([high, low], axis=0)
    product = dot(both, tile_high[...], 1, 1)
    return product[:width] + product[width:] + dot(high, tile_low[...], 1, 1)


def own_product_body(own, h0, l0, out):
    out[...] = product_rows(own[...], h0, l0)


def add_blocks(product, near1, near2, q1, q2, h1, l1, h2, l2, total):
    width, size = near1.shape
    product = product[...] + product_rows(near1, h1, l1) + product_rows(near2, h2, l2)
    total[:width, :] = product[:, :size] + q1[...] + q2[...]
    total[width:, :] = product[:, size:]


def first_block_body(product, seed1, seed2, scale1, scale2, *refs):
    add_blocks(product, seed1[...] * scale1[0:1, :], seed2[...] * scale2[0:1, :], *refs)


def block_body(product, near1, near2, *refs):
    add_blocks(product, near1[...], near2[...], *refs)


def low_body(degree, v0, v1, v2, moments, scaled):
    width = v0.shape[0]
    root = jnp.sqrt(degree[0:1, :])
    x0, x1, x2 = v0[...] * root, v1[...] * root, v2[...] * root
    scaled[...] = jnp.concatenate([x0, x1, x2], axis=0)
    left = jnp.concatenate([x0, x1], axis=0)
    order012 = dot(left, left, 1, 1)
    order34 = dot(jnp.concatenate([x1, x2], axis=0), x2, 1, 1)
    order = [order012[:width, :width], order012[:width, width:], order012[width:, width:],
             order34[:width], order34[width:]]
    for i in range(5):
        moments[i * width:(i + 1) * width, :] = order[i]


def place_of(rows, cols):
    return [lax.broadcasted_iota(jnp.int32, (rows, cols), axis) for axis in range(2)]


def moment_body(core, low, own, other, product, near1, near2, h1, l1, h2, l2, mine, theirs):
    n = own.shape[0]
    last = product_rows(near1[...], h1, l1) + product_rows(near2[...], h2, l2)
    last = 2.0 * last + product[...]
    last = dot(jnp.concatenate([own[...], other[...]], axis=1), last, 1, 1)
    moments = [low[i * n:(i + 1) * n, :] for i in range(5)] + [0.5 * (last + last.T)]
    row, col = place_of(n, n)
    pieces = []
    for i in range(0, 6, 2):
        pair = jnp.where(row >= col, moments[i], moments[i + 1])
        pieces.append(jnp.concatenate([pair[:n // 2], pair[n // 2:]], axis=1))
    d1, d3, d5 = (jnp.sum(moments[i] * unit(n, n), axis=0, keepdims=True) for i in (1, 3, 5))
    row, _ = place_of(8, 2 * n)
    pieces.append(jnp.where(row == 0, jnp.concatenate([d1, d3], axis=1),
                            jnp.where(row == 1, jnp.concatenate([d5, d5], axis=1), 0.0)))
    pieces.append(jnp.zeros((8, 2 * n), F32))
    packed = jnp.concatenate(pieces, axis=0)
    half = packed.shape[0] // 2
    first = core[0] == 0
    mine[...] = jnp.where(first, packed[:half], packed[half:])
    theirs[...] = jnp.where(first, packed[half:], packed[:half])


def unpacked(packed, n):
    row, col = place_of(n, n)
    start = 3 * n // 2
    diagonals = [packed[start:start + 1, :n], packed[start:start + 1, n:], packed[start + 1:start + 2, :n]]
    moments = []
    for i in range(3):
        folded = packed[i * n // 2:(i + 1) * n // 2]
        pair = jnp.concatenate([folded[:, :n], folded[:, n:]], axis=0)
        flipped = pair.T
        moments.append(jnp.where(row >= col, pair, flipped))
        moments.append(jnp.where(row == col, diagonals[i], jnp.where(row < col, pair, flipped)))
    return moments


def unit(rows, cols):
    return (lax.broadcasted_iota(jnp.int32, (rows, cols), 0)
            == lax.broadcasted_iota(jnp.int32, (rows, cols), 1)).astype(F32)


def lane(values, k):
    return jnp.take_along_axis(values, jnp.full(values.shape, k, jnp.int32), axis=1, mode="promise_in_bounds")


def sublane(values, k):
    return jnp.broadcast_to(values[k:k + 1, :], values.shape)


def inverse_factor(matrix):
    size = matrix.shape[0]
    work = jnp.concatenate([matrix, unit(size, size)], axis=1)
    blocks = [work[8 * i:8 * i + 8, :] for i in range(size // 8)]
    place = lax.broadcasted_iota(jnp.int32, (8, 2 * size), 0)
    done = [None] * (size // 8)
    for k in range(0, size, 4):
        top, r = divmod(k, 8)
        pivot = blocks[top]
        cols = [lane(pivot, k + j) for j in range(4)]
        u0, u1, u2, u3 = (sublane(pivot, r + j) for j in range(4))
        a00, a10, a20, a30 = (sublane(cols[0], r + j) for j in range(4))
        a11, a21, a31 = (sublane(cols[1], r + j) for j in range(1, 4))
        a22, a32 = (sublane(cols[2], r + j) for j in range(2, 4))
        a33 = sublane(cols[3], r + 3)
        det_a = a00 * a11 - a10 * a10
        inv_a = 1.0 / det_a
        p00, p10, p11 = a11 * inv_a, a10 * inv_a, a00 * inv_a
        b00, b01 = a20 * p00 - a21 * p10, a21 * p11 - a20 * p10
        b10, b11 = a30 * p00 - a31 * p10, a31 * p11 - a30 * p10
        s00 = a22 - b00 * a20 - b01 * a21
        s10 = a32 - b10 * a20 - b11 * a21
        s11 = a33 - b10 * a30 - b11 * a31
        det_s = s00 * s11 - s10 * s10
        inv_s = 1.0 / det_s
        u2 = u2 - b00 * u0 - b01 * u1
        u3 = u3 - b10 * u0 - b11 * u1
        t2 = (s11 * u2 - s10 * u3) * inv_s
        t3 = (s00 * u3 - s10 * u2) * inv_s
        t0 = (p00 * u0 - p10 * u1) - b00 * t2 - b10 * t3
        t1 = (p11 * u1 - p10 * u0) - b01 * t2 - b11 * t3
        for i in range(top, size // 8):
            if i == top:
                if r:
                    continue
                c = cols
            else:
                c = [lane(blocks[i], k + j) for j in range(4)]
            change = (c[0] * t0 + c[1] * t1) + (c[2] * t2 + c[3] * t3)
            blocks[i] = blocks[i] - (jnp.where(place > 3, change, 0.0) if i == top else change)
        v0 = u0 * lax.rsqrt(a00)
        v1 = (a00 * u1 - a10 * u0) * lax.rsqrt(a00 * det_a)
        v2 = u2 * lax.rsqrt(s00)
        v3 = (s00 * u3 - s10 * u2) * lax.rsqrt(s00 * det_s)
        four = jnp.where(place % 4 == 0, v0, jnp.where(place % 4 == 1, v1, jnp.where(place % 4 == 2, v2, v3)))
        done[top] = jnp.where(place > 3, four, done[top]) if r else four
    return jnp.concatenate(done, axis=0)[:, size:]


def trace(matrix):
    return jnp.sum(matrix * unit(*matrix.shape))


def dense(moments, index, rows, data):
    n = NVEC
    eye = unit(n, n)
    pick = ((lax.broadcasted_iota(jnp.int32, (n, n), 0) == index)
            & (lax.broadcasted_iota(jnp.int32, (n, n), 1) == index)).astype(F32)

    def part(stacked, i):
        return stacked[i * n:(i + 1) * n]

    def below(*parts):
        return jnp.concatenate(parts, axis=0)

    def beside(*parts):
        return jnp.concatenate(parts, axis=1)

    base = inverse_factor(moments[0])
    right = dot(below(*moments[1:]), base, 1, 1)
    m1, m2, m3, m4, m5 = (dot(base, part(right, i)) for i in range(5))
    y0, y1, y2 = (dot(base, part(data, i)) for i in range(3))

    by1 = dot(below(m1, m2, m3, m4), m1)
    square, m21, m31, m41 = (part(by1, i) for i in range(4))
    tri = dot(m1, beside(square, m21, m31))
    gram_r = m2 - square
    image_r = m3 - m21 - m21.T + tri[:, :n]
    mixed_r = m3 - m21
    square_r = m4 - m31 - m31.T + tri[:, n:2 * n]
    cubic_r = m5 - m41 - m41.T + tri[:, 2 * n:]
    shift = 3.0 - jnp.sum(m1 * pick)
    ridge = RIDGE_WEIGHT * (n + trace(gram_r)) / (2 * n)
    ridged = gram_r + ridge * eye
    factor = inverse_factor(ridged)
    inverse = dot(factor, factor, 0, 0)
    keep = 1.0 / (1.0 + ridge)
    step = below(
        beside(m1 * keep + shift * eye, gram_r * keep),
        beside(eye - ridge * inverse, dot(inverse, image_r) + shift * eye),
    )
    twice = dot(step, step)
    power = dot(twice, dot(twice, twice[:, :n]))
    top, bottom = power[:n], power[n:]
    weighted = dot(below(ridged, gram_r, image_r), bottom)
    norm = (1.0 + ridge) * dot(top, top, 0, 0) + dot(bottom, part(weighted, 0), 0, 0)
    factor = inverse_factor(norm)

    middle = m4 - m31
    images = dot(below(
        beside(m1, gram_r), beside(gram_r, image_r),
        beside(m2, mixed_r), beside(mixed_r.T, square_r),
        beside(m3, middle), beside(middle.T, cubic_r),
    ), power)
    whole = dot(power, beside(images[:2 * n], images[2 * n:4 * n], images[4 * n:], power), 0, 0)
    lower = dot(bottom, beside(part(images, 1), part(images, 3), part(weighted, 1), part(weighted, 2)), 0, 0)
    raw = [whole[:, i * n:(i + 1) * n] for i in range(4)] + [lower[:, i * n:(i + 1) * n] for i in range(4)]
    right = dot(below(*raw), factor, 1, 1)
    ritz, image2, image3, excess, p_image, p_image2, p_gram, p_ritz = (dot(factor, part(right, i)) for i in range(8))
    excess = ridge * excess

    shift = 3.0 - jnp.sum(ritz * pick)
    by_ritz = dot(below(ritz, p_gram, excess, p_image, image2), ritz)
    squared, gram_pr, gram_cr = part(by_ritz, 0), p_image - part(by_ritz, 1), part(by_ritz, 2)
    tri = dot(ritz, squared), dot(ritz, gram_cr)
    gram_rr = image2 - squared - tri[1]
    image_cr = image2 - squared
    image_pr = p_image2 - part(by_ritz, 3)
    image_rr = image3 - part(by_ritz, 4) - part(by_ritz, 4).T + tri[0]
    ridge = RIDGE_WEIGHT * (n - trace(excess) + trace(p_gram) + trace(gram_rr)) / (3 * n)
    g_cc = eye - excess + ridge * eye
    g_pp = p_gram + ridge * eye
    g_rr = gram_rr + ridge * eye
    image_gram = below(
        beside(ritz, p_image.T, image_cr), beside(p_image, p_ritz, image_pr), beside(image_cr.T, image_pr.T, image_rr),
    )
    v0 = inverse_factor(g_cc)
    side = dot(below(p_gram, gram_cr.T), v0, 1, 1)
    l10, l20 = side[:n], side[n:]
    outer = dot(side, side, 1, 1)
    v1 = inverse_factor(g_pp - outer[:n, :n])
    l21 = dot(gram_pr.T - outer[n:, :n], v1, 1, 1)
    v2 = inverse_factor(g_rr - outer[n:, n:] - dot(l21, l21, 1, 1))
    zero = jnp.zeros((n, n), F32)
    row0 = beside(v0, zero, zero)
    row1 = dot(v1, beside(-dot(l10, v0), eye, zero))
    row2 = beside(zero, zero, eye) - dot(l20, row0) - dot(l21, row1)
    known = below(row0, row1)
    solved = dot(known, dot(known, image_gram), 0, 0)
    row2 = dot(v2, beside(row2, dot(row2, image_gram)))
    step = solved + dot(row2[:, :3 * n], row2[:, 3 * n:], 0, 0) + shift * unit(3 * n, 3 * n)
    twice = dot(step, step)
    power2 = dot(twice, dot(twice, twice[:, :n]))
    gram = below(
        beside(g_cc, p_gram, gram_cr), beside(p_gram, g_pp, gram_pr), beside(gram_cr.T, gram_pr.T, g_rr),
    )
    norm = dot(power2, dot(gram, power2), 0, 0)

    start = dot(power, below(y0, y1), 0, 0) - dot(dot(m1, bottom), y0, 0, 0)
    image = dot(power, below(y1, y2), 0, 0) - dot(dot(m1, bottom), y1, 0, 0)
    residue = dot(bottom, y1 - dot(m1, y0), 0, 0)
    current = dot(factor, start)
    vectors = below(current, dot(factor, residue), dot(factor, image) - dot(ritz, current))
    return dot(inverse_factor(norm), dot(power2, vectors, 0, 0)) * math.sqrt(rows)


def dense_body(rows, core, index, mine, theirs, scaled, out):
    first = core[0] == 0
    packed = jnp.concatenate([
        jnp.where(first, mine[...], theirs[...]), jnp.where(first, theirs[...], mine[...])], axis=0)
    out[...] = dense(unpacked(packed, NVEC), index[0], rows, scaled[...])


def moved(shard, axis, by):
    length = lax.axis_size(axis)
    return lax.ppermute(shard, axis, [(i, (i + by) % length) for i in range(length)])


def total_over_blocks(values):
    blocks = lax.axis_size("blk")
    span = 1
    while blocks % (2 * span) == 0:
        other = lax.ppermute(values, "blk", [(i, i ^ span) for i in range(blocks)])
        values = values + other
        span *= 2
    if span < blocks:
        groups = [list(range(i, blocks, span)) for i in range(span)]
        values = lax.psum(values, "blk", axis_index_groups=groups)
    return values


def shards(embeddings, pair_mask, shift_index, start_seed):
    size = embeddings.shape[0]
    blocks = lax.axis_size("blk")
    where = lax.axis_index("blk")
    core = lax.axis_index("narrow").astype(jnp.int32).reshape(1)
    chunk = 128 if size % 128 == 0 else size
    count = size // chunk
    other_emb = moved(embeddings, "narrow", 1)
    near2 = [moved(embeddings[i * chunk:(i + 1) * chunk], "blk", -2) for i in range(count)]
    keep = lax.dynamic_slice_in_dim(pair_mask, where, 1, 0)[0]
    seed16 = start_seed.astype(jnp.int16).T
    seeds = [seed16, moved(seed16, "narrow", 1), moved(seed16, "blk", -1), moved(seed16, "blk", -2)]
    seed, other_seed, seed1, seed2 = [part.astype(F32) / 1000.0 for part in seeds]

    emb_args = [embeddings, other_emb]
    h0, l0, sums, row_sq, own_copy = make_tile(
        own_body, emb_args, size, extra=(((2 * size, 128), F32), (embeddings.shape, BF16)))
    if blocks % 2 == 0:
        direct = lax.ppermute(own_copy, "blk", [(i, i - 1) for i in range(1, blocks, 2)])
        relayed = [lax.ppermute(part, "blk", [(i, i + 1) for i in range(0, blocks, 2)]) for part in near2]
    else:
        direct, relayed = moved(own_copy, "blk", -1), near2
    odd = (where % 2 * (blocks % 2 == 0)).astype(jnp.int32).reshape(1)
    col_shape = ((8, size), F32)
    h2, l2, sums, cols2 = make_tile(
        lambda *refs: near_body(count, *refs), [keep[1:2], *emb_args, row_sq, *near2, sums], size, (0,), (col_shape,))
    behind2 = moved(cols2, "blk", 2)
    h1, l1, sums, cols1 = make_tile(
        lambda *refs: relayed_body(count, *refs),
        [keep[0:1], odd, *emb_args, row_sq, direct, *relayed, sums, behind2], size, (0, 1), (col_shape,))
    behind1 = moved(cols1, "blk", 1)
    other_sums = moved(sums + jnp.pad(behind1, ((0, 8), (0, 0))), "narrow", 1)

    pair_shape, half_shape = ((2 * NVEC, size), F32), ((NVEC, size), F32)
    small = dict(flops=10**6, nbytes=10**5)
    middle = dict(flops=10**9, nbytes=10**6)
    degree, scale, own, other = call(
        degree_body, [((16, size), F32), col_shape, half_shape, half_shape],
        [sums, behind1, other_sums, seed, other_seed], **small)
    far = [h1, l1, h2, l2]
    history = [own]
    for repeat in range(2):
        if repeat == 0:
            body, near = first_block_body, [seed1, seed2, moved(scale, "blk", -1), moved(scale, "blk", -2)]
        else:
            body, near = block_body, [moved(own, "blk", -1), moved(own, "blk", -2)]
        ahead1, ahead2 = call(ahead_body, [half_shape] * 2, [own, other, *far], **middle)
        q1, q2 = moved(ahead1, "blk", 1), moved(ahead2, "blk", 2)
        (product,) = call(own_product_body, [((NVEC, 2 * size), F32)], [own, h0, l0], **middle)
        (total,) = call(body, [pair_shape], [product, *near, q1, q2, *far], **middle)
        other_total = moved(total, "narrow", 1)
        own, other = call(combine_body, [half_shape] * 2, [total, other_total, degree], **small)
        history.append(own)
    near = [moved(own, "blk", -1), moved(own, "blk", -2)]
    low, scaled = call(
        low_body, [((5 * NVEC, NVEC), F32), ((3 * NVEC, size), F32)], [degree] + history, **middle)
    (product,) = call(own_product_body, [((NVEC, 2 * size), F32)], [own, h0, l0], **middle)
    packed_shape = ((3 * NVEC // 4 + 8, 2 * NVEC), F32)
    mine, theirs = call(
        moment_body, [packed_shape] * 2, [core, low, own, other, product, *near, *far], smem=(0,), **middle)
    mine = total_over_blocks(mine + moved(theirs, "narrow", 1))
    rows = size * blocks * lax.axis_size("narrow")
    (out,) = call(
        lambda *refs: dense_body(rows, *refs), [half_shape],
        [core, shift_index, mine, moved(mine, "narrow", 1), scaled], smem=(0, 1), flops=2 * 10**10, nbytes=10**6,
    )
    return out.T


def solution(mesh):
    return jax.shard_map(
        shards,
        mesh=mesh,
        in_specs=(
            P(("groups", "blk", "narrow"), None),
            P("groups", None),
            P("groups"),
            P(("groups", "blk", "narrow"), None),
        ),
        out_specs=P(("groups", "blk", "narrow"), None),
        check_vma=False,
    )
```

```python
import math

import jax
import jax.numpy as jnp
from jax import lax
from jax.experimental import pallas as pl
from jax.experimental.pallas import tpu as pltpu
from jax.sharding import PartitionSpec as P

KERNEL_GAMMA = 2.0
RIDGE_WEIGHT = 1e-05
NVEC = 64
F32 = jnp.float32
BF16 = jnp.bfloat16
VMEM_LIMIT = 48 * 1024 * 1024


def dot(left, right, left_dim=1, right_dim=0):
    precision = lax.Precision.HIGHEST if left.dtype == F32 else None
    return lax.dot_general(
        left, right, (((left_dim,), (right_dim,)), ((), ())),
        precision=precision, preferred_element_type=F32,
    )


def halves(values):
    high = values.astype(BF16)
    return high, (values - high.astype(F32)).astype(BF16)


def call(body, out_shapes, args, smem=(), flops=0, nbytes=0):
    specs = [
        pl.BlockSpec(memory_space=pltpu.SMEM if i in smem else pltpu.VMEM)
        for i in range(len(args))
    ]
    out = pl.pallas_call(
        body,
        out_shape=[jax.ShapeDtypeStruct(shape, dtype) for shape, dtype in out_shapes],
        in_specs=specs,
        out_specs=[pl.BlockSpec(memory_space=pltpu.VMEM) for _ in out_shapes],
        compiler_params=pltpu.CompilerParams(vmem_limit_bytes=VMEM_LIMIT),
        cost_estimate=pl.CostEstimate(flops=flops, bytes_accessed=nbytes, transcendentals=0),
    )(*args)
    return out


LOG2_E = 1.4426950408889634


def sums_along(values):
    rows, depth = values.shape
    folded = values[:, :128]
    for j in range(128, depth, 128):
        folded = folded + values[:, j:j + 128]
    return dot(jnp.ones((8, 128), F32), folded, 1, 1)


def fill_tile(weight, row_embs, row_sq, col_emb, high, low, row_sum):
    size = col_emb.shape[0]
    col32 = col_emb.astype(F32)
    col_sq = (2.0 * LOG2_E) * sums_along(col32 * col32)[0:1, :]
    total = jnp.zeros((1, size), F32)
    for half in range(2):
        rows = slice(half * size, (half + 1) * size)
        inner = dot(row_embs[half], col_emb, 1, 1)
        squares = jnp.concatenate([row_sq[rows, :]] * (size // 128), axis=1)
        tile = jnp.exp2((4.0 * LOG2_E) * inner - (squares + col_sq)) * weight
        tile_high, tile_low = halves(tile)
        high[rows, :] = tile_high
        low[rows, :] = tile_low
        row_sum[half * 8:(half + 1) * 8, :] = row_sum[half * 8:(half + 1) * 8, :] + sums_along(tile)
        total = total + jnp.sum(tile, axis=0, keepdims=True)
    return jnp.broadcast_to(total, (8, size))


def own_body(own, other, high, low, row_sum, row_sq):
    size = own.shape[0]
    embs = [own[...], other[...]]
    for half in range(2):
        row32 = embs[half].astype(F32)
        squares = (2.0 * LOG2_E) * jnp.sum(row32 * row32, axis=1, keepdims=True)
        row_sq[half * size:(half + 1) * size, :] = jnp.broadcast_to(squares, (size, 128))
    row_sum[...] = jnp.zeros(row_sum.shape, F32)
    fill_tile(1.0, embs, row_sq, embs[0], high, low, row_sum)


def far_body(keep, own, other, row_sq, col, before, seeds, near_seeds,
             high, low, row_sum, col_sum, seeds_out, near_seeds_out):
    row_sum[...] = before[...]
    col_sum[...] = fill_tile(keep[0].astype(F32), [own[...], other[...]], row_sq, col[...], high, low, row_sum)
    seeds_out[...] = seeds[...].astype(jnp.int32).astype(F32) / 1000.0
    near_seeds_out[...] = near_seeds[...].astype(jnp.int32).astype(F32) / 1000.0


def relayed_body(keep, choice, own, other, row_sq, direct, relayed, before, first_cols,
                 high, low, row_sum, col_sum):
    row_sum[...] = before[...]
    col = jnp.where(choice[0] > 0, relayed[...], direct[...])
    col_sum[:8, :] = first_cols[...]
    col_sum[8:, :] = fill_tile(keep[0].astype(F32), [own[...], other[...]], row_sq, col, high, low, row_sum)


def make_tile(body, args, rows, smem=(), extra=()):
    return call(
        body, [((2 * rows, rows), BF16), ((2 * rows, rows), BF16), ((16, rows), F32), *extra],
        args, smem=smem, flops=2 * 10**9, nbytes=10**6,
    )


def swapped(values):
    middle = values.shape[0] // 2
    return jnp.concatenate([values[middle:], values[:middle]], axis=0)


def per_row(values, width):
    shape = (width, values.shape[1])
    return jnp.concatenate([jnp.broadcast_to(values[i:i + 1, :], shape) for i in (0, 8)], axis=0)


def degree_body(sums, other_sums, seeds, degree_out, scale_out, vectors_out):
    degree = sums[...] + swapped(other_sums[...])
    scale = lax.rsqrt(degree)
    degree_out[...] = degree
    scale_out[...] = scale
    vectors_out[...] = seeds[...] * per_row(scale, seeds.shape[0] // 2)


def ahead_body(vectors, h1, l1, h2, l2, ahead):
    width = vectors.shape[0] // 2
    high, low = halves(jnp.concatenate([vectors[:width, :], vectors[width:, :]], axis=1))
    both = jnp.concatenate([high, low], axis=0)
    for half, (tile_high, tile_low) in enumerate(((h1, l1), (h2, l2))):
        product = dot(both, tile_high[...])
        product = product[:width] + product[width:] + dot(high, tile_low[...])
        ahead[half * width:(half + 1) * width, :] = product


def combine_body(total, other_total, degree, vectors_out):
    vectors_out[...] = (total[...] + swapped(other_total[...])) / per_row(degree[...], total.shape[0] // 2)


def product_rows(vectors, tile_high, tile_low):
    width = vectors.shape[0]
    high, low = halves(vectors)
    both = jnp.concatenate([high, low], axis=0)
    product = dot(both, tile_high[...], 1, 1)
    return product[:width] + product[width:] + dot(high, tile_low[...], 1, 1)


def stacked(product):
    size = product.shape[1] // 2
    return jnp.concatenate([product[:, :size], product[:, size:]], axis=0)


def own_product_body(vectors, h0, l0, out):
    out[...] = stacked(product_rows(vectors[:vectors.shape[0] // 2, :], h0, l0))


def add_blocks(product, near, behind, h1, l1, h2, l2, total):
    width = near.shape[0] // 2
    far = product_rows(near[:width], h1, l1) + product_rows(near[width:], h2, l2)
    total[...] = product[...] + behind[...] + stacked(far)


def first_block_body(product, near_seeds, near_scale, *refs):
    add_blocks(product, near_seeds[...] * per_row(near_scale[...], near_seeds.shape[0] // 2), *refs)


def block_body(product, near, *refs):
    add_blocks(product, near[...], *refs)


def low_body(degree, v0, v1, v2, moments, scaled):
    width = v0.shape[0] // 2
    root = jnp.sqrt(degree[0:1, :])
    x0, x1, x2 = v0[:width, :] * root, v1[:width, :] * root, v2[:width, :] * root
    scaled[...] = jnp.concatenate([x0, x1, x2], axis=0)
    left = jnp.concatenate([x0, x1], axis=0)
    order012 = dot(left, left, 1, 1)
    order34 = dot(jnp.concatenate([x1, x2], axis=0), x2, 1, 1)
    order = [order012[:width, :width], order012[:width, width:], order012[width:, width:],
             order34[:width], order34[width:]]
    for i in range(5):
        moments[i * width:(i + 1) * width, :] = order[i]


def place_of(rows, cols):
    return [lax.broadcasted_iota(jnp.int32, (rows, cols), axis) for axis in range(2)]


def moment_body(core, low, vectors, product, near, h1, l1, h2, l2, mine, theirs):
    n = vectors.shape[0] // 2
    last = product_rows(near[:n, :], h1, l1) + product_rows(near[n:, :], h2, l2)
    last = 2.0 * last + jnp.concatenate([product[:n, :], product[n:, :]], axis=1)
    last = dot(jnp.concatenate([vectors[:n, :], vectors[n:, :]], axis=1), last, 1, 1)
    moments = [low[i * n:(i + 1) * n, :] for i in range(5)] + [0.5 * (last + last.T)]
    row, col = place_of(n, n)
    pieces = []
    for i in range(0, 6, 2):
        pair = jnp.where(row >= col, moments[i], moments[i + 1])
        pieces.append(jnp.concatenate([pair[:n // 2], pair[n // 2:]], axis=1))
    d1, d3, d5 = (jnp.sum(moments[i] * unit(n, n), axis=0, keepdims=True) for i in (1, 3, 5))
    row, _ = place_of(8, 2 * n)
    pieces.append(jnp.where(row == 0, jnp.concatenate([d1, d3], axis=1),
                            jnp.where(row == 1, jnp.concatenate([d5, d5], axis=1), 0.0)))
    pieces.append(jnp.zeros((8, 2 * n), F32))
    packed = jnp.concatenate(pieces, axis=0)
    half = packed.shape[0] // 2
    first = core[0] == 0
    mine[...] = jnp.where(first, packed[:half], packed[half:])
    theirs[...] = jnp.where(first, packed[half:], packed[:half])


def unpacked(packed, n):
    row, col = place_of(n, n)
    start = 3 * n // 2
    diagonals = [packed[start:start + 1, :n], packed[start:start + 1, n:], packed[start + 1:start + 2, :n]]
    moments = []
    for i in range(3):
        folded = packed[i * n // 2:(i + 1) * n // 2]
        pair = jnp.concatenate([folded[:, :n], folded[:, n:]], axis=0)
        flipped = pair.T
        moments.append(jnp.where(row >= col, pair, flipped))
        moments.append(jnp.where(row == col, diagonals[i], jnp.where(row < col, pair, flipped)))
    return moments


def unit(rows, cols):
    return (lax.broadcasted_iota(jnp.int32, (rows, cols), 0)
            == lax.broadcasted_iota(jnp.int32, (rows, cols), 1)).astype(F32)


def lane(values, k):
    return jnp.take_along_axis(values, jnp.full(values.shape, k, jnp.int32), axis=1, mode="promise_in_bounds")


def sublane(values, k):
    return jnp.broadcast_to(values[k:k + 1, :], values.shape)


def inverse_factor(matrix):
    size = matrix.shape[0]
    work = jnp.concatenate([matrix, unit(size, size)], axis=1)
    blocks = [work[8 * i:8 * i + 8, :] for i in range(size // 8)]
    place = lax.broadcasted_iota(jnp.int32, (8, 2 * size), 0)
    done = [None] * (size // 8)
    for k in range(0, size, 4):
        top, r = divmod(k, 8)
        pivot = blocks[top]
        cols = [lane(pivot, k + j) for j in range(4)]
        u0, u1, u2, u3 = (sublane(pivot, r + j) for j in range(4))
        a00, a10, a20, a30 = (sublane(cols[0], r + j) for j in range(4))
        a11, a21, a31 = (sublane(cols[1], r + j) for j in range(1, 4))
        a22, a32 = (sublane(cols[2], r + j) for j in range(2, 4))
        a33 = sublane(cols[3], r + 3)
        det_a = a00 * a11 - a10 * a10
        inv_a = 1.0 / det_a
        p00, p10, p11 = a11 * inv_a, a10 * inv_a, a00 * inv_a
        b00, b01 = a20 * p00 - a21 * p10, a21 * p11 - a20 * p10
        b10, b11 = a30 * p00 - a31 * p10, a31 * p11 - a30 * p10
        s00 = a22 - b00 * a20 - b01 * a21
        s10 = a32 - b10 * a20 - b11 * a21
        s11 = a33 - b10 * a30 - b11 * a31
        det_s = s00 * s11 - s10 * s10
        inv_s = 1.0 / det_s
        u2 = u2 - b00 * u0 - b01 * u1
        u3 = u3 - b10 * u0 - b11 * u1
        t2 = (s11 * u2 - s10 * u3) * inv_s
        t3 = (s00 * u3 - s10 * u2) * inv_s
        t0 = (p00 * u0 - p10 * u1) - b00 * t2 - b10 * t3
        t1 = (p11 * u1 - p10 * u0) - b01 * t2 - b11 * t3
        for i in range(top, size // 8):
            if i == top:
                if r:
                    continue
                c = cols
            else:
                c = [lane(blocks[i], k + j) for j in range(4)]
            change = (c[0] * t0 + c[1] * t1) + (c[2] * t2 + c[3] * t3)
            blocks[i] = blocks[i] - (jnp.where(place > 3, change, 0.0) if i == top else change)
        v0 = u0 * lax.rsqrt(a00)
        v1 = (a00 * u1 - a10 * u0) * lax.rsqrt(a00 * det_a)
        v2 = u2 * lax.rsqrt(s00)
        v3 = (s00 * u3 - s10 * u2) * lax.rsqrt(s00 * det_s)
        four = jnp.where(place % 4 == 0, v0, jnp.where(place % 4 == 1, v1, jnp.where(place % 4 == 2, v2, v3)))
        done[top] = jnp.where(place > 3, four, done[top]) if r else four
    return jnp.concatenate(done, axis=0)[:, size:]


def trace(matrix):
    return jnp.sum(matrix * unit(*matrix.shape))


def dense(moments, index, rows, data):
    n = NVEC
    eye = unit(n, n)
    pick = ((lax.broadcasted_iota(jnp.int32, (n, n), 0) == index)
            & (lax.broadcasted_iota(jnp.int32, (n, n), 1) == index)).astype(F32)

    def part(stacked, i):
        return stacked[i * n:(i + 1) * n]

    def below(*parts):
        return jnp.concatenate(parts, axis=0)

    def beside(*parts):
        return jnp.concatenate(parts, axis=1)

    base = inverse_factor(moments[0])
    right = dot(below(*moments[1:]), base, 1, 1)
    m1, m2, m3, m4, m5 = (dot(base, part(right, i)) for i in range(5))
    y0, y1, y2 = (dot(base, part(data, i)) for i in range(3))

    by1 = dot(below(m1, m2, m3, m4), m1)
    square, m21, m31, m41 = (part(by1, i) for i in range(4))
    tri = dot(m1, beside(square, m21, m31))
    gram_r = m2 - square
    image_r = m3 - m21 - m21.T + tri[:, :n]
    mixed_r = m3 - m21
    square_r = m4 - m31 - m31.T + tri[:, n:2 * n]
    cubic_r = m5 - m41 - m41.T + tri[:, 2 * n:]
    shift = 3.0 - jnp.sum(m1 * pick)
    ridge = RIDGE_WEIGHT * (n + trace(gram_r)) / (2 * n)
    ridged = gram_r + ridge * eye
    factor = inverse_factor(ridged)
    inverse = dot(factor, factor, 0, 0)
    keep = 1.0 / (1.0 + ridge)
    step = below(
        beside(m1 * keep + shift * eye, gram_r * keep),
        beside(eye - ridge * inverse, dot(inverse, image_r) + shift * eye),
    )
    twice = dot(step, step)
    power = dot(twice, dot(twice, twice[:, :n]))
    top, bottom = power[:n], power[n:]
    weighted = dot(below(ridged, gram_r, image_r), bottom)
    norm = (1.0 + ridge) * dot(top, top, 0, 0) + dot(bottom, part(weighted, 0), 0, 0)
    factor = inverse_factor(norm)

    middle = m4 - m31
    images = dot(below(
        beside(m1, gram_r), beside(gram_r, image_r),
        beside(m2, mixed_r), beside(mixed_r.T, square_r),
        beside(m3, middle), beside(middle.T, cubic_r),
    ), power)
    whole = dot(power, beside(images[:2 * n], images[2 * n:4 * n], images[4 * n:], power), 0, 0)
    lower = dot(bottom, beside(part(images, 1), part(images, 3), part(weighted, 1), part(weighted, 2)), 0, 0)
    raw = [whole[:, i * n:(i + 1) * n] for i in range(4)] + [lower[:, i * n:(i + 1) * n] for i in range(4)]
    right = dot(below(*raw), factor, 1, 1)
    ritz, image2, image3, excess, p_image, p_image2, p_gram, p_ritz = (dot(factor, part(right, i)) for i in range(8))
    excess = ridge * excess

    shift = 3.0 - jnp.sum(ritz * pick)
    by_ritz = dot(below(ritz, p_gram, excess, p_image, image2), ritz)
    squared, gram_pr, gram_cr = part(by_ritz, 0), p_image - part(by_ritz, 1), part(by_ritz, 2)
    tri = dot(ritz, squared), dot(ritz, gram_cr)
    gram_rr = image2 - squared - tri[1]
    image_cr = image2 - squared
    image_pr = p_image2 - part(by_ritz, 3)
    image_rr = image3 - part(by_ritz, 4) - part(by_ritz, 4).T + tri[0]
    ridge = RIDGE_WEIGHT * (n - trace(excess) + trace(p_gram) + trace(gram_rr)) / (3 * n)
    g_cc = eye - excess + ridge * eye
    g_pp = p_gram + ridge * eye
    g_rr = gram_rr + ridge * eye
    image_gram = below(
        beside(ritz, p_image.T, image_cr), beside(p_image, p_ritz, image_pr), beside(image_cr.T, image_pr.T, image_rr),
    )
    v0 = inverse_factor(g_cc)
    side = dot(below(p_gram, gram_cr.T), v0, 1, 1)
    l10, l20 = side[:n], side[n:]
    outer = dot(side, side, 1, 1)
    v1 = inverse_factor(g_pp - outer[:n, :n])
    l21 = dot(gram_pr.T - outer[n:, :n], v1, 1, 1)
    v2 = inverse_factor(g_rr - outer[n:, n:] - dot(l21, l21, 1, 1))
    zero = jnp.zeros((n, n), F32)
    row0 = beside(v0, zero, zero)
    row1 = dot(v1, beside(-dot(l10, v0), eye, zero))
    row2 = beside(zero, zero, eye) - dot(l20, row0) - dot(l21, row1)
    known = below(row0, row1)
    solved = dot(known, dot(known, image_gram), 0, 0)
    row2 = dot(v2, beside(row2, dot(row2, image_gram)))
    step = solved + dot(row2[:, :3 * n], row2[:, 3 * n:], 0, 0) + shift * unit(3 * n, 3 * n)
    twice = dot(step, step)
    power2 = dot(twice, dot(twice, twice[:, :n]))
    gram = below(
        beside(g_cc, p_gram, gram_cr), beside(p_gram, g_pp, gram_pr), beside(gram_cr.T, gram_pr.T, g_rr),
    )
    norm = dot(power2, dot(gram, power2), 0, 0)

    start = dot(power, below(y0, y1), 0, 0) - dot(dot(m1, bottom), y0, 0, 0)
    image = dot(power, below(y1, y2), 0, 0) - dot(dot(m1, bottom), y1, 0, 0)
    residue = dot(bottom, y1 - dot(m1, y0), 0, 0)
    current = dot(factor, start)
    vectors = below(current, dot(factor, residue), dot(factor, image) - dot(ritz, current))
    return dot(inverse_factor(norm), dot(power2, vectors, 0, 0)) * math.sqrt(rows)


def dense_body(rows, core, index, mine, theirs, scaled, out):
    first = core[0] == 0
    packed = jnp.concatenate([
        jnp.where(first, mine[...], theirs[...]), jnp.where(first, theirs[...], mine[...])], axis=0)
    out[...] = dense(unpacked(packed, NVEC), index[0], rows, scaled[...])


def between_blocks(shard, sign):
    blocks, cores = lax.axis_size("blk"), lax.axis_size("narrow")
    pairs = [(i * cores + j, (i + sign * (1 + j)) % blocks * cores + j) for i in range(blocks) for j in range(cores)]
    return lax.ppermute(shard, ("blk", "narrow"), pairs)


def between_cores(shard):
    return lax.ppermute(shard, "narrow", [(0, 1), (1, 0)])


def total_over_blocks(values):
    blocks = lax.axis_size("blk")
    span = 1
    while blocks % (2 * span) == 0:
        other = lax.ppermute(values, "blk", [(i, i ^ span) for i in range(blocks)])
        values = values + other
        span *= 2
    if span < blocks:
        groups = [list(range(i, blocks, span)) for i in range(span)]
        values = lax.psum(values, "blk", axis_index_groups=groups)
    return values


def shards(embeddings, pair_mask, shift_index, start_seed):
    size = embeddings.shape[0]
    blocks = lax.axis_size("blk")
    where = lax.axis_index("blk")
    core = lax.axis_index("narrow").astype(jnp.int32).reshape(1)
    other_emb = between_cores(embeddings)
    far_emb = between_blocks(embeddings, -1)
    pairs = [(2 * i, (i - 2) % blocks * 2 + 1) for i in range(blocks)]
    pairs += [(2 * i + 1, (i - 1) % blocks * 2) for i in range(blocks) if blocks % 2 or i % 2]
    direct = lax.ppermute(embeddings, ("blk", "narrow"), pairs)
    choice = (1 - core) * (where % 2 * (1 - blocks % 2)).astype(jnp.int32)
    keep = lax.dynamic_slice(pair_mask, (where, core[0]), (1, 1))[0]
    seed16 = start_seed.astype(jnp.int16).T
    seeds16 = jnp.concatenate([seed16, between_cores(seed16)], axis=0)
    near_seeds16 = between_blocks(seeds16, -1)

    emb_args = [embeddings, other_emb]
    pair_shape, row_shape = ((2 * NVEC, size), F32), ((16, size), F32)
    h0, l0, sums, row_sq = make_tile(own_body, emb_args, size, extra=(((2 * size, 128), F32),))
    far_emb, sums, near_seeds16 = lax.optimization_barrier((far_emb, sums, near_seeds16))
    relayed = direct
    if blocks % 2 == 0:
        relayed = lax.ppermute(far_emb, ("blk", "narrow"), [(2 * i + 1, 2 * i + 2) for i in range(0, blocks, 2)])
    h1, l1, sums, cols, seeds, near_seeds = make_tile(
        far_body, [keep, *emb_args, row_sq, far_emb, sums, seeds16, near_seeds16], size, (0,),
        (((8, size), F32), pair_shape, pair_shape))
    h2, l2, sums, cols = make_tile(
        relayed_body, [keep, choice, *emb_args, row_sq, direct, relayed, sums, cols], size, (0, 1), (row_shape,))
    sums = sums + between_blocks(cols, 1)

    small = dict(flops=10**6, nbytes=10**5)
    middle = dict(flops=10**9, nbytes=10**6)
    degree, scale, vectors = call(
        degree_body, [row_shape, row_shape, pair_shape], [sums, between_cores(sums), seeds], **small)
    far = [h1, l1, h2, l2]
    history = [vectors]
    for repeat in range(2):
        if repeat == 0:
            body, near = first_block_body, [near_seeds, between_blocks(scale, -1)]
        else:
            body, near = block_body, [between_blocks(vectors, -1)]
        (ahead,) = call(ahead_body, [pair_shape], [vectors, *far], **middle)
        behind = between_blocks(ahead, 1)
        (product,) = call(own_product_body, [pair_shape], [vectors, h0, l0], **middle)
        (total,) = call(body, [pair_shape], [product, *near, behind, *far], **middle)
        (vectors,) = call(combine_body, [pair_shape], [total, between_cores(total), degree], **small)
        history.append(vectors)
    near = between_blocks(vectors, -1)
    low, scaled = call(
        low_body, [((5 * NVEC, NVEC), F32), ((3 * NVEC, size), F32)], [degree] + history, **middle)
    (product,) = call(own_product_body, [pair_shape], [vectors, h0, l0], **middle)
    packed_shape = ((3 * NVEC // 4 + 8, 2 * NVEC), F32)
    mine, theirs = call(
        moment_body, [packed_shape] * 2, [core, low, vectors, product, near, *far], smem=(0,), **middle)
    mine = total_over_blocks(mine + between_cores(theirs))
    rows = size * blocks * lax.axis_size("narrow")
    (out,) = call(
        lambda *refs: dense_body(rows, *refs), [((NVEC, size), F32)],
        [core, shift_index, mine, between_cores(mine), scaled], smem=(0, 1), flops=2 * 10**10, nbytes=10**6,
    )
    return out.T


def solution(mesh):
    return jax.shard_map(
        shards,
        mesh=mesh,
        in_specs=(
            P(("groups", "blk", "narrow"), None),
            P("groups", None),
            P("groups"),
            P(("groups", "blk", "narrow"), None),
        ),
        out_specs=P(("groups", "blk", "narrow"), None),
        check_vma=False,
    )
```

```python
import math

import jax
import jax.numpy as jnp
from jax import lax
from jax.experimental import pallas as pl
from jax.experimental.pallas import tpu as pltpu
from jax.sharding import PartitionSpec as P

KERNEL_GAMMA = 2.0
RIDGE_WEIGHT = 1e-05
NVEC = 64
F32 = jnp.float32
BF16 = jnp.bfloat16
VMEM_LIMIT = 48 * 1024 * 1024


def dot(left, right, left_dim=1, right_dim=0):
    precision = lax.Precision.HIGHEST if left.dtype == F32 else None
    return lax.dot_general(
        left, right, (((left_dim,), (right_dim,)), ((), ())),
        precision=precision, preferred_element_type=F32,
    )


def halves(values):
    high = values.astype(BF16)
    return high, (values - high.astype(F32)).astype(BF16)


def call(body, out_shapes, args, smem=(), flops=0, nbytes=0):
    specs = [
        pl.BlockSpec(memory_space=pltpu.SMEM if i in smem else pltpu.VMEM)
        for i in range(len(args))
    ]
    out = pl.pallas_call(
        body,
        out_shape=[jax.ShapeDtypeStruct(shape, dtype) for shape, dtype in out_shapes],
        in_specs=specs,
        out_specs=[pl.BlockSpec(memory_space=pltpu.VMEM) for _ in out_shapes],
        compiler_params=pltpu.CompilerParams(vmem_limit_bytes=VMEM_LIMIT),
        cost_estimate=pl.CostEstimate(flops=flops, bytes_accessed=nbytes, transcendentals=0),
    )(*args)
    return out


LOG2_E = 1.4426950408889634


def sums_along(values):
    rows, depth = values.shape
    folded = values[:, :128]
    for j in range(128, depth, 128):
        folded = folded + values[:, j:j + 128]
    return dot(jnp.ones((8, 128), F32), folded, 1, 1)


def fill_tile(weight, row_embs, row_sq, col_emb, high, low, row_sum):
    size = col_emb.shape[0]
    col32 = col_emb.astype(F32)
    col_sq = (2.0 * LOG2_E) * sums_along(col32 * col32)[0:1, :]
    total = jnp.zeros((1, size), F32)
    for half in range(2):
        rows = slice(half * size, (half + 1) * size)
        inner = dot(row_embs[half], col_emb, 1, 1)
        squares = jnp.concatenate([row_sq[rows, :]] * (size // 128), axis=1)
        tile = jnp.exp2((4.0 * LOG2_E) * inner - (squares + col_sq)) * weight
        tile_high, tile_low = halves(tile)
        high[rows, :] = tile_high
        low[rows, :] = tile_low
        row_sum[half * 8:(half + 1) * 8, :] = row_sum[half * 8:(half + 1) * 8, :] + sums_along(tile)
        total = total + jnp.sum(tile, axis=0, keepdims=True)
    return jnp.broadcast_to(total, (8, size))


def seed_values(seeds):
    return seeds[...].astype(jnp.int32).astype(F32) / 1000.0


def own_body(own, other, high, low, row_sum, row_sq):
    size = own.shape[0]
    embs = [own[...], other[...]]
    for half in range(2):
        row32 = embs[half].astype(F32)
        squares = (2.0 * LOG2_E) * jnp.sum(row32 * row32, axis=1, keepdims=True)
        row_sq[half * size:(half + 1) * size, :] = jnp.broadcast_to(squares, (size, 128))
    row_sum[...] = jnp.zeros(row_sum.shape, F32)
    fill_tile(1.0, embs, row_sq, embs[0], high, low, row_sum)


def far_body(keep, own, other, row_sq, col, before, high, low, row_sum, col_sum):
    row_sum[...] = before[...]
    col_sum[...] = fill_tile(keep[0].astype(F32), [own[...], other[...]], row_sq, col[...], high, low, row_sum)


def relayed_body(keep, choice, own, other, row_sq, direct, relayed, before, first_cols, near_seeds,
                 high, low, row_sum, col_sum, near_seeds_out):
    row_sum[...] = before[...]
    near_seeds_out[...] = seed_values(near_seeds)
    col = jnp.where(choice[0] > 0, relayed[...], direct[...])
    col_sum[:8, :] = first_cols[...]
    col_sum[8:, :] = fill_tile(keep[0].astype(F32), [own[...], other[...]], row_sq, col, high, low, row_sum)


def make_tile(body, args, rows, smem=(), extra=()):
    return call(
        body, [((2 * rows, rows), BF16), ((2 * rows, rows), BF16), ((16, rows), F32), *extra],
        args, smem=smem, flops=2 * 10**9, nbytes=10**6,
    )


def swapped(values):
    middle = values.shape[0] // 2
    return jnp.concatenate([values[middle:], values[:middle]], axis=0)


def per_row(values, width):
    shape = (width, values.shape[1])
    return jnp.concatenate([jnp.broadcast_to(values[i:i + 1, :], shape) for i in (0, 8)], axis=0)


def degree_body(sums, other_sums, seeds, degree_out, scale_out, vectors_out):
    degree = sums[...] + swapped(other_sums[...])
    scale = lax.rsqrt(degree)
    degree_out[...] = degree
    scale_out[...] = scale
    vectors_out[...] = seed_values(seeds) * per_row(scale, seeds.shape[0] // 2)


def ahead_body(vectors, h1, l1, h2, l2, ahead):
    width = vectors.shape[0] // 2
    high, low = halves(jnp.concatenate([vectors[:width, :], vectors[width:, :]], axis=1))
    both = jnp.concatenate([high, low], axis=0)
    for half, (tile_high, tile_low) in enumerate(((h1, l1), (h2, l2))):
        product = dot(both, tile_high[...])
        product = product[:width] + product[width:] + dot(high, tile_low[...])
        ahead[half * width:(half + 1) * width, :] = product


def combine_body(total, other_total, degree, vectors_out):
    vectors_out[...] = (total[...] + swapped(other_total[...])) / per_row(degree[...], total.shape[0] // 2)


def product_rows(vectors, tile_high, tile_low):
    width = vectors.shape[0]
    high, low = halves(vectors)
    both = jnp.concatenate([high, low], axis=0)
    product = dot(both, tile_high[...], 1, 1)
    return product[:width] + product[width:] + dot(high, tile_low[...], 1, 1)


def stacked(product):
    size = product.shape[1] // 2
    return jnp.concatenate([product[:, :size], product[:, size:]], axis=0)


def own_product_body(vectors, h0, l0, out):
    out[...] = stacked(product_rows(vectors[:vectors.shape[0] // 2, :], h0, l0))


def add_blocks(product, near, behind, h1, l1, h2, l2, total):
    width = near.shape[0] // 2
    far = product_rows(near[:width], h1, l1) + product_rows(near[width:], h2, l2)
    total[...] = product[...] + behind[...] + stacked(far)


def first_block_body(product, near_seeds, near_scale, *refs):
    add_blocks(product, near_seeds[...] * per_row(near_scale[...], near_seeds.shape[0] // 2), *refs)


def block_body(product, near, *refs):
    add_blocks(product, near[...], *refs)


def low_body(degree, v0, v1, v2, moments, scaled):
    width = v0.shape[0] // 2
    root = jnp.sqrt(degree[0:1, :])
    x0, x1, x2 = v0[:width, :] * root, v1[:width, :] * root, v2[:width, :] * root
    scaled[...] = jnp.concatenate([x0, x1, x2], axis=0)
    left = jnp.concatenate([x0, x1], axis=0)
    order012 = dot(left, left, 1, 1)
    order34 = dot(jnp.concatenate([x1, x2], axis=0), x2, 1, 1)
    order = [order012[:width, :width], order012[:width, width:], order012[width:, width:],
             order34[:width], order34[width:]]
    for i in range(5):
        moments[i * width:(i + 1) * width, :] = order[i]


def place_of(rows, cols):
    return [lax.broadcasted_iota(jnp.int32, (rows, cols), axis) for axis in range(2)]


def moment_body(core, low, vectors, product, near, h1, l1, h2, l2, mine, theirs):
    n = vectors.shape[0] // 2
    last = product_rows(near[:n, :], h1, l1) + product_rows(near[n:, :], h2, l2)
    last = 2.0 * last + jnp.concatenate([product[:n, :], product[n:, :]], axis=1)
    last = dot(jnp.concatenate([vectors[:n, :], vectors[n:, :]], axis=1), last, 1, 1)
    moments = [low[i * n:(i + 1) * n, :] for i in range(5)] + [0.5 * (last + last.T)]
    row, col = place_of(n, n)
    pieces = []
    for i in range(0, 6, 2):
        pair = jnp.where(row >= col, moments[i], moments[i + 1])
        pieces.append(jnp.concatenate([pair[:n // 2], pair[n // 2:]], axis=1))
    d1, d3, d5 = (jnp.sum(moments[i] * unit(n, n), axis=0, keepdims=True) for i in (1, 3, 5))
    row, _ = place_of(8, 2 * n)
    pieces.append(jnp.where(row == 0, jnp.concatenate([d1, d3], axis=1),
                            jnp.where(row == 1, jnp.concatenate([d5, d5], axis=1), 0.0)))
    pieces.append(jnp.zeros((8, 2 * n), F32))
    packed = jnp.concatenate(pieces, axis=0)
    half = packed.shape[0] // 2
    first = core[0] == 0
    mine[...] = jnp.where(first, packed[:half], packed[half:])
    theirs[...] = jnp.where(first, packed[half:], packed[:half])


def unpacked(packed, n):
    row, col = place_of(n, n)
    start = 3 * n // 2
    diagonals = [packed[start:start + 1, :n], packed[start:start + 1, n:], packed[start + 1:start + 2, :n]]
    moments = []
    for i in range(3):
        folded = packed[i * n // 2:(i + 1) * n // 2]
        pair = jnp.concatenate([folded[:, :n], folded[:, n:]], axis=0)
        flipped = pair.T
        moments.append(jnp.where(row >= col, pair, flipped))
        moments.append(jnp.where(row == col, diagonals[i], jnp.where(row < col, pair, flipped)))
    return moments


def unit(rows, cols):
    return (lax.broadcasted_iota(jnp.int32, (rows, cols), 0)
            == lax.broadcasted_iota(jnp.int32, (rows, cols), 1)).astype(F32)


def lane(values, k):
    return jnp.take_along_axis(values, jnp.full(values.shape, k, jnp.int32), axis=1, mode="promise_in_bounds")


def sublane(values, k):
    return jnp.broadcast_to(values[k:k + 1, :], values.shape)


def inverse_factor(matrix):
    size = matrix.shape[0]
    work = jnp.concatenate([matrix, unit(size, size)], axis=1)
    blocks = [work[8 * i:8 * i + 8, :] for i in range(size // 8)]
    place = lax.broadcasted_iota(jnp.int32, (8, 2 * size), 0)
    done = [None] * (size // 8)
    for k in range(0, size, 4):
        top, r = divmod(k, 8)
        pivot = blocks[top]
        cols = [lane(pivot, k + j) for j in range(4)]
        u0, u1, u2, u3 = (sublane(pivot, r + j) for j in range(4))
        a00, a10, a20, a30 = (sublane(cols[0], r + j) for j in range(4))
        a11, a21, a31 = (sublane(cols[1], r + j) for j in range(1, 4))
        a22, a32 = (sublane(cols[2], r + j) for j in range(2, 4))
        a33 = sublane(cols[3], r + 3)
        det_a = a00 * a11 - a10 * a10
        inv_a = 1.0 / det_a
        p00, p10, p11 = a11 * inv_a, a10 * inv_a, a00 * inv_a
        b00, b01 = a20 * p00 - a21 * p10, a21 * p11 - a20 * p10
        b10, b11 = a30 * p00 - a31 * p10, a31 * p11 - a30 * p10
        s00 = a22 - b00 * a20 - b01 * a21
        s10 = a32 - b10 * a20 - b11 * a21
        s11 = a33 - b10 * a30 - b11 * a31
        det_s = s00 * s11 - s10 * s10
        inv_s = 1.0 / det_s
        u2 = u2 - b00 * u0 - b01 * u1
        u3 = u3 - b10 * u0 - b11 * u1
        t2 = (s11 * u2 - s10 * u3) * inv_s
        t3 = (s00 * u3 - s10 * u2) * inv_s
        t0 = (p00 * u0 - p10 * u1) - b00 * t2 - b10 * t3
        t1 = (p11 * u1 - p10 * u0) - b01 * t2 - b11 * t3
        for i in range(top, size // 8):
            if i == top:
                if r:
                    continue
                c = cols
            else:
                c = [lane(blocks[i], k + j) for j in range(4)]
            change = (c[0] * t0 + c[1] * t1) + (c[2] * t2 + c[3] * t3)
            blocks[i] = blocks[i] - (jnp.where(place > 3, change, 0.0) if i == top else change)
        v0 = u0 * lax.rsqrt(a00)
        v1 = (a00 * u1 - a10 * u0) * lax.rsqrt(a00 * det_a)
        v2 = u2 * lax.rsqrt(s00)
        v3 = (s00 * u3 - s10 * u2) * lax.rsqrt(s00 * det_s)
        four = jnp.where(place % 4 == 0, v0, jnp.where(place % 4 == 1, v1, jnp.where(place % 4 == 2, v2, v3)))
        done[top] = jnp.where(place > 3, four, done[top]) if r else four
    return jnp.concatenate(done, axis=0)[:, size:]


def total(matrix):
    return jnp.sum(jnp.sum(matrix, axis=0, keepdims=True), axis=1, keepdims=True)


def trace(matrix):
    return total(matrix * unit(*matrix.shape))


def inverse_root(matrix):
    eye = unit(*matrix.shape)
    rest = matrix - eye

    def series():
        return eye - 0.5 * rest + 0.375 * dot(rest, rest)

    return lax.cond(jnp.sum(rest * rest) < 1e-4, series, lambda: inverse_factor(matrix))


def dense(moments, index, rows, data):
    n = NVEC
    eye = unit(n, n)
    pick = ((lax.broadcasted_iota(jnp.int32, (n, n), 0) == index)
            & (lax.broadcasted_iota(jnp.int32, (n, n), 1) == index)).astype(F32)

    def part(stacked, i):
        return stacked[i * n:(i + 1) * n]

    def below(*parts):
        return jnp.concatenate(parts, axis=0)

    def beside(*parts):
        return jnp.concatenate(parts, axis=1)

    base = inverse_factor(moments[0])
    right = dot(below(*moments[1:]), base, 1, 1)
    m1, m2, m3, m4, m5 = (dot(base, part(right, i)) for i in range(5))
    y0, y1, y2 = (dot(base, part(data, i)) for i in range(3))

    by1 = dot(below(m1, m2, m3, m4), m1)
    square, m21, m31, m41 = (part(by1, i) for i in range(4))
    tri = dot(m1, beside(square, m21, m31))
    gram_r = m2 - square
    image_r = m3 - m21 - m21.T + tri[:, :n]
    mixed_r = m3 - m21
    square_r = m4 - m31 - m31.T + tri[:, n:2 * n]
    cubic_r = m5 - m41 - m41.T + tri[:, 2 * n:]
    shift = 3.0 - total(m1 * pick)
    ridge = RIDGE_WEIGHT * (n + trace(gram_r)) / (2 * n)
    ridged = gram_r + ridge * eye
    factor = inverse_factor(ridged)
    inverse = dot(factor, factor, 0, 0)
    keep = 1.0 / (1.0 + ridge)
    step = below(
        beside(m1 * keep + shift * eye, gram_r * keep),
        beside(eye - ridge * inverse, dot(inverse, image_r) + shift * eye),
    )
    twice = dot(step, step)
    power = dot(twice, dot(twice, twice[:, :n]))
    top, bottom = power[:n], power[n:]
    weighted = dot(below(ridged, gram_r, image_r), bottom)
    norm = (1.0 + ridge) * dot(top, top, 0, 0) + dot(bottom, part(weighted, 0), 0, 0)
    factor = inverse_factor(norm)

    middle = m4 - m31
    images = dot(below(
        beside(m1, gram_r), beside(gram_r, image_r),
        beside(m2, mixed_r), beside(mixed_r.T, square_r),
        beside(m3, middle), beside(middle.T, cubic_r),
    ), power)
    whole = dot(power, beside(images[:2 * n], images[2 * n:4 * n], images[4 * n:], power), 0, 0)
    lower = dot(bottom, beside(part(images, 1), part(images, 3), part(weighted, 1), part(weighted, 2)), 0, 0)
    raw = [whole[:, i * n:(i + 1) * n] for i in range(4)] + [lower[:, i * n:(i + 1) * n] for i in range(4)]
    right = dot(below(*raw), factor, 1, 1)
    ritz, image2, image3, excess, p_image, p_image2, p_gram, p_ritz = (dot(factor, part(right, i)) for i in range(8))
    excess = ridge * excess

    shift = 3.0 - total(ritz * pick)
    by_ritz = dot(below(ritz, p_gram, excess, p_image, image2), ritz)
    squared, gram_pr, gram_cr = part(by_ritz, 0), p_image - part(by_ritz, 1), part(by_ritz, 2)
    tri = dot(ritz, squared), dot(ritz, gram_cr)
    gram_rr = image2 - squared - tri[1]
    image_cr = image2 - squared
    image_pr = p_image2 - part(by_ritz, 3)
    image_rr = image3 - part(by_ritz, 4) - part(by_ritz, 4).T + tri[0]
    ridge = RIDGE_WEIGHT * (n - trace(excess) + trace(p_gram) + trace(gram_rr)) / (3 * n)
    g_cc = eye - excess + ridge * eye
    g_pp = p_gram + ridge * eye
    g_rr = gram_rr + ridge * eye
    image_gram = below(
        beside(ritz, p_image.T, image_cr), beside(p_image, p_ritz, image_pr), beside(image_cr.T, image_pr.T, image_rr),
    )
    v0 = inverse_root(g_cc)
    side = dot(below(p_gram, gram_cr.T), v0, 1, 1)
    l10, l20 = side[:n], side[n:]
    outer = dot(side, side, 1, 1)
    v1 = inverse_factor(g_pp - outer[:n, :n])
    l21 = dot(gram_pr.T - outer[n:, :n], v1, 1, 1)
    v2 = inverse_factor(g_rr - outer[n:, n:] - dot(l21, l21, 1, 1))
    zero = jnp.zeros((n, n), F32)
    row0 = beside(v0, zero, zero)
    row1 = dot(v1, beside(-dot(l10, v0), eye, zero))
    row2 = beside(zero, zero, eye) - dot(l20, row0) - dot(l21, row1)
    known = below(row0, row1)
    solved = dot(known, dot(known, image_gram), 0, 0)
    row2 = dot(v2, beside(row2, dot(row2, image_gram)))
    step = solved + dot(row2[:, :3 * n], row2[:, 3 * n:], 0, 0) + shift * unit(3 * n, 3 * n)
    twice = dot(step, step)
    power2 = dot(twice, dot(twice, twice[:, :n]))
    gram = below(
        beside(g_cc, p_gram, gram_cr), beside(p_gram, g_pp, gram_pr), beside(gram_cr.T, gram_pr.T, g_rr),
    )
    norm = dot(power2, dot(gram, power2), 0, 0)

    start = dot(power, below(y0, y1), 0, 0) - dot(dot(m1, bottom), y0, 0, 0)
    image = dot(power, below(y1, y2), 0, 0) - dot(dot(m1, bottom), y1, 0, 0)
    residue = dot(bottom, y1 - dot(m1, y0), 0, 0)
    current = dot(factor, start)
    vectors = below(current, dot(factor, residue), dot(factor, image) - dot(ritz, current))
    return dot(inverse_factor(norm), dot(power2, vectors, 0, 0)) * math.sqrt(rows)


def dense_body(rows, core, index, mine, theirs, scaled, out):
    first = core[0] == 0
    packed = jnp.concatenate([
        jnp.where(first, mine[...], theirs[...]), jnp.where(first, theirs[...], mine[...])], axis=0)
    out[...] = dense(unpacked(packed, NVEC), index[0], rows, scaled[...])


def between_blocks(shard, sign):
    blocks, cores = lax.axis_size("blk"), lax.axis_size("narrow")
    pairs = [(i * cores + j, (i + sign * (1 + j)) % blocks * cores + j) for i in range(blocks) for j in range(cores)]
    return lax.ppermute(shard, ("blk", "narrow"), pairs)


def between_cores(shard):
    return lax.ppermute(shard, "narrow", [(0, 1), (1, 0)])


def total_over_blocks(values):
    blocks = lax.axis_size("blk")

    def exchanged(distance):
        return lax.ppermute(values, "blk", [(i, i ^ distance) for i in range(blocks)])

    span = 1
    while blocks % (4 * span) == 0:
        first, second, third = exchanged(span), exchanged(2 * span), exchanged(3 * span)
        values = (values + first) + (second + third)
        span *= 4
    if blocks % (2 * span) == 0:
        values = values + exchanged(span)
        span *= 2
    if span < blocks:
        groups = [list(range(i, blocks, span)) for i in range(span)]
        values = lax.psum(values, "blk", axis_index_groups=groups)
    return values


def shards(embeddings, pair_mask, shift_index, start_seed):
    size = embeddings.shape[0]
    blocks = lax.axis_size("blk")
    where = lax.axis_index("blk")
    core = lax.axis_index("narrow").astype(jnp.int32).reshape(1)
    other_emb = between_cores(embeddings)
    far_emb = between_blocks(embeddings, -1)
    emb_args = [embeddings, other_emb]
    pair_shape, row_shape = ((2 * NVEC, size), F32), ((16, size), F32)
    h0, l0, sums, row_sq = make_tile(own_body, emb_args, size, extra=(((2 * size, 128), F32),))
    far_emb, sums = lax.optimization_barrier((far_emb, sums))
    pairs = [(2 * i, (i - 2) % blocks * 2 + 1) for i in range(blocks)]
    pairs += [(2 * i + 1, (i - 1) % blocks * 2) for i in range(blocks) if blocks % 2 or i % 2]
    direct = lax.ppermute(embeddings, ("blk", "narrow"), pairs)
    relayed = direct
    if blocks % 2 == 0:
        relayed = lax.ppermute(far_emb, ("blk", "narrow"), [(2 * i + 1, 2 * i + 2) for i in range(0, blocks, 2)])
    choice = (1 - core) * (where % 2 * (1 - blocks % 2)).astype(jnp.int32)
    keep = lax.dynamic_slice(pair_mask, (where, core[0]), (1, 1))[0]
    h1, l1, sums, cols = make_tile(
        far_body, [keep, *emb_args, row_sq, far_emb, sums], size, (0,), (((8, size), F32),))
    seed16 = start_seed.astype(jnp.int16).T
    seeds = jnp.concatenate([seed16, between_cores(seed16)], axis=0)
    near_seeds, sums = lax.optimization_barrier((seeds, sums))
    near_seeds = between_blocks(near_seeds, -1)
    h2, l2, sums, cols, near_seeds = make_tile(
        relayed_body, [keep, choice, *emb_args, row_sq, direct, relayed, sums, cols, near_seeds], size, (0, 1),
        (row_shape, pair_shape))
    sums = sums + between_blocks(cols, 1)

    small = dict(flops=10**6, nbytes=10**5)
    middle = dict(flops=10**9, nbytes=10**6)
    degree, scale, vectors = call(
        degree_body, [row_shape, row_shape, pair_shape], [sums, between_cores(sums), seeds], **small)
    far = [h1, l1, h2, l2]
    history = [vectors]
    for repeat in range(2):
        if repeat == 0:
            body, near = first_block_body, [near_seeds, between_blocks(scale, -1)]
        else:
            body, near = block_body, [between_blocks(vectors, -1)]
        (ahead,) = call(ahead_body, [pair_shape], [vectors, *far], **middle)
        behind = between_blocks(ahead, 1)
        (product,) = call(own_product_body, [pair_shape], [vectors, h0, l0], **middle)
        (total,) = call(body, [pair_shape], [product, *near, behind, *far], **middle)
        (vectors,) = call(combine_body, [pair_shape], [total, between_cores(total), degree], **small)
        history.append(vectors)
    near = between_blocks(vectors, -1)
    low, scaled = call(
        low_body, [((5 * NVEC, NVEC), F32), ((3 * NVEC, size), F32)], [degree] + history, **middle)
    (product,) = call(own_product_body, [pair_shape], [vectors, h0, l0], **middle)
    packed_shape = ((3 * NVEC // 4 + 8, 2 * NVEC), F32)
    mine, theirs = call(
        moment_body, [packed_shape] * 2, [core, low, vectors, product, near, *far], smem=(0,), **middle)
    mine = total_over_blocks(mine + between_cores(theirs))
    rows = size * blocks * lax.axis_size("narrow")
    (out,) = call(
        lambda *refs: dense_body(rows, *refs), [((NVEC, size), F32)],
        [core, shift_index, mine, between_cores(mine), scaled], smem=(0, 1), flops=2 * 10**10, nbytes=10**6,
    )
    return out.T


def solution(mesh):
    return jax.shard_map(
        shards,
        mesh=mesh,
        in_specs=(
            P(("groups", "blk", "narrow"), None),
            P("groups", None),
            P("groups"),
            P(("groups", "blk", "narrow"), None),
        ),
        out_specs=P(("groups", "blk", "narrow"), None),
        check_vma=False,
    )
```

```python
import math

import jax
import jax.numpy as jnp
from jax import lax
from jax.experimental import pallas as pl
from jax.experimental.pallas import tpu as pltpu
from jax.sharding import PartitionSpec as P

KERNEL_GAMMA = 2.0
RIDGE_WEIGHT = 1e-05
NVEC = 64
F32 = jnp.float32
BF16 = jnp.bfloat16
VMEM_LIMIT = 16 * 1024 * 1024


def dot(left, right, left_dim=1, right_dim=0):
    precision = lax.Precision.HIGHEST if left.dtype == F32 else None
    return lax.dot_general(
        left, right, (((left_dim,), (right_dim,)), ((), ())),
        precision=precision, preferred_element_type=F32,
    )


def halves(values):
    high = values.astype(BF16)
    return high, (values - high.astype(F32)).astype(BF16)


def call(body, out_shapes, args, smem=(), flops=0, nbytes=0):
    specs = [
        pl.BlockSpec(memory_space=pltpu.SMEM if i in smem else pltpu.VMEM)
        for i in range(len(args))
    ]
    out = pl.pallas_call(
        body,
        out_shape=[jax.ShapeDtypeStruct(shape, dtype) for shape, dtype in out_shapes],
        in_specs=specs,
        out_specs=[pl.BlockSpec(memory_space=pltpu.VMEM) for _ in out_shapes],
        compiler_params=pltpu.CompilerParams(vmem_limit_bytes=VMEM_LIMIT),
        cost_estimate=pl.CostEstimate(flops=flops, bytes_accessed=nbytes, transcendentals=0),
    )(*args)
    return out


LOG2_E = 1.4426950408889634


def sums_along(values):
    rows, depth = values.shape
    folded = values[:, :128]
    for j in range(128, depth, 128):
        folded = folded + values[:, j:j + 128]
    return dot(jnp.ones((8, 128), F32), folded, 1, 1)


def fill_tile(weight, row_embs, row_sq, col_emb, high, low, row_sum):
    size = col_emb.shape[0]
    col32 = col_emb.astype(F32)
    col_sq = (2.0 * LOG2_E) * sums_along(col32 * col32)[0:1, :]
    total = jnp.zeros((1, size), F32)
    for half in range(2):
        rows = slice(half * size, (half + 1) * size)
        inner = dot(row_embs[half], col_emb, 1, 1)
        squares = jnp.concatenate([row_sq[rows, :]] * (size // 128), axis=1)
        tile = jnp.exp2((4.0 * LOG2_E) * inner - (squares + col_sq)) * weight
        tile_high, tile_low = halves(tile)
        high[rows, :] = tile_high
        low[rows, :] = tile_low
        row_sum[half * 8:(half + 1) * 8, :] = row_sum[half * 8:(half + 1) * 8, :] + sums_along(tile)
        total = total + jnp.sum(tile, axis=0, keepdims=True)
    return jnp.broadcast_to(total, (8, size))


def seed_values(seeds):
    return seeds[...].astype(jnp.int32).astype(F32) / 1000.0


def own_body(own, other, high, low, row_sum, row_sq):
    size = own.shape[0]
    embs = [own[...], other[...]]
    for half in range(2):
        row32 = embs[half].astype(F32)
        squares = (2.0 * LOG2_E) * jnp.sum(row32 * row32, axis=1, keepdims=True)
        row_sq[half * size:(half + 1) * size, :] = jnp.broadcast_to(squares, (size, 128))
    row_sum[...] = jnp.zeros(row_sum.shape, F32)
    fill_tile(1.0, embs, row_sq, embs[0], high, low, row_sum)


def far_body(keep, own, other, row_sq, col, before, near_seeds, high, low, row_sum, col_sum, near_seeds_out):
    row_sum[...] = before[...]
    near_seeds_out[...] = seed_values(near_seeds)
    col_sum[...] = fill_tile(keep[0].astype(F32), [own[...], other[...]], row_sq, col[...], high, low, row_sum)


def relayed_body(keep, choice, own, other, row_sq, direct, relayed, before, first_cols,
                 high, low, row_sum, col_sum):
    row_sum[...] = before[...]
    col = jnp.where(choice[0] > 0, relayed[...], direct[...])
    col_sum[:8, :] = first_cols[...]
    col_sum[8:, :] = fill_tile(keep[0].astype(F32), [own[...], other[...]], row_sq, col, high, low, row_sum)


def make_tile(body, args, rows, smem=(), extra=()):
    return call(
        body, [((2 * rows, rows), BF16), ((2 * rows, rows), BF16), ((16, rows), F32), *extra],
        args, smem=smem, flops=2 * 10**9, nbytes=10**6,
    )


def swapped(values):
    middle = values.shape[0] // 2
    return jnp.concatenate([values[middle:], values[:middle]], axis=0)


def per_row(values, width):
    shape = (width, values.shape[1])
    return jnp.concatenate([jnp.broadcast_to(values[i:i + 1, :], shape) for i in (0, 8)], axis=0)


def degree_body(sums, other_sums, seeds, degree_out, scale_out, vectors_out):
    degree = sums[...] + swapped(other_sums[...])
    scale = lax.rsqrt(degree)
    degree_out[...] = degree
    scale_out[...] = scale
    vectors_out[...] = seed_values(seeds) * per_row(scale, seeds.shape[0] // 2)


def ahead_body(vectors, h1, l1, h2, l2, ahead):
    width = vectors.shape[0] // 2
    high, low = halves(jnp.concatenate([vectors[:width, :], vectors[width:, :]], axis=1))
    both = jnp.concatenate([high, low], axis=0)
    for half, (tile_high, tile_low) in enumerate(((h1, l1), (h2, l2))):
        product = dot(both, tile_high[...])
        product = product[:width] + product[width:] + dot(high, tile_low[...])
        ahead[half * width:(half + 1) * width, :] = product


def combine_body(total, other_total, degree, vectors_out):
    vectors_out[...] = (total[...] + swapped(other_total[...])) / per_row(degree[...], total.shape[0] // 2)


def product_rows(vectors, tile_high, tile_low):
    width = vectors.shape[0]
    high, low = halves(vectors)
    both = jnp.concatenate([high, low], axis=0)
    product = dot(both, tile_high[...], 1, 1)
    return product[:width] + product[width:] + dot(high, tile_low[...], 1, 1)


def stacked(product):
    size = product.shape[1] // 2
    return jnp.concatenate([product[:, :size], product[:, size:]], axis=0)


def own_product_body(vectors, h0, l0, out):
    out[...] = stacked(product_rows(vectors[:vectors.shape[0] // 2, :], h0, l0))


def add_blocks(product, near, behind, h1, l1, h2, l2, total):
    width = near.shape[0] // 2
    far = product_rows(near[:width], h1, l1) + product_rows(near[width:], h2, l2)
    total[...] = product[...] + behind[...] + stacked(far)


def first_block_body(product, near_seeds, near_scale, *refs):
    add_blocks(product, near_seeds[...] * per_row(near_scale[...], near_seeds.shape[0] // 2), *refs)


def block_body(product, near, *refs):
    add_blocks(product, near[...], *refs)


def low_body(degree, v0, v1, v2, moments, scaled):
    width = v0.shape[0] // 2
    root = jnp.sqrt(degree[0:1, :])
    x0, x1, x2 = v0[:width, :] * root, v1[:width, :] * root, v2[:width, :] * root
    scaled[...] = jnp.concatenate([x0, x1, x2], axis=0)
    left = jnp.concatenate([x0, x1], axis=0)
    order012 = dot(left, left, 1, 1)
    order34 = dot(jnp.concatenate([x1, x2], axis=0), x2, 1, 1)
    order = [order012[:width, :width], order012[:width, width:], order012[width:, width:],
             order34[:width], order34[width:]]
    for i in range(5):
        moments[i * width:(i + 1) * width, :] = order[i]


def place_of(rows, cols):
    return [lax.broadcasted_iota(jnp.int32, (rows, cols), axis) for axis in range(2)]


def moment_body(core, low, vectors, product, near, h1, l1, h2, l2, mine, theirs):
    n = vectors.shape[0] // 2
    last = product_rows(near[:n, :], h1, l1) + product_rows(near[n:, :], h2, l2)
    last = 2.0 * last + jnp.concatenate([product[:n, :], product[n:, :]], axis=1)
    last = dot(jnp.concatenate([vectors[:n, :], vectors[n:, :]], axis=1), last, 1, 1)
    moments = [low[i * n:(i + 1) * n, :] for i in range(5)] + [0.5 * (last + last.T)]
    row, col = place_of(n, n)
    pieces = []
    for i in range(0, 6, 2):
        pair = jnp.where(row >= col, moments[i], moments[i + 1])
        pieces.append(jnp.concatenate([pair[:n // 2], pair[n // 2:]], axis=1))
    d1, d3, d5 = (jnp.sum(moments[i] * unit(n, n), axis=0, keepdims=True) for i in (1, 3, 5))
    row, _ = place_of(8, 2 * n)
    pieces.append(jnp.where(row == 0, jnp.concatenate([d1, d3], axis=1),
                            jnp.where(row == 1, jnp.concatenate([d5, d5], axis=1), 0.0)))
    pieces.append(jnp.zeros((8, 2 * n), F32))
    packed = jnp.concatenate(pieces, axis=0)
    half = packed.shape[0] // 2
    first = core[0] == 0
    mine[...] = jnp.where(first, packed[:half], packed[half:])
    theirs[...] = jnp.where(first, packed[half:], packed[:half])


def unpacked(packed, n):
    row, col = place_of(n, n)
    start = 3 * n // 2
    diagonals = [packed[start:start + 1, :n], packed[start:start + 1, n:], packed[start + 1:start + 2, :n]]
    moments = []
    for i in range(3):
        folded = packed[i * n // 2:(i + 1) * n // 2]
        pair = jnp.concatenate([folded[:, :n], folded[:, n:]], axis=0)
        flipped = pair.T
        moments.append(jnp.where(row >= col, pair, flipped))
        moments.append(jnp.where(row == col, diagonals[i], jnp.where(row < col, pair, flipped)))
    return moments


def unit(rows, cols):
    return (lax.broadcasted_iota(jnp.int32, (rows, cols), 0)
            == lax.broadcasted_iota(jnp.int32, (rows, cols), 1)).astype(F32)


def lane(values, k):
    return jnp.take_along_axis(values, jnp.full(values.shape, k, jnp.int32), axis=1, mode="promise_in_bounds")


def sublane(values, k):
    return jnp.broadcast_to(values[k:k + 1, :], values.shape)


def inverse_factor(matrix):
    size = matrix.shape[0]
    work = jnp.concatenate([matrix, unit(size, size)], axis=1)
    blocks = [work[8 * i:8 * i + 8, :] for i in range(size // 8)]
    place = lax.broadcasted_iota(jnp.int32, (8, 2 * size), 0)
    done = [None] * (size // 8)
    for k in range(0, size, 4):
        top, r = divmod(k, 8)
        pivot = blocks[top]
        cols = [lane(pivot, k + j) for j in range(4)]
        u0, u1, u2, u3 = (sublane(pivot, r + j) for j in range(4))
        a00, a10, a20, a30 = (sublane(cols[0], r + j) for j in range(4))
        a11, a21, a31 = (sublane(cols[1], r + j) for j in range(1, 4))
        a22, a32 = (sublane(cols[2], r + j) for j in range(2, 4))
        a33 = sublane(cols[3], r + 3)
        det_a = a00 * a11 - a10 * a10
        inv_a = 1.0 / det_a
        p00, p10, p11 = a11 * inv_a, a10 * inv_a, a00 * inv_a
        b00, b01 = a20 * p00 - a21 * p10, a21 * p11 - a20 * p10
        b10, b11 = a30 * p00 - a31 * p10, a31 * p11 - a30 * p10
        s00 = a22 - b00 * a20 - b01 * a21
        s10 = a32 - b10 * a20 - b11 * a21
        s11 = a33 - b10 * a30 - b11 * a31
        det_s = s00 * s11 - s10 * s10
        inv_s = 1.0 / det_s
        u2 = u2 - b00 * u0 - b01 * u1
        u3 = u3 - b10 * u0 - b11 * u1
        t2 = (s11 * u2 - s10 * u3) * inv_s
        t3 = (s00 * u3 - s10 * u2) * inv_s
        t0 = (p00 * u0 - p10 * u1) - b00 * t2 - b10 * t3
        t1 = (p11 * u1 - p10 * u0) - b01 * t2 - b11 * t3
        for i in range(top, size // 8):
            if i == top:
                if r:
                    continue
                c = cols
            else:
                c = [lane(blocks[i], k + j) for j in range(4)]
            change = (c[0] * t0 + c[1] * t1) + (c[2] * t2 + c[3] * t3)
            blocks[i] = blocks[i] - (jnp.where(place > 3, change, 0.0) if i == top else change)
        v0 = u0 * lax.rsqrt(a00)
        v1 = (a00 * u1 - a10 * u0) * lax.rsqrt(a00 * det_a)
        v2 = u2 * lax.rsqrt(s00)
        v3 = (s00 * u3 - s10 * u2) * lax.rsqrt(s00 * det_s)
        four = jnp.where(place % 4 == 0, v0, jnp.where(place % 4 == 1, v1, jnp.where(place % 4 == 2, v2, v3)))
        done[top] = jnp.where(place > 3, four, done[top]) if r else four
    return jnp.concatenate(done, axis=0)[:, size:]


def total(matrix):
    return jnp.sum(jnp.sum(matrix, axis=0, keepdims=True), axis=1, keepdims=True)


def trace(matrix):
    return total(matrix * unit(*matrix.shape))


def inverse_root(matrix):
    eye = unit(*matrix.shape)
    rest = matrix - eye

    def series():
        return eye - 0.5 * rest + 0.375 * dot(rest, rest)

    return lax.cond(jnp.sum(rest * rest) < 1e-4, series, lambda: inverse_factor(matrix))


def dense(moments, index, rows, data):
    n = NVEC
    eye = unit(n, n)
    pick = ((lax.broadcasted_iota(jnp.int32, (n, n), 0) == index)
            & (lax.broadcasted_iota(jnp.int32, (n, n), 1) == index)).astype(F32)

    def part(stacked, i):
        return stacked[i * n:(i + 1) * n]

    def below(*parts):
        return jnp.concatenate(parts, axis=0)

    def beside(*parts):
        return jnp.concatenate(parts, axis=1)

    base = inverse_factor(moments[0])
    right = dot(below(*moments[1:]), base, 1, 1)
    m1, m2, m3, m4, m5 = (dot(base, part(right, i)) for i in range(5))
    y0, y1, y2 = (dot(base, part(data, i)) for i in range(3))

    by1 = dot(below(m1, m2, m3, m4), m1)
    square, m21, m31, m41 = (part(by1, i) for i in range(4))
    tri = dot(m1, beside(square, m21, m31))
    gram_r = m2 - square
    image_r = m3 - m21 - m21.T + tri[:, :n]
    mixed_r = m3 - m21
    square_r = m4 - m31 - m31.T + tri[:, n:2 * n]
    cubic_r = m5 - m41 - m41.T + tri[:, 2 * n:]
    shift = 3.0 - total(m1 * pick)
    ridge = RIDGE_WEIGHT * (n + trace(gram_r)) / (2 * n)
    ridged = gram_r + ridge * eye
    factor = inverse_factor(ridged)
    inverse = dot(factor, factor, 0, 0)
    keep = 1.0 / (1.0 + ridge)
    step = below(
        beside(m1 * keep + shift * eye, gram_r * keep),
        beside(eye - ridge * inverse, dot(inverse, image_r) + shift * eye),
    )
    twice = dot(step, step)
    power = dot(twice, dot(twice, twice[:, :n]))
    top, bottom = power[:n], power[n:]
    weighted = dot(below(ridged, gram_r, image_r), bottom)
    norm = (1.0 + ridge) * dot(top, top, 0, 0) + dot(bottom, part(weighted, 0), 0, 0)
    factor = inverse_factor(norm)

    middle = m4 - m31
    images = dot(below(
        beside(m1, gram_r), beside(gram_r, image_r),
        beside(m2, mixed_r), beside(mixed_r.T, square_r),
        beside(m3, middle), beside(middle.T, cubic_r),
    ), power)
    whole = dot(power, beside(images[:2 * n], images[2 * n:4 * n], images[4 * n:], power), 0, 0)
    lower = dot(bottom, beside(part(images, 1), part(images, 3), part(weighted, 1), part(weighted, 2)), 0, 0)
    raw = [whole[:, i * n:(i + 1) * n] for i in range(4)] + [lower[:, i * n:(i + 1) * n] for i in range(4)]
    right = dot(below(*raw), factor, 1, 1)
    ritz, image2, image3, excess, p_image, p_image2, p_gram, p_ritz = (dot(factor, part(right, i)) for i in range(8))
    excess = ridge * excess

    shift = 3.0 - total(ritz * pick)
    by_ritz = dot(below(ritz, p_gram, excess, p_image, image2), ritz)
    squared, gram_pr, gram_cr = part(by_ritz, 0), p_image - part(by_ritz, 1), part(by_ritz, 2)
    tri = dot(ritz, squared), dot(ritz, gram_cr)
    gram_rr = image2 - squared - tri[1]
    image_cr = image2 - squared
    image_pr = p_image2 - part(by_ritz, 3)
    image_rr = image3 - part(by_ritz, 4) - part(by_ritz, 4).T + tri[0]
    ridge = RIDGE_WEIGHT * (n - trace(excess) + trace(p_gram) + trace(gram_rr)) / (3 * n)
    g_cc = eye - excess + ridge * eye
    g_pp = p_gram + ridge * eye
    g_rr = gram_rr + ridge * eye
    image_gram = below(
        beside(ritz, p_image.T, image_cr), beside(p_image, p_ritz, image_pr), beside(image_cr.T, image_pr.T, image_rr),
    )
    v0 = inverse_root(g_cc)
    side = dot(below(p_gram, gram_cr.T), v0, 1, 1)
    l10, l20 = side[:n], side[n:]
    outer = dot(side, side, 1, 1)
    v1 = inverse_factor(g_pp - outer[:n, :n])
    l21 = dot(gram_pr.T - outer[n:, :n], v1, 1, 1)
    v2 = inverse_factor(g_rr - outer[n:, n:] - dot(l21, l21, 1, 1))
    zero = jnp.zeros((n, n), F32)
    row0 = beside(v0, zero, zero)
    row1 = dot(v1, beside(-dot(l10, v0), eye, zero))
    row2 = beside(zero, zero, eye) - dot(l20, row0) - dot(l21, row1)
    known = below(row0, row1)
    solved = dot(known, dot(known, image_gram), 0, 0)
    row2 = dot(v2, beside(row2, dot(row2, image_gram)))
    step = solved + dot(row2[:, :3 * n], row2[:, 3 * n:], 0, 0) + shift * unit(3 * n, 3 * n)
    twice = dot(step, step)
    power2 = dot(twice, dot(twice, twice[:, :n]))
    gram = below(
        beside(g_cc, p_gram, gram_cr), beside(p_gram, g_pp, gram_pr), beside(gram_cr.T, gram_pr.T, g_rr),
    )
    norm = dot(power2, dot(gram, power2), 0, 0)

    start = dot(power, below(y0, y1), 0, 0) - dot(dot(m1, bottom), y0, 0, 0)
    image = dot(power, below(y1, y2), 0, 0) - dot(dot(m1, bottom), y1, 0, 0)
    residue = dot(bottom, y1 - dot(m1, y0), 0, 0)
    current = dot(factor, start)
    vectors = below(current, dot(factor, residue), dot(factor, image) - dot(ritz, current))
    return dot(inverse_factor(norm), dot(power2, vectors, 0, 0)) * math.sqrt(rows)


def dense_body(rows, core, index, mine, theirs, scaled, out):
    first = core[0] == 0
    packed = jnp.concatenate([
        jnp.where(first, mine[...], theirs[...]), jnp.where(first, theirs[...], mine[...])], axis=0)
    out[...] = dense(unpacked(packed, NVEC), index[0], rows, scaled[...])


def between_blocks(shard, sign):
    blocks, cores = lax.axis_size("blk"), lax.axis_size("narrow")
    pairs = [(i * cores + j, (i + sign * (1 + j)) % blocks * cores + j) for i in range(blocks) for j in range(cores)]
    return lax.ppermute(shard, ("blk", "narrow"), pairs)


def between_cores(shard):
    return lax.ppermute(shard, "narrow", [(0, 1), (1, 0)])


def total_over_blocks(values):
    blocks = lax.axis_size("blk")
    if blocks <= 8:
        copies = jnp.broadcast_to(values[None], (blocks, *values.shape))
        return jnp.sum(lax.all_to_all(copies, "blk", 0, 0), axis=0)
    span = 1
    while blocks % (2 * span) == 0:
        values = values + lax.ppermute(values, "blk", [(i, i ^ span) for i in range(blocks)])
        span *= 2
    if span < blocks:
        groups = [list(range(i, blocks, span)) for i in range(span)]
        values = lax.psum(values, "blk", axis_index_groups=groups)
    return values


def shards(embeddings, pair_mask, shift_index, start_seed):
    size = embeddings.shape[0]
    blocks = lax.axis_size("blk")
    where = lax.axis_index("blk")
    core = lax.axis_index("narrow").astype(jnp.int32).reshape(1)
    other_emb = between_cores(embeddings)
    far_emb = between_blocks(embeddings, -1)
    seed16 = start_seed.astype(jnp.int16).T
    seeds = jnp.concatenate([seed16, between_cores(seed16)], axis=0)
    near_seeds = between_blocks(seeds, -1)
    keep = lax.dynamic_slice(pair_mask, (where, core[0]), (1, 1))[0]
    emb_args = [embeddings, other_emb]
    pair_shape, row_shape = ((2 * NVEC, size), F32), ((16, size), F32)
    h0, l0, sums, row_sq = make_tile(own_body, emb_args, size, extra=(((2 * size, 128), F32),))
    far_emb, sums, near_seeds, keep = lax.optimization_barrier((far_emb, sums, near_seeds, keep))
    second, sums = lax.optimization_barrier((embeddings, sums))
    pairs = [(2 * i, (i - 2) % blocks * 2 + 1) for i in range(blocks)]
    pairs += [(2 * i + 1, (i - 1) % blocks * 2) for i in range(blocks) if blocks % 2 or i % 2]
    direct = lax.ppermute(second, ("blk", "narrow"), pairs)
    relayed = direct
    if blocks % 2 == 0:
        relayed = lax.ppermute(far_emb, ("blk", "narrow"), [(2 * i + 1, 2 * i + 2) for i in range(0, blocks, 2)])
    choice = (1 - core) * (where % 2 * (1 - blocks % 2)).astype(jnp.int32)
    h1, l1, sums, cols, near_seeds = make_tile(
        far_body, [keep, *emb_args, row_sq, far_emb, sums, near_seeds], size, (0,), (((8, size), F32), pair_shape))
    h2, l2, sums, cols = make_tile(
        relayed_body, [keep, choice, *emb_args, row_sq, direct, relayed, sums, cols], size, (0, 1), (row_shape,))
    sums = sums + between_blocks(cols, 1)

    small = dict(flops=10**6, nbytes=10**5)
    middle = dict(flops=10**9, nbytes=10**6)
    degree, scale, vectors = call(
        degree_body, [row_shape, row_shape, pair_shape], [sums, between_cores(sums), seeds], **small)
    far = [h1, l1, h2, l2]
    history = [vectors]
    for repeat in range(2):
        if repeat == 0:
            body, near = first_block_body, [near_seeds, between_blocks(scale, -1)]
        else:
            body, near = block_body, [between_blocks(vectors, -1)]
        (ahead,) = call(ahead_body, [pair_shape], [vectors, *far], **middle)
        behind = between_blocks(ahead, 1)
        (product,) = call(own_product_body, [pair_shape], [vectors, h0, l0], **middle)
        (total,) = call(body, [pair_shape], [product, *near, behind, *far], **middle)
        (vectors,) = call(combine_body, [pair_shape], [total, between_cores(total), degree], **small)
        history.append(vectors)
    near = between_blocks(vectors, -1)
    low, scaled = call(
        low_body, [((5 * NVEC, NVEC), F32), ((3 * NVEC, size), F32)], [degree] + history, **middle)
    (product,) = call(own_product_body, [pair_shape], [vectors, h0, l0], **middle)
    packed_shape = ((3 * NVEC // 4 + 8, 2 * NVEC), F32)
    mine, theirs = call(
        moment_body, [packed_shape] * 2, [core, low, vectors, product, near, *far], smem=(0,), **middle)
    mine = total_over_blocks(mine + between_cores(theirs))
    rows = size * blocks * lax.axis_size("narrow")
    (out,) = call(
        lambda *refs: dense_body(rows, *refs), [((NVEC, size), F32)],
        [core, shift_index, mine, between_cores(mine), scaled], smem=(0, 1), flops=2 * 10**10, nbytes=10**6,
    )
    return out.T


def solution(mesh):
    return jax.shard_map(
        shards,
        mesh=mesh,
        in_specs=(
            P(("groups", "blk", "narrow"), None),
            P("groups", None),
            P("groups"),
            P(("groups", "blk", "narrow"), None),
        ),
        out_specs=P(("groups", "blk", "narrow"), None),
        check_vma=False,
    )
```

```python
import math

import jax
import jax.numpy as jnp
from jax import lax
from jax.experimental import pallas as pl
from jax.experimental.pallas import tpu as pltpu
from jax.sharding import PartitionSpec as P

KERNEL_GAMMA = 2.0
RIDGE_WEIGHT = 1e-05
NVEC = 64
F32 = jnp.float32
BF16 = jnp.bfloat16
VMEM_LIMIT = 16 * 1024 * 1024


def dot(left, right, left_dim=1, right_dim=0):
    precision = lax.Precision.HIGHEST if left.dtype == F32 else None
    return lax.dot_general(
        left, right, (((left_dim,), (right_dim,)), ((), ())),
        precision=precision, preferred_element_type=F32,
    )


def halves(values):
    high = values.astype(BF16)
    return high, (values - high.astype(F32)).astype(BF16)


def call(body, out_shapes, args, smem=(), flops=0, nbytes=0):
    specs = [
        pl.BlockSpec(memory_space=pltpu.SMEM if i in smem else pltpu.VMEM)
        for i in range(len(args))
    ]
    out = pl.pallas_call(
        body,
        out_shape=[jax.ShapeDtypeStruct(shape, dtype) for shape, dtype in out_shapes],
        in_specs=specs,
        out_specs=[pl.BlockSpec(memory_space=pltpu.VMEM) for _ in out_shapes],
        compiler_params=pltpu.CompilerParams(vmem_limit_bytes=VMEM_LIMIT),
        cost_estimate=pl.CostEstimate(flops=flops, bytes_accessed=nbytes, transcendentals=0),
    )(*args)
    return out


LOG2_E = 1.4426950408889634


def sums_along(values):
    rows, depth = values.shape
    folded = values[:, :128]
    for j in range(128, depth, 128):
        folded = folded + values[:, j:j + 128]
    return dot(jnp.ones((8, 128), F32), folded, 1, 1)


def fill_tile(weight, row_embs, row_sq, col_emb, high, low, row_sum):
    size = col_emb.shape[0]
    col32 = col_emb.astype(F32)
    col_sq = (2.0 * LOG2_E) * sums_along(col32 * col32)[0:1, :]
    total = jnp.zeros((1, size), F32)
    for half in range(2):
        rows = slice(half * size, (half + 1) * size)
        inner = dot(row_embs[half], col_emb, 1, 1)
        squares = jnp.concatenate([row_sq[rows, :]] * (size // 128), axis=1)
        tile = jnp.exp2((4.0 * LOG2_E) * inner - (squares + col_sq)) * weight
        tile_high, tile_low = halves(tile)
        high[rows, :] = tile_high
        low[rows, :] = tile_low
        row_sum[half * 8:(half + 1) * 8, :] = row_sum[half * 8:(half + 1) * 8, :] + sums_along(tile)
        total = total + jnp.sum(tile, axis=0, keepdims=True)
    return jnp.broadcast_to(total, (8, size))


def own_body(own, other, high, low, row_sum, row_sq, copy):
    size = own.shape[0]
    embs = [own[...], other[...]]
    copy[...] = embs[0]
    for half in range(2):
        row32 = embs[half].astype(F32)
        squares = (2.0 * LOG2_E) * jnp.sum(row32 * row32, axis=1, keepdims=True)
        row_sq[half * size:(half + 1) * size, :] = jnp.broadcast_to(squares, (size, 128))
    row_sum[...] = jnp.zeros(row_sum.shape, F32)
    fill_tile(1.0, embs, row_sq, embs[0], high, low, row_sum)


def far_body(keep, own, other, row_sq, col, before, high, low, row_sum, col_sum):
    row_sum[...] = before[...]
    col_sum[...] = fill_tile(keep[0].astype(F32), [own[...], other[...]], row_sq, col[...], high, low, row_sum)


def relayed_body(keep, choice, own, other, row_sq, direct, relayed, before, first_cols,
                 high, low, row_sum, col_sum):
    row_sum[...] = before[...]
    col = jnp.where(choice[0] > 0, relayed[...], direct[...])
    col_sum[:8, :] = first_cols[...]
    col_sum[8:, :] = fill_tile(keep[0].astype(F32), [own[...], other[...]], row_sq, col, high, low, row_sum)


def make_tile(body, args, rows, smem=(), extra=()):
    return call(
        body, [((2 * rows, rows), BF16), ((2 * rows, rows), BF16), ((16, rows), F32), *extra],
        args, smem=smem, flops=2 * 10**9, nbytes=10**6,
    )


def swapped(values):
    middle = values.shape[0] // 2
    return jnp.concatenate([values[middle:], values[:middle]], axis=0)


def per_row(values, width):
    shape = (width, values.shape[1])
    return jnp.concatenate([jnp.broadcast_to(values[i:i + 1, :], shape) for i in (0, 8)], axis=0)


def degree_body(sums, other_sums, seeds, degree_out, vectors_out):
    degree = sums[...] + swapped(other_sums[...])
    scale = lax.rsqrt(degree)
    degree_out[...] = degree
    vectors_out[...] = seeds[...] * per_row(scale, seeds.shape[0] // 2)


def ahead_body(vectors, h1, l1, h2, l2, ahead):
    width = vectors.shape[0] // 2
    high, low = halves(jnp.concatenate([vectors[:width, :], vectors[width:, :]], axis=1))
    both = jnp.concatenate([high, low], axis=0)
    for half, (tile_high, tile_low) in enumerate(((h1, l1), (h2, l2))):
        product = dot(both, tile_high[...])
        product = product[:width] + product[width:] + dot(high, tile_low[...])
        ahead[half * width:(half + 1) * width, :] = product


def combine_body(total, other_total, degree, vectors_out):
    vectors_out[...] = (total[...] + swapped(other_total[...])) / per_row(degree[...], total.shape[0] // 2)


def product_rows(vectors, tile_high, tile_low):
    width = vectors.shape[0]
    high, low = halves(vectors)
    both = jnp.concatenate([high, low], axis=0)
    product = dot(both, tile_high[...], 1, 1)
    return product[:width] + product[width:] + dot(high, tile_low[...], 1, 1)


def stacked(product):
    size = product.shape[1] // 2
    return jnp.concatenate([product[:, :size], product[:, size:]], axis=0)


def own_product_body(vectors, h0, l0, out):
    out[...] = stacked(product_rows(vectors[:vectors.shape[0] // 2, :], h0, l0))


def block_body(product, near, behind, h1, l1, h2, l2, total):
    width = near.shape[0] // 2
    far = product_rows(near[:width, :], h1, l1) + product_rows(near[width:, :], h2, l2)
    total[...] = product[...] + behind[...] + stacked(far)


def low_body(degree, v0, v1, v2, moments, scaled):
    width = v0.shape[0] // 2
    root = jnp.sqrt(degree[0:1, :])
    x0, x1, x2 = v0[:width, :] * root, v1[:width, :] * root, v2[:width, :] * root
    scaled[...] = jnp.concatenate([x0, x1, x2], axis=0)
    left = jnp.concatenate([x0, x1], axis=0)
    order012 = dot(left, left, 1, 1)
    order34 = dot(jnp.concatenate([x1, x2], axis=0), x2, 1, 1)
    order = [order012[:width, :width], order012[:width, width:], order012[width:, width:],
             order34[:width], order34[width:]]
    for i in range(5):
        moments[i * width:(i + 1) * width, :] = order[i]


def place_of(rows, cols):
    return [lax.broadcasted_iota(jnp.int32, (rows, cols), axis) for axis in range(2)]


def moment_body(core, low, vectors, product, near, h1, l1, h2, l2, mine, theirs):
    n = vectors.shape[0] // 2
    last = product_rows(near[:n, :], h1, l1) + product_rows(near[n:, :], h2, l2)
    last = 2.0 * last + jnp.concatenate([product[:n, :], product[n:, :]], axis=1)
    last = dot(jnp.concatenate([vectors[:n, :], vectors[n:, :]], axis=1), last, 1, 1)
    moments = [low[i * n:(i + 1) * n, :] for i in range(5)] + [0.5 * (last + last.T)]
    row, col = place_of(n, n)
    pieces = []
    for i in range(0, 6, 2):
        pair = jnp.where(row >= col, moments[i], moments[i + 1])
        pieces.append(jnp.concatenate([pair[:n // 2], pair[n // 2:]], axis=1))
    d1, d3, d5 = (jnp.sum(moments[i] * unit(n, n), axis=0, keepdims=True) for i in (1, 3, 5))
    row, _ = place_of(8, 2 * n)
    pieces.append(jnp.where(row == 0, jnp.concatenate([d1, d3], axis=1),
                            jnp.where(row == 1, jnp.concatenate([d5, d5], axis=1), 0.0)))
    pieces.append(jnp.zeros((8, 2 * n), F32))
    packed = jnp.concatenate(pieces, axis=0)
    half = packed.shape[0] // 2
    first = core[0] == 0
    mine[...] = jnp.where(first, packed[:half], packed[half:])
    theirs[...] = jnp.where(first, packed[half:], packed[:half])


def unpacked(packed, n):
    row, col = place_of(n, n)
    start = 3 * n // 2
    diagonals = [packed[start:start + 1, :n], packed[start:start + 1, n:], packed[start + 1:start + 2, :n]]
    moments = []
    for i in range(3):
        folded = packed[i * n // 2:(i + 1) * n // 2]
        pair = jnp.concatenate([folded[:, :n], folded[:, n:]], axis=0)
        flipped = pair.T
        moments.append(jnp.where(row >= col, pair, flipped))
        moments.append(jnp.where(row == col, diagonals[i], jnp.where(row < col, pair, flipped)))
    return moments


def unit(rows, cols):
    return (lax.broadcasted_iota(jnp.int32, (rows, cols), 0)
            == lax.broadcasted_iota(jnp.int32, (rows, cols), 1)).astype(F32)


def lane(values, k):
    return jnp.take_along_axis(values, jnp.full(values.shape, k, jnp.int32), axis=1, mode="promise_in_bounds")


def sublane(values, k):
    return jnp.broadcast_to(values[k:k + 1, :], values.shape)


def inverse_factor(matrix):
    size = matrix.shape[0]
    work = jnp.concatenate([matrix, unit(size, size)], axis=1)
    blocks = [work[8 * i:8 * i + 8, :] for i in range(size // 8)]
    place = lax.broadcasted_iota(jnp.int32, (8, 2 * size), 0)
    done = [None] * (size // 8)
    for k in range(0, size, 4):
        top, r = divmod(k, 8)
        pivot = blocks[top]
        cols = [lane(pivot, k + j) for j in range(4)]
        u0, u1, u2, u3 = (sublane(pivot, r + j) for j in range(4))
        a00, a10, a20, a30 = (sublane(cols[0], r + j) for j in range(4))
        a11, a21, a31 = (sublane(cols[1], r + j) for j in range(1, 4))
        a22, a32 = (sublane(cols[2], r + j) for j in range(2, 4))
        a33 = sublane(cols[3], r + 3)
        det_a = a00 * a11 - a10 * a10
        inv_a = 1.0 / det_a
        p00, p10, p11 = a11 * inv_a, a10 * inv_a, a00 * inv_a
        b00, b01 = a20 * p00 - a21 * p10, a21 * p11 - a20 * p10
        b10, b11 = a30 * p00 - a31 * p10, a31 * p11 - a30 * p10
        s00 = a22 - b00 * a20 - b01 * a21
        s10 = a32 - b10 * a20 - b11 * a21
        s11 = a33 - b10 * a30 - b11 * a31
        det_s = s00 * s11 - s10 * s10
        inv_s = 1.0 / det_s
        u2 = u2 - b00 * u0 - b01 * u1
        u3 = u3 - b10 * u0 - b11 * u1
        t2 = (s11 * u2 - s10 * u3) * inv_s
        t3 = (s00 * u3 - s10 * u2) * inv_s
        t0 = (p00 * u0 - p10 * u1) - b00 * t2 - b10 * t3
        t1 = (p11 * u1 - p10 * u0) - b01 * t2 - b11 * t3
        for i in range(top, size // 8):
            if i == top:
                if r:
                    continue
                c = cols
            else:
                c = [lane(blocks[i], k + j) for j in range(4)]
            change = (c[0] * t0 + c[1] * t1) + (c[2] * t2 + c[3] * t3)
            blocks[i] = blocks[i] - (jnp.where(place > 3, change, 0.0) if i == top else change)
        v0 = u0 * lax.rsqrt(a00)
        v1 = (a00 * u1 - a10 * u0) * lax.rsqrt(a00 * det_a)
        v2 = u2 * lax.rsqrt(s00)
        v3 = (s00 * u3 - s10 * u2) * lax.rsqrt(s00 * det_s)
        four = jnp.where(place % 4 == 0, v0, jnp.where(place % 4 == 1, v1, jnp.where(place % 4 == 2, v2, v3)))
        done[top] = jnp.where(place > 3, four, done[top]) if r else four
    return jnp.concatenate(done, axis=0)[:, size:]


def total(matrix):
    return jnp.sum(jnp.sum(matrix, axis=0, keepdims=True), axis=1, keepdims=True)


def trace(matrix):
    return total(matrix * unit(*matrix.shape))


def inverse_root(matrix):
    eye = unit(*matrix.shape)
    rest = matrix - eye

    def series():
        return eye - 0.5 * rest + 0.375 * dot(rest, rest)

    return lax.cond(jnp.sum(rest * rest) < 1e-4, series, lambda: inverse_factor(matrix))


def dense(moments, index, rows, data):
    n = NVEC
    eye = unit(n, n)
    pick = ((lax.broadcasted_iota(jnp.int32, (n, n), 0) == index)
            & (lax.broadcasted_iota(jnp.int32, (n, n), 1) == index)).astype(F32)

    def part(stacked, i):
        return stacked[i * n:(i + 1) * n]

    def below(*parts):
        return jnp.concatenate(parts, axis=0)

    def beside(*parts):
        return jnp.concatenate(parts, axis=1)

    base = inverse_factor(moments[0])
    right = dot(below(*moments[1:]), base, 1, 1)
    m1, m2, m3, m4, m5 = (dot(base, part(right, i)) for i in range(5))
    y0, y1, y2 = (dot(base, part(data, i)) for i in range(3))

    by1 = dot(below(m1, m2, m3, m4), m1)
    square, m21, m31, m41 = (part(by1, i) for i in range(4))
    tri = dot(m1, beside(square, m21, m31))
    gram_r = m2 - square
    image_r = m3 - m21 - m21.T + tri[:, :n]
    mixed_r = m3 - m21
    square_r = m4 - m31 - m31.T + tri[:, n:2 * n]
    cubic_r = m5 - m41 - m41.T + tri[:, 2 * n:]
    shift = 3.0 - total(m1 * pick)
    ridge = RIDGE_WEIGHT * (n + trace(gram_r)) / (2 * n)
    ridged = gram_r + ridge * eye
    factor = inverse_factor(ridged)
    inverse = dot(factor, factor, 0, 0)
    keep = 1.0 / (1.0 + ridge)
    step = below(
        beside(m1 * keep + shift * eye, gram_r * keep),
        beside(eye - ridge * inverse, dot(inverse, image_r) + shift * eye),
    )
    twice = dot(step, step)
    power = dot(twice, dot(twice, twice[:, :n]))
    top, bottom = power[:n], power[n:]
    weighted = dot(below(ridged, gram_r, image_r), bottom)
    norm = (1.0 + ridge) * dot(top, top, 0, 0) + dot(bottom, part(weighted, 0), 0, 0)
    factor = inverse_factor(norm)

    middle = m4 - m31
    images = dot(below(
        beside(m1, gram_r), beside(gram_r, image_r),
        beside(m2, mixed_r), beside(mixed_r.T, square_r),
        beside(m3, middle), beside(middle.T, cubic_r),
    ), power)
    whole = dot(power, beside(images[:2 * n], images[2 * n:4 * n], images[4 * n:], power), 0, 0)
    lower = dot(bottom, beside(part(images, 1), part(images, 3), part(weighted, 1), part(weighted, 2)), 0, 0)
    raw = [whole[:, i * n:(i + 1) * n] for i in range(4)] + [lower[:, i * n:(i + 1) * n] for i in range(4)]
    right = dot(below(*raw), factor, 1, 1)
    ritz, image2, image3, excess, p_image, p_image2, p_gram, p_ritz = (dot(factor, part(right, i)) for i in range(8))
    excess = ridge * excess

    shift = 3.0 - total(ritz * pick)
    by_ritz = dot(below(ritz, p_gram, excess, p_image, image2), ritz)
    squared, gram_pr, gram_cr = part(by_ritz, 0), p_image - part(by_ritz, 1), part(by_ritz, 2)
    tri = dot(ritz, squared), dot(ritz, gram_cr)
    gram_rr = image2 - squared - tri[1]
    image_cr = image2 - squared
    image_pr = p_image2 - part(by_ritz, 3)
    image_rr = image3 - part(by_ritz, 4) - part(by_ritz, 4).T + tri[0]
    ridge = RIDGE_WEIGHT * (n - trace(excess) + trace(p_gram) + trace(gram_rr)) / (3 * n)
    g_cc = eye - excess + ridge * eye
    g_pp = p_gram + ridge * eye
    g_rr = gram_rr + ridge * eye
    image_gram = below(
        beside(ritz, p_image.T, image_cr), beside(p_image, p_ritz, image_pr), beside(image_cr.T, image_pr.T, image_rr),
    )
    v0 = inverse_root(g_cc)
    side = dot(below(p_gram, gram_cr.T), v0, 1, 1)
    l10, l20 = side[:n], side[n:]
    outer = dot(side, side, 1, 1)
    v1 = inverse_factor(g_pp - outer[:n, :n])
    l21 = dot(gram_pr.T - outer[n:, :n], v1, 1, 1)
    v2 = inverse_factor(g_rr - outer[n:, n:] - dot(l21, l21, 1, 1))
    zero = jnp.zeros((n, n), F32)
    row0 = beside(v0, zero, zero)
    row1 = dot(v1, beside(-dot(l10, v0), eye, zero))
    row2 = beside(zero, zero, eye) - dot(l20, row0) - dot(l21, row1)
    known = below(row0, row1)
    solved = dot(known, dot(known, image_gram), 0, 0)
    row2 = dot(v2, beside(row2, dot(row2, image_gram)))
    step = solved + dot(row2[:, :3 * n], row2[:, 3 * n:], 0, 0) + shift * unit(3 * n, 3 * n)
    twice = dot(step, step)
    power2 = dot(twice, dot(twice, twice[:, :n]))
    gram = below(
        beside(g_cc, p_gram, gram_cr), beside(p_gram, g_pp, gram_pr), beside(gram_cr.T, gram_pr.T, g_rr),
    )
    norm = dot(power2, dot(gram, power2), 0, 0)

    start = dot(power, below(y0, y1), 0, 0) - dot(dot(m1, bottom), y0, 0, 0)
    image = dot(power, below(y1, y2), 0, 0) - dot(dot(m1, bottom), y1, 0, 0)
    residue = dot(bottom, y1 - dot(m1, y0), 0, 0)
    current = dot(factor, start)
    vectors = below(current, dot(factor, residue), dot(factor, image) - dot(ritz, current))
    return dot(inverse_factor(norm), dot(power2, vectors, 0, 0)) * math.sqrt(rows)


def dense_body(rows, core, index, mine, theirs, scaled, out):
    first = core[0] == 0
    packed = jnp.concatenate([
        jnp.where(first, mine[...], theirs[...]), jnp.where(first, theirs[...], mine[...])], axis=0)
    out[...] = dense(unpacked(packed, NVEC), index[0], rows, scaled[...])


def between_blocks(shard, sign):
    blocks, cores = lax.axis_size("blk"), lax.axis_size("narrow")
    pairs = [(i * cores + j, (i + sign * (1 + j)) % blocks * cores + j) for i in range(blocks) for j in range(cores)]
    return lax.ppermute(shard, ("blk", "narrow"), pairs)


def between_cores(shard):
    return lax.ppermute(shard, "narrow", [(0, 1), (1, 0)])


def total_over_blocks(values):
    blocks = lax.axis_size("blk")
    span = 1
    while blocks % (2 * span) == 0:
        values = values + lax.ppermute(values, "blk", [(i, i ^ span) for i in range(blocks)])
        span *= 2
    if span < blocks:
        groups = [list(range(i, blocks, span)) for i in range(span)]
        values = lax.psum(values, "blk", axis_index_groups=groups)
    return values


def shards(embeddings, pair_mask, shift_index, start_seed):
    size = embeddings.shape[0]
    blocks = lax.axis_size("blk")
    where = lax.axis_index("blk")
    core = lax.axis_index("narrow").astype(jnp.int32).reshape(1)
    other_emb = between_cores(embeddings)
    far_emb = between_blocks(embeddings, -1)
    seed = start_seed.astype(F32).T / 1000.0
    seeds = jnp.concatenate([seed, between_cores(seed)], axis=0)
    keep = lax.dynamic_slice(pair_mask, (where, core[0]), (1, 1))[0]
    emb_args = [embeddings, other_emb]
    pair_shape, row_shape = ((2 * NVEC, size), F32), ((16, size), F32)
    h0, l0, sums, row_sq, own_copy = make_tile(
        own_body, emb_args, size, extra=(((2 * size, 128), F32), (embeddings.shape, BF16)))
    emb_args = [own_copy, other_emb]
    far_emb, sums, seeds, keep = lax.optimization_barrier((far_emb, sums, seeds, keep))
    pairs = [(2 * i, (i - 2) % blocks * 2 + 1) for i in range(blocks)]
    pairs += [(2 * i + 1, (i - 1) % blocks * 2) for i in range(blocks) if blocks % 2 or i % 2]
    direct = lax.ppermute(own_copy, ("blk", "narrow"), pairs)
    relayed = direct
    if blocks % 2 == 0:
        relayed = lax.ppermute(far_emb, ("blk", "narrow"), [(2 * i + 1, 2 * i + 2) for i in range(0, blocks, 2)])
    choice = (1 - core) * (where % 2 * (1 - blocks % 2)).astype(jnp.int32)
    h1, l1, sums, cols = make_tile(
        far_body, [keep, *emb_args, row_sq, far_emb, sums], size, (0,), (((8, size), F32),))
    h2, l2, sums, cols = make_tile(
        relayed_body, [keep, choice, *emb_args, row_sq, direct, relayed, sums, cols], size, (0, 1), (row_shape,))
    sums = sums + between_blocks(cols, 1)

    small = dict(flops=10**6, nbytes=10**5)
    middle = dict(flops=10**9, nbytes=10**6)
    degree, vectors = call(
        degree_body, [row_shape, pair_shape], [sums, between_cores(sums), seeds], **small)
    far = [h1, l1, h2, l2]
    history = [vectors]
    for _ in range(2):
        near = between_blocks(vectors, -1)
        (ahead,) = call(ahead_body, [pair_shape], [vectors, *far], **middle)
        behind = between_blocks(ahead, 1)
        (product,) = call(own_product_body, [pair_shape], [vectors, h0, l0], **middle)
        (total,) = call(block_body, [pair_shape], [product, near, behind, *far], **middle)
        (vectors,) = call(combine_body, [pair_shape], [total, between_cores(total), degree], **small)
        history.append(vectors)
    near = between_blocks(vectors, -1)
    low, scaled = call(
        low_body, [((5 * NVEC, NVEC), F32), ((3 * NVEC, size), F32)], [degree] + history, **middle)
    (product,) = call(own_product_body, [pair_shape], [vectors, h0, l0], **middle)
    packed_shape = ((3 * NVEC // 4 + 8, 2 * NVEC), F32)
    mine, theirs = call(
        moment_body, [packed_shape] * 2, [core, low, vectors, product, near, *far], smem=(0,), **middle)
    mine = total_over_blocks(mine + between_cores(theirs))
    rows = size * blocks * lax.axis_size("narrow")
    (out,) = call(
        lambda *refs: dense_body(rows, *refs), [((NVEC, size), F32)],
        [core, shift_index, mine, between_cores(mine), scaled], smem=(0, 1), flops=2 * 10**10, nbytes=10**6,
    )
    return out.T


def solution(mesh):
    return jax.shard_map(
        shards,
        mesh=mesh,
        in_specs=(
            P(("groups", "blk", "narrow"), None),
            P("groups", None),
            P("groups"),
            P(("groups", "blk", "narrow"), None),
        ),
        out_specs=P(("groups", "blk", "narrow"), None),
        check_vma=False,
    )
```

```python
import math

import jax
import jax.numpy as jnp
from jax import lax
from jax.experimental import pallas as pl
from jax.experimental.pallas import tpu as pltpu
from jax.sharding import PartitionSpec as P

KERNEL_GAMMA = 2.0
RIDGE_WEIGHT = 1e-05
NVEC = 64
F32 = jnp.float32
BF16 = jnp.bfloat16
VMEM_LIMIT = 16 * 1024 * 1024


def dot(left, right, left_dim=1, right_dim=0):
    precision = lax.Precision.HIGHEST if left.dtype == F32 else None
    return lax.dot_general(
        left, right, (((left_dim,), (right_dim,)), ((), ())),
        precision=precision, preferred_element_type=F32,
    )


def halves(values):
    high = values.astype(BF16)
    return high, (values - high.astype(F32)).astype(BF16)


def call(body, out_shapes, args, flops=0, nbytes=0):
    return pl.pallas_call(
        body,
        out_shape=[jax.ShapeDtypeStruct(shape, dtype) for shape, dtype in out_shapes],
        in_specs=[pl.BlockSpec(memory_space=pltpu.VMEM) for _ in args],
        out_specs=[pl.BlockSpec(memory_space=pltpu.VMEM) for _ in out_shapes],
        compiler_params=pltpu.CompilerParams(vmem_limit_bytes=VMEM_LIMIT),
        cost_estimate=pl.CostEstimate(flops=flops, bytes_accessed=nbytes, transcendentals=0),
    )(*args)


def spread(value):
    return jnp.broadcast_to(value.astype(F32), (8, 128))


def chosen(flag, first, second):
    rows, cols = first.shape
    wide = jnp.concatenate([flag[0:1, :]] * (cols // 128), axis=1)
    return jnp.where(jnp.broadcast_to(wide, (rows, cols)) > 0.5, first, second)


LOG2_E = 1.4426950408889634


def sums_along(values):
    rows, depth = values.shape
    folded = values[:, :128]
    for j in range(128, depth, 128):
        folded = folded + values[:, j:j + 128]
    return dot(jnp.ones((8, 128), F32), folded, 1, 1)


def fill_tile(weight, row_embs, row_sq, col_emb, high, low, row_sum):
    size = col_emb.shape[0]
    col32 = col_emb.astype(F32)
    col_sq = (2.0 * LOG2_E) * sums_along(col32 * col32)[0:1, :]
    total = jnp.zeros((1, size), F32)
    for half in range(2):
        rows = slice(half * size, (half + 1) * size)
        inner = dot(row_embs[half], col_emb, 1, 1)
        squares = jnp.concatenate([row_sq[rows, :]] * (size // 128), axis=1)
        tile = jnp.exp2((4.0 * LOG2_E) * inner - (squares + col_sq))
        if weight is not None:
            tile = tile * weight
        tile_high, tile_low = halves(tile)
        high[rows, :] = tile_high
        low[rows, :] = tile_low
        row_sum[half * 8:(half + 1) * 8, :] = row_sum[half * 8:(half + 1) * 8, :] + sums_along(tile)
        total = total + jnp.sum(tile, axis=0, keepdims=True)
    return jnp.broadcast_to(total, (8, size))


def own_body(own, other, high, low, row_sum, row_sq, copy, token):
    size = own.shape[0]
    embs = [own[...], other[...]]
    copy[...] = embs[0]
    for half in range(2):
        row32 = embs[half].astype(F32)
        squares = (2.0 * LOG2_E) * jnp.sum(row32 * row32, axis=1, keepdims=True)
        row_sq[half * size:(half + 1) * size, :] = jnp.broadcast_to(squares, (size, 128))
    row_sum[...] = jnp.zeros(row_sum.shape, F32)
    token[...] = jnp.zeros(token.shape, F32)
    fill_tile(None, embs, row_sq, embs[0], high, low, row_sum)


def far_body(keep, relays, own, other, row_sq, direct, relayed, before, high, low, row_sum, col_sum):
    row_sum[...] = before[...]
    size = own.shape[0]
    weight = jnp.concatenate([keep[0:1, :]] * (size // 128), axis=1)
    col = chosen(relays, relayed[...], direct[...])
    col_sum[...] = fill_tile(weight, [own[...], other[...]], row_sq, col, high, low, row_sum)


def make_tile(body, args, rows, extra=()):
    return call(
        body, [((2 * rows, rows), BF16), ((2 * rows, rows), BF16), ((16, rows), F32), *extra],
        args, flops=2 * 10**9, nbytes=10**6,
    )


def swapped(values):
    middle = values.shape[0] // 2
    return jnp.concatenate([values[middle:], values[:middle]], axis=0)


def per_row(values, width):
    shape = (width, values.shape[1])
    return jnp.concatenate([jnp.broadcast_to(values[i:i + 1, :], shape) for i in (0, 8)], axis=0)


def degree_body(sums, other_sums, seeds, degree_out, vectors_out):
    degree = sums[...] + swapped(other_sums[...])
    scale = lax.rsqrt(degree)
    degree_out[...] = degree
    vectors_out[...] = seeds[...] * per_row(scale, seeds.shape[0] // 2)


def ahead_body(relays, vectors, h1, l1, h2, l2, ahead):
    width = vectors.shape[0] // 2
    high, low = halves(jnp.concatenate([vectors[:width, :], vectors[width:, :]], axis=1))
    both = jnp.concatenate([high, low], axis=0)
    products = []
    for tile_high, tile_low in ((h1, l1), (h2, l2)):
        product = dot(both, tile_high[...])
        products.append(product[:width] + product[width:] + dot(high, tile_low[...]))
    ahead[:width, :] = chosen(relays, products[1], products[0])
    ahead[width:, :] = chosen(relays, products[0], products[1])


def combine_body(total, other_total, degree, vectors_out):
    vectors_out[...] = (total[...] + swapped(other_total[...])) / per_row(degree[...], total.shape[0] // 2)


def product_rows(vectors, tile_high, tile_low):
    width = vectors.shape[0]
    high, low = halves(vectors)
    both = jnp.concatenate([high, low], axis=0)
    product = dot(both, tile_high[...], 1, 1)
    return product[:width] + product[width:] + dot(high, tile_low[...], 1, 1)


def stacked(product):
    size = product.shape[1] // 2
    return jnp.concatenate([product[:, :size], product[:, size:]], axis=0)


def own_product_body(vectors, h0, l0, out):
    out[...] = stacked(product_rows(vectors[:vectors.shape[0] // 2, :], h0, l0))


def far_product(relays, near, h1, l1, h2, l2):
    width = near.shape[0] // 2
    first = chosen(relays, near[width:, :], near[:width, :])
    second = chosen(relays, near[:width, :], near[width:, :])
    return product_rows(first, h1, l1) + product_rows(second, h2, l2)


def block_body(relays, product, near, behind, h1, l1, h2, l2, total):
    total[...] = product[...] + behind[...] + stacked(far_product(relays, near, h1, l1, h2, l2))


def low_body(degree, v0, v1, v2, moments, scaled):
    width = v0.shape[0] // 2
    root = jnp.sqrt(degree[0:1, :])
    x0, x1, x2 = v0[:width, :] * root, v1[:width, :] * root, v2[:width, :] * root
    scaled[...] = jnp.concatenate([x0, x1, x2], axis=0)
    left = jnp.concatenate([x0, x1], axis=0)
    order012 = dot(left, left, 1, 1)
    order34 = dot(jnp.concatenate([x1, x2], axis=0), x2, 1, 1)
    order = [order012[:width, :width], order012[:width, width:], order012[width:, width:],
             order34[:width], order34[width:]]
    for i in range(5):
        moments[i * width:(i + 1) * width, :] = order[i]


def place_of(rows, cols):
    return [lax.broadcasted_iota(jnp.int32, (rows, cols), axis) for axis in range(2)]


def moment_body(core, relays, low, vectors, product, near, h1, l1, h2, l2, mine, theirs):
    n = vectors.shape[0] // 2
    last = far_product(relays, near, h1, l1, h2, l2)
    last = 2.0 * last + jnp.concatenate([product[:n, :], product[n:, :]], axis=1)
    last = dot(jnp.concatenate([vectors[:n, :], vectors[n:, :]], axis=1), last, 1, 1)
    moments = [low[i * n:(i + 1) * n, :] for i in range(5)] + [0.5 * (last + last.T)]
    row, col = place_of(n, n)
    pieces = []
    for i in range(0, 6, 2):
        pair = jnp.where(row >= col, moments[i], moments[i + 1])
        pieces.append(jnp.concatenate([pair[:n // 2], pair[n // 2:]], axis=1))
    d1, d3, d5 = (jnp.sum(moments[i] * unit(n, n), axis=0, keepdims=True) for i in (1, 3, 5))
    row, _ = place_of(8, 2 * n)
    pieces.append(jnp.where(row == 0, jnp.concatenate([d1, d3], axis=1),
                            jnp.where(row == 1, jnp.concatenate([d5, d5], axis=1), 0.0)))
    pieces.append(jnp.zeros((8, 2 * n), F32))
    packed = jnp.concatenate(pieces, axis=0)
    half = packed.shape[0] // 2
    mine[...] = chosen(core, packed[half:], packed[:half])
    theirs[...] = chosen(core, packed[:half], packed[half:])


def unpacked(packed, n):
    row, col = place_of(n, n)
    start = 3 * n // 2
    diagonals = [packed[start:start + 1, :n], packed[start:start + 1, n:], packed[start + 1:start + 2, :n]]
    moments = []
    for i in range(3):
        folded = packed[i * n // 2:(i + 1) * n // 2]
        pair = jnp.concatenate([folded[:, :n], folded[:, n:]], axis=0)
        flipped = pair.T
        moments.append(jnp.where(row >= col, pair, flipped))
        moments.append(jnp.where(row == col, diagonals[i], jnp.where(row < col, pair, flipped)))
    return moments


def unit(rows, cols):
    return (lax.broadcasted_iota(jnp.int32, (rows, cols), 0)
            == lax.broadcasted_iota(jnp.int32, (rows, cols), 1)).astype(F32)


def lane(values, k):
    return jnp.take_along_axis(values, jnp.full(values.shape, k, jnp.int32), axis=1, mode="promise_in_bounds")


def sublane(values, k):
    return jnp.broadcast_to(values[k:k + 1, :], values.shape)


def inverse_factor(matrix):
    size = matrix.shape[0]
    work = jnp.concatenate([matrix, unit(size, size)], axis=1)
    blocks = [work[8 * i:8 * i + 8, :] for i in range(size // 8)]
    place = lax.broadcasted_iota(jnp.int32, (8, 2 * size), 0)
    done = [None] * (size // 8)
    for k in range(0, size, 4):
        top, r = divmod(k, 8)
        pivot = blocks[top]
        cols = [lane(pivot, k + j) for j in range(4)]
        u0, u1, u2, u3 = (sublane(pivot, r + j) for j in range(4))
        a00, a10, a20, a30 = (sublane(cols[0], r + j) for j in range(4))
        a11, a21, a31 = (sublane(cols[1], r + j) for j in range(1, 4))
        a22, a32 = (sublane(cols[2], r + j) for j in range(2, 4))
        a33 = sublane(cols[3], r + 3)
        det_a = a00 * a11 - a10 * a10
        inv_a = 1.0 / det_a
        p00, p10, p11 = a11 * inv_a, a10 * inv_a, a00 * inv_a
        b00, b01 = a20 * p00 - a21 * p10, a21 * p11 - a20 * p10
        b10, b11 = a30 * p00 - a31 * p10, a31 * p11 - a30 * p10
        s00 = a22 - b00 * a20 - b01 * a21
        s10 = a32 - b10 * a20 - b11 * a21
        s11 = a33 - b10 * a30 - b11 * a31
        det_s = s00 * s11 - s10 * s10
        inv_s = 1.0 / det_s
        u2 = u2 - b00 * u0 - b01 * u1
        u3 = u3 - b10 * u0 - b11 * u1
        t2 = (s11 * u2 - s10 * u3) * inv_s
        t3 = (s00 * u3 - s10 * u2) * inv_s
        t0 = (p00 * u0 - p10 * u1) - b00 * t2 - b10 * t3
        t1 = (p11 * u1 - p10 * u0) - b01 * t2 - b11 * t3
        for i in range(top, size // 8):
            if i == top:
                if r:
                    continue
                c = cols
            else:
                c = [lane(blocks[i], k + j) for j in range(4)]
            change = (c[0] * t0 + c[1] * t1) + (c[2] * t2 + c[3] * t3)
            blocks[i] = blocks[i] - (jnp.where(place > 3, change, 0.0) if i == top else change)
        v0 = u0 * lax.rsqrt(a00)
        v1 = (a00 * u1 - a10 * u0) * lax.rsqrt(a00 * det_a)
        v2 = u2 * lax.rsqrt(s00)
        v3 = (s00 * u3 - s10 * u2) * lax.rsqrt(s00 * det_s)
        four = jnp.where(place % 4 == 0, v0, jnp.where(place % 4 == 1, v1, jnp.where(place % 4 == 2, v2, v3)))
        done[top] = jnp.where(place > 3, four, done[top]) if r else four
    return jnp.concatenate(done, axis=0)[:, size:]


def total(matrix):
    return jnp.sum(jnp.sum(matrix, axis=0, keepdims=True), axis=1, keepdims=True)


def trace(matrix):
    return total(matrix * unit(*matrix.shape))


def inverse_root(matrix):
    eye = unit(*matrix.shape)
    rest = matrix - eye

    def series():
        return eye - 0.5 * rest + 0.375 * dot(rest, rest)

    return lax.cond(jnp.sum(rest * rest) < 1e-4, series, lambda: inverse_factor(matrix))


def dense(moments, index, rows, data):
    n = NVEC
    eye = unit(n, n)
    pick = ((lax.broadcasted_iota(jnp.int32, (n, n), 0) == index)
            & (lax.broadcasted_iota(jnp.int32, (n, n), 1) == index)).astype(F32)

    def part(stacked, i):
        return stacked[i * n:(i + 1) * n]

    def below(*parts):
        return jnp.concatenate(parts, axis=0)

    def beside(*parts):
        return jnp.concatenate(parts, axis=1)

    base = inverse_factor(moments[0])
    right = dot(below(*moments[1:]), base, 1, 1)
    m1, m2, m3, m4, m5 = (dot(base, part(right, i)) for i in range(5))
    y0, y1, y2 = (dot(base, part(data, i)) for i in range(3))

    by1 = dot(below(m1, m2, m3, m4), m1)
    square, m21, m31, m41 = (part(by1, i) for i in range(4))
    tri = dot(m1, beside(square, m21, m31))
    gram_r = m2 - square
    image_r = m3 - m21 - m21.T + tri[:, :n]
    mixed_r = m3 - m21
    square_r = m4 - m31 - m31.T + tri[:, n:2 * n]
    cubic_r = m5 - m41 - m41.T + tri[:, 2 * n:]
    shift = 3.0 - total(m1 * pick)
    ridge = RIDGE_WEIGHT * (n + trace(gram_r)) / (2 * n)
    ridged = gram_r + ridge * eye
    factor = inverse_factor(ridged)
    inverse = dot(factor, factor, 0, 0)
    keep = 1.0 / (1.0 + ridge)
    step = below(
        beside(m1 * keep + shift * eye, gram_r * keep),
        beside(eye - ridge * inverse, dot(inverse, image_r) + shift * eye),
    )
    twice = dot(step, step)
    power = dot(twice, dot(twice, twice[:, :n]))
    top, bottom = power[:n], power[n:]
    weighted = dot(below(ridged, gram_r, image_r), bottom)
    norm = (1.0 + ridge) * dot(top, top, 0, 0) + dot(bottom, part(weighted, 0), 0, 0)
    factor = inverse_factor(norm)

    middle = m4 - m31
    images = dot(below(
        beside(m1, gram_r), beside(gram_r, image_r),
        beside(m2, mixed_r), beside(mixed_r.T, square_r),
        beside(m3, middle), beside(middle.T, cubic_r),
    ), power)
    whole = dot(power, beside(images[:2 * n], images[2 * n:4 * n], images[4 * n:], power), 0, 0)
    lower = dot(bottom, beside(part(images, 1), part(images, 3), part(weighted, 1), part(weighted, 2)), 0, 0)
    raw = [whole[:, i * n:(i + 1) * n] for i in range(4)] + [lower[:, i * n:(i + 1) * n] for i in range(4)]
    right = dot(below(*raw), factor, 1, 1)
    ritz, image2, image3, excess, p_image, p_image2, p_gram, p_ritz = (dot(factor, part(right, i)) for i in range(8))
    excess = ridge * excess

    shift = 3.0 - total(ritz * pick)
    by_ritz = dot(below(ritz, p_gram, excess, p_image, image2), ritz)
    squared, gram_pr, gram_cr = part(by_ritz, 0), p_image - part(by_ritz, 1), part(by_ritz, 2)
    tri = dot(ritz, squared), dot(ritz, gram_cr)
    gram_rr = image2 - squared - tri[1]
    image_cr = image2 - squared
    image_pr = p_image2 - part(by_ritz, 3)
    image_rr = image3 - part(by_ritz, 4) - part(by_ritz, 4).T + tri[0]
    ridge = RIDGE_WEIGHT * (n - trace(excess) + trace(p_gram) + trace(gram_rr)) / (3 * n)
    g_cc = eye - excess + ridge * eye
    g_pp = p_gram + ridge * eye
    g_rr = gram_rr + ridge * eye
    image_gram = below(
        beside(ritz, p_image.T, image_cr), beside(p_image, p_ritz, image_pr), beside(image_cr.T, image_pr.T, image_rr),
    )
    v0 = inverse_root(g_cc)
    side = dot(below(p_gram, gram_cr.T), v0, 1, 1)
    l10, l20 = side[:n], side[n:]
    outer = dot(side, side, 1, 1)
    v1 = inverse_factor(g_pp - outer[:n, :n])
    l21 = dot(gram_pr.T - outer[n:, :n], v1, 1, 1)
    v2 = inverse_factor(g_rr - outer[n:, n:] - dot(l21, l21, 1, 1))
    zero = jnp.zeros((n, n), F32)
    row0 = beside(v0, zero, zero)
    row1 = dot(v1, beside(-dot(l10, v0), eye, zero))
    row2 = beside(zero, zero, eye) - dot(l20, row0) - dot(l21, row1)
    known = below(row0, row1)
    solved = dot(known, dot(known, image_gram), 0, 0)
    row2 = dot(v2, beside(row2, dot(row2, image_gram)))
    step = solved + dot(row2[:, :3 * n], row2[:, 3 * n:], 0, 0) + shift * unit(3 * n, 3 * n)
    twice = dot(step, step)
    power2 = dot(twice, dot(twice, twice[:, :n]))
    gram = below(
        beside(g_cc, p_gram, gram_cr), beside(p_gram, g_pp, gram_pr), beside(gram_cr.T, gram_pr.T, g_rr),
    )
    norm = dot(power2, dot(gram, power2), 0, 0)

    start = dot(power, below(y0, y1), 0, 0) - dot(dot(m1, bottom), y0, 0, 0)
    image = dot(power, below(y1, y2), 0, 0) - dot(dot(m1, bottom), y1, 0, 0)
    residue = dot(bottom, y1 - dot(m1, y0), 0, 0)
    current = dot(factor, start)
    vectors = below(current, dot(factor, residue), dot(factor, image) - dot(ritz, current))
    return dot(inverse_factor(norm), dot(power2, vectors, 0, 0)) * math.sqrt(rows)


def dense_body(rows, core, index, mine, theirs, scaled, out):
    packed = jnp.concatenate([
        chosen(core, theirs[...], mine[...]), chosen(core, mine[...], theirs[...])], axis=0)
    index = jnp.broadcast_to(index[0:1, :NVEC], (NVEC, NVEC)).astype(jnp.int32)
    out[...] = dense(unpacked(packed, NVEC), index, rows, scaled[...])


def between_blocks(shard, sign):
    blocks, cores = lax.axis_size("blk"), lax.axis_size("narrow")
    pairs = [(i * cores + j, (i + sign * (1 + j)) % blocks * cores + j) for i in range(blocks) for j in range(cores)]
    return lax.ppermute(shard, ("blk", "narrow"), pairs)


def between_cores(shard):
    return lax.ppermute(shard, "narrow", [(0, 1), (1, 0)])


def total_over_blocks(values):
    blocks = lax.axis_size("blk")
    span = 1
    while blocks % (2 * span) == 0:
        values = values + lax.ppermute(values, "blk", [(i, i ^ span) for i in range(blocks)])
        span *= 2
    if span < blocks:
        groups = [list(range(i, blocks, span)) for i in range(span)]
        values = lax.psum(values, "blk", axis_index_groups=groups)
    return values


def shards(embeddings, pair_mask, shift_index, start_seed):
    size = embeddings.shape[0]
    blocks = lax.axis_size("blk")
    where = lax.axis_index("blk")
    core = lax.axis_index("narrow")
    other_emb = between_cores(embeddings)
    relaying = blocks % 2 == 0
    back1 = [(i, (i - 1) % blocks) for i in range(blocks) if i % 2 or not relaying]
    back2 = [(i, (i - 2) % blocks) for i in range(blocks)]
    orders = [
        [(2 * i + j, 2 * k) for i, k in back1] + [(2 * i + 1 - j, 2 * k + 1) for i, k in back2] for j in range(2)]

    def between_shards(shard, pairs):
        return lax.ppermute(shard, ("blk", "narrow"), pairs)

    def relay(shard):
        pairs = [(2 * i + 1, 2 * i + 2) for i in range(0, blocks, 2)]
        return between_shards(shard, pairs) if relaying else shard

    first = between_shards(embeddings, orders[0])
    seed = start_seed.astype(F32).T / 1000.0
    seeds = jnp.concatenate([seed, between_cores(seed)], axis=0)
    keep = spread(lax.dynamic_slice(pair_mask, (where, core), (1, 1)))
    relays = spread((1 - core) * (where % 2) * int(relaying))
    pair_shape, row_shape = ((2 * NVEC, size), F32), ((16, size), F32)
    h0, l0, sums, row_sq, own_copy, token = make_tile(
        own_body, [embeddings, other_emb], size,
        (((2 * size, 128), F32), (embeddings.shape, BF16), ((8, 128), F32)))
    first, seeds, keep, relays, token = lax.optimization_barrier((first, seeds, keep, relays, token))
    second = between_shards(own_copy, orders[1])
    tile_args = [keep, relays, own_copy, other_emb, row_sq]
    h1, l1, sums, cols1 = make_tile(
        far_body, [*tile_args, first, relay(first), sums], size, (((8, size), F32),))
    h2, l2, sums, cols2 = make_tile(
        far_body, [*tile_args, second, relay(second), sums], size, (((8, size), F32),))
    cols = jnp.concatenate([jnp.where(relays[0, 0] > 0.5, cols2, cols1), jnp.where(relays[0, 0] > 0.5, cols1, cols2)])
    sums = sums + between_blocks(cols, 1)

    small = dict(flops=10**6, nbytes=10**5)
    middle = dict(flops=10**9, nbytes=10**6)
    degree, vectors = call(
        degree_body, [row_shape, pair_shape], [sums, between_cores(sums), seeds], **small)
    far = [h1, l1, h2, l2]
    history = [vectors]
    for _ in range(2):
        near = between_blocks(vectors, -1)
        (ahead,) = call(ahead_body, [pair_shape], [relays, vectors, *far], **middle)
        behind = between_blocks(ahead, 1)
        (product,) = call(own_product_body, [pair_shape], [vectors, h0, l0], **middle)
        (total,) = call(block_body, [pair_shape], [relays, product, near, behind, *far], **middle)
        (vectors,) = call(combine_body, [pair_shape], [total, between_cores(total), degree], **small)
        history.append(vectors)
    near = between_blocks(vectors, -1)
    low, scaled = call(
        low_body, [((5 * NVEC, NVEC), F32), ((3 * NVEC, size), F32)], [degree] + history, **middle)
    (product,) = call(own_product_body, [pair_shape], [vectors, h0, l0], **middle)
    packed_shape = ((3 * NVEC // 4 + 8, 2 * NVEC), F32)
    mine, theirs = call(
        moment_body, [packed_shape] * 2, [spread(core), relays, low, vectors, product, near, *far], **middle)
    mine = total_over_blocks(mine + between_cores(theirs))
    rows = size * blocks * lax.axis_size("narrow")
    (out,) = call(
        lambda *refs: dense_body(rows, *refs), [((NVEC, size), F32)],
        [spread(core), spread(shift_index), mine, between_cores(mine), scaled], flops=2 * 10**10, nbytes=10**6,
    )
    return out.T


def solution(mesh):
    return jax.shard_map(
        shards,
        mesh=mesh,
        in_specs=(
            P(("groups", "blk", "narrow"), None),
            P("groups", None),
            P("groups"),
            P(("groups", "blk", "narrow"), None),
        ),
        out_specs=P(("groups", "blk", "narrow"), None),
        check_vma=False,
    )
```

```python
import math

import jax
import jax.numpy as jnp
from jax import lax
from jax.experimental import pallas as pl
from jax.experimental.pallas import tpu as pltpu
from jax.sharding import PartitionSpec as P

KERNEL_GAMMA = 2.0
RIDGE_WEIGHT = 1e-05
NVEC = 64
F32 = jnp.float32
BF16 = jnp.bfloat16
VMEM_LIMIT = 16 * 1024 * 1024


def dot(left, right, left_dim=1, right_dim=0):
    precision = lax.Precision.HIGHEST if left.dtype == F32 else None
    return lax.dot_general(
        left, right, (((left_dim,), (right_dim,)), ((), ())),
        precision=precision, preferred_element_type=F32,
    )


def halves(values):
    high = values.astype(BF16)
    return high, (values - high.astype(F32)).astype(BF16)


def call(body, out_shapes, args, flops=0, nbytes=0):
    return pl.pallas_call(
        body,
        out_shape=[jax.ShapeDtypeStruct(shape, dtype) for shape, dtype in out_shapes],
        in_specs=[pl.BlockSpec(memory_space=pltpu.VMEM) for _ in args],
        out_specs=[pl.BlockSpec(memory_space=pltpu.VMEM) for _ in out_shapes],
        compiler_params=pltpu.CompilerParams(vmem_limit_bytes=VMEM_LIMIT),
        cost_estimate=pl.CostEstimate(flops=flops, bytes_accessed=nbytes, transcendentals=0),
    )(*args)


def spread(value):
    return jnp.broadcast_to(value.astype(F32), (8, 128))


def chosen(flag, first, second):
    rows, cols = first.shape
    wide = jnp.concatenate([flag[0:1, :]] * (cols // 128), axis=1)
    return jnp.where(jnp.broadcast_to(wide, (rows, cols)) > 0.5, first, second)


LOG2_E = 1.4426950408889634


def sums_along(values):
    rows, depth = values.shape
    folded = values[:, :128]
    for j in range(128, depth, 128):
        folded = folded + values[:, j:j + 128]
    return dot(jnp.ones((8, 128), F32), folded, 1, 1)


def fill_tile(weight, row_embs, row_sq, col_emb, high, low, row_sum):
    size = col_emb.shape[0]
    col32 = col_emb.astype(F32)
    col_sq = (2.0 * LOG2_E) * sums_along(col32 * col32)[0:1, :]
    total = jnp.zeros((1, size), F32)
    for half in range(2):
        rows = slice(half * size, (half + 1) * size)
        inner = dot(row_embs[half], col_emb, 1, 1)
        squares = jnp.concatenate([row_sq[rows, :]] * (size // 128), axis=1)
        tile = jnp.exp2((4.0 * LOG2_E) * inner - (squares + col_sq))
        if weight is not None:
            tile = tile * weight
        tile_high, tile_low = halves(tile)
        high[rows, :] = tile_high
        low[rows, :] = tile_low
        row_sum[half * 8:(half + 1) * 8, :] = row_sum[half * 8:(half + 1) * 8, :] + sums_along(tile)
        total = total + jnp.sum(tile, axis=0, keepdims=True)
    return jnp.broadcast_to(total, (8, size))


def own_body(own, other, high, low, row_sum, row_sq, copy, token):
    size = own.shape[0]
    embs = [own[...], other[...]]
    copy[...] = embs[0]
    for half in range(2):
        row32 = embs[half].astype(F32)
        squares = (2.0 * LOG2_E) * jnp.sum(row32 * row32, axis=1, keepdims=True)
        row_sq[half * size:(half + 1) * size, :] = jnp.broadcast_to(squares, (size, 128))
    row_sum[...] = jnp.zeros(row_sum.shape, F32)
    token[...] = jnp.zeros(token.shape, F32)
    fill_tile(None, embs, row_sq, embs[0], high, low, row_sum)


def far_body(keep, relays, token, own, other, row_sq, direct, relayed, before, high, low, row_sum, col_sum):
    row_sum[...] = before[...] + token[0:1, 0:1]
    size = own.shape[0]
    weight = jnp.concatenate([keep[0:1, :]] * (size // 128), axis=1)
    col = chosen(relays, relayed[...], direct[...])
    col_sum[...] = fill_tile(weight, [own[...], other[...]], row_sq, col, high, low, row_sum)


def make_tile(body, args, rows, extra=()):
    return call(
        body, [((2 * rows, rows), BF16), ((2 * rows, rows), BF16), ((16, rows), F32), *extra],
        args, flops=2 * 10**9, nbytes=10**6,
    )


def swapped(values):
    middle = values.shape[0] // 2
    return jnp.concatenate([values[middle:], values[:middle]], axis=0)


def per_row(values, width):
    shape = (width, values.shape[1])
    return jnp.concatenate([jnp.broadcast_to(values[i:i + 1, :], shape) for i in (0, 8)], axis=0)


def degree_body(sums, other_sums, seeds, degree_out, vectors_out):
    degree = sums[...] + swapped(other_sums[...])
    scale = lax.rsqrt(degree)
    degree_out[...] = degree
    vectors_out[...] = seeds[...] * per_row(scale, seeds.shape[0] // 2)


def ahead_body(relays, vectors, h1, l1, h2, l2, ahead):
    width = vectors.shape[0] // 2
    high, low = halves(jnp.concatenate([vectors[:width, :], vectors[width:, :]], axis=1))
    both = jnp.concatenate([high, low], axis=0)
    products = []
    for tile_high, tile_low in ((h1, l1), (h2, l2)):
        product = dot(both, tile_high[...])
        products.append(product[:width] + product[width:] + dot(high, tile_low[...]))
    ahead[:width, :] = chosen(relays, products[1], products[0])
    ahead[width:, :] = chosen(relays, products[0], products[1])


def combine_body(total, other_total, degree, vectors_out):
    vectors_out[...] = (total[...] + swapped(other_total[...])) / per_row(degree[...], total.shape[0] // 2)


def product_rows(vectors, tile_high, tile_low):
    width = vectors.shape[0]
    high, low = halves(vectors)
    both = jnp.concatenate([high, low], axis=0)
    product = dot(both, tile_high[...], 1, 1)
    return product[:width] + product[width:] + dot(high, tile_low[...], 1, 1)


def stacked(product):
    size = product.shape[1] // 2
    return jnp.concatenate([product[:, :size], product[:, size:]], axis=0)


def own_product_body(vectors, h0, l0, out):
    out[...] = stacked(product_rows(vectors[:vectors.shape[0] // 2, :], h0, l0))


def far_product(relays, near, h1, l1, h2, l2):
    width = near.shape[0] // 2
    first = chosen(relays, near[width:, :], near[:width, :])
    second = chosen(relays, near[:width, :], near[width:, :])
    return product_rows(first, h1, l1) + product_rows(second, h2, l2)


def block_body(relays, product, near, behind, h1, l1, h2, l2, total):
    total[...] = product[...] + behind[...] + stacked(far_product(relays, near, h1, l1, h2, l2))


def low_body(degree, v0, v1, v2, moments, scaled):
    width = v0.shape[0] // 2
    root = jnp.sqrt(degree[0:1, :])
    x0, x1, x2 = v0[:width, :] * root, v1[:width, :] * root, v2[:width, :] * root
    scaled[...] = jnp.concatenate([x0, x1, x2], axis=0)
    left = jnp.concatenate([x0, x1], axis=0)
    order012 = dot(left, left, 1, 1)
    order34 = dot(jnp.concatenate([x1, x2], axis=0), x2, 1, 1)
    order = [order012[:width, :width], order012[:width, width:], order012[width:, width:],
             order34[:width], order34[width:]]
    for i in range(5):
        moments[i * width:(i + 1) * width, :] = order[i]


def place_of(rows, cols):
    return [lax.broadcasted_iota(jnp.int32, (rows, cols), axis) for axis in range(2)]


def moment_body(core, relays, low, vectors, product, near, h1, l1, h2, l2, mine, theirs):
    n = vectors.shape[0] // 2
    last = far_product(relays, near, h1, l1, h2, l2)
    last = 2.0 * last + jnp.concatenate([product[:n, :], product[n:, :]], axis=1)
    last = dot(jnp.concatenate([vectors[:n, :], vectors[n:, :]], axis=1), last, 1, 1)
    moments = [low[i * n:(i + 1) * n, :] for i in range(5)] + [0.5 * (last + last.T)]
    row, col = place_of(n, n)
    pieces = []
    for i in range(0, 6, 2):
        pair = jnp.where(row >= col, moments[i], moments[i + 1])
        pieces.append(jnp.concatenate([pair[:n // 2], pair[n // 2:]], axis=1))
    d1, d3, d5 = (jnp.sum(moments[i] * unit(n, n), axis=0, keepdims=True) for i in (1, 3, 5))
    row, _ = place_of(8, 2 * n)
    pieces.append(jnp.where(row == 0, jnp.concatenate([d1, d3], axis=1),
                            jnp.where(row == 1, jnp.concatenate([d5, d5], axis=1), 0.0)))
    pieces.append(jnp.zeros((8, 2 * n), F32))
    packed = jnp.concatenate(pieces, axis=0)
    half = packed.shape[0] // 2
    mine[...] = chosen(core, packed[half:], packed[:half])
    theirs[...] = chosen(core, packed[:half], packed[half:])


def unpacked(packed, n):
    row, col = place_of(n, n)
    start = 3 * n // 2
    diagonals = [packed[start:start + 1, :n], packed[start:start + 1, n:], packed[start + 1:start + 2, :n]]
    moments = []
    for i in range(3):
        folded = packed[i * n // 2:(i + 1) * n // 2]
        pair = jnp.concatenate([folded[:, :n], folded[:, n:]], axis=0)
        flipped = pair.T
        moments.append(jnp.where(row >= col, pair, flipped))
        moments.append(jnp.where(row == col, diagonals[i], jnp.where(row < col, pair, flipped)))
    return moments


def unit(rows, cols):
    return (lax.broadcasted_iota(jnp.int32, (rows, cols), 0)
            == lax.broadcasted_iota(jnp.int32, (rows, cols), 1)).astype(F32)


def lane(values, k):
    return jnp.take_along_axis(values, jnp.full(values.shape, k, jnp.int32), axis=1, mode="promise_in_bounds")


def sublane(values, k):
    return jnp.broadcast_to(values[k:k + 1, :], values.shape)


def inverse_factor(matrix):
    size = matrix.shape[0]
    work = jnp.concatenate([matrix, unit(size, size)], axis=1)
    blocks = [work[8 * i:8 * i + 8, :] for i in range(size // 8)]
    place = lax.broadcasted_iota(jnp.int32, (8, 2 * size), 0)
    done = [None] * (size // 8)

    def corner(cols, r):
        return [[sublane(cols[j], r + i) for j in range(i + 1)] for i in range(4)]

    pivot = corner([lane(blocks[0], j) for j in range(4)], 0)
    for k in range(0, size, 4):
        top, r = divmod(k, 8)
        (a00,), (a10, a11), (a20, a21, a22), (a30, a31, a32, a33) = pivot
        u0, u1, u2, u3 = u = [sublane(blocks[top], r + j) for j in range(4)]
        det_a = a00 * a11 - a10 * a10
        inv_a = 1.0 / det_a
        p00, p10, p11 = a11 * inv_a, a10 * inv_a, a00 * inv_a
        b00, b01 = a20 * p00 - a21 * p10, a21 * p11 - a20 * p10
        b10, b11 = a30 * p00 - a31 * p10, a31 * p11 - a30 * p10
        s00 = a22 - (b00 * a20 + b01 * a21)
        s10 = a32 - (b10 * a20 + b11 * a21)
        s11 = a33 - (b10 * a30 + b11 * a31)
        det_s = s00 * s11 - s10 * s10
        inv_s = 1.0 / det_s
        q22, q32, q33 = s11 * inv_s, -s10 * inv_s, s00 * inv_s
        q20, q21 = -(q22 * b00 + q32 * b10), -(q22 * b01 + q32 * b11)
        q30, q31 = -(q32 * b00 + q33 * b10), -(q32 * b01 + q33 * b11)
        q00 = p00 - (b00 * q20 + b10 * q30)
        q10 = -p10 - (b01 * q20 + b11 * q30)
        q11 = p11 - (b01 * q21 + b11 * q31)
        inverse = [[q00, q10, q20, q30], [q10, q11, q21, q31], [q20, q21, q22, q32], [q30, q31, q32, q33]]

        def applied(values):
            return [(row[0] * values[0] + row[1] * values[1]) + (row[2] * values[2] + row[3] * values[3])
                    for row in inverse]

        if k + 4 < size:
            across = [lane(blocks[top], k + 4 + j) for j in range(4)]
            cross = [[sublane(across[j], r + i) for i in range(4)] for j in range(4)]
            after = across if r == 0 else [lane(blocks[top + 1], k + 4 + j) for j in range(4)]
            plain = corner(after, 4 - r)
            solved = [applied(column) for column in cross]
            pivot = [[plain[i][j] - ((cross[i][0] * solved[j][0] + cross[i][1] * solved[j][1])
                                     + (cross[i][2] * solved[j][2] + cross[i][3] * solved[j][3]))
                      for j in range(i + 1)] for i in range(4)]
        t = applied(u)
        for i in range(top, size // 8):
            if i == top and r:
                continue
            c = [lane(blocks[i], k + j) for j in range(4)]
            change = (c[0] * t[0] + c[1] * t[1]) + (c[2] * t[2] + c[3] * t[3])
            blocks[i] = blocks[i] - (jnp.where(place > 3, change, 0.0) if i == top else change)
        v0 = u0 * lax.rsqrt(a00)
        v1 = (a00 * u1 - a10 * u0) * lax.rsqrt(a00 * det_a)
        u2 = u2 - b00 * u0 - b01 * u1
        u3 = u3 - b10 * u0 - b11 * u1
        v2 = u2 * lax.rsqrt(s00)
        v3 = (s00 * u3 - s10 * u2) * lax.rsqrt(s00 * det_s)
        four = jnp.where(place % 4 == 0, v0, jnp.where(place % 4 == 1, v1, jnp.where(place % 4 == 2, v2, v3)))
        done[top] = jnp.where(place > 3, four, done[top]) if r else four
    return jnp.concatenate(done, axis=0)[:, size:]


def total(matrix):
    return jnp.sum(jnp.sum(matrix, axis=0, keepdims=True), axis=1, keepdims=True)


def trace(matrix):
    return total(matrix * unit(*matrix.shape))


def inverse_root(matrix):
    eye = unit(*matrix.shape)
    rest = matrix - eye

    def series():
        return eye - 0.5 * rest + 0.375 * dot(rest, rest)

    return lax.cond(jnp.sum(rest * rest) < 1e-4, series, lambda: inverse_factor(matrix))


def dense(moments, index, rows, data):
    n = NVEC
    eye = unit(n, n)
    pick = ((lax.broadcasted_iota(jnp.int32, (n, n), 0) == index)
            & (lax.broadcasted_iota(jnp.int32, (n, n), 1) == index)).astype(F32)

    def part(stacked, i):
        return stacked[i * n:(i + 1) * n]

    def below(*parts):
        return jnp.concatenate(parts, axis=0)

    def beside(*parts):
        return jnp.concatenate(parts, axis=1)

    base = inverse_factor(moments[0])
    right = dot(below(*moments[1:]), base, 1, 1)
    m1, m2, m3, m4, m5 = (dot(base, part(right, i)) for i in range(5))
    y0, y1, y2 = (dot(base, part(data, i)) for i in range(3))

    by1 = dot(below(m1, m2, m3, m4), m1)
    square, m21, m31, m41 = (part(by1, i) for i in range(4))
    tri = dot(m1, beside(square, m21, m31))
    gram_r = m2 - square
    image_r = m3 - m21 - m21.T + tri[:, :n]
    mixed_r = m3 - m21
    square_r = m4 - m31 - m31.T + tri[:, n:2 * n]
    cubic_r = m5 - m41 - m41.T + tri[:, 2 * n:]
    shift = 3.0 - total(m1 * pick)
    ridge = RIDGE_WEIGHT * (n + trace(gram_r)) / (2 * n)
    ridged = gram_r + ridge * eye
    factor = inverse_factor(ridged)
    inverse = dot(factor, factor, 0, 0)
    keep = 1.0 / (1.0 + ridge)
    step = below(
        beside(m1 * keep + shift * eye, gram_r * keep),
        beside(eye - ridge * inverse, dot(inverse, image_r) + shift * eye),
    )
    twice = dot(step, step)
    power = dot(twice, dot(twice, twice[:, :n]))
    top, bottom = power[:n], power[n:]
    weighted = dot(below(ridged, gram_r, image_r), bottom)
    norm = (1.0 + ridge) * dot(top, top, 0, 0) + dot(bottom, part(weighted, 0), 0, 0)
    factor = inverse_factor(norm)

    middle = m4 - m31
    images = dot(below(
        beside(m1, gram_r), beside(gram_r, image_r),
        beside(m2, mixed_r), beside(mixed_r.T, square_r),
        beside(m3, middle), beside(middle.T, cubic_r),
    ), power)
    whole = dot(power, beside(images[:2 * n], images[2 * n:4 * n], images[4 * n:], power), 0, 0)
    lower = dot(bottom, beside(part(images, 1), part(images, 3), part(weighted, 1), part(weighted, 2)), 0, 0)
    raw = [whole[:, i * n:(i + 1) * n] for i in range(4)] + [lower[:, i * n:(i + 1) * n] for i in range(4)]
    right = dot(below(*raw), factor, 1, 1)
    ritz, image2, image3, excess, p_image, p_image2, p_gram, p_ritz = (dot(factor, part(right, i)) for i in range(8))
    excess = ridge * excess

    shift = 3.0 - total(ritz * pick)
    by_ritz = dot(below(ritz, p_gram, excess, p_image, image2), ritz)
    squared, gram_pr, gram_cr = part(by_ritz, 0), p_image - part(by_ritz, 1), part(by_ritz, 2)
    tri = dot(ritz, squared), dot(ritz, gram_cr)
    gram_rr = image2 - squared - tri[1]
    image_cr = image2 - squared
    image_pr = p_image2 - part(by_ritz, 3)
    image_rr = image3 - part(by_ritz, 4) - part(by_ritz, 4).T + tri[0]
    ridge = RIDGE_WEIGHT * (n - trace(excess) + trace(p_gram) + trace(gram_rr)) / (3 * n)
    g_cc = eye - excess + ridge * eye
    g_pp = p_gram + ridge * eye
    g_rr = gram_rr + ridge * eye
    image_gram = below(
        beside(ritz, p_image.T, image_cr), beside(p_image, p_ritz, image_pr), beside(image_cr.T, image_pr.T, image_rr),
    )
    v0 = inverse_root(g_cc)
    side = dot(below(p_gram, gram_cr.T), v0, 1, 1)
    l10, l20 = side[:n], side[n:]
    outer = dot(side, side, 1, 1)
    v1 = inverse_factor(g_pp - outer[:n, :n])
    l21 = dot(gram_pr.T - outer[n:, :n], v1, 1, 1)
    v2 = inverse_factor(g_rr - outer[n:, n:] - dot(l21, l21, 1, 1))
    zero = jnp.zeros((n, n), F32)
    row0 = beside(v0, zero, zero)
    row1 = dot(v1, beside(-dot(l10, v0), eye, zero))
    row2 = beside(zero, zero, eye) - dot(l20, row0) - dot(l21, row1)
    known = below(row0, row1)
    solved = dot(known, dot(known, image_gram), 0, 0)
    row2 = dot(v2, beside(row2, dot(row2, image_gram)))
    step = solved + dot(row2[:, :3 * n], row2[:, 3 * n:], 0, 0) + shift * unit(3 * n, 3 * n)
    twice = dot(step, step)
    power2 = dot(twice, dot(twice, twice[:, :n]))
    gram = below(
        beside(g_cc, p_gram, gram_cr), beside(p_gram, g_pp, gram_pr), beside(gram_cr.T, gram_pr.T, g_rr),
    )
    norm = dot(power2, dot(gram, power2), 0, 0)

    start = dot(power, below(y0, y1), 0, 0) - dot(dot(m1, bottom), y0, 0, 0)
    image = dot(power, below(y1, y2), 0, 0) - dot(dot(m1, bottom), y1, 0, 0)
    residue = dot(bottom, y1 - dot(m1, y0), 0, 0)
    current = dot(factor, start)
    vectors = below(current, dot(factor, residue), dot(factor, image) - dot(ritz, current))
    return dot(inverse_factor(norm), dot(power2, vectors, 0, 0)) * math.sqrt(rows)


def dense_body(rows, core, index, mine, theirs, scaled, out):
    packed = jnp.concatenate([
        chosen(core, theirs[...], mine[...]), chosen(core, mine[...], theirs[...])], axis=0)
    index = jnp.broadcast_to(index[0:1, :NVEC], (NVEC, NVEC)).astype(jnp.int32)
    out[...] = dense(unpacked(packed, NVEC), index, rows, scaled[...])


def between_blocks(shard, sign):
    blocks, cores = lax.axis_size("blk"), lax.axis_size("narrow")
    pairs = [(i * cores + j, (i + sign * (1 + j)) % blocks * cores + j) for i in range(blocks) for j in range(cores)]
    return lax.ppermute(shard, ("blk", "narrow"), pairs)


def between_cores(shard):
    return lax.ppermute(shard, "narrow", [(0, 1), (1, 0)])


def total_over_blocks(values):
    blocks = lax.axis_size("blk")
    span = 1
    while blocks % (2 * span) == 0:
        values = values + lax.ppermute(values, "blk", [(i, i ^ span) for i in range(blocks)])
        span *= 2
    if span < blocks:
        groups = [list(range(i, blocks, span)) for i in range(span)]
        values = lax.psum(values, "blk", axis_index_groups=groups)
    return values


def shards(embeddings, pair_mask, shift_index, start_seed):
    size = embeddings.shape[0]
    blocks = lax.axis_size("blk")
    where = lax.axis_index("blk")
    core = lax.axis_index("narrow")
    other_emb = between_cores(embeddings)
    relaying = blocks % 2 == 0
    back1 = [(i, (i - 1) % blocks) for i in range(blocks) if i % 2 or not relaying]
    back2 = [(i, (i - 2) % blocks) for i in range(blocks)]
    orders = [
        [(2 * i + j, 2 * k) for i, k in back1] + [(2 * i + 1 - j, 2 * k + 1) for i, k in back2] for j in range(2)]
    if relaying:
        orders[0] += [(2 * i, 2 * i + 2) for i in range(0, blocks, 2)]

    def between_shards(shard, pairs):
        return lax.ppermute(shard, ("blk", "narrow"), pairs)

    first = between_shards(embeddings, orders[0])
    seed = start_seed.astype(F32).T / 1000.0
    seeds = jnp.concatenate([seed, between_cores(seed)], axis=0)
    keep = spread(lax.dynamic_slice(pair_mask, (where, core), (1, 1)))
    relays = spread((1 - core) * (where % 2) * int(relaying))
    pair_shape, row_shape = ((2 * NVEC, size), F32), ((16, size), F32)
    h0, l0, sums, row_sq, own_copy, token = make_tile(
        own_body, [embeddings, other_emb], size,
        (((2 * size, 128), F32), (embeddings.shape, BF16), ((8, 128), F32)))
    first, seeds, keep, relays, token = lax.optimization_barrier((first, seeds, keep, relays, token))
    relayed = [first, own_copy]
    if relaying:
        relayed[1] = between_shards(first, [(2 * i, (i - 2) % blocks * 2) for i in range(1, blocks, 2)])
    second = between_shards(own_copy, orders[1])
    if relaying:
        relayed[0] = between_shards(first, [(2 * i + 1, 2 * i + 2) for i in range(0, blocks, 2)])
    tile_args = [keep, relays, token, own_copy, other_emb, row_sq]
    h1, l1, sums, cols1 = make_tile(
        far_body, [*tile_args, first, relayed[0], sums], size, (((8, size), F32),))
    h2, l2, sums, cols2 = make_tile(
        far_body, [*tile_args, second, relayed[1], sums], size, (((8, size), F32),))
    cols = jnp.concatenate([jnp.where(relays[0, 0] > 0.5, cols2, cols1), jnp.where(relays[0, 0] > 0.5, cols1, cols2)])
    sums = sums + between_blocks(cols, 1)

    small = dict(flops=10**6, nbytes=10**5)
    middle = dict(flops=10**9, nbytes=10**6)
    degree, vectors = call(
        degree_body, [row_shape, pair_shape], [sums, between_cores(sums), seeds], **small)
    far = [h1, l1, h2, l2]
    history = [vectors]
    for _ in range(2):
        near = between_blocks(vectors, -1)
        (ahead,) = call(ahead_body, [pair_shape], [relays, vectors, *far], **middle)
        behind = between_blocks(ahead, 1)
        (product,) = call(own_product_body, [pair_shape], [vectors, h0, l0], **middle)
        (total,) = call(block_body, [pair_shape], [relays, product, near, behind, *far], **middle)
        (vectors,) = call(combine_body, [pair_shape], [total, between_cores(total), degree], **small)
        history.append(vectors)
    near = between_blocks(vectors, -1)
    low, scaled = call(
        low_body, [((5 * NVEC, NVEC), F32), ((3 * NVEC, size), F32)], [degree] + history, **middle)
    (product,) = call(own_product_body, [pair_shape], [vectors, h0, l0], **middle)
    packed_shape = ((3 * NVEC // 4 + 8, 2 * NVEC), F32)
    mine, theirs = call(
        moment_body, [packed_shape] * 2, [spread(core), relays, low, vectors, product, near, *far], **middle)
    mine = total_over_blocks(mine + between_cores(theirs))
    rows = size * blocks * lax.axis_size("narrow")
    (out,) = call(
        lambda *refs: dense_body(rows, *refs), [((NVEC, size), F32)],
        [spread(core), spread(shift_index), mine, between_cores(mine), scaled], flops=2 * 10**10, nbytes=10**6,
    )
    return out.T


def solution(mesh):
    return jax.shard_map(
        shards,
        mesh=mesh,
        in_specs=(
            P(("groups", "blk", "narrow"), None),
            P("groups", None),
            P("groups"),
            P(("groups", "blk", "narrow"), None),
        ),
        out_specs=P(("groups", "blk", "narrow"), None),
        check_vma=False,
    )
```

```python
import math

import jax
import jax.numpy as jnp
from jax import lax
from jax.experimental import pallas as pl
from jax.experimental.pallas import tpu as pltpu
from jax.sharding import PartitionSpec as P

KERNEL_GAMMA = 2.0
RIDGE_WEIGHT = 1e-05
NVEC = 64
F32 = jnp.float32
BF16 = jnp.bfloat16
VMEM_LIMIT = 16 * 1024 * 1024


def dot(left, right, left_dim=1, right_dim=0):
    precision = lax.Precision.HIGHEST if left.dtype == F32 else None
    return lax.dot_general(
        left, right, (((left_dim,), (right_dim,)), ((), ())),
        precision=precision, preferred_element_type=F32,
    )


def halves(values):
    high = values.astype(BF16)
    return high, (values - high.astype(F32)).astype(BF16)


def call(body, out_shapes, args, flops=0, nbytes=0):
    return pl.pallas_call(
        body,
        out_shape=[jax.ShapeDtypeStruct(shape, dtype) for shape, dtype in out_shapes],
        in_specs=[pl.BlockSpec(memory_space=pltpu.VMEM) for _ in args],
        out_specs=[pl.BlockSpec(memory_space=pltpu.VMEM) for _ in out_shapes],
        compiler_params=pltpu.CompilerParams(vmem_limit_bytes=VMEM_LIMIT),
        cost_estimate=pl.CostEstimate(flops=flops, bytes_accessed=nbytes, transcendentals=0),
    )(*args)


def spread(value):
    return jnp.broadcast_to(value.astype(F32), (8, 128))


def chosen(flag, first, second):
    rows, cols = first.shape
    wide = jnp.concatenate([flag[0:1, :]] * (cols // 128), axis=1)
    return jnp.where(jnp.broadcast_to(wide, (rows, cols)) > 0.5, first, second)


LOG2_E = 1.4426950408889634


def sums_along(values):
    rows, depth = values.shape
    folded = values[:, :128]
    for j in range(128, depth, 128):
        folded = folded + values[:, j:j + 128]
    return dot(jnp.ones((8, 128), F32), folded, 1, 1)


def fill_tile(weight, row_embs, row_sq, col_emb, high, low, row_sum):
    size = col_emb.shape[0]
    col32 = col_emb.astype(F32)
    col_sq = (2.0 * LOG2_E) * sums_along(col32 * col32)[0:1, :]
    total = jnp.zeros((1, size), F32)
    for half in range(2):
        rows = slice(half * size, (half + 1) * size)
        inner = dot(row_embs[half], col_emb, 1, 1)
        squares = jnp.concatenate([row_sq[rows, :]] * (size // 128), axis=1)
        tile = jnp.exp2((4.0 * LOG2_E) * inner - (squares + col_sq))
        if weight is not None:
            tile = tile * weight
        tile_high, tile_low = halves(tile)
        high[rows, :] = tile_high
        low[rows, :] = tile_low
        row_sum[half * 8:(half + 1) * 8, :] = row_sum[half * 8:(half + 1) * 8, :] + sums_along(tile)
        total = total + jnp.sum(tile, axis=0, keepdims=True)
    return jnp.broadcast_to(total, (8, size))


def own_body(own, other, high, low, row_sum, row_sq, copy, token):
    size = own.shape[0]
    embs = [own[...], other[...]]
    copy[...] = embs[0]
    for half in range(2):
        row32 = embs[half].astype(F32)
        squares = (2.0 * LOG2_E) * jnp.sum(row32 * row32, axis=1, keepdims=True)
        row_sq[half * size:(half + 1) * size, :] = jnp.broadcast_to(squares, (size, 128))
    row_sum[...] = jnp.zeros(row_sum.shape, F32)
    token[...] = jnp.zeros(token.shape, F32)
    fill_tile(None, embs, row_sq, embs[0], high, low, row_sum)


def far_body(keep, relays, token, own, other, row_sq, direct, relayed, before, high, low, row_sum, col_sum):
    row_sum[...] = before[...] + token[0:1, 0:1]
    size = own.shape[0]
    weight = jnp.concatenate([keep[0:1, :]] * (size // 128), axis=1)
    col = chosen(relays, relayed[...], direct[...])
    col_sum[...] = fill_tile(weight, [own[...], other[...]], row_sq, col, high, low, row_sum)


def make_tile(body, args, rows, extra=()):
    return call(
        body, [((2 * rows, rows), BF16), ((2 * rows, rows), BF16), ((16, rows), F32), *extra],
        args, flops=2 * 10**9, nbytes=10**6,
    )


def swapped(values):
    middle = values.shape[0] // 2
    return jnp.concatenate([values[middle:], values[:middle]], axis=0)


def per_row(values, width):
    shape = (width, values.shape[1])
    return jnp.concatenate([jnp.broadcast_to(values[i:i + 1, :], shape) for i in (0, 8)], axis=0)


def degree_body(sums, other_sums, seeds, degree_out, vectors_out):
    degree = sums[...] + swapped(other_sums[...])
    scale = lax.rsqrt(degree)
    degree_out[...] = degree
    vectors_out[...] = seeds[...] * per_row(scale, seeds.shape[0] // 2)


def ahead_body(relays, vectors, h1, l1, h2, l2, ahead):
    width = vectors.shape[0] // 2
    high, low = halves(jnp.concatenate([vectors[:width, :], vectors[width:, :]], axis=1))
    both = jnp.concatenate([high, low], axis=0)
    products = []
    for tile_high, tile_low in ((h1, l1), (h2, l2)):
        product = dot(both, tile_high[...])
        products.append(product[:width] + product[width:] + dot(high, tile_low[...]))
    ahead[:width, :] = chosen(relays, products[1], products[0])
    ahead[width:, :] = chosen(relays, products[0], products[1])


def combine_body(total, other_total, degree, vectors_out):
    vectors_out[...] = (total[...] + swapped(other_total[...])) / per_row(degree[...], total.shape[0] // 2)


def product_rows(vectors, tile_high, tile_low):
    width = vectors.shape[0]
    high, low = halves(vectors)
    both = jnp.concatenate([high, low], axis=0)
    product = dot(both, tile_high[...], 1, 1)
    return product[:width] + product[width:] + dot(high, tile_low[...], 1, 1)


def stacked(product):
    size = product.shape[1] // 2
    return jnp.concatenate([product[:, :size], product[:, size:]], axis=0)


def own_product_body(vectors, h0, l0, out):
    out[...] = stacked(product_rows(vectors[:vectors.shape[0] // 2, :], h0, l0))


def far_product(relays, near, h1, l1, h2, l2):
    width = near.shape[0] // 2
    first = chosen(relays, near[width:, :], near[:width, :])
    second = chosen(relays, near[:width, :], near[width:, :])
    return product_rows(first, h1, l1) + product_rows(second, h2, l2)


def near_product_body(relays, product, near, h1, l1, h2, l2, total):
    total[...] = product[...] + stacked(far_product(relays, near, h1, l1, h2, l2))


def add_body(total, behind, out):
    out[...] = total[...] + behind[...]


def low_body(degree, v0, v1, v2, moments, scaled):
    width = v0.shape[0] // 2
    root = jnp.sqrt(degree[0:1, :])
    x0, x1, x2 = v0[:width, :] * root, v1[:width, :] * root, v2[:width, :] * root
    scaled[...] = jnp.concatenate([x0, x1, x2], axis=0)
    left = jnp.concatenate([x0, x1], axis=0)
    order012 = dot(left, left, 1, 1)
    order34 = dot(jnp.concatenate([x1, x2], axis=0), x2, 1, 1)
    order = [order012[:width, :width], order012[:width, width:], order012[width:, width:],
             order34[:width], order34[width:]]
    for i in range(5):
        moments[i * width:(i + 1) * width, :] = order[i]


def place_of(rows, cols):
    return [lax.broadcasted_iota(jnp.int32, (rows, cols), axis) for axis in range(2)]


def moment_body(core, relays, low, vectors, product, near, h1, l1, h2, l2, mine, theirs):
    n = vectors.shape[0] // 2
    last = far_product(relays, near, h1, l1, h2, l2)
    last = 2.0 * last + jnp.concatenate([product[:n, :], product[n:, :]], axis=1)
    last = dot(jnp.concatenate([vectors[:n, :], vectors[n:, :]], axis=1), last, 1, 1)
    moments = [low[i * n:(i + 1) * n, :] for i in range(5)] + [0.5 * (last + last.T)]
    row, col = place_of(n, n)
    pieces = []
    for i in range(0, 6, 2):
        pair = jnp.where(row >= col, moments[i], moments[i + 1])
        pieces.append(jnp.concatenate([pair[:n // 2], pair[n // 2:]], axis=1))
    d1, d3, d5 = (jnp.sum(moments[i] * unit(n, n), axis=0, keepdims=True) for i in (1, 3, 5))
    row, _ = place_of(8, 2 * n)
    pieces.append(jnp.where(row == 0, jnp.concatenate([d1, d3], axis=1),
                            jnp.where(row == 1, jnp.concatenate([d5, d5], axis=1), 0.0)))
    pieces.append(jnp.zeros((8, 2 * n), F32))
    packed = jnp.concatenate(pieces, axis=0)
    half = packed.shape[0] // 2
    mine[...] = chosen(core, packed[half:], packed[:half])
    theirs[...] = chosen(core, packed[:half], packed[half:])


def unpacked(packed, n):
    row, col = place_of(n, n)
    start = 3 * n // 2
    diagonals = [packed[start:start + 1, :n], packed[start:start + 1, n:], packed[start + 1:start + 2, :n]]
    moments = []
    for i in range(3):
        folded = packed[i * n // 2:(i + 1) * n // 2]
        pair = jnp.concatenate([folded[:, :n], folded[:, n:]], axis=0)
        flipped = pair.T
        moments.append(jnp.where(row >= col, pair, flipped))
        moments.append(jnp.where(row == col, diagonals[i], jnp.where(row < col, pair, flipped)))
    return moments


def unit(rows, cols):
    return (lax.broadcasted_iota(jnp.int32, (rows, cols), 0)
            == lax.broadcasted_iota(jnp.int32, (rows, cols), 1)).astype(F32)


def lane(values, k):
    return jnp.take_along_axis(values, jnp.full(values.shape, k, jnp.int32), axis=1, mode="promise_in_bounds")


def sublane(values, k):
    return jnp.broadcast_to(values[k:k + 1, :], values.shape)


def inverse_factor(matrix):
    size = matrix.shape[0]
    work = jnp.concatenate([matrix, unit(size, size)], axis=1)
    blocks = [work[8 * i:8 * i + 8, :] for i in range(size // 8)]
    place = lax.broadcasted_iota(jnp.int32, (8, 2 * size), 0)
    done = [None] * (size // 8)

    def corner(cols, r):
        return [[sublane(cols[j], r + i) for j in range(i + 1)] for i in range(4)]

    pivot = corner([lane(blocks[0], j) for j in range(4)], 0)
    for k in range(0, size, 4):
        top, r = divmod(k, 8)
        (a00,), (a10, a11), (a20, a21, a22), (a30, a31, a32, a33) = pivot
        u0, u1, u2, u3 = u = [sublane(blocks[top], r + j) for j in range(4)]
        det_a = a00 * a11 - a10 * a10
        inv_a = 1.0 / det_a
        p00, p10, p11 = a11 * inv_a, a10 * inv_a, a00 * inv_a
        b00, b01 = a20 * p00 - a21 * p10, a21 * p11 - a20 * p10
        b10, b11 = a30 * p00 - a31 * p10, a31 * p11 - a30 * p10
        s00 = a22 - (b00 * a20 + b01 * a21)
        s10 = a32 - (b10 * a20 + b11 * a21)
        s11 = a33 - (b10 * a30 + b11 * a31)
        det_s = s00 * s11 - s10 * s10
        inv_s = 1.0 / det_s
        q22, q32, q33 = s11 * inv_s, -s10 * inv_s, s00 * inv_s
        q20, q21 = -(q22 * b00 + q32 * b10), -(q22 * b01 + q32 * b11)
        q30, q31 = -(q32 * b00 + q33 * b10), -(q32 * b01 + q33 * b11)
        q00 = p00 - (b00 * q20 + b10 * q30)
        q10 = -p10 - (b01 * q20 + b11 * q30)
        q11 = p11 - (b01 * q21 + b11 * q31)
        inverse = [[q00, q10, q20, q30], [q10, q11, q21, q31], [q20, q21, q22, q32], [q30, q31, q32, q33]]

        def applied(values):
            return [(row[0] * values[0] + row[1] * values[1]) + (row[2] * values[2] + row[3] * values[3])
                    for row in inverse]

        if k + 4 < size:
            across = [lane(blocks[top], k + 4 + j) for j in range(4)]
            cross = [[sublane(across[j], r + i) for i in range(4)] for j in range(4)]
            after = across if r == 0 else [lane(blocks[top + 1], k + 4 + j) for j in range(4)]
            plain = corner(after, 4 - r)
            solved = [applied(column) for column in cross]
            pivot = [[plain[i][j] - ((cross[i][0] * solved[j][0] + cross[i][1] * solved[j][1])
                                     + (cross[i][2] * solved[j][2] + cross[i][3] * solved[j][3]))
                      for j in range(i + 1)] for i in range(4)]
        t = applied(u)
        for i in range(top, size // 8):
            if i == top and r:
                continue
            c = [lane(blocks[i], k + j) for j in range(4)]
            change = (c[0] * t[0] + c[1] * t[1]) + (c[2] * t[2] + c[3] * t[3])
            blocks[i] = blocks[i] - (jnp.where(place > 3, change, 0.0) if i == top else change)
        v0 = u0 * lax.rsqrt(a00)
        v1 = (a00 * u1 - a10 * u0) * lax.rsqrt(a00 * det_a)
        u2 = u2 - b00 * u0 - b01 * u1
        u3 = u3 - b10 * u0 - b11 * u1
        v2 = u2 * lax.rsqrt(s00)
        v3 = (s00 * u3 - s10 * u2) * lax.rsqrt(s00 * det_s)
        four = jnp.where(place % 4 == 0, v0, jnp.where(place % 4 == 1, v1, jnp.where(place % 4 == 2, v2, v3)))
        done[top] = jnp.where(place > 3, four, done[top]) if r else four
    return jnp.concatenate(done, axis=0)[:, size:]


def total(matrix):
    return jnp.sum(jnp.sum(matrix, axis=0, keepdims=True), axis=1, keepdims=True)


def trace(matrix):
    return total(matrix * unit(*matrix.shape))


def inverse_root(matrix):
    eye = unit(*matrix.shape)
    rest = matrix - eye

    def series():
        return eye - 0.5 * rest + 0.375 * dot(rest, rest)

    return lax.cond(jnp.sum(rest * rest) < 1e-4, series, lambda: inverse_factor(matrix))


def dense(moments, index, rows, data):
    n = NVEC
    eye = unit(n, n)
    pick = ((lax.broadcasted_iota(jnp.int32, (n, n), 0) == index)
            & (lax.broadcasted_iota(jnp.int32, (n, n), 1) == index)).astype(F32)

    def part(stacked, i):
        return stacked[i * n:(i + 1) * n]

    def below(*parts):
        return jnp.concatenate(parts, axis=0)

    def beside(*parts):
        return jnp.concatenate(parts, axis=1)

    base = inverse_factor(moments[0])
    right = dot(below(*moments[1:]), base, 1, 1)
    m1, m2, m3, m4, m5 = (dot(base, part(right, i)) for i in range(5))
    y0, y1, y2 = (dot(base, part(data, i)) for i in range(3))

    by1 = dot(below(m1, m2, m3, m4), m1)
    square, m21, m31, m41 = (part(by1, i) for i in range(4))
    tri = dot(m1, beside(square, m21, m31))
    gram_r = m2 - square
    image_r = m3 - m21 - m21.T + tri[:, :n]
    mixed_r = m3 - m21
    square_r = m4 - m31 - m31.T + tri[:, n:2 * n]
    cubic_r = m5 - m41 - m41.T + tri[:, 2 * n:]
    shift = 3.0 - total(m1 * pick)
    ridge = RIDGE_WEIGHT * (n + trace(gram_r)) / (2 * n)
    ridged = gram_r + ridge * eye
    factor = inverse_factor(ridged)
    inverse = dot(factor, factor, 0, 0)
    keep = 1.0 / (1.0 + ridge)
    step = below(
        beside(m1 * keep + shift * eye, gram_r * keep),
        beside(eye - ridge * inverse, dot(inverse, image_r) + shift * eye),
    )
    twice = dot(step, step)
    power = dot(twice, dot(twice, twice[:, :n]))
    top, bottom = power[:n], power[n:]
    weighted = dot(below(ridged, gram_r, image_r), bottom)
    norm = (1.0 + ridge) * dot(top, top, 0, 0) + dot(bottom, part(weighted, 0), 0, 0)
    factor = inverse_factor(norm)

    middle = m4 - m31
    images = dot(below(
        beside(m1, gram_r), beside(gram_r, image_r),
        beside(m2, mixed_r), beside(mixed_r.T, square_r),
        beside(m3, middle), beside(middle.T, cubic_r),
    ), power)
    whole = dot(power, beside(images[:2 * n], images[2 * n:4 * n], images[4 * n:], power), 0, 0)
    lower = dot(bottom, beside(part(images, 1), part(images, 3), part(weighted, 1), part(weighted, 2)), 0, 0)
    raw = [whole[:, i * n:(i + 1) * n] for i in range(4)] + [lower[:, i * n:(i + 1) * n] for i in range(4)]
    right = dot(below(*raw), factor, 1, 1)
    ritz, image2, image3, excess, p_image, p_image2, p_gram, p_ritz = (dot(factor, part(right, i)) for i in range(8))
    excess = ridge * excess

    shift = 3.0 - total(ritz * pick)
    by_ritz = dot(below(ritz, p_gram, excess, p_image, image2), ritz)
    squared, gram_pr, gram_cr = part(by_ritz, 0), p_image - part(by_ritz, 1), part(by_ritz, 2)
    tri = dot(ritz, squared), dot(ritz, gram_cr)
    gram_rr = image2 - squared - tri[1]
    image_cr = image2 - squared
    image_pr = p_image2 - part(by_ritz, 3)
    image_rr = image3 - part(by_ritz, 4) - part(by_ritz, 4).T + tri[0]
    ridge = RIDGE_WEIGHT * (n - trace(excess) + trace(p_gram) + trace(gram_rr)) / (3 * n)
    g_cc = eye - excess + ridge * eye
    g_pp = p_gram + ridge * eye
    g_rr = gram_rr + ridge * eye
    image_gram = below(
        beside(ritz, p_image.T, image_cr), beside(p_image, p_ritz, image_pr), beside(image_cr.T, image_pr.T, image_rr),
    )
    v0 = inverse_root(g_cc)
    side = dot(below(p_gram, gram_cr.T), v0, 1, 1)
    l10, l20 = side[:n], side[n:]
    outer = dot(side, side, 1, 1)
    v1 = inverse_factor(g_pp - outer[:n, :n])
    l21 = dot(gram_pr.T - outer[n:, :n], v1, 1, 1)
    v2 = inverse_factor(g_rr - outer[n:, n:] - dot(l21, l21, 1, 1))
    zero = jnp.zeros((n, n), F32)
    row0 = beside(v0, zero, zero)
    row1 = dot(v1, beside(-dot(l10, v0), eye, zero))
    row2 = beside(zero, zero, eye) - dot(l20, row0) - dot(l21, row1)
    known = below(row0, row1)
    solved = dot(known, dot(known, image_gram), 0, 0)
    row2 = dot(v2, beside(row2, dot(row2, image_gram)))
    step = solved + dot(row2[:, :3 * n], row2[:, 3 * n:], 0, 0) + shift * unit(3 * n, 3 * n)
    twice = dot(step, step)
    power2 = dot(twice, dot(twice, twice[:, :n]))
    gram = below(
        beside(g_cc, p_gram, gram_cr), beside(p_gram, g_pp, gram_pr), beside(gram_cr.T, gram_pr.T, g_rr),
    )
    norm = dot(power2, dot(gram, power2), 0, 0)

    start = dot(power, below(y0, y1), 0, 0) - dot(dot(m1, bottom), y0, 0, 0)
    image = dot(power, below(y1, y2), 0, 0) - dot(dot(m1, bottom), y1, 0, 0)
    residue = dot(bottom, y1 - dot(m1, y0), 0, 0)
    current = dot(factor, start)
    vectors = below(current, dot(factor, residue), dot(factor, image) - dot(ritz, current))
    return dot(inverse_factor(norm), dot(power2, vectors, 0, 0)) * math.sqrt(rows)


def dense_body(rows, core, index, mine, theirs, scaled, out):
    packed = jnp.concatenate([
        chosen(core, theirs[...], mine[...]), chosen(core, mine[...], theirs[...])], axis=0)
    index = jnp.broadcast_to(index[0:1, :NVEC], (NVEC, NVEC)).astype(jnp.int32)
    out[...] = dense(unpacked(packed, NVEC), index, rows, scaled[...])


def between_blocks(shard, sign):
    blocks, cores = lax.axis_size("blk"), lax.axis_size("narrow")
    pairs = [(i * cores + j, (i + sign * (1 + j)) % blocks * cores + j) for i in range(blocks) for j in range(cores)]
    return lax.ppermute(shard, ("blk", "narrow"), pairs)


def between_cores(shard):
    return lax.ppermute(shard, "narrow", [(0, 1), (1, 0)])


def total_over_blocks(values):
    blocks = lax.axis_size("blk")
    span = 1
    while blocks % (2 * span) == 0:
        values = values + lax.ppermute(values, "blk", [(i, i ^ span) for i in range(blocks)])
        span *= 2
    if span < blocks:
        groups = [list(range(i, blocks, span)) for i in range(span)]
        values = lax.psum(values, "blk", axis_index_groups=groups)
    return values


def shards(embeddings, pair_mask, shift_index, start_seed):
    size = embeddings.shape[0]
    blocks = lax.axis_size("blk")
    where = lax.axis_index("blk")
    core = lax.axis_index("narrow")
    other_emb = between_cores(embeddings)
    relaying = blocks % 2 == 0
    back1 = [(i, (i - 1) % blocks) for i in range(blocks) if i % 2 or not relaying]
    back2 = [(i, (i - 2) % blocks) for i in range(blocks)]
    orders = [
        [(2 * i + j, 2 * k) for i, k in back1] + [(2 * i + 1 - j, 2 * k + 1) for i, k in back2] for j in range(2)]
    if relaying:
        orders[0] += [(2 * i, 2 * i + 2) for i in range(0, blocks, 2)]

    def between_shards(shard, pairs):
        return lax.ppermute(shard, ("blk", "narrow"), pairs)

    first, second = between_shards(embeddings, orders[0]), between_shards(embeddings, orders[1])
    seed = start_seed.astype(F32).T / 1000.0
    seeds = jnp.concatenate([seed, between_cores(seed)], axis=0)
    keep = spread(lax.dynamic_slice(pair_mask, (where, core), (1, 1)))
    relays = spread((1 - core) * (where % 2) * int(relaying))
    pair_shape, row_shape = ((2 * NVEC, size), F32), ((16, size), F32)
    h0, l0, sums, row_sq, own_copy, token = make_tile(
        own_body, [embeddings, other_emb], size,
        (((2 * size, 128), F32), (embeddings.shape, BF16), ((8, 128), F32)))
    first, second, seeds, keep, relays, token = lax.optimization_barrier(
        (first, second, seeds, keep, relays, token))
    relayed = [first, own_copy]
    if relaying:
        relayed[1] = between_shards(first, [(2 * i, (i - 2) % blocks * 2) for i in range(1, blocks, 2)])
    if relaying:
        relayed[0] = between_shards(first, [(2 * i + 1, 2 * i + 2) for i in range(0, blocks, 2)])
    tile_args = [keep, relays, token, own_copy, other_emb, row_sq]
    h1, l1, sums, cols1 = make_tile(
        far_body, [*tile_args, first, relayed[0], sums], size, (((8, size), F32),))
    h2, l2, sums, cols2 = make_tile(
        far_body, [*tile_args, second, relayed[1], sums], size, (((8, size), F32),))
    cols = jnp.concatenate([jnp.where(relays[0, 0] > 0.5, cols2, cols1), jnp.where(relays[0, 0] > 0.5, cols1, cols2)])
    sums = sums + between_blocks(cols, 1)

    small = dict(flops=10**6, nbytes=10**5)
    middle = dict(flops=10**9, nbytes=10**6)
    degree, vectors = call(
        degree_body, [row_shape, pair_shape], [sums, between_cores(sums), seeds], **small)
    far = [h1, l1, h2, l2]
    history = [vectors]
    for _ in range(2):
        near = between_blocks(vectors, -1)
        (ahead,) = call(ahead_body, [pair_shape], [relays, vectors, *far], **middle)
        behind = between_blocks(ahead, 1)
        (product,) = call(own_product_body, [pair_shape], [vectors, h0, l0], **middle)
        (total,) = call(near_product_body, [pair_shape], [relays, product, near, *far], **middle)
        (total,) = call(add_body, [pair_shape], [total, behind], **small)
        (vectors,) = call(combine_body, [pair_shape], [total, between_cores(total), degree], **small)
        history.append(vectors)
    near = between_blocks(vectors, -1)
    low, scaled = call(
        low_body, [((5 * NVEC, NVEC), F32), ((3 * NVEC, size), F32)], [degree] + history, **middle)
    (product,) = call(own_product_body, [pair_shape], [vectors, h0, l0], **middle)
    packed_shape = ((3 * NVEC // 4 + 8, 2 * NVEC), F32)
    mine, theirs = call(
        moment_body, [packed_shape] * 2, [spread(core), relays, low, vectors, product, near, *far], **middle)
    mine = total_over_blocks(mine + between_cores(theirs))
    rows = size * blocks * lax.axis_size("narrow")
    (out,) = call(
        lambda *refs: dense_body(rows, *refs), [((NVEC, size), F32)],
        [spread(core), spread(shift_index), mine, between_cores(mine), scaled], flops=2 * 10**10, nbytes=10**6,
    )
    return out.T


def solution(mesh):
    return jax.shard_map(
        shards,
        mesh=mesh,
        in_specs=(
            P(("groups", "blk", "narrow"), None),
            P("groups", None),
            P("groups"),
            P(("groups", "blk", "narrow"), None),
        ),
        out_specs=P(("groups", "blk", "narrow"), None),
        check_vma=False,
    )
```

```python
import math

import jax
import jax.numpy as jnp
from jax import lax
from jax.experimental import pallas as pl
from jax.experimental.pallas import tpu as pltpu
from jax.sharding import PartitionSpec as P

KERNEL_GAMMA = 2.0
RIDGE_WEIGHT = 1e-05
NVEC = 64
F32 = jnp.float32
BF16 = jnp.bfloat16
VMEM_LIMIT = 16 * 1024 * 1024


def dot(left, right, left_dim=1, right_dim=0):
    precision = lax.Precision.HIGHEST if left.dtype == F32 else None
    return lax.dot_general(
        left, right, (((left_dim,), (right_dim,)), ((), ())),
        precision=precision, preferred_element_type=F32,
    )


def halves(values):
    high = values.astype(BF16)
    return high, (values - high.astype(F32)).astype(BF16)


def call(body, out_shapes, args, flops=0, nbytes=0):
    return pl.pallas_call(
        body,
        out_shape=[jax.ShapeDtypeStruct(shape, dtype) for shape, dtype in out_shapes],
        in_specs=[pl.BlockSpec(memory_space=pltpu.VMEM) for _ in args],
        out_specs=[pl.BlockSpec(memory_space=pltpu.VMEM) for _ in out_shapes],
        compiler_params=pltpu.CompilerParams(vmem_limit_bytes=VMEM_LIMIT),
        cost_estimate=pl.CostEstimate(flops=flops, bytes_accessed=nbytes, transcendentals=0),
    )(*args)


def spread(value):
    return jnp.broadcast_to(value.astype(F32), (8, 128))


def chosen(flag, first, second):
    rows, cols = first.shape
    wide = jnp.concatenate([flag[0:1, :]] * (cols // 128), axis=1)
    return jnp.where(jnp.broadcast_to(wide, (rows, cols)) > 0.5, first, second)


LOG2_E = 1.4426950408889634


def sums_along(values):
    rows, depth = values.shape
    folded = values[:, :128]
    for j in range(128, depth, 128):
        folded = folded + values[:, j:j + 128]
    return dot(jnp.ones((8, 128), F32), folded, 1, 1)


def fill_tile(weight, row_embs, row_sq, col_emb, high, low, row_sum):
    size = col_emb.shape[0]
    col32 = col_emb.astype(F32)
    col_sq = (2.0 * LOG2_E) * sums_along(col32 * col32)[0:1, :]
    total = jnp.zeros((1, size), F32)
    for half in range(2):
        rows = slice(half * size, (half + 1) * size)
        inner = dot(row_embs[half], col_emb, 1, 1)
        squares = jnp.concatenate([row_sq[rows, :]] * (size // 128), axis=1)
        tile = jnp.exp2((4.0 * LOG2_E) * inner - (squares + col_sq))
        if weight is not None:
            tile = tile * weight
        tile_high, tile_low = halves(tile)
        high[rows, :] = tile_high
        low[rows, :] = tile_low
        row_sum[half * 8:(half + 1) * 8, :] = row_sum[half * 8:(half + 1) * 8, :] + sums_along(tile)
        total = total + jnp.sum(tile, axis=0, keepdims=True)
    return jnp.broadcast_to(total, (8, size))


def own_body(own, other, high, low, row_sum, row_sq, copy, token):
    size = own.shape[0]
    embs = [own[...], other[...]]
    copy[...] = embs[0]
    for half in range(2):
        row32 = embs[half].astype(F32)
        squares = (2.0 * LOG2_E) * jnp.sum(row32 * row32, axis=1, keepdims=True)
        row_sq[half * size:(half + 1) * size, :] = jnp.broadcast_to(squares, (size, 128))
    row_sum[...] = jnp.zeros(row_sum.shape, F32)
    token[...] = jnp.zeros(token.shape, F32)
    fill_tile(None, embs, row_sq, embs[0], high, low, row_sum)


def far_body(keep, relays, token, own, other, row_sq, direct, relayed, before, high, low, row_sum, col_sum):
    row_sum[...] = before[...] + token[0:1, 0:1]
    size = own.shape[0]
    weight = jnp.concatenate([keep[0:1, :]] * (size // 128), axis=1)
    col = chosen(relays, relayed[...], direct[...])
    col_sum[...] = fill_tile(weight, [own[...], other[...]], row_sq, col, high, low, row_sum)


def make_tile(body, args, rows, extra=()):
    return call(
        body, [((2 * rows, rows), BF16), ((2 * rows, rows), BF16), ((16, rows), F32), *extra],
        args, flops=2 * 10**9, nbytes=10**6,
    )


def swapped(values):
    middle = values.shape[0] // 2
    return jnp.concatenate([values[middle:], values[:middle]], axis=0)


def per_row(values, width):
    shape = (width, values.shape[1])
    return jnp.concatenate([jnp.broadcast_to(values[i:i + 1, :], shape) for i in (0, 8)], axis=0)


def degree_body(sums, other_sums, seeds, degree_out, vectors_out):
    degree = sums[...] + swapped(other_sums[...])
    scale = lax.rsqrt(degree)
    degree_out[...] = degree
    vectors_out[...] = seeds[...] * per_row(scale, seeds.shape[0] // 2)


def ahead_body(relays, vectors, h1, l1, h2, l2, ahead):
    width = vectors.shape[0] // 2
    high, low = halves(jnp.concatenate([vectors[:width, :], vectors[width:, :]], axis=1))
    both = jnp.concatenate([high, low], axis=0)
    products = []
    for tile_high, tile_low in ((h1, l1), (h2, l2)):
        product = dot(both, tile_high[...])
        products.append(product[:width] + product[width:] + dot(high, tile_low[...]))
    ahead[:width, :] = chosen(relays, products[1], products[0])
    ahead[width:, :] = chosen(relays, products[0], products[1])


def combine_body(total, other_total, degree, vectors_out):
    vectors_out[...] = (total[...] + swapped(other_total[...])) / per_row(degree[...], total.shape[0] // 2)


def product_rows(vectors, tile_high, tile_low):
    width = vectors.shape[0]
    high, low = halves(vectors)
    both = jnp.concatenate([high, low], axis=0)
    product = dot(both, tile_high[...], 1, 1)
    return product[:width] + product[width:] + dot(high, tile_low[...], 1, 1)


def stacked(product):
    size = product.shape[1] // 2
    return jnp.concatenate([product[:, :size], product[:, size:]], axis=0)


def own_product_body(vectors, h0, l0, out):
    out[...] = stacked(product_rows(vectors[:vectors.shape[0] // 2, :], h0, l0))


def far_product(relays, near, h1, l1, h2, l2):
    width = near.shape[0] // 2
    first = chosen(relays, near[width:, :], near[:width, :])
    second = chosen(relays, near[:width, :], near[width:, :])
    return product_rows(first, h1, l1) + product_rows(second, h2, l2)


def near_product_body(relays, product, near, h1, l1, h2, l2, total):
    total[...] = product[...] + stacked(far_product(relays, near, h1, l1, h2, l2))


def add_body(total, behind, out):
    out[...] = total[...] + behind[...]


def low_body(degree, v0, v1, v2, moments, scaled):
    width = v0.shape[0] // 2
    root = jnp.sqrt(degree[0:1, :])
    x0, x1, x2 = v0[:width, :] * root, v1[:width, :] * root, v2[:width, :] * root
    scaled[...] = jnp.concatenate([x0, x1, x2], axis=0)
    left = jnp.concatenate([x0, x1], axis=0)
    order012 = dot(left, left, 1, 1)
    order34 = dot(jnp.concatenate([x1, x2], axis=0), x2, 1, 1)
    order = [order012[:width, :width], order012[:width, width:], order012[width:, width:],
             order34[:width], order34[width:]]
    for i in range(5):
        moments[i * width:(i + 1) * width, :] = order[i]


def place_of(rows, cols):
    return [lax.broadcasted_iota(jnp.int32, (rows, cols), axis) for axis in range(2)]


def moment_body(core, relays, low, vectors, product, near, h1, l1, h2, l2, mine, theirs):
    n = vectors.shape[0] // 2
    last = far_product(relays, near, h1, l1, h2, l2)
    last = 2.0 * last + jnp.concatenate([product[:n, :], product[n:, :]], axis=1)
    last = dot(jnp.concatenate([vectors[:n, :], vectors[n:, :]], axis=1), last, 1, 1)
    moments = [low[i * n:(i + 1) * n, :] for i in range(5)] + [0.5 * (last + last.T)]
    row, col = place_of(n, n)
    pieces = []
    for i in range(0, 6, 2):
        pair = jnp.where(row >= col, moments[i], moments[i + 1])
        pieces.append(jnp.concatenate([pair[:n // 2], pair[n // 2:]], axis=1))
    d1, d3, d5 = (jnp.sum(moments[i] * unit(n, n), axis=0, keepdims=True) for i in (1, 3, 5))
    row, _ = place_of(8, 2 * n)
    pieces.append(jnp.where(row == 0, jnp.concatenate([d1, d3], axis=1),
                            jnp.where(row == 1, jnp.concatenate([d5, d5], axis=1), 0.0)))
    pieces.append(jnp.zeros((8, 2 * n), F32))
    packed = jnp.concatenate(pieces, axis=0)
    half = packed.shape[0] // 2
    mine[...] = chosen(core, packed[half:], packed[:half])
    theirs[...] = chosen(core, packed[:half], packed[half:])


def unpacked(packed, n):
    row, col = place_of(n, n)
    start = 3 * n // 2
    diagonals = [packed[start:start + 1, :n], packed[start:start + 1, n:], packed[start + 1:start + 2, :n]]
    moments = []
    for i in range(3):
        folded = packed[i * n // 2:(i + 1) * n // 2]
        pair = jnp.concatenate([folded[:, :n], folded[:, n:]], axis=0)
        flipped = pair.T
        moments.append(jnp.where(row >= col, pair, flipped))
        moments.append(jnp.where(row == col, diagonals[i], jnp.where(row < col, pair, flipped)))
    return moments


def unit(rows, cols):
    return (lax.broadcasted_iota(jnp.int32, (rows, cols), 0)
            == lax.broadcasted_iota(jnp.int32, (rows, cols), 1)).astype(F32)


def lane(values, k):
    return jnp.take_along_axis(values, jnp.full(values.shape, k, jnp.int32), axis=1, mode="promise_in_bounds")


def sublane(values, k):
    return jnp.broadcast_to(values[k:k + 1, :], values.shape)


def inverse_factor(matrix):
    size = matrix.shape[0]
    work = jnp.concatenate([matrix, unit(size, size)], axis=1)
    blocks = [work[8 * i:8 * i + 8, :] for i in range(size // 8)]
    place = lax.broadcasted_iota(jnp.int32, (8, 2 * size), 0)
    done = [None] * (size // 8)

    def corner(cols, r):
        return [[sublane(cols[j], r + i) for j in range(i + 1)] for i in range(4)]

    pivot = corner([lane(blocks[0], j) for j in range(4)], 0)
    for k in range(0, size, 4):
        top, r = divmod(k, 8)
        (a00,), (a10, a11), (a20, a21, a22), (a30, a31, a32, a33) = pivot
        u0, u1, u2, u3 = u = [sublane(blocks[top], r + j) for j in range(4)]
        det_a = a00 * a11 - a10 * a10
        inv_a = 1.0 / det_a
        p00, p10, p11 = a11 * inv_a, a10 * inv_a, a00 * inv_a
        b00, b01 = a20 * p00 - a21 * p10, a21 * p11 - a20 * p10
        b10, b11 = a30 * p00 - a31 * p10, a31 * p11 - a30 * p10
        s00 = a22 - (b00 * a20 + b01 * a21)
        s10 = a32 - (b10 * a20 + b11 * a21)
        s11 = a33 - (b10 * a30 + b11 * a31)
        det_s = s00 * s11 - s10 * s10
        inv_s = 1.0 / det_s
        q22, q32, q33 = s11 * inv_s, -s10 * inv_s, s00 * inv_s
        q20, q21 = -(q22 * b00 + q32 * b10), -(q22 * b01 + q32 * b11)
        q30, q31 = -(q32 * b00 + q33 * b10), -(q32 * b01 + q33 * b11)
        q00 = p00 - (b00 * q20 + b10 * q30)
        q10 = -p10 - (b01 * q20 + b11 * q30)
        q11 = p11 - (b01 * q21 + b11 * q31)
        inverse = [[q00, q10, q20, q30], [q10, q11, q21, q31], [q20, q21, q22, q32], [q30, q31, q32, q33]]

        def applied(values):
            return [(row[0] * values[0] + row[1] * values[1]) + (row[2] * values[2] + row[3] * values[3])
                    for row in inverse]

        if k + 4 < size:
            across = [lane(blocks[top], k + 4 + j) for j in range(4)]
            cross = [[sublane(across[j], r + i) for i in range(4)] for j in range(4)]
            after = across if r == 0 else [lane(blocks[top + 1], k + 4 + j) for j in range(4)]
            plain = corner(after, 4 - r)
            solved = [applied(column) for column in cross]
            pivot = [[plain[i][j] - ((cross[i][0] * solved[j][0] + cross[i][1] * solved[j][1])
                                     + (cross[i][2] * solved[j][2] + cross[i][3] * solved[j][3]))
                      for j in range(i + 1)] for i in range(4)]
        t = applied(u)
        for i in range(top, size // 8):
            if i == top and r:
                continue
            c = [lane(blocks[i], k + j) for j in range(4)]
            change = (c[0] * t[0] + c[1] * t[1]) + (c[2] * t[2] + c[3] * t[3])
            blocks[i] = blocks[i] - (jnp.where(place > 3, change, 0.0) if i == top else change)
        v0 = u0 * lax.rsqrt(a00)
        v1 = (a00 * u1 - a10 * u0) * lax.rsqrt(a00 * det_a)
        u2 = u2 - b00 * u0 - b01 * u1
        u3 = u3 - b10 * u0 - b11 * u1
        v2 = u2 * lax.rsqrt(s00)
        v3 = (s00 * u3 - s10 * u2) * lax.rsqrt(s00 * det_s)
        four = jnp.where(place % 4 == 0, v0, jnp.where(place % 4 == 1, v1, jnp.where(place % 4 == 2, v2, v3)))
        done[top] = jnp.where(place > 3, four, done[top]) if r else four
    return jnp.concatenate(done, axis=0)[:, size:]


def total(matrix):
    return jnp.sum(jnp.sum(matrix, axis=0, keepdims=True), axis=1, keepdims=True)


def trace(matrix):
    return total(matrix * unit(*matrix.shape))


def inverse_root(matrix):
    eye = unit(*matrix.shape)
    rest = matrix - eye

    def series():
        return eye - 0.5 * rest + 0.375 * dot(rest, rest)

    return lax.cond(jnp.sum(rest * rest) < 1e-4, series, lambda: inverse_factor(matrix))


def dense(moments, index, rows, data):
    n = NVEC
    eye = unit(n, n)
    pick = ((lax.broadcasted_iota(jnp.int32, (n, n), 0) == index)
            & (lax.broadcasted_iota(jnp.int32, (n, n), 1) == index)).astype(F32)

    def part(stacked, i):
        return stacked[i * n:(i + 1) * n]

    def below(*parts):
        return jnp.concatenate(parts, axis=0)

    def beside(*parts):
        return jnp.concatenate(parts, axis=1)

    base = inverse_factor(moments[0])
    right = dot(below(*moments[1:]), base, 1, 1)
    m1, m2, m3, m4, m5 = (dot(base, part(right, i)) for i in range(5))
    y0, y1, y2 = (dot(base, part(data, i)) for i in range(3))

    by1 = dot(below(m1, m2, m3, m4), m1)
    square, m21, m31, m41 = (part(by1, i) for i in range(4))
    tri = dot(m1, beside(square, m21, m31))
    gram_r = m2 - square
    image_r = m3 - m21 - m21.T + tri[:, :n]
    mixed_r = m3 - m21
    square_r = m4 - m31 - m31.T + tri[:, n:2 * n]
    cubic_r = m5 - m41 - m41.T + tri[:, 2 * n:]
    shift = 3.0 - total(m1 * pick)
    ridge = RIDGE_WEIGHT * (n + trace(gram_r)) / (2 * n)
    ridged = gram_r + ridge * eye
    factor = inverse_factor(ridged)
    inverse = dot(factor, factor, 0, 0)
    keep = 1.0 / (1.0 + ridge)
    step = below(
        beside(m1 * keep + shift * eye, gram_r * keep),
        beside(eye - ridge * inverse, dot(inverse, image_r) + shift * eye),
    )
    twice = dot(step, step)
    power = dot(twice, dot(twice, twice[:, :n]))
    top, bottom = power[:n], power[n:]
    weighted = dot(below(ridged, gram_r, image_r), bottom)
    norm = (1.0 + ridge) * dot(top, top, 0, 0) + dot(bottom, part(weighted, 0), 0, 0)
    factor = inverse_factor(norm)

    middle = m4 - m31
    images = dot(below(
        beside(m1, gram_r), beside(gram_r, image_r),
        beside(m2, mixed_r), beside(mixed_r.T, square_r),
        beside(m3, middle), beside(middle.T, cubic_r),
    ), power)
    whole = dot(power, beside(images[:2 * n], images[2 * n:4 * n], images[4 * n:], power), 0, 0)
    lower = dot(bottom, beside(part(images, 1), part(images, 3), part(weighted, 1), part(weighted, 2)), 0, 0)
    raw = [whole[:, i * n:(i + 1) * n] for i in range(4)] + [lower[:, i * n:(i + 1) * n] for i in range(4)]
    right = dot(below(*raw), factor, 1, 1)
    ritz, image2, image3, excess, p_image, p_image2, p_gram, p_ritz = (dot(factor, part(right, i)) for i in range(8))
    excess = ridge * excess

    shift = 3.0 - total(ritz * pick)
    by_ritz = dot(below(ritz, p_gram, excess, p_image, image2), ritz)
    squared, gram_pr, gram_cr = part(by_ritz, 0), p_image - part(by_ritz, 1), part(by_ritz, 2)
    tri = dot(ritz, squared), dot(ritz, gram_cr)
    gram_rr = image2 - squared - tri[1]
    image_cr = image2 - squared
    image_pr = p_image2 - part(by_ritz, 3)
    image_rr = image3 - part(by_ritz, 4) - part(by_ritz, 4).T + tri[0]
    ridge = RIDGE_WEIGHT * (n - trace(excess) + trace(p_gram) + trace(gram_rr)) / (3 * n)
    g_cc = eye - excess + ridge * eye
    g_pp = p_gram + ridge * eye
    g_rr = gram_rr + ridge * eye
    image_gram = below(
        beside(ritz, p_image.T, image_cr), beside(p_image, p_ritz, image_pr), beside(image_cr.T, image_pr.T, image_rr),
    )
    v0 = inverse_root(g_cc)
    side = dot(below(p_gram, gram_cr.T), v0, 1, 1)
    l10, l20 = side[:n], side[n:]
    outer = dot(side, side, 1, 1)
    v1 = inverse_factor(g_pp - outer[:n, :n])
    l21 = dot(gram_pr.T - outer[n:, :n], v1, 1, 1)
    v2 = inverse_factor(g_rr - outer[n:, n:] - dot(l21, l21, 1, 1))
    zero = jnp.zeros((n, n), F32)
    row0 = beside(v0, zero, zero)
    row1 = dot(v1, beside(-dot(l10, v0), eye, zero))
    row2 = beside(zero, zero, eye) - dot(l20, row0) - dot(l21, row1)
    known = below(row0, row1)
    solved = dot(known, dot(known, image_gram), 0, 0)
    row2 = dot(v2, beside(row2, dot(row2, image_gram)))
    step = solved + dot(row2[:, :3 * n], row2[:, 3 * n:], 0, 0) + shift * unit(3 * n, 3 * n)
    twice = dot(step, step)
    power2 = dot(twice, dot(twice, twice[:, :n]))
    gram = below(
        beside(g_cc, p_gram, gram_cr), beside(p_gram, g_pp, gram_pr), beside(gram_cr.T, gram_pr.T, g_rr),
    )
    norm = dot(power2, dot(gram, power2), 0, 0)

    start = dot(power, below(y0, y1), 0, 0) - dot(dot(m1, bottom), y0, 0, 0)
    image = dot(power, below(y1, y2), 0, 0) - dot(dot(m1, bottom), y1, 0, 0)
    residue = dot(bottom, y1 - dot(m1, y0), 0, 0)
    current = dot(factor, start)
    vectors = below(current, dot(factor, residue), dot(factor, image) - dot(ritz, current))
    return dot(inverse_factor(norm), dot(power2, vectors, 0, 0)) * math.sqrt(rows)


def dense_body(rows, core, index, mine, theirs, scaled, out):
    packed = jnp.concatenate([
        chosen(core, theirs[...], mine[...]), chosen(core, mine[...], theirs[...])], axis=0)
    index = jnp.broadcast_to(index[0:1, :NVEC], (NVEC, NVEC)).astype(jnp.int32)
    out[...] = dense(unpacked(packed, NVEC), index, rows, scaled[...])


def between_blocks(shard, sign):
    blocks, cores = lax.axis_size("blk"), lax.axis_size("narrow")
    pairs = [(i * cores + j, (i + sign * (1 + j)) % blocks * cores + j) for i in range(blocks) for j in range(cores)]
    return lax.ppermute(shard, ("blk", "narrow"), pairs)


def between_cores(shard):
    return lax.ppermute(shard, "narrow", [(0, 1), (1, 0)])


def total_over_blocks(values):
    blocks = lax.axis_size("blk")
    span = 1
    while blocks % (2 * span) == 0:
        values = values + lax.ppermute(values, "blk", [(i, i ^ span) for i in range(blocks)])
        span *= 2
    if span < blocks:
        groups = [list(range(i, blocks, span)) for i in range(span)]
        values = lax.psum(values, "blk", axis_index_groups=groups)
    return values


def shards(embeddings, pair_mask, shift_index, start_seed):
    size = embeddings.shape[0]
    blocks = lax.axis_size("blk")
    where = lax.axis_index("blk")
    core = lax.axis_index("narrow")
    other_emb = between_cores(embeddings)
    relaying = blocks % 2 == 0
    back1 = [(i, (i - 1) % blocks) for i in range(blocks) if i % 2 or not relaying]
    back2 = [(i, (i - 2) % blocks) for i in range(blocks)]
    orders = [
        [(2 * i + j, 2 * k) for i, k in back1] + [(2 * i + 1 - j, 2 * k + 1) for i, k in back2] for j in range(2)]
    if relaying:
        orders[0] += [(2 * i, 2 * i + 2) for i in range(0, blocks, 2)]

    def between_shards(shard, pairs):
        return lax.ppermute(shard, ("blk", "narrow"), pairs)

    first, second = between_shards(embeddings, orders[0]), between_shards(embeddings, orders[1])
    seed = start_seed.astype(F32).T / 1000.0
    seeds = jnp.concatenate([seed, between_cores(seed)], axis=0)
    keep = spread(lax.dynamic_slice(pair_mask, (where, core), (1, 1)))
    relays = spread((1 - core) * (where % 2) * int(relaying))
    pair_shape, row_shape = ((2 * NVEC, size), F32), ((16, size), F32)
    h0, l0, sums, row_sq, own_copy, token = make_tile(
        own_body, [embeddings, other_emb], size,
        (((2 * size, 128), F32), (embeddings.shape, BF16), ((8, 128), F32)))
    first, seeds, keep, relays, token = lax.optimization_barrier((first, seeds, keep, relays, token))
    relayed = [first, own_copy]
    if relaying:
        forward, second = lax.optimization_barrier((first, second))
        relayed[1] = between_shards(forward, [(2 * i, (i - 2) % blocks * 2) for i in range(1, blocks, 2)])
    if relaying:
        relayed[0] = between_shards(first, [(2 * i + 1, 2 * i + 2) for i in range(0, blocks, 2)])
    tile_args = [keep, relays, token, own_copy, other_emb, row_sq]
    h1, l1, sums, cols1 = make_tile(
        far_body, [*tile_args, first, relayed[0], sums], size, (((8, size), F32),))
    h2, l2, sums, cols2 = make_tile(
        far_body, [*tile_args, second, relayed[1], sums], size, (((8, size), F32),))
    cols = jnp.concatenate([jnp.where(relays[0, 0] > 0.5, cols2, cols1), jnp.where(relays[0, 0] > 0.5, cols1, cols2)])
    sums = sums + between_blocks(cols, 1)

    small = dict(flops=10**6, nbytes=10**5)
    middle = dict(flops=10**9, nbytes=10**6)
    degree, vectors = call(
        degree_body, [row_shape, pair_shape], [sums, between_cores(sums), seeds], **small)
    far = [h1, l1, h2, l2]
    history = [vectors]
    for _ in range(2):
        near = between_blocks(vectors, -1)
        (ahead,) = call(ahead_body, [pair_shape], [relays, vectors, *far], **middle)
        behind = between_blocks(ahead, 1)
        (product,) = call(own_product_body, [pair_shape], [vectors, h0, l0], **middle)
        (total,) = call(near_product_body, [pair_shape], [relays, product, near, *far], **middle)
        (total,) = call(add_body, [pair_shape], [total, behind], **small)
        (vectors,) = call(combine_body, [pair_shape], [total, between_cores(total), degree], **small)
        history.append(vectors)
    near = between_blocks(vectors, -1)
    low, scaled = call(
        low_body, [((5 * NVEC, NVEC), F32), ((3 * NVEC, size), F32)], [degree] + history, **middle)
    (product,) = call(own_product_body, [pair_shape], [vectors, h0, l0], **middle)
    packed_shape = ((3 * NVEC // 4 + 8, 2 * NVEC), F32)
    mine, theirs = call(
        moment_body, [packed_shape] * 2, [spread(core), relays, low, vectors, product, near, *far], **middle)
    mine = total_over_blocks(mine + between_cores(theirs))
    rows = size * blocks * lax.axis_size("narrow")
    (out,) = call(
        lambda *refs: dense_body(rows, *refs), [((NVEC, size), F32)],
        [spread(core), spread(shift_index), mine, between_cores(mine), scaled], flops=2 * 10**10, nbytes=10**6,
    )
    return out.T


def solution(mesh):
    return jax.shard_map(
        shards,
        mesh=mesh,
        in_specs=(
            P(("groups", "blk", "narrow"), None),
            P("groups", None),
            P("groups"),
            P(("groups", "blk", "narrow"), None),
        ),
        out_specs=P(("groups", "blk", "narrow"), None),
        check_vma=False,
    )
```

```python
import math

import jax
import jax.numpy as jnp
from jax import lax
from jax.experimental import pallas as pl
from jax.experimental.pallas import tpu as pltpu
from jax.sharding import PartitionSpec as P

KERNEL_GAMMA = 2.0
RIDGE_WEIGHT = 1e-05
NVEC = 64
F32 = jnp.float32
BF16 = jnp.bfloat16
VMEM_LIMIT = 16 * 1024 * 1024


def dot(left, right, left_dim=1, right_dim=0):
    precision = lax.Precision.HIGHEST if left.dtype == F32 else None
    return lax.dot_general(
        left, right, (((left_dim,), (right_dim,)), ((), ())),
        precision=precision, preferred_element_type=F32,
    )


def halves(values):
    high = values.astype(BF16)
    return high, (values - high.astype(F32)).astype(BF16)


def call(body, out_shapes, args, flops=0, nbytes=0):
    return pl.pallas_call(
        body,
        out_shape=[jax.ShapeDtypeStruct(shape, dtype) for shape, dtype in out_shapes],
        in_specs=[pl.BlockSpec(memory_space=pltpu.VMEM) for _ in args],
        out_specs=[pl.BlockSpec(memory_space=pltpu.VMEM) for _ in out_shapes],
        compiler_params=pltpu.CompilerParams(vmem_limit_bytes=VMEM_LIMIT),
        cost_estimate=pl.CostEstimate(flops=flops, bytes_accessed=nbytes, transcendentals=0),
    )(*args)


def spread(value):
    return jnp.broadcast_to(value.astype(F32), (8, 128))


def chosen(flag, first, second):
    rows, cols = first.shape
    wide = jnp.concatenate([flag[0:1, :]] * (cols // 128), axis=1)
    return jnp.where(jnp.broadcast_to(wide, (rows, cols)) > 0.5, first, second)


LOG2_E = 1.4426950408889634


def sums_along(values):
    rows, depth = values.shape
    folded = values[:, :128]
    for j in range(128, depth, 128):
        folded = folded + values[:, j:j + 128]
    return dot(jnp.ones((8, 128), F32), folded, 1, 1)


def fill_tile(weight, row_embs, row_sq, col_emb, high, low, row_sum):
    size = col_emb.shape[0]
    col32 = col_emb.astype(F32)
    col_sq = (2.0 * LOG2_E) * sums_along(col32 * col32)[0:1, :]
    total = jnp.zeros((1, size), F32)
    for half in range(2):
        rows = slice(half * size, (half + 1) * size)
        inner = dot(row_embs[half], col_emb, 1, 1)
        squares = jnp.concatenate([row_sq[rows, :]] * (size // 128), axis=1)
        tile = jnp.exp2((4.0 * LOG2_E) * inner - (squares + col_sq))
        if weight is not None:
            tile = tile * weight
        tile_high, tile_low = halves(tile)
        high[rows, :] = tile_high
        low[rows, :] = tile_low
        row_sum[half * 8:(half + 1) * 8, :] = row_sum[half * 8:(half + 1) * 8, :] + sums_along(tile)
        total = total + jnp.sum(tile, axis=0, keepdims=True)
    return jnp.broadcast_to(total, (8, size))


def own_body(own, other, high, low, row_sum, row_sq, copy, token):
    size = own.shape[0]
    embs = [own[...], other[...]]
    copy[...] = embs[0]
    for half in range(2):
        row32 = embs[half].astype(F32)
        squares = (2.0 * LOG2_E) * jnp.sum(row32 * row32, axis=1, keepdims=True)
        row_sq[half * size:(half + 1) * size, :] = jnp.broadcast_to(squares, (size, 128))
    row_sum[...] = jnp.zeros(row_sum.shape, F32)
    token[...] = jnp.zeros(token.shape, F32)
    fill_tile(None, embs, row_sq, embs[0], high, low, row_sum)


def far_body(keep, relays, token, own, other, row_sq, direct, relayed, before, high, low, row_sum, col_sum):
    row_sum[...] = before[...] + token[0:1, 0:1]
    size = own.shape[0]
    weight = jnp.concatenate([keep[0:1, :]] * (size // 128), axis=1)
    col = chosen(relays, relayed[...], direct[...])
    col_sum[...] = fill_tile(weight, [own[...], other[...]], row_sq, col, high, low, row_sum)


def make_tile(body, args, rows, extra=()):
    return call(
        body, [((2 * rows, rows), BF16), ((2 * rows, rows), BF16), ((16, rows), F32), *extra],
        args, flops=2 * 10**9, nbytes=10**6,
    )


def swapped(values):
    middle = values.shape[0] // 2
    return jnp.concatenate([values[middle:], values[:middle]], axis=0)


def per_row(values, width):
    shape = (width, values.shape[1])
    return jnp.concatenate([jnp.broadcast_to(values[i:i + 1, :], shape) for i in (0, 8)], axis=0)


def packed_rows(values):
    rows, cols = values.shape
    biggest = jnp.max(jnp.abs(values), axis=1, keepdims=True)
    power = jnp.floor(jnp.log2(jnp.maximum(biggest, 1e-30)) + 1e-3)
    whole = jnp.round(values * jnp.exp2(14.0 - power)).astype(jnp.int32).astype(jnp.int16)
    powers = jnp.broadcast_to(power, (rows, 128)).T[:16, :]
    powers = jnp.concatenate([powers] * (cols // 128), axis=1)
    return jnp.concatenate([whole, powers.astype(jnp.int32).astype(jnp.int16)], axis=0)


def unpacked_rows(message):
    rows, cols = message.shape[0] - 16, message.shape[1]
    whole = message[:rows, :].astype(jnp.int32).astype(F32)
    powers = message[rows:, :128].astype(jnp.int32).astype(F32)[0:1, :]
    scale = jnp.exp2(jnp.broadcast_to(powers, (128, 128)).T[:rows, :] - 14.0)
    return whole * jnp.concatenate([scale] * (cols // 128), axis=1)


def degree_body(sums, other_sums, seeds, degree_out, vectors_out, message):
    degree = sums[...] + swapped(other_sums[...])
    scale = lax.rsqrt(degree)
    degree_out[...] = degree
    vectors = seeds[...] * per_row(scale, seeds.shape[0] // 2)
    vectors_out[...] = vectors
    message[...] = packed_rows(vectors)


def ahead_body(relays, vectors, h1, l1, h2, l2, ahead):
    width = vectors.shape[0] // 2
    high, low = halves(jnp.concatenate([vectors[:width, :], vectors[width:, :]], axis=1))
    both = jnp.concatenate([high, low], axis=0)
    products = []
    for tile_high, tile_low in ((h1, l1), (h2, l2)):
        product = dot(both, tile_high[...])
        products.append(product[:width] + product[width:] + dot(high, tile_low[...]))
    ahead[...] = packed_rows(jnp.concatenate([
        chosen(relays, products[1], products[0]), chosen(relays, products[0], products[1])], axis=0))


def combine_body(total, other_total, degree, vectors_out, message):
    vectors = (total[...] + swapped(other_total[...])) / per_row(degree[...], total.shape[0] // 2)
    vectors_out[...] = vectors
    message[...] = packed_rows(vectors)


def product_rows(vectors, tile_high, tile_low):
    width = vectors.shape[0]
    high, low = halves(vectors)
    both = jnp.concatenate([high, low], axis=0)
    product = dot(both, tile_high[...], 1, 1)
    return product[:width] + product[width:] + dot(high, tile_low[...], 1, 1)


def stacked(product):
    size = product.shape[1] // 2
    return jnp.concatenate([product[:, :size], product[:, size:]], axis=0)


def own_product_body(vectors, h0, l0, out):
    out[...] = stacked(product_rows(vectors[:vectors.shape[0] // 2, :], h0, l0))


def far_product(relays, message, h1, l1, h2, l2):
    near = unpacked_rows(message)
    width = near.shape[0] // 2
    first = chosen(relays, near[width:], near[:width])
    second = chosen(relays, near[:width], near[width:])
    return product_rows(first, h1, l1) + product_rows(second, h2, l2)


def near_product_body(relays, product, near, h1, l1, h2, l2, total):
    total[...] = product[...] + stacked(far_product(relays, near, h1, l1, h2, l2))


def add_body(total, behind, out):
    out[...] = total[...] + unpacked_rows(behind)


def low_body(degree, v0, v1, v2, moments, scaled):
    width = v0.shape[0] // 2
    root = jnp.sqrt(degree[0:1, :])
    x0, x1, x2 = v0[:width, :] * root, v1[:width, :] * root, v2[:width, :] * root
    scaled[...] = jnp.concatenate([x0, x1, x2], axis=0)
    left = jnp.concatenate([x0, x1], axis=0)
    order012 = dot(left, left, 1, 1)
    order34 = dot(jnp.concatenate([x1, x2], axis=0), x2, 1, 1)
    order = [order012[:width, :width], order012[:width, width:], order012[width:, width:],
             order34[:width], order34[width:]]
    for i in range(5):
        moments[i * width:(i + 1) * width, :] = order[i]


def place_of(rows, cols):
    return [lax.broadcasted_iota(jnp.int32, (rows, cols), axis) for axis in range(2)]


def moment_body(core, relays, low, vectors, product, near, h1, l1, h2, l2, mine, theirs):
    n = vectors.shape[0] // 2
    last = far_product(relays, near, h1, l1, h2, l2)
    last = 2.0 * last + jnp.concatenate([product[:n, :], product[n:, :]], axis=1)
    last = dot(jnp.concatenate([vectors[:n, :], vectors[n:, :]], axis=1), last, 1, 1)
    moments = [low[i * n:(i + 1) * n, :] for i in range(5)] + [0.5 * (last + last.T)]
    row, col = place_of(n, n)
    pieces = []
    for i in range(0, 6, 2):
        pair = jnp.where(row >= col, moments[i], moments[i + 1])
        pieces.append(jnp.concatenate([pair[:n // 2], pair[n // 2:]], axis=1))
    d1, d3, d5 = (jnp.sum(moments[i] * unit(n, n), axis=0, keepdims=True) for i in (1, 3, 5))
    row, _ = place_of(8, 2 * n)
    pieces.append(jnp.where(row == 0, jnp.concatenate([d1, d3], axis=1),
                            jnp.where(row == 1, jnp.concatenate([d5, d5], axis=1), 0.0)))
    pieces.append(jnp.zeros((8, 2 * n), F32))
    packed = jnp.concatenate(pieces, axis=0)
    half = packed.shape[0] // 2
    mine[...] = chosen(core, packed[half:], packed[:half])
    theirs[...] = chosen(core, packed[:half], packed[half:])


def unpacked(packed, n):
    row, col = place_of(n, n)
    start = 3 * n // 2
    diagonals = [packed[start:start + 1, :n], packed[start:start + 1, n:], packed[start + 1:start + 2, :n]]
    moments = []
    for i in range(3):
        folded = packed[i * n // 2:(i + 1) * n // 2]
        pair = jnp.concatenate([folded[:, :n], folded[:, n:]], axis=0)
        flipped = pair.T
        moments.append(jnp.where(row >= col, pair, flipped))
        moments.append(jnp.where(row == col, diagonals[i], jnp.where(row < col, pair, flipped)))
    return moments


def unit(rows, cols):
    return (lax.broadcasted_iota(jnp.int32, (rows, cols), 0)
            == lax.broadcasted_iota(jnp.int32, (rows, cols), 1)).astype(F32)


def lane(values, k):
    return jnp.take_along_axis(values, jnp.full(values.shape, k, jnp.int32), axis=1, mode="promise_in_bounds")


def sublane(values, k):
    return jnp.broadcast_to(values[k:k + 1, :], values.shape)


def inverse_factor(matrix):
    size = matrix.shape[0]
    work = jnp.concatenate([matrix, unit(size, size)], axis=1)
    blocks = [work[8 * i:8 * i + 8, :] for i in range(size // 8)]
    place = lax.broadcasted_iota(jnp.int32, (8, 2 * size), 0)
    done = [None] * (size // 8)

    def corner(cols, r):
        return [[sublane(cols[j], r + i) for j in range(i + 1)] for i in range(4)]

    pivot = corner([lane(blocks[0], j) for j in range(4)], 0)
    for k in range(0, size, 4):
        top, r = divmod(k, 8)
        (a00,), (a10, a11), (a20, a21, a22), (a30, a31, a32, a33) = pivot
        u0, u1, u2, u3 = u = [sublane(blocks[top], r + j) for j in range(4)]
        det_a = a00 * a11 - a10 * a10
        inv_a = 1.0 / det_a
        p00, p10, p11 = a11 * inv_a, a10 * inv_a, a00 * inv_a
        b00, b01 = a20 * p00 - a21 * p10, a21 * p11 - a20 * p10
        b10, b11 = a30 * p00 - a31 * p10, a31 * p11 - a30 * p10
        s00 = a22 - (b00 * a20 + b01 * a21)
        s10 = a32 - (b10 * a20 + b11 * a21)
        s11 = a33 - (b10 * a30 + b11 * a31)
        det_s = s00 * s11 - s10 * s10
        inv_s = 1.0 / det_s
        q22, q32, q33 = s11 * inv_s, -s10 * inv_s, s00 * inv_s
        q20, q21 = -(q22 * b00 + q32 * b10), -(q22 * b01 + q32 * b11)
        q30, q31 = -(q32 * b00 + q33 * b10), -(q32 * b01 + q33 * b11)
        q00 = p00 - (b00 * q20 + b10 * q30)
        q10 = -p10 - (b01 * q20 + b11 * q30)
        q11 = p11 - (b01 * q21 + b11 * q31)
        inverse = [[q00, q10, q20, q30], [q10, q11, q21, q31], [q20, q21, q22, q32], [q30, q31, q32, q33]]

        def applied(values):
            return [(row[0] * values[0] + row[1] * values[1]) + (row[2] * values[2] + row[3] * values[3])
                    for row in inverse]

        if k + 4 < size:
            across = [lane(blocks[top], k + 4 + j) for j in range(4)]
            cross = [[sublane(across[j], r + i) for i in range(4)] for j in range(4)]
            after = across if r == 0 else [lane(blocks[top + 1], k + 4 + j) for j in range(4)]
            plain = corner(after, 4 - r)
            solved = [applied(column) for column in cross]
            pivot = [[plain[i][j] - ((cross[i][0] * solved[j][0] + cross[i][1] * solved[j][1])
                                     + (cross[i][2] * solved[j][2] + cross[i][3] * solved[j][3]))
                      for j in range(i + 1)] for i in range(4)]
        t = applied(u)
        for i in range(top, size // 8):
            if i == top and r:
                continue
            c = [lane(blocks[i], k + j) for j in range(4)]
            change = (c[0] * t[0] + c[1] * t[1]) + (c[2] * t[2] + c[3] * t[3])
            blocks[i] = blocks[i] - (jnp.where(place > 3, change, 0.0) if i == top else change)
        v0 = u0 * lax.rsqrt(a00)
        v1 = (a00 * u1 - a10 * u0) * lax.rsqrt(a00 * det_a)
        u2 = u2 - b00 * u0 - b01 * u1
        u3 = u3 - b10 * u0 - b11 * u1
        v2 = u2 * lax.rsqrt(s00)
        v3 = (s00 * u3 - s10 * u2) * lax.rsqrt(s00 * det_s)
        four = jnp.where(place % 4 == 0, v0, jnp.where(place % 4 == 1, v1, jnp.where(place % 4 == 2, v2, v3)))
        done[top] = jnp.where(place > 3, four, done[top]) if r else four
    return jnp.concatenate(done, axis=0)[:, size:]


def total(matrix):
    return jnp.sum(jnp.sum(matrix, axis=0, keepdims=True), axis=1, keepdims=True)


def trace(matrix):
    return total(matrix * unit(*matrix.shape))


def inverse_root(matrix):
    eye = unit(*matrix.shape)
    rest = matrix - eye

    def series():
        return eye - 0.5 * rest + 0.375 * dot(rest, rest)

    return lax.cond(jnp.sum(rest * rest) < 1e-4, series, lambda: inverse_factor(matrix))


def dense(moments, index, rows, data):
    n = NVEC
    eye = unit(n, n)
    pick = ((lax.broadcasted_iota(jnp.int32, (n, n), 0) == index)
            & (lax.broadcasted_iota(jnp.int32, (n, n), 1) == index)).astype(F32)

    def part(stacked, i):
        return stacked[i * n:(i + 1) * n]

    def below(*parts):
        return jnp.concatenate(parts, axis=0)

    def beside(*parts):
        return jnp.concatenate(parts, axis=1)

    base = inverse_factor(moments[0])
    right = dot(below(*moments[1:]), base, 1, 1)
    m1, m2, m3, m4, m5 = (dot(base, part(right, i)) for i in range(5))
    y0, y1, y2 = (dot(base, part(data, i)) for i in range(3))

    by1 = dot(below(m1, m2, m3, m4), m1)
    square, m21, m31, m41 = (part(by1, i) for i in range(4))
    tri = dot(m1, beside(square, m21, m31))
    gram_r = m2 - square
    image_r = m3 - m21 - m21.T + tri[:, :n]
    mixed_r = m3 - m21
    square_r = m4 - m31 - m31.T + tri[:, n:2 * n]
    cubic_r = m5 - m41 - m41.T + tri[:, 2 * n:]
    shift = 3.0 - total(m1 * pick)
    ridge = RIDGE_WEIGHT * (n + trace(gram_r)) / (2 * n)
    ridged = gram_r + ridge * eye
    factor = inverse_factor(ridged)
    inverse = dot(factor, factor, 0, 0)
    keep = 1.0 / (1.0 + ridge)
    step = below(
        beside(m1 * keep + shift * eye, gram_r * keep),
        beside(eye - ridge * inverse, dot(inverse, image_r) + shift * eye),
    )
    twice = dot(step, step)
    power = dot(twice, dot(twice, twice[:, :n]))
    top, bottom = power[:n], power[n:]
    weighted = dot(below(ridged, gram_r, image_r), bottom)
    norm = (1.0 + ridge) * dot(top, top, 0, 0) + dot(bottom, part(weighted, 0), 0, 0)
    factor = inverse_factor(norm)

    middle = m4 - m31
    images = dot(below(
        beside(m1, gram_r), beside(gram_r, image_r),
        beside(m2, mixed_r), beside(mixed_r.T, square_r),
        beside(m3, middle), beside(middle.T, cubic_r),
    ), power)
    whole = dot(power, beside(images[:2 * n], images[2 * n:4 * n], images[4 * n:], power), 0, 0)
    lower = dot(bottom, beside(part(images, 1), part(images, 3), part(weighted, 1), part(weighted, 2)), 0, 0)
    raw = [whole[:, i * n:(i + 1) * n] for i in range(4)] + [lower[:, i * n:(i + 1) * n] for i in range(4)]
    right = dot(below(*raw), factor, 1, 1)
    ritz, image2, image3, excess, p_image, p_image2, p_gram, p_ritz = (dot(factor, part(right, i)) for i in range(8))
    excess = ridge * excess

    shift = 3.0 - total(ritz * pick)
    by_ritz = dot(below(ritz, p_gram, excess, p_image, image2), ritz)
    squared, gram_pr, gram_cr = part(by_ritz, 0), p_image - part(by_ritz, 1), part(by_ritz, 2)
    tri = dot(ritz, squared), dot(ritz, gram_cr)
    gram_rr = image2 - squared - tri[1]
    image_cr = image2 - squared
    image_pr = p_image2 - part(by_ritz, 3)
    image_rr = image3 - part(by_ritz, 4) - part(by_ritz, 4).T + tri[0]
    ridge = RIDGE_WEIGHT * (n - trace(excess) + trace(p_gram) + trace(gram_rr)) / (3 * n)
    g_cc = eye - excess + ridge * eye
    g_pp = p_gram + ridge * eye
    g_rr = gram_rr + ridge * eye
    image_gram = below(
        beside(ritz, p_image.T, image_cr), beside(p_image, p_ritz, image_pr), beside(image_cr.T, image_pr.T, image_rr),
    )
    v0 = inverse_root(g_cc)
    side = dot(below(p_gram, gram_cr.T), v0, 1, 1)
    l10, l20 = side[:n], side[n:]
    outer = dot(side, side, 1, 1)
    v1 = inverse_factor(g_pp - outer[:n, :n])
    l21 = dot(gram_pr.T - outer[n:, :n], v1, 1, 1)
    v2 = inverse_factor(g_rr - outer[n:, n:] - dot(l21, l21, 1, 1))
    zero = jnp.zeros((n, n), F32)
    row0 = beside(v0, zero, zero)
    row1 = dot(v1, beside(-dot(l10, v0), eye, zero))
    row2 = beside(zero, zero, eye) - dot(l20, row0) - dot(l21, row1)
    known = below(row0, row1)
    solved = dot(known, dot(known, image_gram), 0, 0)
    row2 = dot(v2, beside(row2, dot(row2, image_gram)))
    step = solved + dot(row2[:, :3 * n], row2[:, 3 * n:], 0, 0) + shift * unit(3 * n, 3 * n)
    twice = dot(step, step)
    power2 = dot(twice, dot(twice, twice[:, :n]))
    gram = below(
        beside(g_cc, p_gram, gram_cr), beside(p_gram, g_pp, gram_pr), beside(gram_cr.T, gram_pr.T, g_rr),
    )
    norm = dot(power2, dot(gram, power2), 0, 0)

    start = dot(power, below(y0, y1), 0, 0) - dot(dot(m1, bottom), y0, 0, 0)
    image = dot(power, below(y1, y2), 0, 0) - dot(dot(m1, bottom), y1, 0, 0)
    residue = dot(bottom, y1 - dot(m1, y0), 0, 0)
    current = dot(factor, start)
    vectors = below(current, dot(factor, residue), dot(factor, image) - dot(ritz, current))
    return dot(inverse_factor(norm), dot(power2, vectors, 0, 0)) * math.sqrt(rows)


def dense_body(rows, core, index, mine, theirs, scaled, out):
    packed = jnp.concatenate([
        chosen(core, theirs[...], mine[...]), chosen(core, mine[...], theirs[...])], axis=0)
    index = jnp.broadcast_to(index[0:1, :NVEC], (NVEC, NVEC)).astype(jnp.int32)
    out[...] = dense(unpacked(packed, NVEC), index, rows, scaled[...])


def between_blocks(shard, sign):
    blocks, cores = lax.axis_size("blk"), lax.axis_size("narrow")
    pairs = [(i * cores + j, (i + sign * (1 + j)) % blocks * cores + j) for i in range(blocks) for j in range(cores)]
    return lax.ppermute(shard, ("blk", "narrow"), pairs)


def between_cores(shard):
    return lax.ppermute(shard, "narrow", [(0, 1), (1, 0)])


def total_over_blocks(values):
    blocks = lax.axis_size("blk")
    span = 1
    while blocks % (2 * span) == 0:
        values = values + lax.ppermute(values, "blk", [(i, i ^ span) for i in range(blocks)])
        span *= 2
    if span < blocks:
        groups = [list(range(i, blocks, span)) for i in range(span)]
        values = lax.psum(values, "blk", axis_index_groups=groups)
    return values


def shards(embeddings, pair_mask, shift_index, start_seed):
    size = embeddings.shape[0]
    blocks = lax.axis_size("blk")
    where = lax.axis_index("blk")
    core = lax.axis_index("narrow")
    other_emb = between_cores(embeddings)
    relaying = blocks % 2 == 0
    back1 = [(i, (i - 1) % blocks) for i in range(blocks) if i % 2 or not relaying]
    back2 = [(i, (i - 2) % blocks) for i in range(blocks)]
    orders = [
        [(2 * i + j, 2 * k) for i, k in back1] + [(2 * i + 1 - j, 2 * k + 1) for i, k in back2] for j in range(2)]
    if relaying:
        orders[0] += [(2 * i, 2 * i + 2) for i in range(0, blocks, 2)]

    def between_shards(shard, pairs):
        return lax.ppermute(shard, ("blk", "narrow"), pairs)

    first, second = between_shards(embeddings, orders[0]), between_shards(embeddings, orders[1])
    seed = start_seed.astype(F32).T / 1000.0
    seeds = jnp.concatenate([seed, between_cores(seed)], axis=0)
    keep = spread(lax.dynamic_slice(pair_mask, (where, core), (1, 1)))
    relays = spread((1 - core) * (where % 2) * int(relaying))
    pair_shape, row_shape = ((2 * NVEC, size), F32), ((16, size), F32)
    h0, l0, sums, row_sq, own_copy, token = make_tile(
        own_body, [embeddings, other_emb], size,
        (((2 * size, 128), F32), (embeddings.shape, BF16), ((8, 128), F32)))
    first, seeds, keep, relays, token = lax.optimization_barrier((first, seeds, keep, relays, token))
    relayed = [first, own_copy]
    if relaying:
        forward, second = lax.optimization_barrier((first, second))
        relayed[1] = between_shards(forward, [(2 * i, (i - 2) % blocks * 2) for i in range(1, blocks, 2)])
    if relaying:
        relayed[0] = between_shards(first, [(2 * i + 1, 2 * i + 2) for i in range(0, blocks, 2)])
    tile_args = [keep, relays, token, own_copy, other_emb, row_sq]
    h1, l1, sums, cols1 = make_tile(
        far_body, [*tile_args, first, relayed[0], sums], size, (((8, size), F32),))
    h2, l2, sums, cols2 = make_tile(
        far_body, [*tile_args, second, relayed[1], sums], size, (((8, size), F32),))
    cols = jnp.concatenate([jnp.where(relays[0, 0] > 0.5, cols2, cols1), jnp.where(relays[0, 0] > 0.5, cols1, cols2)])
    sums = sums + between_blocks(cols, 1)

    small = dict(flops=10**6, nbytes=10**5)
    middle = dict(flops=10**9, nbytes=10**6)
    message_shape = ((2 * NVEC + 16, size), jnp.int16)
    degree, vectors, message = call(
        degree_body, [row_shape, pair_shape, message_shape], [sums, between_cores(sums), seeds], **small)
    far = [h1, l1, h2, l2]
    history = [vectors]
    for _ in range(2):
        near = between_blocks(message, -1)
        (ahead,) = call(ahead_body, [message_shape], [relays, vectors, *far], **middle)
        behind = between_blocks(ahead, 1)
        (product,) = call(own_product_body, [pair_shape], [vectors, h0, l0], **middle)
        (total,) = call(near_product_body, [pair_shape], [relays, product, near, *far], **middle)
        (total,) = call(add_body, [pair_shape], [total, behind], **small)
        vectors, message = call(
            combine_body, [pair_shape, message_shape], [total, between_cores(total), degree], **small)
        history.append(vectors)
    near = between_blocks(message, -1)
    low, scaled = call(
        low_body, [((5 * NVEC, NVEC), F32), ((3 * NVEC, size), F32)], [degree] + history, **middle)
    (product,) = call(own_product_body, [pair_shape], [vectors, h0, l0], **middle)
    packed_shape = ((3 * NVEC // 4 + 8, 2 * NVEC), F32)
    mine, theirs = call(
        moment_body, [packed_shape] * 2, [spread(core), relays, low, vectors, product, near, *far], **middle)
    mine = total_over_blocks(mine + between_cores(theirs))
    rows = size * blocks * lax.axis_size("narrow")
    (out,) = call(
        lambda *refs: dense_body(rows, *refs), [((NVEC, size), F32)],
        [spread(core), spread(shift_index), mine, between_cores(mine), scaled], flops=2 * 10**10, nbytes=10**6,
    )
    return out.T


def solution(mesh):
    return jax.shard_map(
        shards,
        mesh=mesh,
        in_specs=(
            P(("groups", "blk", "narrow"), None),
            P("groups", None),
            P("groups"),
            P(("groups", "blk", "narrow"), None),
        ),
        out_specs=P(("groups", "blk", "narrow"), None),
        check_vma=False,
    )
```

```python
import math

import jax
import jax.numpy as jnp
from jax import lax
from jax.experimental import pallas as pl
from jax.experimental.pallas import tpu as pltpu
from jax.sharding import PartitionSpec as P

KERNEL_GAMMA = 2.0
RIDGE_WEIGHT = 1e-05
NVEC = 64
F32 = jnp.float32
BF16 = jnp.bfloat16
VMEM_LIMIT = 16 * 1024 * 1024


def dot(left, right, left_dim=1, right_dim=0):
    precision = lax.Precision.HIGHEST if left.dtype == F32 else None
    return lax.dot_general(
        left, right, (((left_dim,), (right_dim,)), ((), ())),
        precision=precision, preferred_element_type=F32,
    )


def halves(values):
    high = values.astype(BF16)
    return high, (values - high.astype(F32)).astype(BF16)


def call(body, out_shapes, args, flops=0, nbytes=0):
    return pl.pallas_call(
        body,
        out_shape=[jax.ShapeDtypeStruct(shape, dtype) for shape, dtype in out_shapes],
        in_specs=[pl.BlockSpec(memory_space=pltpu.VMEM) for _ in args],
        out_specs=[pl.BlockSpec(memory_space=pltpu.VMEM) for _ in out_shapes],
        compiler_params=pltpu.CompilerParams(vmem_limit_bytes=VMEM_LIMIT),
        cost_estimate=pl.CostEstimate(flops=flops, bytes_accessed=nbytes, transcendentals=0),
    )(*args)


def spread(value):
    return jnp.broadcast_to(value.astype(F32), (8, 128))


def chosen(flag, first, second):
    rows, cols = first.shape
    wide = jnp.concatenate([flag[0:1, :]] * (cols // 128), axis=1)
    return jnp.where(jnp.broadcast_to(wide, (rows, cols)) > 0.5, first, second)


LOG2_E = 1.4426950408889634


def sums_along(values):
    rows, depth = values.shape
    folded = values[:, :128]
    for j in range(128, depth, 128):
        folded = folded + values[:, j:j + 128]
    return dot(jnp.ones((8, 128), F32), folded, 1, 1)


def fill_tile(weight, row_embs, row_sq, col_emb, high, low, row_sum):
    size = col_emb.shape[0]
    col32 = col_emb.astype(F32)
    col_sq = (2.0 * LOG2_E) * sums_along(col32 * col32)[0:1, :]
    total = jnp.zeros((1, size), F32)
    for half in range(2):
        rows = slice(half * size, (half + 1) * size)
        inner = dot(row_embs[half], col_emb, 1, 1)
        squares = jnp.concatenate([row_sq[rows, :]] * (size // 128), axis=1)
        tile = jnp.exp2((4.0 * LOG2_E) * inner - (squares + col_sq))
        if weight is not None:
            tile = tile * weight
        tile_high, tile_low = halves(tile)
        high[rows, :] = tile_high
        low[rows, :] = tile_low
        row_sum[half * 8:(half + 1) * 8, :] = row_sum[half * 8:(half + 1) * 8, :] + sums_along(tile)
        total = total + jnp.sum(tile, axis=0, keepdims=True)
    return jnp.broadcast_to(total, (8, size))


def own_body(own, other, high, low, row_sum, row_sq, copy, token):
    size = own.shape[0]
    embs = [own[...], other[...]]
    copy[...] = embs[0]
    for half in range(2):
        row32 = embs[half].astype(F32)
        squares = (2.0 * LOG2_E) * jnp.sum(row32 * row32, axis=1, keepdims=True)
        row_sq[half * size:(half + 1) * size, :] = jnp.broadcast_to(squares, (size, 128))
    row_sum[...] = jnp.zeros(row_sum.shape, F32)
    token[...] = jnp.zeros(token.shape, F32)
    fill_tile(None, embs, row_sq, embs[0], high, low, row_sum)


def far_body(keep, relays, token, own, other, row_sq, direct, relayed, before, high, low, row_sum, col_sum):
    row_sum[...] = before[...] + token[0:1, 0:1]
    size = own.shape[0]
    weight = jnp.concatenate([keep[0:1, :]] * (size // 128), axis=1)
    col = chosen(relays, relayed[...], direct[...])
    col_sum[...] = fill_tile(weight, [own[...], other[...]], row_sq, col, high, low, row_sum)


def make_tile(body, args, rows, extra=()):
    return call(
        body, [((2 * rows, rows), BF16), ((2 * rows, rows), BF16), ((16, rows), F32), *extra],
        args, flops=2 * 10**9, nbytes=10**6,
    )


def swapped(values):
    middle = values.shape[0] // 2
    return jnp.concatenate([values[middle:], values[:middle]], axis=0)


def per_row(values, width):
    shape = (width, values.shape[1])
    return jnp.concatenate([jnp.broadcast_to(values[i:i + 1, :], shape) for i in (0, 8)], axis=0)


def packed_rows(values):
    rows, cols = values.shape
    biggest = jnp.max(jnp.abs(values), axis=1, keepdims=True)
    power = jnp.floor(jnp.log2(jnp.maximum(biggest, 1e-30)) + 1e-3)
    whole = jnp.round(values * jnp.exp2(14.0 - power)).astype(jnp.int32).astype(jnp.int16)
    powers = jnp.broadcast_to(power, (rows, 128)).T[:16, :]
    powers = jnp.concatenate([powers] * (cols // 128), axis=1)
    return jnp.concatenate([whole, powers.astype(jnp.int32).astype(jnp.int16)], axis=0)


def unpacked_rows(message):
    rows, cols = message.shape[0] - 16, message.shape[1]
    whole = message[:rows, :].astype(jnp.int32).astype(F32)
    powers = message[rows:, :128].astype(jnp.int32).astype(F32)[0:1, :]
    scale = jnp.exp2(jnp.broadcast_to(powers, (128, 128)).T[:rows, :] - 14.0)
    return whole * jnp.concatenate([scale] * (cols // 128), axis=1)


def degree_body(sums, other_sums, seeds, degree_out, vectors_out, message):
    degree = sums[...] + swapped(other_sums[...])
    scale = lax.rsqrt(degree)
    degree_out[...] = degree
    vectors = seeds[...] * per_row(scale, seeds.shape[0] // 2)
    vectors_out[...] = vectors
    message[...] = packed_rows(vectors)


def ahead_body(vectors, h1, l1, h2, l2, ahead):
    width = vectors.shape[0] // 2
    high, low = halves(jnp.concatenate([vectors[:width, :], vectors[width:, :]], axis=1))
    both = jnp.concatenate([high, low], axis=0)
    products = []
    for tile_high, tile_low in ((h1, l1), (h2, l2)):
        product = dot(both, tile_high[...])
        products.append(product[:width] + product[width:] + dot(high, tile_low[...]))
    ahead[...] = packed_rows(jnp.concatenate(products, axis=0))


def combine_body(total, other_total, degree, vectors_out, message):
    vectors = (total[...] + swapped(other_total[...])) / per_row(degree[...], total.shape[0] // 2)
    vectors_out[...] = vectors
    message[...] = packed_rows(vectors)


def product_rows(vectors, tile_high, tile_low):
    width = vectors.shape[0]
    high, low = halves(vectors)
    both = jnp.concatenate([high, low], axis=0)
    product = dot(both, tile_high[...], 1, 1)
    return product[:width] + product[width:] + dot(high, tile_low[...], 1, 1)


def stacked(product):
    size = product.shape[1] // 2
    return jnp.concatenate([product[:, :size], product[:, size:]], axis=0)


def own_product_body(vectors, h0, l0, out):
    out[...] = stacked(product_rows(vectors[:vectors.shape[0] // 2, :], h0, l0))


def far_product(message, h1, l1, h2, l2):
    near = unpacked_rows(message)
    width = near.shape[0] // 2
    return product_rows(near[:width], h1, l1) + product_rows(near[width:], h2, l2)


def near_product_body(product, near, h1, l1, h2, l2, total):
    total[...] = product[...] + stacked(far_product(near, h1, l1, h2, l2))


def add_body(total, behind, out):
    out[...] = total[...] + unpacked_rows(behind)


def low_body(degree, v0, v1, v2, moments, scaled):
    width = v0.shape[0] // 2
    root = jnp.sqrt(degree[0:1, :])
    x0, x1, x2 = v0[:width, :] * root, v1[:width, :] * root, v2[:width, :] * root
    scaled[...] = jnp.concatenate([x0, x1, x2], axis=0)
    left = jnp.concatenate([x0, x1], axis=0)
    order012 = dot(left, left, 1, 1)
    order34 = dot(jnp.concatenate([x1, x2], axis=0), x2, 1, 1)
    order = [order012[:width, :width], order012[:width, width:], order012[width:, width:],
             order34[:width], order34[width:]]
    for i in range(5):
        moments[i * width:(i + 1) * width, :] = order[i]


def place_of(rows, cols):
    return [lax.broadcasted_iota(jnp.int32, (rows, cols), axis) for axis in range(2)]


def moment_body(core, low, vectors, product, near, h1, l1, h2, l2, mine, theirs):
    n = vectors.shape[0] // 2
    last = far_product(near, h1, l1, h2, l2)
    last = 2.0 * last + jnp.concatenate([product[:n, :], product[n:, :]], axis=1)
    last = dot(jnp.concatenate([vectors[:n, :], vectors[n:, :]], axis=1), last, 1, 1)
    moments = [low[i * n:(i + 1) * n, :] for i in range(5)] + [0.5 * (last + last.T)]
    row, col = place_of(n, n)
    pieces = []
    for i in range(0, 6, 2):
        pair = jnp.where(row >= col, moments[i], moments[i + 1])
        pieces.append(jnp.concatenate([pair[:n // 2], pair[n // 2:]], axis=1))
    d1, d3, d5 = (jnp.sum(moments[i] * unit(n, n), axis=0, keepdims=True) for i in (1, 3, 5))
    row, _ = place_of(8, 2 * n)
    pieces.append(jnp.where(row == 0, jnp.concatenate([d1, d3], axis=1),
                            jnp.where(row == 1, jnp.concatenate([d5, d5], axis=1), 0.0)))
    pieces.append(jnp.zeros((8, 2 * n), F32))
    packed = jnp.concatenate(pieces, axis=0)
    half = packed.shape[0] // 2
    mine[...] = chosen(core, packed[half:], packed[:half])
    theirs[...] = chosen(core, packed[:half], packed[half:])


def unpacked(packed, n):
    row, col = place_of(n, n)
    start = 3 * n // 2
    diagonals = [packed[start:start + 1, :n], packed[start:start + 1, n:], packed[start + 1:start + 2, :n]]
    moments = []
    for i in range(3):
        folded = packed[i * n // 2:(i + 1) * n // 2]
        pair = jnp.concatenate([folded[:, :n], folded[:, n:]], axis=0)
        flipped = pair.T
        moments.append(jnp.where(row >= col, pair, flipped))
        moments.append(jnp.where(row == col, diagonals[i], jnp.where(row < col, pair, flipped)))
    return moments


def unit(rows, cols):
    return (lax.broadcasted_iota(jnp.int32, (rows, cols), 0)
            == lax.broadcasted_iota(jnp.int32, (rows, cols), 1)).astype(F32)


def lane(values, k):
    return jnp.take_along_axis(values, jnp.full(values.shape, k, jnp.int32), axis=1, mode="promise_in_bounds")


def sublane(values, k):
    return jnp.broadcast_to(values[k:k + 1, :], values.shape)


def inverse_factor(matrix):
    size = matrix.shape[0]
    work = jnp.concatenate([matrix, unit(size, size)], axis=1)
    blocks = [work[8 * i:8 * i + 8, :] for i in range(size // 8)]
    place = lax.broadcasted_iota(jnp.int32, (8, 2 * size), 0)
    done = [None] * (size // 8)

    def corner(cols, r):
        return [[sublane(cols[j], r + i) for j in range(i + 1)] for i in range(4)]

    pivot = corner([lane(blocks[0], j) for j in range(4)], 0)
    for k in range(0, size, 4):
        top, r = divmod(k, 8)
        (a00,), (a10, a11), (a20, a21, a22), (a30, a31, a32, a33) = pivot
        u0, u1, u2, u3 = u = [sublane(blocks[top], r + j) for j in range(4)]
        det_a = a00 * a11 - a10 * a10
        inv_a = 1.0 / det_a
        p00, p10, p11 = a11 * inv_a, a10 * inv_a, a00 * inv_a
        b00, b01 = a20 * p00 - a21 * p10, a21 * p11 - a20 * p10
        b10, b11 = a30 * p00 - a31 * p10, a31 * p11 - a30 * p10
        s00 = a22 - (b00 * a20 + b01 * a21)
        s10 = a32 - (b10 * a20 + b11 * a21)
        s11 = a33 - (b10 * a30 + b11 * a31)
        det_s = s00 * s11 - s10 * s10
        inv_s = 1.0 / det_s
        q22, q32, q33 = s11 * inv_s, -s10 * inv_s, s00 * inv_s
        q20, q21 = -(q22 * b00 + q32 * b10), -(q22 * b01 + q32 * b11)
        q30, q31 = -(q32 * b00 + q33 * b10), -(q32 * b01 + q33 * b11)
        q00 = p00 - (b00 * q20 + b10 * q30)
        q10 = -p10 - (b01 * q20 + b11 * q30)
        q11 = p11 - (b01 * q21 + b11 * q31)
        inverse = [[q00, q10, q20, q30], [q10, q11, q21, q31], [q20, q21, q22, q32], [q30, q31, q32, q33]]

        def applied(values):
            return [(row[0] * values[0] + row[1] * values[1]) + (row[2] * values[2] + row[3] * values[3])
                    for row in inverse]

        if k + 4 < size:
            across = [lane(blocks[top], k + 4 + j) for j in range(4)]
            cross = [[sublane(across[j], r + i) for i in range(4)] for j in range(4)]
            after = across if r == 0 else [lane(blocks[top + 1], k + 4 + j) for j in range(4)]
            plain = corner(after, 4 - r)
            solved = [applied(column) for column in cross]
            pivot = [[plain[i][j] - ((cross[i][0] * solved[j][0] + cross[i][1] * solved[j][1])
                                     + (cross[i][2] * solved[j][2] + cross[i][3] * solved[j][3]))
                      for j in range(i + 1)] for i in range(4)]
        t = applied(u)
        for i in range(top, size // 8):
            if i == top and r:
                continue
            c = [lane(blocks[i], k + j) for j in range(4)]
            change = (c[0] * t[0] + c[1] * t[1]) + (c[2] * t[2] + c[3] * t[3])
            blocks[i] = blocks[i] - (jnp.where(place > 3, change, 0.0) if i == top else change)
        v0 = u0 * lax.rsqrt(a00)
        v1 = (a00 * u1 - a10 * u0) * lax.rsqrt(a00 * det_a)
        u2 = u2 - b00 * u0 - b01 * u1
        u3 = u3 - b10 * u0 - b11 * u1
        v2 = u2 * lax.rsqrt(s00)
        v3 = (s00 * u3 - s10 * u2) * lax.rsqrt(s00 * det_s)
        four = jnp.where(place % 4 == 0, v0, jnp.where(place % 4 == 1, v1, jnp.where(place % 4 == 2, v2, v3)))
        done[top] = jnp.where(place > 3, four, done[top]) if r else four
    return jnp.concatenate(done, axis=0)[:, size:]


def total(matrix):
    return jnp.sum(jnp.sum(matrix, axis=0, keepdims=True), axis=1, keepdims=True)


def trace(matrix):
    return total(matrix * unit(*matrix.shape))


def inverse_root(matrix):
    eye = unit(*matrix.shape)
    rest = matrix - eye

    def series():
        return eye - 0.5 * rest + 0.375 * dot(rest, rest)

    return lax.cond(jnp.sum(rest * rest) < 1e-4, series, lambda: inverse_factor(matrix))


def dense(moments, index, rows, data):
    n = NVEC
    eye = unit(n, n)
    pick = ((lax.broadcasted_iota(jnp.int32, (n, n), 0) == index)
            & (lax.broadcasted_iota(jnp.int32, (n, n), 1) == index)).astype(F32)

    def part(stacked, i):
        return stacked[i * n:(i + 1) * n]

    def below(*parts):
        return jnp.concatenate(parts, axis=0)

    def beside(*parts):
        return jnp.concatenate(parts, axis=1)

    base = inverse_factor(moments[0])
    right = dot(below(*moments[1:]), base, 1, 1)
    m1, m2, m3, m4, m5 = (dot(base, part(right, i)) for i in range(5))
    y0, y1, y2 = (dot(base, part(data, i)) for i in range(3))

    by1 = dot(below(m1, m2, m3, m4), m1)
    square, m21, m31, m41 = (part(by1, i) for i in range(4))
    tri = dot(m1, beside(square, m21, m31))
    gram_r = m2 - square
    image_r = m3 - m21 - m21.T + tri[:, :n]
    mixed_r = m3 - m21
    square_r = m4 - m31 - m31.T + tri[:, n:2 * n]
    cubic_r = m5 - m41 - m41.T + tri[:, 2 * n:]
    shift = 3.0 - total(m1 * pick)
    ridge = RIDGE_WEIGHT * (n + trace(gram_r)) / (2 * n)
    ridged = gram_r + ridge * eye
    factor = inverse_factor(ridged)
    inverse = dot(factor, factor, 0, 0)
    keep = 1.0 / (1.0 + ridge)
    step = below(
        beside(m1 * keep + shift * eye, gram_r * keep),
        beside(eye - ridge * inverse, dot(inverse, image_r) + shift * eye),
    )
    twice = dot(step, step)
    power = dot(twice, dot(twice, twice[:, :n]))
    top, bottom = power[:n], power[n:]
    weighted = dot(below(ridged, gram_r, image_r), bottom)
    norm = (1.0 + ridge) * dot(top, top, 0, 0) + dot(bottom, part(weighted, 0), 0, 0)
    factor = inverse_factor(norm)

    middle = m4 - m31
    images = dot(below(
        beside(m1, gram_r), beside(gram_r, image_r),
        beside(m2, mixed_r), beside(mixed_r.T, square_r),
        beside(m3, middle), beside(middle.T, cubic_r),
    ), power)
    whole = dot(power, beside(images[:2 * n], images[2 * n:4 * n], images[4 * n:], power), 0, 0)
    lower = dot(bottom, beside(part(images, 1), part(images, 3), part(weighted, 1), part(weighted, 2)), 0, 0)
    raw = [whole[:, i * n:(i + 1) * n] for i in range(4)] + [lower[:, i * n:(i + 1) * n] for i in range(4)]
    right = dot(below(*raw), factor, 1, 1)
    ritz, image2, image3, excess, p_image, p_image2, p_gram, p_ritz = (dot(factor, part(right, i)) for i in range(8))
    excess = ridge * excess

    shift = 3.0 - total(ritz * pick)
    by_ritz = dot(below(ritz, p_gram, excess, p_image, image2), ritz)
    squared, gram_pr, gram_cr = part(by_ritz, 0), p_image - part(by_ritz, 1), part(by_ritz, 2)
    tri = dot(ritz, squared), dot(ritz, gram_cr)
    gram_rr = image2 - squared - tri[1]
    image_cr = image2 - squared
    image_pr = p_image2 - part(by_ritz, 3)
    image_rr = image3 - part(by_ritz, 4) - part(by_ritz, 4).T + tri[0]
    ridge = RIDGE_WEIGHT * (n - trace(excess) + trace(p_gram) + trace(gram_rr)) / (3 * n)
    g_cc = eye - excess + ridge * eye
    g_pp = p_gram + ridge * eye
    g_rr = gram_rr + ridge * eye
    image_gram = below(
        beside(ritz, p_image.T, image_cr), beside(p_image, p_ritz, image_pr), beside(image_cr.T, image_pr.T, image_rr),
    )
    v0 = inverse_root(g_cc)
    side = dot(below(p_gram, gram_cr.T), v0, 1, 1)
    l10, l20 = side[:n], side[n:]
    outer = dot(side, side, 1, 1)
    v1 = inverse_factor(g_pp - outer[:n, :n])
    l21 = dot(gram_pr.T - outer[n:, :n], v1, 1, 1)
    v2 = inverse_factor(g_rr - outer[n:, n:] - dot(l21, l21, 1, 1))
    zero = jnp.zeros((n, n), F32)
    row0 = beside(v0, zero, zero)
    row1 = dot(v1, beside(-dot(l10, v0), eye, zero))
    row2 = beside(zero, zero, eye) - dot(l20, row0) - dot(l21, row1)
    known = below(row0, row1)
    solved = dot(known, dot(known, image_gram), 0, 0)
    row2 = dot(v2, beside(row2, dot(row2, image_gram)))
    step = solved + dot(row2[:, :3 * n], row2[:, 3 * n:], 0, 0) + shift * unit(3 * n, 3 * n)
    twice = dot(step, step)
    power2 = dot(twice, dot(twice, twice[:, :n]))
    gram = below(
        beside(g_cc, p_gram, gram_cr), beside(p_gram, g_pp, gram_pr), beside(gram_cr.T, gram_pr.T, g_rr),
    )
    norm = dot(power2, dot(gram, power2), 0, 0)

    start = dot(power, below(y0, y1), 0, 0) - dot(dot(m1, bottom), y0, 0, 0)
    image = dot(power, below(y1, y2), 0, 0) - dot(dot(m1, bottom), y1, 0, 0)
    residue = dot(bottom, y1 - dot(m1, y0), 0, 0)
    current = dot(factor, start)
    vectors = below(current, dot(factor, residue), dot(factor, image) - dot(ritz, current))
    return dot(inverse_factor(norm), dot(power2, vectors, 0, 0)) * math.sqrt(rows)


def dense_body(rows, core, index, mine, theirs, scaled, out):
    packed = jnp.concatenate([
        chosen(core, theirs[...], mine[...]), chosen(core, mine[...], theirs[...])], axis=0)
    index = jnp.broadcast_to(index[0:1, :NVEC], (NVEC, NVEC)).astype(jnp.int32)
    out[...] = dense(unpacked(packed, NVEC), index, rows, scaled[...])


def between_blocks(shard, sign):
    blocks, cores = lax.axis_size("blk"), lax.axis_size("narrow")
    pairs = [(i * cores + j, (i + sign * (1 + j)) % blocks * cores + j) for i in range(blocks) for j in range(cores)]
    return lax.ppermute(shard, ("blk", "narrow"), pairs)


def between_cores(shard):
    return lax.ppermute(shard, "narrow", [(0, 1), (1, 0)])


def total_over_blocks(values):
    blocks = lax.axis_size("blk")
    span = 1
    while blocks % (2 * span) == 0:
        values = values + lax.ppermute(values, "blk", [(i, i ^ span) for i in range(blocks)])
        span *= 2
    if span < blocks:
        groups = [list(range(i, blocks, span)) for i in range(span)]
        values = lax.psum(values, "blk", axis_index_groups=groups)
    return values


def shards(embeddings, pair_mask, shift_index, start_seed):
    size = embeddings.shape[0]
    blocks = lax.axis_size("blk")
    where = lax.axis_index("blk")
    core = lax.axis_index("narrow")
    other_emb = between_cores(embeddings)
    relaying = blocks % 2 == 0
    back1 = [(i, (i - 1) % blocks) for i in range(blocks) if i % 2 or not relaying]
    back2 = [(i, (i - 2) % blocks) for i in range(blocks)]
    orders = [
        [(2 * i + j, 2 * k) for i, k in back1] + [(2 * i + 1 - j, 2 * k + 1) for i, k in back2] for j in range(2)]
    if relaying:
        orders[0] += [(2 * i, 2 * i + 2) for i in range(0, blocks, 2)]

    def between_shards(shard, pairs):
        return lax.ppermute(shard, ("blk", "narrow"), pairs)

    first, second = between_shards(embeddings, orders[0]), between_shards(embeddings, orders[1])
    seed = start_seed.astype(F32).T / 1000.0
    seeds = jnp.concatenate([seed, between_cores(seed)], axis=0)
    keep = spread(lax.dynamic_slice(pair_mask, (where, core), (1, 1)))
    relays = spread((1 - core) * (where % 2) * int(relaying))
    pair_shape, row_shape = ((2 * NVEC, size), F32), ((16, size), F32)
    h0, l0, sums, row_sq, own_copy, token = make_tile(
        own_body, [embeddings, other_emb], size,
        (((2 * size, 128), F32), (embeddings.shape, BF16), ((8, 128), F32)))
    first, seeds, keep, relays, token = lax.optimization_barrier((first, seeds, keep, relays, token))
    relayed = [first, own_copy]
    if relaying:
        relayed[0] = between_shards(first, [(2 * i, (i - 2) % blocks * 2) for i in range(1, blocks, 2)])
        forward, second = lax.optimization_barrier((first, second))
        relayed[1] = between_shards(forward, [(2 * i + 1, 2 * i + 2) for i in range(0, blocks, 2)])
    tile_args = [keep, relays, token, own_copy, other_emb, row_sq]
    h1, l1, sums, cols1 = make_tile(
        far_body, [*tile_args, first, relayed[0], sums], size, (((8, size), F32),))
    h2, l2, sums, cols2 = make_tile(
        far_body, [*tile_args, second, relayed[1], sums], size, (((8, size), F32),))
    cols = jnp.concatenate([cols1, cols2], axis=0)
    sums = sums + between_blocks(cols, 1)

    small = dict(flops=10**6, nbytes=10**5)
    middle = dict(flops=10**9, nbytes=10**6)
    message_shape = ((2 * NVEC + 16, size), jnp.int16)
    degree, vectors, message = call(
        degree_body, [row_shape, pair_shape, message_shape], [sums, between_cores(sums), seeds], **small)
    far = [h1, l1, h2, l2]
    history = [vectors]
    for _ in range(2):
        near = between_blocks(message, -1)
        (ahead,) = call(ahead_body, [message_shape], [vectors, *far], **middle)
        behind = between_blocks(ahead, 1)
        (product,) = call(own_product_body, [pair_shape], [vectors, h0, l0], **middle)
        (total,) = call(near_product_body, [pair_shape], [product, near, *far], **middle)
        (total,) = call(add_body, [pair_shape], [total, behind], **small)
        vectors, message = call(
            combine_body, [pair_shape, message_shape], [total, between_cores(total), degree], **small)
        history.append(vectors)
    near = between_blocks(message, -1)
    low, scaled = call(
        low_body, [((5 * NVEC, NVEC), F32), ((3 * NVEC, size), F32)], [degree] + history, **middle)
    (product,) = call(own_product_body, [pair_shape], [vectors, h0, l0], **middle)
    packed_shape = ((3 * NVEC // 4 + 8, 2 * NVEC), F32)
    mine, theirs = call(
        moment_body, [packed_shape] * 2, [spread(core), low, vectors, product, near, *far], **middle)
    mine = total_over_blocks(mine + between_cores(theirs))
    rows = size * blocks * lax.axis_size("narrow")
    (out,) = call(
        lambda *refs: dense_body(rows, *refs), [((NVEC, size), F32)],
        [spread(core), spread(shift_index), mine, between_cores(mine), scaled], flops=2 * 10**10, nbytes=10**6,
    )
    return out.T


def solution(mesh):
    return jax.shard_map(
        shards,
        mesh=mesh,
        in_specs=(
            P(("groups", "blk", "narrow"), None),
            P("groups", None),
            P("groups"),
            P(("groups", "blk", "narrow"), None),
        ),
        out_specs=P(("groups", "blk", "narrow"), None),
        check_vma=False,
    )
```

```python
import math

import jax
import jax.numpy as jnp
from jax import lax
from jax.experimental import pallas as pl
from jax.experimental.pallas import tpu as pltpu
from jax.sharding import PartitionSpec as P

KERNEL_GAMMA = 2.0
RIDGE_WEIGHT = 1e-05
NVEC = 64
F32 = jnp.float32
BF16 = jnp.bfloat16
VMEM_LIMIT = 16 * 1024 * 1024


def dot(left, right, left_dim=1, right_dim=0):
    precision = lax.Precision.HIGHEST if left.dtype == F32 else None
    return lax.dot_general(
        left, right, (((left_dim,), (right_dim,)), ((), ())),
        precision=precision, preferred_element_type=F32,
    )


def halves(values):
    high = values.astype(BF16)
    return high, (values - high.astype(F32)).astype(BF16)


def call(body, out_shapes, args, flops=0, nbytes=0):
    return pl.pallas_call(
        body,
        out_shape=[jax.ShapeDtypeStruct(shape, dtype) for shape, dtype in out_shapes],
        in_specs=[pl.BlockSpec(memory_space=pltpu.VMEM) for _ in args],
        out_specs=[pl.BlockSpec(memory_space=pltpu.VMEM) for _ in out_shapes],
        compiler_params=pltpu.CompilerParams(vmem_limit_bytes=VMEM_LIMIT),
        cost_estimate=pl.CostEstimate(flops=flops, bytes_accessed=nbytes, transcendentals=0),
    )(*args)


def spread(value):
    return jnp.broadcast_to(value.astype(F32), (8, 128))


def chosen(flag, first, second):
    rows, cols = first.shape
    wide = jnp.concatenate([flag[0:1, :]] * (cols // 128), axis=1)
    return jnp.where(jnp.broadcast_to(wide, (rows, cols)) > 0.5, first, second)


LOG2_E = 1.4426950408889634


def sums_along(values):
    rows, depth = values.shape
    folded = values[:, :128]
    for j in range(128, depth, 128):
        folded = folded + values[:, j:j + 128]
    return dot(jnp.ones((8, 128), F32), folded, 1, 1)


def fill_tile(weight, row_embs, row_sq, col_emb, high, low, row_sum):
    size = col_emb.shape[0]
    col32 = col_emb.astype(F32)
    col_sq = (2.0 * LOG2_E) * sums_along(col32 * col32)[0:1, :]
    total = jnp.zeros((1, size), F32)
    for half in range(2):
        rows = slice(half * size, (half + 1) * size)
        inner = dot(row_embs[half], col_emb, 1, 1)
        squares = jnp.concatenate([row_sq[rows, :]] * (size // 128), axis=1)
        tile = jnp.exp2((4.0 * LOG2_E) * inner - (squares + col_sq))
        if weight is not None:
            tile = tile * weight
        tile_high, tile_low = halves(tile)
        high[rows, :] = tile_high
        low[rows, :] = tile_low
        row_sum[half * 8:(half + 1) * 8, :] = row_sum[half * 8:(half + 1) * 8, :] + sums_along(tile)
        total = total + jnp.sum(tile, axis=0, keepdims=True)
    return jnp.broadcast_to(total, (8, size))


def own_body(own, other, high, low, row_sum, row_sq, copy, token):
    size = own.shape[0]
    embs = [own[...], other[...]]
    copy[...] = embs[0]
    for half in range(2):
        row32 = embs[half].astype(F32)
        squares = (2.0 * LOG2_E) * jnp.sum(row32 * row32, axis=1, keepdims=True)
        row_sq[half * size:(half + 1) * size, :] = jnp.broadcast_to(squares, (size, 128))
    row_sum[...] = jnp.zeros(row_sum.shape, F32)
    token[...] = jnp.zeros(token.shape, F32)
    fill_tile(None, embs, row_sq, embs[0], high, low, row_sum)


def far_body(keep, relays, token, own, other, row_sq, direct, relayed, before, high, low, row_sum, col_sum):
    row_sum[...] = before[...] + token[0:1, 0:1]
    size = own.shape[0]
    weight = jnp.concatenate([keep[0:1, :]] * (size // 128), axis=1)
    col = chosen(relays, relayed[...], direct[...])
    col_sum[...] = fill_tile(weight, [own[...], other[...]], row_sq, col, high, low, row_sum)


def make_tile(body, args, rows, extra=()):
    return call(
        body, [((2 * rows, rows), BF16), ((2 * rows, rows), BF16), ((16, rows), F32), *extra],
        args, flops=2 * 10**9, nbytes=10**6,
    )


def swapped(values):
    middle = values.shape[0] // 2
    return jnp.concatenate([values[middle:], values[:middle]], axis=0)


def per_row(values, width):
    shape = (width, values.shape[1])
    return jnp.concatenate([jnp.broadcast_to(values[i:i + 1, :], shape) for i in (0, 8)], axis=0)


def packed_rows(values):
    rows, cols = values.shape
    biggest = jnp.max(jnp.abs(values), axis=1, keepdims=True)
    power = jnp.floor(jnp.log2(jnp.maximum(biggest, 1e-30)) + 1e-3)
    whole = jnp.round(values * jnp.exp2(14.0 - power)).astype(jnp.int32).astype(jnp.int16)
    powers = jnp.broadcast_to(power, (rows, 128)).T[:16, :]
    powers = jnp.concatenate([powers] * (cols // 128), axis=1)
    return jnp.concatenate([whole, powers.astype(jnp.int32).astype(jnp.int16)], axis=0)


def unpacked_rows(message):
    rows, cols = message.shape[0] - 16, message.shape[1]
    whole = message[:rows, :].astype(jnp.int32).astype(F32)
    powers = message[rows:, :128].astype(jnp.int32).astype(F32)[0:1, :]
    scale = jnp.exp2(jnp.broadcast_to(powers, (128, 128)).T[:rows, :] - 14.0)
    return whole * jnp.concatenate([scale] * (cols // 128), axis=1)


def degree_body(sums, other_sums, seeds, degree_out, vectors_out, message):
    degree = sums[...] + swapped(other_sums[...])
    scale = lax.rsqrt(degree)
    degree_out[...] = degree
    vectors = seeds[...] * per_row(scale, seeds.shape[0] // 2)
    vectors_out[...] = vectors
    message[...] = packed_rows(vectors)


def ahead_body(vectors, h1, l1, h2, l2, ahead):
    width = vectors.shape[0] // 2
    high, low = halves(jnp.concatenate([vectors[:width, :], vectors[width:, :]], axis=1))
    both = jnp.concatenate([high, low], axis=0)
    products = []
    for tile_high, tile_low in ((h1, l1), (h2, l2)):
        product = dot(both, tile_high[...])
        products.append(product[:width] + product[width:] + dot(high, tile_low[...]))
    ahead[...] = packed_rows(jnp.concatenate(products, axis=0))


def combine_body(total, other_total, degree, vectors_out, message):
    vectors = (total[...] + swapped(other_total[...])) / per_row(degree[...], total.shape[0] // 2)
    vectors_out[...] = vectors
    message[...] = packed_rows(vectors)


def product_rows(vectors, tile_high, tile_low):
    width = vectors.shape[0]
    high, low = halves(vectors)
    both = jnp.concatenate([high, low], axis=0)
    product = dot(both, tile_high[...], 1, 1)
    return product[:width] + product[width:] + dot(high, tile_low[...], 1, 1)


def stacked(product):
    size = product.shape[1] // 2
    return jnp.concatenate([product[:, :size], product[:, size:]], axis=0)


def own_product_body(vectors, h0, l0, out):
    out[...] = stacked(product_rows(vectors[:vectors.shape[0] // 2, :], h0, l0))


def far_product(message, h1, l1, h2, l2):
    near = unpacked_rows(message)
    width = near.shape[0] // 2
    return product_rows(near[:width], h1, l1) + product_rows(near[width:], h2, l2)


def near_product_body(product, near, h1, l1, h2, l2, total):
    total[...] = product[...] + stacked(far_product(near, h1, l1, h2, l2))


def add_body(total, behind, out):
    out[...] = total[...] + unpacked_rows(behind)


def low_body(degree, v0, v1, v2, moments, scaled):
    width = v0.shape[0] // 2
    root = jnp.sqrt(degree[0:1, :])
    x0, x1, x2 = v0[:width, :] * root, v1[:width, :] * root, v2[:width, :] * root
    scaled[...] = jnp.concatenate([x0, x1, x2], axis=0)
    left = jnp.concatenate([x0, x1], axis=0)
    order012 = dot(left, left, 1, 1)
    order34 = dot(jnp.concatenate([x1, x2], axis=0), x2, 1, 1)
    order = [order012[:width, :width], order012[:width, width:], order012[width:, width:],
             order34[:width], order34[width:]]
    for i in range(5):
        moments[i * width:(i + 1) * width, :] = order[i]


def place_of(rows, cols):
    return [lax.broadcasted_iota(jnp.int32, (rows, cols), axis) for axis in range(2)]


def moment_body(low, vectors, product, near, h1, l1, h2, l2, packed):
    n = vectors.shape[0] // 2
    last = far_product(near, h1, l1, h2, l2)
    last = 2.0 * last + jnp.concatenate([product[:n, :], product[n:, :]], axis=1)
    last = dot(jnp.concatenate([vectors[:n, :], vectors[n:, :]], axis=1), last, 1, 1)
    moments = [low[i * n:(i + 1) * n, :] for i in range(5)] + [0.5 * (last + last.T)]
    row, col = place_of(n, n)
    pieces = []
    for i in range(0, 6, 2):
        pair = jnp.where(row >= col, moments[i], moments[i + 1])
        pieces.append(jnp.concatenate([pair[:n // 2], pair[n // 2:]], axis=1))
    d1, d3, d5 = (jnp.sum(moments[i] * unit(n, n), axis=0, keepdims=True) for i in (1, 3, 5))
    row, _ = place_of(8, 2 * n)
    pieces.append(jnp.where(row == 0, jnp.concatenate([d1, d3], axis=1),
                            jnp.where(row == 1, jnp.concatenate([d5, d5], axis=1), 0.0)))
    packed[...] = jnp.concatenate(pieces, axis=0)


def unpacked(packed, n):
    row, col = place_of(n, n)
    start = 3 * n // 2
    diagonals = [packed[start:start + 1, :n], packed[start:start + 1, n:], packed[start + 1:start + 2, :n]]
    moments = []
    for i in range(3):
        folded = packed[i * n // 2:(i + 1) * n // 2]
        pair = jnp.concatenate([folded[:, :n], folded[:, n:]], axis=0)
        flipped = pair.T
        moments.append(jnp.where(row >= col, pair, flipped))
        moments.append(jnp.where(row == col, diagonals[i], jnp.where(row < col, pair, flipped)))
    return moments


def unit(rows, cols):
    return (lax.broadcasted_iota(jnp.int32, (rows, cols), 0)
            == lax.broadcasted_iota(jnp.int32, (rows, cols), 1)).astype(F32)


def lane(values, k):
    return jnp.take_along_axis(values, jnp.full(values.shape, k, jnp.int32), axis=1, mode="promise_in_bounds")


def sublane(values, k):
    return jnp.broadcast_to(values[k:k + 1, :], values.shape)


def inverse_factor(matrix):
    size = matrix.shape[0]
    work = jnp.concatenate([matrix, unit(size, size)], axis=1)
    blocks = [work[8 * i:8 * i + 8, :] for i in range(size // 8)]
    place = lax.broadcasted_iota(jnp.int32, (8, 2 * size), 0)
    done = [None] * (size // 8)

    def corner(cols, r):
        return [[sublane(cols[j], r + i) for j in range(i + 1)] for i in range(4)]

    pivot = corner([lane(blocks[0], j) for j in range(4)], 0)
    for k in range(0, size, 4):
        top, r = divmod(k, 8)
        (a00,), (a10, a11), (a20, a21, a22), (a30, a31, a32, a33) = pivot
        u0, u1, u2, u3 = u = [sublane(blocks[top], r + j) for j in range(4)]
        det_a = a00 * a11 - a10 * a10
        inv_a = 1.0 / det_a
        p00, p10, p11 = a11 * inv_a, a10 * inv_a, a00 * inv_a
        b00, b01 = a20 * p00 - a21 * p10, a21 * p11 - a20 * p10
        b10, b11 = a30 * p00 - a31 * p10, a31 * p11 - a30 * p10
        s00 = a22 - (b00 * a20 + b01 * a21)
        s10 = a32 - (b10 * a20 + b11 * a21)
        s11 = a33 - (b10 * a30 + b11 * a31)
        det_s = s00 * s11 - s10 * s10
        inv_s = 1.0 / det_s
        q22, q32, q33 = s11 * inv_s, -s10 * inv_s, s00 * inv_s
        q20, q21 = -(q22 * b00 + q32 * b10), -(q22 * b01 + q32 * b11)
        q30, q31 = -(q32 * b00 + q33 * b10), -(q32 * b01 + q33 * b11)
        q00 = p00 - (b00 * q20 + b10 * q30)
        q10 = -p10 - (b01 * q20 + b11 * q30)
        q11 = p11 - (b01 * q21 + b11 * q31)
        inverse = [[q00, q10, q20, q30], [q10, q11, q21, q31], [q20, q21, q22, q32], [q30, q31, q32, q33]]

        def applied(values):
            return [(row[0] * values[0] + row[1] * values[1]) + (row[2] * values[2] + row[3] * values[3])
                    for row in inverse]

        if k + 4 < size:
            across = [lane(blocks[top], k + 4 + j) for j in range(4)]
            cross = [[sublane(across[j], r + i) for i in range(4)] for j in range(4)]
            after = across if r == 0 else [lane(blocks[top + 1], k + 4 + j) for j in range(4)]
            plain = corner(after, 4 - r)
            solved = [applied(column) for column in cross]
            pivot = [[plain[i][j] - ((cross[i][0] * solved[j][0] + cross[i][1] * solved[j][1])
                                     + (cross[i][2] * solved[j][2] + cross[i][3] * solved[j][3]))
                      for j in range(i + 1)] for i in range(4)]
        t = applied(u)
        for i in range(top, size // 8):
            if i == top and r:
                continue
            c = [lane(blocks[i], k + j) for j in range(4)]
            change = (c[0] * t[0] + c[1] * t[1]) + (c[2] * t[2] + c[3] * t[3])
            blocks[i] = blocks[i] - (jnp.where(place > 3, change, 0.0) if i == top else change)
        v0 = u0 * lax.rsqrt(a00)
        v1 = (a00 * u1 - a10 * u0) * lax.rsqrt(a00 * det_a)
        u2 = u2 - b00 * u0 - b01 * u1
        u3 = u3 - b10 * u0 - b11 * u1
        v2 = u2 * lax.rsqrt(s00)
        v3 = (s00 * u3 - s10 * u2) * lax.rsqrt(s00 * det_s)
        four = jnp.where(place % 4 == 0, v0, jnp.where(place % 4 == 1, v1, jnp.where(place % 4 == 2, v2, v3)))
        done[top] = jnp.where(place > 3, four, done[top]) if r else four
    return jnp.concatenate(done, axis=0)[:, size:]


def total(matrix):
    return jnp.sum(jnp.sum(matrix, axis=0, keepdims=True), axis=1, keepdims=True)


def trace(matrix):
    return total(matrix * unit(*matrix.shape))


def inverse_root(matrix):
    eye = unit(*matrix.shape)
    rest = matrix - eye

    def series():
        return eye - 0.5 * rest + 0.375 * dot(rest, rest)

    return lax.cond(jnp.sum(rest * rest) < 1e-4, series, lambda: inverse_factor(matrix))


def dense(moments, index, rows, data):
    n = NVEC
    eye = unit(n, n)
    pick = ((lax.broadcasted_iota(jnp.int32, (n, n), 0) == index)
            & (lax.broadcasted_iota(jnp.int32, (n, n), 1) == index)).astype(F32)

    def part(stacked, i):
        return stacked[i * n:(i + 1) * n]

    def below(*parts):
        return jnp.concatenate(parts, axis=0)

    def beside(*parts):
        return jnp.concatenate(parts, axis=1)

    base = inverse_factor(moments[0])
    right = dot(below(*moments[1:]), base, 1, 1)
    m1, m2, m3, m4, m5 = (dot(base, part(right, i)) for i in range(5))
    y0, y1, y2 = (dot(base, part(data, i)) for i in range(3))

    by1 = dot(below(m1, m2, m3, m4), m1)
    square, m21, m31, m41 = (part(by1, i) for i in range(4))
    tri = dot(m1, beside(square, m21, m31))
    gram_r = m2 - square
    image_r = m3 - m21 - m21.T + tri[:, :n]
    mixed_r = m3 - m21
    square_r = m4 - m31 - m31.T + tri[:, n:2 * n]
    cubic_r = m5 - m41 - m41.T + tri[:, 2 * n:]
    shift = 3.0 - total(m1 * pick)
    ridge = RIDGE_WEIGHT * (n + trace(gram_r)) / (2 * n)
    ridged = gram_r + ridge * eye
    factor = inverse_factor(ridged)
    inverse = dot(factor, factor, 0, 0)
    keep = 1.0 / (1.0 + ridge)
    step = below(
        beside(m1 * keep + shift * eye, gram_r * keep),
        beside(eye - ridge * inverse, dot(inverse, image_r) + shift * eye),
    )
    twice = dot(step, step)
    power = dot(twice, dot(twice, twice[:, :n]))
    top, bottom = power[:n], power[n:]
    weighted = dot(below(ridged, gram_r, image_r), bottom)
    norm = (1.0 + ridge) * dot(top, top, 0, 0) + dot(bottom, part(weighted, 0), 0, 0)
    factor = inverse_factor(norm)

    middle = m4 - m31
    images = dot(below(
        beside(m1, gram_r), beside(gram_r, image_r),
        beside(m2, mixed_r), beside(mixed_r.T, square_r),
        beside(m3, middle), beside(middle.T, cubic_r),
    ), power)
    whole = dot(power, beside(images[:2 * n], images[2 * n:4 * n], images[4 * n:], power), 0, 0)
    lower = dot(bottom, beside(part(images, 1), part(images, 3), part(weighted, 1), part(weighted, 2)), 0, 0)
    raw = [whole[:, i * n:(i + 1) * n] for i in range(4)] + [lower[:, i * n:(i + 1) * n] for i in range(4)]
    right = dot(below(*raw), factor, 1, 1)
    ritz, image2, image3, excess, p_image, p_image2, p_gram, p_ritz = (dot(factor, part(right, i)) for i in range(8))
    excess = ridge * excess

    shift = 3.0 - total(ritz * pick)
    by_ritz = dot(below(ritz, p_gram, excess, p_image, image2), ritz)
    squared, gram_pr, gram_cr = part(by_ritz, 0), p_image - part(by_ritz, 1), part(by_ritz, 2)
    tri = dot(ritz, squared), dot(ritz, gram_cr)
    gram_rr = image2 - squared - tri[1]
    image_cr = image2 - squared
    image_pr = p_image2 - part(by_ritz, 3)
    image_rr = image3 - part(by_ritz, 4) - part(by_ritz, 4).T + tri[0]
    ridge = RIDGE_WEIGHT * (n - trace(excess) + trace(p_gram) + trace(gram_rr)) / (3 * n)
    g_cc = eye - excess + ridge * eye
    g_pp = p_gram + ridge * eye
    g_rr = gram_rr + ridge * eye
    image_gram = below(
        beside(ritz, p_image.T, image_cr), beside(p_image, p_ritz, image_pr), beside(image_cr.T, image_pr.T, image_rr),
    )
    v0 = inverse_root(g_cc)
    side = dot(below(p_gram, gram_cr.T), v0, 1, 1)
    l10, l20 = side[:n], side[n:]
    outer = dot(side, side, 1, 1)
    v1 = inverse_factor(g_pp - outer[:n, :n])
    l21 = dot(gram_pr.T - outer[n:, :n], v1, 1, 1)
    v2 = inverse_factor(g_rr - outer[n:, n:] - dot(l21, l21, 1, 1))
    zero = jnp.zeros((n, n), F32)
    row0 = beside(v0, zero, zero)
    row1 = dot(v1, beside(-dot(l10, v0), eye, zero))
    row2 = beside(zero, zero, eye) - dot(l20, row0) - dot(l21, row1)
    known = below(row0, row1)
    solved = dot(known, dot(known, image_gram), 0, 0)
    row2 = dot(v2, beside(row2, dot(row2, image_gram)))
    step = solved + dot(row2[:, :3 * n], row2[:, 3 * n:], 0, 0) + shift * unit(3 * n, 3 * n)
    twice = dot(step, step)
    power2 = dot(twice, dot(twice, twice[:, :n]))
    gram = below(
        beside(g_cc, p_gram, gram_cr), beside(p_gram, g_pp, gram_pr), beside(gram_cr.T, gram_pr.T, g_rr),
    )
    norm = dot(power2, dot(gram, power2), 0, 0)

    start = dot(power, below(y0, y1), 0, 0) - dot(dot(m1, bottom), y0, 0, 0)
    image = dot(power, below(y1, y2), 0, 0) - dot(dot(m1, bottom), y1, 0, 0)
    residue = dot(bottom, y1 - dot(m1, y0), 0, 0)
    current = dot(factor, start)
    vectors = below(current, dot(factor, residue), dot(factor, image) - dot(ritz, current))
    return dot(inverse_factor(norm), dot(power2, vectors, 0, 0)) * math.sqrt(rows)


def dense_body(rows, core, index, mine, theirs, scaled, out):
    packed = chosen(core, mine[...], theirs[...])
    index = jnp.broadcast_to(index[0:1, :NVEC], (NVEC, NVEC)).astype(jnp.int32)
    out[...] = dense(unpacked(packed, NVEC), index, rows, scaled[...])


def between_blocks(shard, sign):
    blocks, cores = lax.axis_size("blk"), lax.axis_size("narrow")
    pairs = [(i * cores + j, (i + sign * (1 + j)) % blocks * cores + j) for i in range(blocks) for j in range(cores)]
    return lax.ppermute(shard, ("blk", "narrow"), pairs)


def between_cores(shard):
    return lax.ppermute(shard, "narrow", [(0, 1), (1, 0)])


def total_on_one(values):
    blocks = lax.axis_size("blk")
    values = values + lax.ppermute(values, "narrow", [(0, 1)])
    span = 1
    while blocks % (2 * span) == 0:
        pairs = [(2 * i + 1, 2 * (i ^ span) + 1) for i in range(blocks)]
        values = values + lax.ppermute(values, ("blk", "narrow"), pairs)
        span *= 2
    if span < blocks:
        groups = [list(range(i, blocks, span)) for i in range(span)]
        values = lax.psum(values, "blk", axis_index_groups=groups)
    return values


def shards(embeddings, pair_mask, shift_index, start_seed):
    size = embeddings.shape[0]
    blocks = lax.axis_size("blk")
    where = lax.axis_index("blk")
    core = lax.axis_index("narrow")
    other_emb = between_cores(embeddings)
    relaying = blocks % 2 == 0
    back1 = [(i, (i - 1) % blocks) for i in range(blocks) if i % 2 or not relaying]
    back2 = [(i, (i - 2) % blocks) for i in range(blocks)]
    orders = [
        [(2 * i + j, 2 * k) for i, k in back1] + [(2 * i + 1 - j, 2 * k + 1) for i, k in back2] for j in range(2)]
    if relaying:
        orders[0] += [(2 * i, 2 * i + 2) for i in range(0, blocks, 2)]

    def between_shards(shard, pairs):
        return lax.ppermute(shard, ("blk", "narrow"), pairs)

    first, second = between_shards(embeddings, orders[0]), between_shards(embeddings, orders[1])
    seed = start_seed.astype(F32).T / 1000.0
    seeds = jnp.concatenate([seed, between_cores(seed)], axis=0)
    keep = spread(lax.dynamic_slice(pair_mask, (where, core), (1, 1)))
    relays = spread((1 - core) * (where % 2) * int(relaying))
    pair_shape, row_shape = ((2 * NVEC, size), F32), ((16, size), F32)
    h0, l0, sums, row_sq, own_copy, token = make_tile(
        own_body, [embeddings, other_emb], size,
        (((2 * size, 128), F32), (embeddings.shape, BF16), ((8, 128), F32)))
    first, seeds, keep, relays, token = lax.optimization_barrier((first, seeds, keep, relays, token))
    relayed = [first, own_copy]
    if relaying:
        relayed[0] = between_shards(first, [(2 * i, (i - 2) % blocks * 2) for i in range(1, blocks, 2)])
        forward, second = lax.optimization_barrier((first, second))
        relayed[1] = between_shards(forward, [(2 * i + 1, 2 * i + 2) for i in range(0, blocks, 2)])
    tile_args = [keep, relays, token, own_copy, other_emb, row_sq]
    h1, l1, sums, cols1 = make_tile(
        far_body, [*tile_args, first, relayed[0], sums], size, (((8, size), F32),))
    h2, l2, sums, cols2 = make_tile(
        far_body, [*tile_args, second, relayed[1], sums], size, (((8, size), F32),))
    cols = jnp.concatenate([cols1, cols2], axis=0)
    sums = sums + between_blocks(cols, 1)

    small = dict(flops=10**6, nbytes=10**5)
    middle = dict(flops=10**9, nbytes=10**6)
    message_shape = ((2 * NVEC + 16, size), jnp.int16)
    degree, vectors, message = call(
        degree_body, [row_shape, pair_shape, message_shape], [sums, between_cores(sums), seeds], **small)
    far = [h1, l1, h2, l2]
    history = [vectors]
    for _ in range(2):
        near = between_blocks(message, -1)
        (ahead,) = call(ahead_body, [message_shape], [vectors, *far], **middle)
        behind = between_blocks(ahead, 1)
        (product,) = call(own_product_body, [pair_shape], [vectors, h0, l0], **middle)
        (total,) = call(near_product_body, [pair_shape], [product, near, *far], **middle)
        (total,) = call(add_body, [pair_shape], [total, behind], **small)
        vectors, message = call(
            combine_body, [pair_shape, message_shape], [total, between_cores(total), degree], **small)
        history.append(vectors)
    near = between_blocks(message, -1)
    low, scaled = call(
        low_body, [((5 * NVEC, NVEC), F32), ((3 * NVEC, size), F32)], [degree] + history, **middle)
    (product,) = call(own_product_body, [pair_shape], [vectors, h0, l0], **middle)
    (packed,) = call(
        moment_body, [((3 * NVEC // 2 + 8, 2 * NVEC), F32)], [low, vectors, product, near, *far], **middle)
    packed = total_on_one(packed)
    handed = lax.ppermute(packed, "narrow", [(1, 0)])
    rows = size * blocks * lax.axis_size("narrow")
    (out,) = call(
        lambda *refs: dense_body(rows, *refs), [((NVEC, size), F32)],
        [spread(core), spread(shift_index), packed, handed, scaled], flops=2 * 10**10, nbytes=10**6,
    )
    return out.T


def solution(mesh):
    return jax.shard_map(
        shards,
        mesh=mesh,
        in_specs=(
            P(("groups", "blk", "narrow"), None),
            P("groups", None),
            P("groups"),
            P(("groups", "blk", "narrow"), None),
        ),
        out_specs=P(("groups", "blk", "narrow"), None),
        check_vma=False,
    )
```

```python
import math

import jax
import jax.numpy as jnp
from jax import lax
from jax.experimental import pallas as pl
from jax.experimental.pallas import tpu as pltpu
from jax.sharding import PartitionSpec as P

KERNEL_GAMMA = 2.0
RIDGE_WEIGHT = 1e-05
NVEC = 64
F32 = jnp.float32
BF16 = jnp.bfloat16
VMEM_LIMIT = 16 * 1024 * 1024


def dot(left, right, left_dim=1, right_dim=0):
    precision = lax.Precision.HIGHEST if left.dtype == F32 else None
    return lax.dot_general(
        left, right, (((left_dim,), (right_dim,)), ((), ())),
        precision=precision, preferred_element_type=F32,
    )


def halves(values):
    high = values.astype(BF16)
    return high, (values - high.astype(F32)).astype(BF16)


def call(body, out_shapes, args, flops=0, nbytes=0):
    return pl.pallas_call(
        body,
        out_shape=[jax.ShapeDtypeStruct(shape, dtype) for shape, dtype in out_shapes],
        in_specs=[pl.BlockSpec(memory_space=pltpu.VMEM) for _ in args],
        out_specs=[pl.BlockSpec(memory_space=pltpu.VMEM) for _ in out_shapes],
        compiler_params=pltpu.CompilerParams(vmem_limit_bytes=VMEM_LIMIT),
        cost_estimate=pl.CostEstimate(flops=flops, bytes_accessed=nbytes, transcendentals=0),
    )(*args)


def spread(value):
    return jnp.broadcast_to(value.astype(F32), (8, 128))


def chosen(flag, first, second):
    rows, cols = first.shape
    wide = jnp.concatenate([flag[0:1, :]] * (cols // 128), axis=1)
    return jnp.where(jnp.broadcast_to(wide, (rows, cols)) > 0.5, first, second)


LOG2_E = 1.4426950408889634


def sums_along(values):
    rows, depth = values.shape
    folded = values[:, :128]
    for j in range(128, depth, 128):
        folded = folded + values[:, j:j + 128]
    return dot(jnp.ones((8, 128), F32), folded, 1, 1)


def fill_tile(weight, row_embs, row_sq, col_emb, high, low, row_sum):
    size = col_emb.shape[0]
    col32 = col_emb.astype(F32)
    col_sq = (2.0 * LOG2_E) * sums_along(col32 * col32)[0:1, :]
    total = jnp.zeros((1, size), F32)
    for half in range(2):
        rows = slice(half * size, (half + 1) * size)
        inner = dot(row_embs[half], col_emb, 1, 1)
        squares = jnp.concatenate([row_sq[rows, :]] * (size // 128), axis=1)
        tile = jnp.exp2((4.0 * LOG2_E) * inner - (squares + col_sq))
        if weight is not None:
            tile = tile * weight
        tile_high, tile_low = halves(tile)
        high[rows, :] = tile_high
        low[rows, :] = tile_low
        row_sum[half * 8:(half + 1) * 8, :] = row_sum[half * 8:(half + 1) * 8, :] + sums_along(tile)
        total = total + jnp.sum(tile, axis=0, keepdims=True)
    return jnp.broadcast_to(total, (8, size))


def own_body(own, other, high, low, row_sum, row_sq, copy, token):
    size = own.shape[0]
    embs = [own[...], other[...]]
    copy[...] = embs[0]
    for half in range(2):
        row32 = embs[half].astype(F32)
        squares = (2.0 * LOG2_E) * jnp.sum(row32 * row32, axis=1, keepdims=True)
        row_sq[half * size:(half + 1) * size, :] = jnp.broadcast_to(squares, (size, 128))
    row_sum[...] = jnp.zeros(row_sum.shape, F32)
    token[...] = jnp.zeros(token.shape, F32)
    fill_tile(None, embs, row_sq, embs[0], high, low, row_sum)


def far_body(keep, relays, token, own, other, row_sq, direct, relayed, before, high, low, row_sum, col_sum):
    row_sum[...] = before[...] + token[0:1, 0:1]
    size = own.shape[0]
    weight = jnp.concatenate([keep[0:1, :]] * (size // 128), axis=1)
    col = chosen(relays, relayed[...], direct[...])
    col_sum[...] = fill_tile(weight, [own[...], other[...]], row_sq, col, high, low, row_sum)


def make_tile(body, args, rows, extra=()):
    return call(
        body, [((2 * rows, rows), BF16), ((2 * rows, rows), BF16), ((16, rows), F32), *extra],
        args, flops=2 * 10**9, nbytes=10**6,
    )


def swapped(values):
    middle = values.shape[0] // 2
    return jnp.concatenate([values[middle:], values[:middle]], axis=0)


def per_row(values, width):
    shape = (width, values.shape[1])
    return jnp.concatenate([jnp.broadcast_to(values[i:i + 1, :], shape) for i in (0, 8)], axis=0)


def packed_rows(values):
    rows, cols = values.shape
    biggest = jnp.max(jnp.abs(values), axis=1, keepdims=True)
    power = jnp.floor(jnp.log2(jnp.maximum(biggest, 1e-30)) + 1e-3)
    whole = jnp.round(values * jnp.exp2(14.0 - power)).astype(jnp.int32).astype(jnp.int16)
    powers = jnp.broadcast_to(power, (rows, 128)).T[:16, :]
    powers = jnp.concatenate([powers] * (cols // 128), axis=1)
    return jnp.concatenate([whole, powers.astype(jnp.int32).astype(jnp.int16)], axis=0)


def unpacked_rows(message):
    rows, cols = message.shape[0] - 16, message.shape[1]
    whole = message[:rows, :].astype(jnp.int32).astype(F32)
    powers = message[rows:, :128].astype(jnp.int32).astype(F32)[0:1, :]
    scale = jnp.exp2(jnp.broadcast_to(powers, (128, 128)).T[:rows, :] - 14.0)
    return whole * jnp.concatenate([scale] * (cols // 128), axis=1)


def degree_body(sums, other_sums, seeds, degree_out, vectors_out, message):
    degree = sums[...] + swapped(other_sums[...])
    scale = lax.rsqrt(degree)
    degree_out[...] = degree
    vectors = seeds[...] * per_row(scale, seeds.shape[0] // 2)
    vectors_out[...] = vectors
    message[...] = packed_rows(vectors)


def ahead_body(vectors, h1, l1, h2, l2, ahead):
    width = vectors.shape[0] // 2
    high, low = halves(jnp.concatenate([vectors[:width, :], vectors[width:, :]], axis=1))
    both = jnp.concatenate([high, low], axis=0)
    products = []
    for tile_high, tile_low in ((h1, l1), (h2, l2)):
        product = dot(both, tile_high[...])
        products.append(product[:width] + product[width:] + dot(high, tile_low[...]))
    ahead[...] = packed_rows(jnp.concatenate(products, axis=0))


def combine_body(total, other_total, degree, vectors_out, message):
    vectors = (total[...] + swapped(other_total[...])) / per_row(degree[...], total.shape[0] // 2)
    vectors_out[...] = vectors
    message[...] = packed_rows(vectors)


def product_rows(vectors, tile_high, tile_low):
    width = vectors.shape[0]
    high, low = halves(vectors)
    both = jnp.concatenate([high, low], axis=0)
    product = dot(both, tile_high[...], 1, 1)
    return product[:width] + product[width:] + dot(high, tile_low[...], 1, 1)


def stacked(product):
    size = product.shape[1] // 2
    return jnp.concatenate([product[:, :size], product[:, size:]], axis=0)


def own_product_body(vectors, h0, l0, out):
    out[...] = stacked(product_rows(vectors[:vectors.shape[0] // 2, :], h0, l0))


def far_product(message, h1, l1, h2, l2):
    near = unpacked_rows(message)
    width = near.shape[0] // 2
    return product_rows(near[:width], h1, l1) + product_rows(near[width:], h2, l2)


def near_product_body(product, near, h1, l1, h2, l2, total):
    total[...] = product[...] + stacked(far_product(near, h1, l1, h2, l2))


def add_body(total, behind, out):
    out[...] = total[...] + unpacked_rows(behind)


def low_body(degree, v0, v1, v2, moments, scaled):
    width = v0.shape[0] // 2
    root = jnp.sqrt(degree[0:1, :])
    x0, x1, x2 = v0[:width, :] * root, v1[:width, :] * root, v2[:width, :] * root
    scaled[...] = jnp.concatenate([x0, x1, x2], axis=0)
    left = jnp.concatenate([x0, x1], axis=0)
    order012 = dot(left, left, 1, 1)
    order34 = dot(jnp.concatenate([x1, x2], axis=0), x2, 1, 1)
    order = [order012[:width, :width], order012[:width, width:], order012[width:, width:],
             order34[:width], order34[width:]]
    for i in range(5):
        moments[i * width:(i + 1) * width, :] = order[i]


def place_of(rows, cols):
    return [lax.broadcasted_iota(jnp.int32, (rows, cols), axis) for axis in range(2)]


def moment_body(core, low, vectors, product, near, h1, l1, h2, l2, mine, theirs):
    n = vectors.shape[0] // 2
    last = far_product(near, h1, l1, h2, l2)
    last = 2.0 * last + jnp.concatenate([product[:n, :], product[n:, :]], axis=1)
    last = dot(jnp.concatenate([vectors[:n, :], vectors[n:, :]], axis=1), last, 1, 1)
    moments = [low[i * n:(i + 1) * n, :] for i in range(5)] + [0.5 * (last + last.T)]
    row, col = place_of(n, n)
    pieces = []
    for i in range(0, 6, 2):
        pair = jnp.where(row >= col, moments[i], moments[i + 1])
        pieces.append(jnp.concatenate([pair[:n // 2], pair[n // 2:]], axis=1))
    d1, d3, d5 = (jnp.sum(moments[i] * unit(n, n), axis=0, keepdims=True) for i in (1, 3, 5))
    row, _ = place_of(8, 2 * n)
    pieces.append(jnp.where(row == 0, jnp.concatenate([d1, d3], axis=1),
                            jnp.where(row == 1, jnp.concatenate([d5, d5], axis=1), 0.0)))
    pieces.append(jnp.zeros((8, 2 * n), F32))
    packed = jnp.concatenate(pieces, axis=0)
    half = packed.shape[0] // 2
    mine[...] = chosen(core, packed[half:], packed[:half])
    theirs[...] = chosen(core, packed[:half], packed[half:])


def unpacked(packed, n):
    row, col = place_of(n, n)
    start = 3 * n // 2
    diagonals = [packed[start:start + 1, :n], packed[start:start + 1, n:], packed[start + 1:start + 2, :n]]
    moments = []
    for i in range(3):
        folded = packed[i * n // 2:(i + 1) * n // 2]
        pair = jnp.concatenate([folded[:, :n], folded[:, n:]], axis=0)
        flipped = pair.T
        moments.append(jnp.where(row >= col, pair, flipped))
        moments.append(jnp.where(row == col, diagonals[i], jnp.where(row < col, pair, flipped)))
    return moments


def unit(rows, cols):
    return (lax.broadcasted_iota(jnp.int32, (rows, cols), 0)
            == lax.broadcasted_iota(jnp.int32, (rows, cols), 1)).astype(F32)


def lane(values, k):
    return jnp.take_along_axis(values, jnp.full(values.shape, k, jnp.int32), axis=1, mode="promise_in_bounds")


def sublane(values, k):
    return jnp.broadcast_to(values[k:k + 1, :], values.shape)


def inverse_factor(matrix):
    size = matrix.shape[0]
    work = jnp.concatenate([matrix, unit(size, size)], axis=1)
    blocks = [work[8 * i:8 * i + 8, :] for i in range(size // 8)]
    place = lax.broadcasted_iota(jnp.int32, (8, 2 * size), 0)
    done = [None] * (size // 8)

    def corner(cols, r):
        return [[sublane(cols[j], r + i) for j in range(i + 1)] for i in range(4)]

    pivot = corner([lane(blocks[0], j) for j in range(4)], 0)
    for k in range(0, size, 4):
        top, r = divmod(k, 8)
        (a00,), (a10, a11), (a20, a21, a22), (a30, a31, a32, a33) = pivot
        u0, u1, u2, u3 = u = [sublane(blocks[top], r + j) for j in range(4)]
        det_a = a00 * a11 - a10 * a10
        inv_a = 1.0 / det_a
        p00, p10, p11 = a11 * inv_a, a10 * inv_a, a00 * inv_a
        b00, b01 = a20 * p00 - a21 * p10, a21 * p11 - a20 * p10
        b10, b11 = a30 * p00 - a31 * p10, a31 * p11 - a30 * p10
        s00 = a22 - (b00 * a20 + b01 * a21)
        s10 = a32 - (b10 * a20 + b11 * a21)
        s11 = a33 - (b10 * a30 + b11 * a31)
        det_s = s00 * s11 - s10 * s10
        inv_s = 1.0 / det_s
        q22, q32, q33 = s11 * inv_s, -s10 * inv_s, s00 * inv_s
        q20, q21 = -(q22 * b00 + q32 * b10), -(q22 * b01 + q32 * b11)
        q30, q31 = -(q32 * b00 + q33 * b10), -(q32 * b01 + q33 * b11)
        q00 = p00 - (b00 * q20 + b10 * q30)
        q10 = -p10 - (b01 * q20 + b11 * q30)
        q11 = p11 - (b01 * q21 + b11 * q31)
        inverse = [[q00, q10, q20, q30], [q10, q11, q21, q31], [q20, q21, q22, q32], [q30, q31, q32, q33]]

        def applied(values):
            return [(row[0] * values[0] + row[1] * values[1]) + (row[2] * values[2] + row[3] * values[3])
                    for row in inverse]

        if k + 4 < size:
            across = [lane(blocks[top], k + 4 + j) for j in range(4)]
            cross = [[sublane(across[j], r + i) for i in range(4)] for j in range(4)]
            after = across if r == 0 else [lane(blocks[top + 1], k + 4 + j) for j in range(4)]
            plain = corner(after, 4 - r)
            solved = [applied(column) for column in cross]
            pivot = [[plain[i][j] - ((cross[i][0] * solved[j][0] + cross[i][1] * solved[j][1])
                                     + (cross[i][2] * solved[j][2] + cross[i][3] * solved[j][3]))
                      for j in range(i + 1)] for i in range(4)]
        t = applied(u)
        for i in range(top, size // 8):
            if i == top and r:
                continue
            c = [lane(blocks[i], k + j) for j in range(4)]
            change = (c[0] * t[0] + c[1] * t[1]) + (c[2] * t[2] + c[3] * t[3])
            blocks[i] = blocks[i] - (jnp.where(place > 3, change, 0.0) if i == top else change)
        v0 = u0 * lax.rsqrt(a00)
        v1 = (a00 * u1 - a10 * u0) * lax.rsqrt(a00 * det_a)
        u2 = u2 - b00 * u0 - b01 * u1
        u3 = u3 - b10 * u0 - b11 * u1
        v2 = u2 * lax.rsqrt(s00)
        v3 = (s00 * u3 - s10 * u2) * lax.rsqrt(s00 * det_s)
        four = jnp.where(place % 4 == 0, v0, jnp.where(place % 4 == 1, v1, jnp.where(place % 4 == 2, v2, v3)))
        done[top] = jnp.where(place > 3, four, done[top]) if r else four
    return jnp.concatenate(done, axis=0)[:, size:]


def total(matrix):
    return jnp.sum(jnp.sum(matrix, axis=0, keepdims=True), axis=1, keepdims=True)


def trace(matrix):
    return total(matrix * unit(*matrix.shape))


def inverse_root(matrix):
    eye = unit(*matrix.shape)
    rest = matrix - eye

    def series():
        return eye - 0.5 * rest + 0.375 * dot(rest, rest)

    return lax.cond(jnp.sum(rest * rest) < 1e-4, series, lambda: inverse_factor(matrix))


def dense(moments, index, rows, data):
    n = NVEC
    eye = unit(n, n)
    pick = ((lax.broadcasted_iota(jnp.int32, (n, n), 0) == index)
            & (lax.broadcasted_iota(jnp.int32, (n, n), 1) == index)).astype(F32)

    def part(stacked, i):
        return stacked[i * n:(i + 1) * n]

    def below(*parts):
        return jnp.concatenate(parts, axis=0)

    def beside(*parts):
        return jnp.concatenate(parts, axis=1)

    base = inverse_factor(moments[0])
    right = dot(below(*moments[1:]), base, 1, 1)
    m1, m2, m3, m4, m5 = (dot(base, part(right, i)) for i in range(5))

    by1 = dot(below(m1, m2, m3, m4), m1)
    square, m21, m31, m41 = (part(by1, i) for i in range(4))
    tri = dot(m1, beside(square, m21, m31))
    gram_r = m2 - square
    image_r = m3 - m21 - m21.T + tri[:, :n]
    mixed_r = m3 - m21
    square_r = m4 - m31 - m31.T + tri[:, n:2 * n]
    cubic_r = m5 - m41 - m41.T + tri[:, 2 * n:]
    shift = 3.0 - total(m1 * pick)
    ridge = RIDGE_WEIGHT * (n + trace(gram_r)) / (2 * n)
    ridged = gram_r + ridge * eye
    factor = inverse_factor(ridged)
    inverse = dot(factor, factor, 0, 0)
    keep = 1.0 / (1.0 + ridge)
    step = below(
        beside(m1 * keep + shift * eye, gram_r * keep),
        beside(eye - ridge * inverse, dot(inverse, image_r) + shift * eye),
    )
    twice = dot(step, step)
    power = dot(twice, dot(twice, twice[:, :n]))
    top, bottom = power[:n], power[n:]
    weighted = dot(below(ridged, gram_r, image_r), bottom)
    norm = (1.0 + ridge) * dot(top, top, 0, 0) + dot(bottom, part(weighted, 0), 0, 0)
    factor = inverse_factor(norm)

    middle = m4 - m31
    images = dot(below(
        beside(m1, gram_r), beside(gram_r, image_r),
        beside(m2, mixed_r), beside(mixed_r.T, square_r),
        beside(m3, middle), beside(middle.T, cubic_r),
    ), power)
    whole = dot(power, beside(images[:2 * n], images[2 * n:4 * n], images[4 * n:], power), 0, 0)
    lower = dot(bottom, beside(part(images, 1), part(images, 3), part(weighted, 1), part(weighted, 2)), 0, 0)
    raw = [whole[:, i * n:(i + 1) * n] for i in range(4)] + [lower[:, i * n:(i + 1) * n] for i in range(4)]
    right = dot(below(*raw), factor, 1, 1)
    ritz, image2, image3, excess, p_image, p_image2, p_gram, p_ritz = (dot(factor, part(right, i)) for i in range(8))
    excess = ridge * excess

    shift = 3.0 - total(ritz * pick)
    by_ritz = dot(below(ritz, p_gram, excess, p_image, image2), ritz)
    squared, gram_pr, gram_cr = part(by_ritz, 0), p_image - part(by_ritz, 1), part(by_ritz, 2)
    tri = dot(ritz, squared), dot(ritz, gram_cr)
    gram_rr = image2 - squared - tri[1]
    image_cr = image2 - squared
    image_pr = p_image2 - part(by_ritz, 3)
    image_rr = image3 - part(by_ritz, 4) - part(by_ritz, 4).T + tri[0]
    ridge = RIDGE_WEIGHT * (n - trace(excess) + trace(p_gram) + trace(gram_rr)) / (3 * n)
    g_cc = eye - excess + ridge * eye
    g_pp = p_gram + ridge * eye
    g_rr = gram_rr + ridge * eye
    image_gram = below(
        beside(ritz, p_image.T, image_cr), beside(p_image, p_ritz, image_pr), beside(image_cr.T, image_pr.T, image_rr),
    )
    v0 = inverse_root(g_cc)
    side = dot(below(p_gram, gram_cr.T), v0, 1, 1)
    l10, l20 = side[:n], side[n:]
    outer = dot(side, side, 1, 1)
    v1 = inverse_factor(g_pp - outer[:n, :n])
    l21 = dot(gram_pr.T - outer[n:, :n], v1, 1, 1)
    v2 = inverse_factor(g_rr - outer[n:, n:] - dot(l21, l21, 1, 1))
    zero = jnp.zeros((n, n), F32)
    row0 = beside(v0, zero, zero)
    row1 = dot(v1, beside(-dot(l10, v0), eye, zero))
    row2 = beside(zero, zero, eye) - dot(l20, row0) - dot(l21, row1)
    known = below(row0, row1)
    solved = dot(known, dot(known, image_gram), 0, 0)
    row2 = dot(v2, beside(row2, dot(row2, image_gram)))
    step = solved + dot(row2[:, :3 * n], row2[:, 3 * n:], 0, 0) + shift * unit(3 * n, 3 * n)
    twice = dot(step, step)
    power2 = dot(twice, dot(twice, twice[:, :n]))
    gram = below(
        beside(g_cc, p_gram, gram_cr), beside(p_gram, g_pp, gram_pr), beside(gram_cr.T, gram_pr.T, g_rr),
    )
    norm = dot(power2, dot(gram, power2), 0, 0)

    back = dot(m1, bottom)
    of_top, of_bottom, of_back = (
        dot(factor, dot(part, base, 0, 0)) for part in (top - back, bottom, back))
    vectors = below(
        beside(of_top, of_bottom, zero),
        beside(-of_back, of_bottom, zero),
        beside(-dot(ritz, of_top), of_top - dot(ritz, of_bottom), of_bottom),
    )
    mixed = dot(power2, vectors, 0, 0)
    return dot(dot(inverse_factor(norm), mixed), data) * math.sqrt(rows)


def dense_body(rows, core, index, mine, theirs, scaled, out):
    packed = jnp.concatenate([
        chosen(core, theirs[...], mine[...]), chosen(core, mine[...], theirs[...])], axis=0)
    index = jnp.broadcast_to(index[0:1, :NVEC], (NVEC, NVEC)).astype(jnp.int32)
    out[...] = dense(unpacked(packed, NVEC), index, rows, scaled[...])


def between_blocks(shard, sign):
    blocks, cores = lax.axis_size("blk"), lax.axis_size("narrow")
    pairs = [(i * cores + j, (i + sign * (1 + j)) % blocks * cores + j) for i in range(blocks) for j in range(cores)]
    return lax.ppermute(shard, ("blk", "narrow"), pairs)


def between_cores(shard):
    return lax.ppermute(shard, "narrow", [(0, 1), (1, 0)])


def total_over_blocks(values):
    blocks = lax.axis_size("blk")
    span = 1
    while blocks % (2 * span) == 0:
        values = values + lax.ppermute(values, "blk", [(i, i ^ span) for i in range(blocks)])
        span *= 2
    if span < blocks:
        groups = [list(range(i, blocks, span)) for i in range(span)]
        values = lax.psum(values, "blk", axis_index_groups=groups)
    return values


def shards(embeddings, pair_mask, shift_index, start_seed):
    size = embeddings.shape[0]
    blocks = lax.axis_size("blk")
    where = lax.axis_index("blk")
    core = lax.axis_index("narrow")
    other_emb = between_cores(embeddings)
    relaying = blocks % 2 == 0
    back1 = [(i, (i - 1) % blocks) for i in range(blocks) if i % 2 or not relaying]
    back2 = [(i, (i - 2) % blocks) for i in range(blocks)]
    orders = [
        [(2 * i + j, 2 * k) for i, k in back1] + [(2 * i + 1 - j, 2 * k + 1) for i, k in back2] for j in range(2)]
    if relaying:
        orders[0] += [(2 * i, 2 * i + 2) for i in range(0, blocks, 2)]

    def between_shards(shard, pairs):
        return lax.ppermute(shard, ("blk", "narrow"), pairs)

    first, second = between_shards(embeddings, orders[0]), between_shards(embeddings, orders[1])
    seed = start_seed.astype(F32).T / 1000.0
    seeds = jnp.concatenate([seed, between_cores(seed)], axis=0)
    keep = spread(lax.dynamic_slice(pair_mask, (where, core), (1, 1)))
    relays = spread((1 - core) * (where % 2) * int(relaying))
    pair_shape, row_shape = ((2 * NVEC, size), F32), ((16, size), F32)
    h0, l0, sums, row_sq, own_copy, token = make_tile(
        own_body, [embeddings, other_emb], size,
        (((2 * size, 128), F32), (embeddings.shape, BF16), ((8, 128), F32)))
    first, seeds, keep, relays, token = lax.optimization_barrier((first, seeds, keep, relays, token))
    relayed = [first, own_copy]
    if relaying:
        relayed[0] = between_shards(first, [(2 * i, (i - 2) % blocks * 2) for i in range(1, blocks, 2)])
        forward, second = lax.optimization_barrier((first, second))
        relayed[1] = between_shards(forward, [(2 * i + 1, 2 * i + 2) for i in range(0, blocks, 2)])
    tile_args = [keep, relays, token, own_copy, other_emb, row_sq]
    h1, l1, sums, cols1 = make_tile(
        far_body, [*tile_args, first, relayed[0], sums], size, (((8, size), F32),))
    h2, l2, sums, cols2 = make_tile(
        far_body, [*tile_args, second, relayed[1], sums], size, (((8, size), F32),))
    cols = jnp.concatenate([cols1, cols2], axis=0)
    sums = sums + between_blocks(cols, 1)

    small = dict(flops=10**6, nbytes=10**5)
    middle = dict(flops=10**9, nbytes=10**6)
    message_shape = ((2 * NVEC + 16, size), jnp.int16)
    degree, vectors, message = call(
        degree_body, [row_shape, pair_shape, message_shape], [sums, between_cores(sums), seeds], **small)
    far = [h1, l1, h2, l2]
    history = [vectors]
    for _ in range(2):
        near = between_blocks(message, -1)
        (ahead,) = call(ahead_body, [message_shape], [vectors, *far], **middle)
        behind = between_blocks(ahead, 1)
        (product,) = call(own_product_body, [pair_shape], [vectors, h0, l0], **middle)
        (total,) = call(near_product_body, [pair_shape], [product, near, *far], **middle)
        (total,) = call(add_body, [pair_shape], [total, behind], **small)
        vectors, message = call(
            combine_body, [pair_shape, message_shape], [total, between_cores(total), degree], **small)
        history.append(vectors)
    near = between_blocks(message, -1)
    low, scaled = call(
        low_body, [((5 * NVEC, NVEC), F32), ((3 * NVEC, size), F32)], [degree] + history, **middle)
    (product,) = call(own_product_body, [pair_shape], [vectors, h0, l0], **middle)
    packed_shape = ((3 * NVEC // 4 + 8, 2 * NVEC), F32)
    mine, theirs = call(
        moment_body, [packed_shape] * 2, [spread(core), low, vectors, product, near, *far], **middle)
    mine = total_over_blocks(mine + between_cores(theirs))
    rows = size * blocks * lax.axis_size("narrow")
    (out,) = call(
        lambda *refs: dense_body(rows, *refs), [((NVEC, size), F32)],
        [spread(core), spread(shift_index), mine, between_cores(mine), scaled], flops=2 * 10**10, nbytes=10**6,
    )
    return out.T


def solution(mesh):
    return jax.shard_map(
        shards,
        mesh=mesh,
        in_specs=(
            P(("groups", "blk", "narrow"), None),
            P("groups", None),
            P("groups"),
            P(("groups", "blk", "narrow"), None),
        ),
        out_specs=P(("groups", "blk", "narrow"), None),
        check_vma=False,
    )
```

```python
import math

import jax
import jax.numpy as jnp
from jax import lax
from jax.experimental import pallas as pl
from jax.experimental.pallas import tpu as pltpu
from jax.sharding import PartitionSpec as P

KERNEL_GAMMA = 2.0
RIDGE_WEIGHT = 1e-05
NVEC = 64
F32 = jnp.float32
BF16 = jnp.bfloat16
VMEM_LIMIT = 16 * 1024 * 1024


def dot(left, right, left_dim=1, right_dim=0):
    precision = lax.Precision.HIGHEST if left.dtype == F32 else None
    return lax.dot_general(
        left, right, (((left_dim,), (right_dim,)), ((), ())),
        precision=precision, preferred_element_type=F32,
    )


def halves(values):
    high = values.astype(BF16)
    return high, (values - high.astype(F32)).astype(BF16)


def call(body, out_shapes, args, flops=0, nbytes=0):
    return pl.pallas_call(
        body,
        out_shape=[jax.ShapeDtypeStruct(shape, dtype) for shape, dtype in out_shapes],
        in_specs=[pl.BlockSpec(memory_space=pltpu.VMEM) for _ in args],
        out_specs=[pl.BlockSpec(memory_space=pltpu.VMEM) for _ in out_shapes],
        compiler_params=pltpu.CompilerParams(vmem_limit_bytes=VMEM_LIMIT),
        cost_estimate=pl.CostEstimate(flops=flops, bytes_accessed=nbytes, transcendentals=0),
    )(*args)


def spread(value):
    return jnp.broadcast_to(value.astype(F32), (8, 128))


def chosen(flag, first, second):
    rows, cols = first.shape
    wide = jnp.concatenate([flag[0:1, :]] * (cols // 128), axis=1)
    return jnp.where(jnp.broadcast_to(wide, (rows, cols)) > 0.5, first, second)


LOG2_E = 1.4426950408889634


def sums_along(values):
    rows, depth = values.shape
    folded = values[:, :128]
    for j in range(128, depth, 128):
        folded = folded + values[:, j:j + 128]
    return dot(jnp.ones((8, 128), F32), folded, 1, 1)


def fill_tile(weight, row_embs, row_sq, col_emb, high, low, row_sum):
    size = col_emb.shape[0]
    col32 = col_emb.astype(F32)
    col_sq = (2.0 * LOG2_E) * sums_along(col32 * col32)[0:1, :]
    total = jnp.zeros((1, size), F32)
    for half in range(2):
        rows = slice(half * size, (half + 1) * size)
        inner = dot(row_embs[half], col_emb, 1, 1)
        squares = jnp.concatenate([row_sq[rows, :]] * (size // 128), axis=1)
        tile = jnp.exp2((4.0 * LOG2_E) * inner - (squares + col_sq))
        if weight is not None:
            tile = tile * weight
        tile_high, tile_low = halves(tile)
        high[rows, :] = tile_high
        low[rows, :] = tile_low
        row_sum[half * 8:(half + 1) * 8, :] = row_sum[half * 8:(half + 1) * 8, :] + sums_along(tile)
        total = total + jnp.sum(tile, axis=0, keepdims=True)
    return jnp.broadcast_to(total, (8, size))


def own_body(own, other, high, low, row_sum, row_sq, copy, token):
    size = own.shape[0]
    embs = [own[...], other[...]]
    copy[...] = embs[0]
    for half in range(2):
        row32 = embs[half].astype(F32)
        squares = (2.0 * LOG2_E) * jnp.sum(row32 * row32, axis=1, keepdims=True)
        row_sq[half * size:(half + 1) * size, :] = jnp.broadcast_to(squares, (size, 128))
    row_sum[...] = jnp.zeros(row_sum.shape, F32)
    token[...] = jnp.zeros(token.shape, F32)
    fill_tile(None, embs, row_sq, embs[0], high, low, row_sum)


def far_body(keep, relays, token, own, other, row_sq, direct, relayed, before, high, low, row_sum, col_sum):
    row_sum[...] = before[...] + token[0:1, 0:1]
    size = own.shape[0]
    weight = jnp.concatenate([keep[0:1, :]] * (size // 128), axis=1)
    col = chosen(relays, relayed[...], direct[...])
    col_sum[...] = fill_tile(weight, [own[...], other[...]], row_sq, col, high, low, row_sum)


def make_tile(body, args, rows, extra=()):
    return call(
        body, [((2 * rows, rows), BF16), ((2 * rows, rows), BF16), ((16, rows), F32), *extra],
        args, flops=2 * 10**9, nbytes=10**6,
    )


def swapped(values):
    middle = values.shape[0] // 2
    return jnp.concatenate([values[middle:], values[:middle]], axis=0)


def per_row(values, width):
    shape = (width, values.shape[1])
    return jnp.concatenate([jnp.broadcast_to(values[i:i + 1, :], shape) for i in (0, 8)], axis=0)


def packed_rows(values):
    rows, cols = values.shape
    biggest = jnp.max(jnp.abs(values), axis=1, keepdims=True)
    power = jnp.floor(jnp.log2(jnp.maximum(biggest, 1e-30)) + 1e-3)
    whole = jnp.round(values * jnp.exp2(14.0 - power)).astype(jnp.int32).astype(jnp.int16)
    powers = jnp.broadcast_to(power, (rows, 128)).T[:16, :]
    powers = jnp.concatenate([powers] * (cols // 128), axis=1)
    return jnp.concatenate([whole, powers.astype(jnp.int32).astype(jnp.int16)], axis=0)


def unpacked_rows(message):
    rows, cols = message.shape[0] - 16, message.shape[1]
    whole = message[:rows, :].astype(jnp.int32).astype(F32)
    powers = message[rows:, :128].astype(jnp.int32).astype(F32)[0:1, :]
    scale = jnp.exp2(jnp.broadcast_to(powers, (128, 128)).T[:rows, :] - 14.0)
    return whole * jnp.concatenate([scale] * (cols // 128), axis=1)


def degree_body(sums, other_sums, seeds, degree_out, vectors_out, message):
    degree = sums[...] + swapped(other_sums[...])
    scale = lax.rsqrt(degree)
    degree_out[...] = degree
    vectors = seeds[...] * per_row(scale, seeds.shape[0] // 2)
    vectors_out[...] = vectors
    message[...] = packed_rows(vectors)


def ahead_body(vectors, h1, l1, h2, l2, ahead):
    width = vectors.shape[0] // 2
    high, low = halves(jnp.concatenate([vectors[:width, :], vectors[width:, :]], axis=1))
    both = jnp.concatenate([high, low], axis=0)
    products = []
    for tile_high, tile_low in ((h1, l1), (h2, l2)):
        product = dot(both, tile_high[...])
        products.append(product[:width] + product[width:] + dot(high, tile_low[...]))
    ahead[...] = packed_rows(jnp.concatenate(products, axis=0))


def combine_body(total, other_total, degree, vectors_out, message):
    vectors = (total[...] + swapped(other_total[...])) / per_row(degree[...], total.shape[0] // 2)
    vectors_out[...] = vectors
    message[...] = packed_rows(vectors)


def product_rows(vectors, tile_high, tile_low):
    width = vectors.shape[0]
    high, low = halves(vectors)
    both = jnp.concatenate([high, low], axis=0)
    product = dot(both, tile_high[...], 1, 1)
    return product[:width] + product[width:] + dot(high, tile_low[...], 1, 1)


def stacked(product):
    size = product.shape[1] // 2
    return jnp.concatenate([product[:, :size], product[:, size:]], axis=0)


def own_product_body(vectors, h0, l0, out):
    out[...] = stacked(product_rows(vectors[:vectors.shape[0] // 2, :], h0, l0))


def far_product(message, h1, l1, h2, l2):
    near = unpacked_rows(message)
    width = near.shape[0] // 2
    return product_rows(near[:width], h1, l1) + product_rows(near[width:], h2, l2)


def near_product_body(product, near, h1, l1, h2, l2, total):
    total[...] = product[...] + stacked(far_product(near, h1, l1, h2, l2))


def add_body(total, behind, out):
    out[...] = total[...] + unpacked_rows(behind)


def low_body(degree, v0, v1, v2, moments, scaled):
    width = v0.shape[0] // 2
    root = jnp.sqrt(degree[0:1, :])
    x0, x1, x2 = v0[:width, :] * root, v1[:width, :] * root, v2[:width, :] * root
    scaled[...] = jnp.concatenate([x0, x1, x2], axis=0)
    left = jnp.concatenate([x0, x1], axis=0)
    order012 = dot(left, left, 1, 1)
    order34 = dot(jnp.concatenate([x1, x2], axis=0), x2, 1, 1)
    order = [order012[:width, :width], order012[:width, width:], order012[width:, width:],
             order34[:width], order34[width:]]
    for i in range(5):
        moments[i * width:(i + 1) * width, :] = order[i]


def place_of(rows, cols):
    return [lax.broadcasted_iota(jnp.int32, (rows, cols), axis) for axis in range(2)]


def moment_body(core, low, vectors, product, near, h1, l1, h2, l2, mine, theirs):
    n = vectors.shape[0] // 2
    last = far_product(near, h1, l1, h2, l2)
    last = 2.0 * last + jnp.concatenate([product[:n, :], product[n:, :]], axis=1)
    last = dot(jnp.concatenate([vectors[:n, :], vectors[n:, :]], axis=1), last, 1, 1)
    moments = [low[i * n:(i + 1) * n, :] for i in range(5)] + [0.5 * (last + last.T)]
    row, col = place_of(n, n)
    pieces = []
    for i in range(0, 6, 2):
        pair = jnp.where(row >= col, moments[i], moments[i + 1])
        pieces.append(jnp.concatenate([pair[:n // 2], pair[n // 2:]], axis=1))
    d1, d3, d5 = (jnp.sum(moments[i] * unit(n, n), axis=0, keepdims=True) for i in (1, 3, 5))
    row, _ = place_of(8, 2 * n)
    pieces.append(jnp.where(row == 0, jnp.concatenate([d1, d3], axis=1),
                            jnp.where(row == 1, jnp.concatenate([d5, d5], axis=1), 0.0)))
    pieces.append(jnp.zeros((8, 2 * n), F32))
    packed = jnp.concatenate(pieces, axis=0)
    half = packed.shape[0] // 2
    mine[...] = chosen(core, packed[half:], packed[:half])
    theirs[...] = chosen(core, packed[:half], packed[half:])


def unpacked(packed, n):
    row, col = place_of(n, n)
    start = 3 * n // 2
    diagonals = [packed[start:start + 1, :n], packed[start:start + 1, n:], packed[start + 1:start + 2, :n]]
    moments = []
    for i in range(3):
        folded = packed[i * n // 2:(i + 1) * n // 2]
        pair = jnp.concatenate([folded[:, :n], folded[:, n:]], axis=0)
        flipped = pair.T
        moments.append(jnp.where(row >= col, pair, flipped))
        moments.append(jnp.where(row == col, diagonals[i], jnp.where(row < col, pair, flipped)))
    return moments


def unit(rows, cols):
    return (lax.broadcasted_iota(jnp.int32, (rows, cols), 0)
            == lax.broadcasted_iota(jnp.int32, (rows, cols), 1)).astype(F32)


def lane(values, k):
    return jnp.take_along_axis(values, jnp.full(values.shape, k, jnp.int32), axis=1, mode="promise_in_bounds")


def sublane(values, k):
    return jnp.broadcast_to(values[k:k + 1, :], values.shape)


def reciprocal(values):
    guess = pl.reciprocal(values, approx=True)
    guess = guess * (2.0 - values * guess)
    return guess * (2.0 - values * guess)


def inverse_factor(matrix):
    size = matrix.shape[0]
    work = jnp.concatenate([matrix, unit(size, size)], axis=1)
    blocks = [work[8 * i:8 * i + 8, :] for i in range(size // 8)]
    place = lax.broadcasted_iota(jnp.int32, (8, 2 * size), 0)
    done = [None] * (size // 8)

    def corner(cols, r):
        return [[sublane(cols[j], r + i) for j in range(i + 1)] for i in range(4)]

    pivot = corner([lane(blocks[0], j) for j in range(4)], 0)
    for k in range(0, size, 4):
        top, r = divmod(k, 8)
        (a00,), (a10, a11), (a20, a21, a22), (a30, a31, a32, a33) = pivot
        u0, u1, u2, u3 = u = [sublane(blocks[top], r + j) for j in range(4)]
        det_a = a00 * a11 - a10 * a10
        inv_a = reciprocal(det_a)
        p00, p10, p11 = a11 * inv_a, a10 * inv_a, a00 * inv_a
        b00, b01 = a20 * p00 - a21 * p10, a21 * p11 - a20 * p10
        b10, b11 = a30 * p00 - a31 * p10, a31 * p11 - a30 * p10
        s00 = a22 - (b00 * a20 + b01 * a21)
        s10 = a32 - (b10 * a20 + b11 * a21)
        s11 = a33 - (b10 * a30 + b11 * a31)
        det_s = s00 * s11 - s10 * s10
        inv_s = reciprocal(det_s)
        q22, q32, q33 = s11 * inv_s, -s10 * inv_s, s00 * inv_s
        q20, q21 = -(q22 * b00 + q32 * b10), -(q22 * b01 + q32 * b11)
        q30, q31 = -(q32 * b00 + q33 * b10), -(q32 * b01 + q33 * b11)
        q00 = p00 - (b00 * q20 + b10 * q30)
        q10 = -p10 - (b01 * q20 + b11 * q30)
        q11 = p11 - (b01 * q21 + b11 * q31)
        inverse = [[q00, q10, q20, q30], [q10, q11, q21, q31], [q20, q21, q22, q32], [q30, q31, q32, q33]]

        def applied(values):
            return [(row[0] * values[0] + row[1] * values[1]) + (row[2] * values[2] + row[3] * values[3])
                    for row in inverse]

        if k + 4 < size:
            across = [lane(blocks[top], k + 4 + j) for j in range(4)]
            cross = [[sublane(across[j], r + i) for i in range(4)] for j in range(4)]
            after = across if r == 0 else [lane(blocks[top + 1], k + 4 + j) for j in range(4)]
            plain = corner(after, 4 - r)
            solved = [applied(column) for column in cross]
            pivot = [[plain[i][j] - ((cross[i][0] * solved[j][0] + cross[i][1] * solved[j][1])
                                     + (cross[i][2] * solved[j][2] + cross[i][3] * solved[j][3]))
                      for j in range(i + 1)] for i in range(4)]
        t = applied(u)
        for i in range(top, size // 8):
            if i == top and r:
                continue
            c = [lane(blocks[i], k + j) for j in range(4)]
            change = (c[0] * t[0] + c[1] * t[1]) + (c[2] * t[2] + c[3] * t[3])
            blocks[i] = blocks[i] - (jnp.where(place > 3, change, 0.0) if i == top else change)
        v0 = u0 * lax.rsqrt(a00)
        v1 = (a00 * u1 - a10 * u0) * lax.rsqrt(a00 * det_a)
        u2 = u2 - b00 * u0 - b01 * u1
        u3 = u3 - b10 * u0 - b11 * u1
        v2 = u2 * lax.rsqrt(s00)
        v3 = (s00 * u3 - s10 * u2) * lax.rsqrt(s00 * det_s)
        four = jnp.where(place % 4 == 0, v0, jnp.where(place % 4 == 1, v1, jnp.where(place % 4 == 2, v2, v3)))
        done[top] = jnp.where(place > 3, four, done[top]) if r else four
    return jnp.concatenate(done, axis=0)[:, size:]


def total(matrix):
    return jnp.sum(jnp.sum(matrix, axis=0, keepdims=True), axis=1, keepdims=True)


def trace(matrix):
    return total(matrix * unit(*matrix.shape))


def inverse_root(matrix):
    eye = unit(*matrix.shape)
    rest = matrix - eye

    def series():
        return eye - 0.5 * rest + 0.375 * dot(rest, rest)

    return lax.cond(jnp.sum(rest * rest) < 1e-4, series, lambda: inverse_factor(matrix))


def dense(moments, index, rows, data):
    n = NVEC
    eye = unit(n, n)
    pick = ((lax.broadcasted_iota(jnp.int32, (n, n), 0) == index)
            & (lax.broadcasted_iota(jnp.int32, (n, n), 1) == index)).astype(F32)

    def part(stacked, i):
        return stacked[i * n:(i + 1) * n]

    def below(*parts):
        return jnp.concatenate(parts, axis=0)

    def beside(*parts):
        return jnp.concatenate(parts, axis=1)

    base = inverse_factor(moments[0])
    right = dot(below(*moments[1:]), base, 1, 1)
    m1, m2, m3, m4, m5 = (dot(base, part(right, i)) for i in range(5))

    by1 = dot(below(m1, m2, m3, m4), m1)
    square, m21, m31, m41 = (part(by1, i) for i in range(4))
    tri = dot(m1, beside(square, m21, m31))
    gram_r = m2 - square
    image_r = m3 - m21 - m21.T + tri[:, :n]
    mixed_r = m3 - m21
    square_r = m4 - m31 - m31.T + tri[:, n:2 * n]
    cubic_r = m5 - m41 - m41.T + tri[:, 2 * n:]
    shift = 3.0 - total(m1 * pick)
    ridge = RIDGE_WEIGHT * (n + trace(gram_r)) / (2 * n)
    ridged = gram_r + ridge * eye
    factor = inverse_factor(ridged)
    inverse = dot(factor, factor, 0, 0)
    keep = 1.0 / (1.0 + ridge)
    step = below(
        beside(m1 * keep + shift * eye, gram_r * keep),
        beside(eye - ridge * inverse, dot(inverse, image_r) + shift * eye),
    )
    twice = dot(step, step)
    power = dot(twice, dot(twice, twice[:, :n]))
    top, bottom = power[:n], power[n:]
    weighted = dot(below(ridged, gram_r, image_r), bottom)
    norm = (1.0 + ridge) * dot(top, top, 0, 0) + dot(bottom, part(weighted, 0), 0, 0)
    factor = inverse_factor(norm)

    middle = m4 - m31
    images = dot(below(
        beside(m1, gram_r), beside(gram_r, image_r),
        beside(m2, mixed_r), beside(mixed_r.T, square_r),
        beside(m3, middle), beside(middle.T, cubic_r),
    ), power)
    whole = dot(power, beside(images[:2 * n], images[2 * n:4 * n], images[4 * n:], power), 0, 0)
    lower = dot(bottom, beside(part(images, 1), part(images, 3), part(weighted, 1), part(weighted, 2)), 0, 0)
    raw = [whole[:, i * n:(i + 1) * n] for i in range(4)] + [lower[:, i * n:(i + 1) * n] for i in range(4)]
    right = dot(below(*raw), factor, 1, 1)
    ritz, image2, image3, excess, p_image, p_image2, p_gram, p_ritz = (dot(factor, part(right, i)) for i in range(8))
    excess = ridge * excess

    shift = 3.0 - total(ritz * pick)
    by_ritz = dot(below(ritz, p_gram, excess, p_image, image2), ritz)
    squared, gram_pr, gram_cr = part(by_ritz, 0), p_image - part(by_ritz, 1), part(by_ritz, 2)
    tri = dot(ritz, squared), dot(ritz, gram_cr)
    gram_rr = image2 - squared - tri[1]
    image_cr = image2 - squared
    image_pr = p_image2 - part(by_ritz, 3)
    image_rr = image3 - part(by_ritz, 4) - part(by_ritz, 4).T + tri[0]
    ridge = RIDGE_WEIGHT * (n - trace(excess) + trace(p_gram) + trace(gram_rr)) / (3 * n)
    g_cc = eye - excess + ridge * eye
    g_pp = p_gram + ridge * eye
    g_rr = gram_rr + ridge * eye
    image_gram = below(
        beside(ritz, p_image.T, image_cr), beside(p_image, p_ritz, image_pr), beside(image_cr.T, image_pr.T, image_rr),
    )
    v0 = inverse_root(g_cc)
    side = dot(below(p_gram, gram_cr.T), v0, 1, 1)
    l10, l20 = side[:n], side[n:]
    outer = dot(side, side, 1, 1)
    v1 = inverse_factor(g_pp - outer[:n, :n])
    l21 = dot(gram_pr.T - outer[n:, :n], v1, 1, 1)
    v2 = inverse_factor(g_rr - outer[n:, n:] - dot(l21, l21, 1, 1))
    zero = jnp.zeros((n, n), F32)
    row0 = beside(v0, zero, zero)
    row1 = dot(v1, beside(-dot(l10, v0), eye, zero))
    row2 = beside(zero, zero, eye) - dot(l20, row0) - dot(l21, row1)
    known = below(row0, row1)
    solved = dot(known, dot(known, image_gram), 0, 0)
    row2 = dot(v2, beside(row2, dot(row2, image_gram)))
    step = solved + dot(row2[:, :3 * n], row2[:, 3 * n:], 0, 0) + shift * unit(3 * n, 3 * n)
    twice = dot(step, step)
    power2 = dot(twice, dot(twice, twice[:, :n]))
    gram = below(
        beside(g_cc, p_gram, gram_cr), beside(p_gram, g_pp, gram_pr), beside(gram_cr.T, gram_pr.T, g_rr),
    )
    norm = dot(power2, dot(gram, power2), 0, 0)

    back = dot(m1, bottom)
    of_top, of_bottom, of_back = (
        dot(factor, dot(part, base, 0, 0)) for part in (top - back, bottom, back))
    vectors = below(
        beside(of_top, of_bottom, zero),
        beside(-of_back, of_bottom, zero),
        beside(-dot(ritz, of_top), of_top - dot(ritz, of_bottom), of_bottom),
    )
    mixed = dot(power2, vectors, 0, 0)
    return dot(dot(inverse_factor(norm), mixed), data) * math.sqrt(rows)


def dense_body(rows, core, index, mine, theirs, scaled, out):
    packed = jnp.concatenate([
        chosen(core, theirs[...], mine[...]), chosen(core, mine[...], theirs[...])], axis=0)
    index = jnp.broadcast_to(index[0:1, :NVEC], (NVEC, NVEC)).astype(jnp.int32)
    out[...] = dense(unpacked(packed, NVEC), index, rows, scaled[...])


def between_blocks(shard, sign):
    blocks, cores = lax.axis_size("blk"), lax.axis_size("narrow")
    pairs = [(i * cores + j, (i + sign * (1 + j)) % blocks * cores + j) for i in range(blocks) for j in range(cores)]
    return lax.ppermute(shard, ("blk", "narrow"), pairs)


def between_cores(shard):
    return lax.ppermute(shard, "narrow", [(0, 1), (1, 0)])


def total_over_blocks(values):
    blocks = lax.axis_size("blk")
    span = 1
    while blocks % (2 * span) == 0:
        values = values + lax.ppermute(values, "blk", [(i, i ^ span) for i in range(blocks)])
        span *= 2
    if span < blocks:
        groups = [list(range(i, blocks, span)) for i in range(span)]
        values = lax.psum(values, "blk", axis_index_groups=groups)
    return values


def shards(embeddings, pair_mask, shift_index, start_seed):
    size = embeddings.shape[0]
    blocks = lax.axis_size("blk")
    where = lax.axis_index("blk")
    core = lax.axis_index("narrow")
    other_emb = between_cores(embeddings)
    relaying = blocks % 2 == 0
    back1 = [(i, (i - 1) % blocks) for i in range(blocks) if i % 2 or not relaying]
    back2 = [(i, (i - 2) % blocks) for i in range(blocks)]
    orders = [
        [(2 * i + j, 2 * k) for i, k in back1] + [(2 * i + 1 - j, 2 * k + 1) for i, k in back2] for j in range(2)]
    if relaying:
        orders[0] += [(2 * i, 2 * i + 2) for i in range(0, blocks, 2)]

    def between_shards(shard, pairs):
        return lax.ppermute(shard, ("blk", "narrow"), pairs)

    first, second = between_shards(embeddings, orders[0]), between_shards(embeddings, orders[1])
    seed = start_seed.astype(F32).T / 1000.0
    seeds = jnp.concatenate([seed, between_cores(seed)], axis=0)
    keep = spread(lax.dynamic_slice(pair_mask, (where, core), (1, 1)))
    relays = spread((1 - core) * (where % 2) * int(relaying))
    pair_shape, row_shape = ((2 * NVEC, size), F32), ((16, size), F32)
    h0, l0, sums, row_sq, own_copy, token = make_tile(
        own_body, [embeddings, other_emb], size,
        (((2 * size, 128), F32), (embeddings.shape, BF16), ((8, 128), F32)))
    first, seeds, keep, relays, token = lax.optimization_barrier((first, seeds, keep, relays, token))
    relayed = [first, own_copy]
    if relaying:
        relayed[0] = between_shards(first, [(2 * i, (i - 2) % blocks * 2) for i in range(1, blocks, 2)])
        forward, second = lax.optimization_barrier((first, second))
        relayed[1] = between_shards(forward, [(2 * i + 1, 2 * i + 2) for i in range(0, blocks, 2)])
    tile_args = [keep, relays, token, own_copy, other_emb, row_sq]
    h1, l1, sums, cols1 = make_tile(
        far_body, [*tile_args, first, relayed[0], sums], size, (((8, size), F32),))
    h2, l2, sums, cols2 = make_tile(
        far_body, [*tile_args, second, relayed[1], sums], size, (((8, size), F32),))
    cols = jnp.concatenate([cols1, cols2], axis=0)
    sums = sums + between_blocks(cols, 1)

    small = dict(flops=10**6, nbytes=10**5)
    middle = dict(flops=10**9, nbytes=10**6)
    message_shape = ((2 * NVEC + 16, size), jnp.int16)
    degree, vectors, message = call(
        degree_body, [row_shape, pair_shape, message_shape], [sums, between_cores(sums), seeds], **small)
    far = [h1, l1, h2, l2]
    history = [vectors]
    for _ in range(2):
        near = between_blocks(message, -1)
        (ahead,) = call(ahead_body, [message_shape], [vectors, *far], **middle)
        behind = between_blocks(ahead, 1)
        (product,) = call(own_product_body, [pair_shape], [vectors, h0, l0], **middle)
        (total,) = call(near_product_body, [pair_shape], [product, near, *far], **middle)
        (total,) = call(add_body, [pair_shape], [total, behind], **small)
        vectors, message = call(
            combine_body, [pair_shape, message_shape], [total, between_cores(total), degree], **small)
        history.append(vectors)
    near = between_blocks(message, -1)
    low, scaled = call(
        low_body, [((5 * NVEC, NVEC), F32), ((3 * NVEC, size), F32)], [degree] + history, **middle)
    (product,) = call(own_product_body, [pair_shape], [vectors, h0, l0], **middle)
    packed_shape = ((3 * NVEC // 4 + 8, 2 * NVEC), F32)
    mine, theirs = call(
        moment_body, [packed_shape] * 2, [spread(core), low, vectors, product, near, *far], **middle)
    mine = total_over_blocks(mine + between_cores(theirs))
    rows = size * blocks * lax.axis_size("narrow")
    (out,) = call(
        lambda *refs: dense_body(rows, *refs), [((NVEC, size), F32)],
        [spread(core), spread(shift_index), mine, between_cores(mine), scaled], flops=2 * 10**10, nbytes=10**6,
    )
    return out.T


def solution(mesh):
    return jax.shard_map(
        shards,
        mesh=mesh,
        in_specs=(
            P(("groups", "blk", "narrow"), None),
            P("groups", None),
            P("groups"),
            P(("groups", "blk", "narrow"), None),
        ),
        out_specs=P(("groups", "blk", "narrow"), None),
        check_vma=False,
    )
```
